32 devices in a mesh: wide: 8 (over y, x, core), narrow: 4 (over z).
Axes of the slice: x: 2, y: 2, z: 4, core: 2. Of those that a mesh axis runs over, the one named last changes fastest.
Arguments:
- tokens: bfloat16 [16, 1024, 768], P('wide', 'narrow'), may hold values from -6 to 6
- positions: int32 [16, 1024], P('wide', 'narrow'), may hold values from 0 to 107, as said below
- segments: int32 [16, 1024], P('wide'), may hold values from 0 to 47, as said below
- position_table: bfloat16 [768, 108], P(('wide', 'narrow')), may hold values from -3 to 3
- input_weight: bfloat16 [768, 2304], P(('wide', 'narrow')), may hold values from -0.21875 to 0.21875
- query_bias: bfloat16 [768], P(('wide', 'narrow')), may hold values from -1.796875 to 1.796875
- value_bias: bfloat16 [768], P(('wide', 'narrow')), may hold values from -3 to 3
- output_weight: bfloat16 [768, 768], P(('wide', 'narrow')), may hold values from -1.75 to 1.75
- output_bias: bfloat16 [768], P(('wide', 'narrow')), may hold values from -1.796875 to 1.796875
- first_gain: bfloat16 [768], P(('wide', 'narrow')), may hold values from 0.5 to 1.5
- first_shift: bfloat16 [768], P(('wide', 'narrow')), may hold values from -1.796875 to 1.796875
- up_weight: bfloat16 [768, 3072], P(('wide', 'narrow')), may hold values from -0.21875 to 0.21875
- up_bias: bfloat16 [3072], P(('wide', 'narrow')), may hold values from -3 to 3
- down_weight: bfloat16 [3072, 768], P(('wide', 'narrow')), may hold values from -0.109375 to 0.109375
- down_bias: bfloat16 [768], P(('wide', 'narrow')), may hold values from -1.796875 to 1.796875
- second_gain: bfloat16 [768], P(('wide', 'narrow')), may hold values from 0.5 to 1.5
- second_shift: bfloat16 [768], P(('wide', 'narrow')), may hold values from -1.796875 to 1.796875
- cotangent: bfloat16 [16, 1024, 768], P('wide', 'narrow'), may hold values from -6 to 6
Outputs:
- outputs: bfloat16 [16, 1024, 768], P('wide', 'narrow')
- grad_tokens: bfloat16 [16, 1024, 768], P('wide', 'narrow')
- grad_position_table: float32 [768, 108], P(('wide', 'narrow'))
- grad_input_weight: float32 [768, 2304], P(('wide', 'narrow'))
- grad_query_bias: float32 [768], P(('wide', 'narrow'))
- grad_value_bias: float32 [768], P(('wide', 'narrow'))
- grad_output_weight: float32 [768, 768], P(('wide', 'narrow'))
- grad_output_bias: float32 [768], P(('wide', 'narrow'))
- grad_first_gain: float32 [768], P(('wide', 'narrow'))
- grad_first_shift: float32 [768], P(('wide', 'narrow'))
- grad_up_weight: float32 [768, 3072], P(('wide', 'narrow'))
- grad_up_bias: float32 [3072], P(('wide', 'narrow'))
- grad_down_weight: float32 [3072, 768], P(('wide', 'narrow'))
- grad_down_bias: float32 [768], P(('wide', 'narrow'))
- grad_second_gain: float32 [768], P(('wide', 'narrow'))
- grad_second_shift: float32 [768], P(('wide', 'narrow'))
The draws below stay inside these ranges and needn't reach their ends.
Inputs may be any that keep to these rules, and one draw needn't show every extreme that they name: `positions`: within each sequence, timesteps of 36, 72 or 108 tokens follow one another; a sequence may begin with the last tokens of a timestep of 36, and the timestep after that has 108 tokens; a token's entry is its index within its timestep. `segments`: sequence s holds episodes 3 s, 3 s + 1 and 3 s + 2 in this order, none empty; the first ends within the sequence's first 256 tokens and the last begins within its last 255.
All inputs are finite; a program needn't handle non-finite values.
Results may differ from the reference program's by a relative error of at most 0.012.
Values may be sent and summed in bfloat16 or wider, within the bound.
No kernel may reach another device: no remote copies, remote signals or barrier semaphores. Data moves between devices by JAX's collectives and lax.ppermute only.
A program may use at most 192 MiB of HBM per device.

```python
import jax
import jax.numpy as jnp
from jax import lax

D = 768
HEADS = 12
HEAD_DIM = 64
FF = 3072
PATCHES = 108
SEQ = 1024
LOCAL = 256
SEQS = 16
TOKENS = 16384


def draw_positions(key, part):
    key = jax.random.fold_in(key, 23)
    lead_key, count_key = jax.random.split(key)
    short_step = PATCHES // 3
    timesteps = SEQ // short_step + 3
    lead_most = min(SEQ - PATCHES, short_step)
    lead = jax.random.randint(lead_key, (SEQS, 1), 0, lead_most + 1).astype(jnp.int32)
    counts = short_step * jax.random.randint(count_key, (SEQS, timesteps), 1, 4)
    counts = counts.astype(jnp.int32)
    counts = jnp.concatenate([lead, jnp.full((SEQS, 1), PATCHES, jnp.int32), counts[:, 2:]], axis=1).astype(jnp.int32)
    step_end = jnp.cumsum(counts, axis=1).astype(jnp.int32)
    step_begin = step_end - counts
    places = jnp.arange(SEQ, dtype=jnp.int32)
    step_index = jnp.sum((step_end[:, None, :] <= places[None, :, None]).astype(jnp.int32), axis=2).astype(jnp.int32)
    step_start = jnp.take_along_axis(step_begin, step_index, axis=1)
    within = places[None, :] - step_start
    offset = jnp.where(step_index == 0, short_step - lead, 0).astype(jnp.int32)
    return (within + offset).astype(jnp.int32)


def draw_segments(key, part):
    key = jax.random.fold_in(key, 11)
    first_key, second_key = jax.random.split(key)
    first_cut = jax.random.randint(first_key, (SEQS, 1), 1, LOCAL)
    second_cut = jax.random.randint(second_key, (SEQS, 1), SEQ - LOCAL + 1, SEQ)
    places = jnp.arange(SEQ, dtype=jnp.int32)[None, :]
    within = (places >= first_cut).astype(jnp.int32) + (places >= second_cut).astype(jnp.int32)
    offsets = 3 * jnp.arange(SEQS, dtype=jnp.int32)[:, None]
    return (within + offsets).astype(jnp.int32)


def block_scale(own_key, extent, cuts, low, top_value):
    level, own = 1.0, jax.random.fold_in(own_key, 6)
    for position, shards_of in cuts:
        heights = jnp.exp(jax.random.uniform(jax.random.fold_in(own, position), (shards_of,), jnp.float32, low / len(cuts), top_value / len(cuts)))
        level = level * jnp.repeat(heights, extent[position] // shards_of).reshape([-1 if axis == position else 1 for axis in range(len(extent))])
    return level


def centred(rng, dims, spread, bound, cuts=(), held_as=jnp.bfloat16):
    values = spread * jax.random.normal(rng, dims, jnp.float32)
    if cuts:
        values = values * block_scale(rng, dims, cuts, -0.22, 0.18)
    return jnp.clip(values, -bound, bound).astype(held_as)


def setup_inputs(seed: int = 0) -> dict:
    arg_keys = jax.random.split(jax.random.key(seed), 19)
    tokens = centred(arg_keys[0], (SEQS, SEQ, D), 1.0, 6.0, ((0, 8), (1, 4)))
    positions = draw_positions(jax.random.fold_in(arg_keys[18], 71), 0)
    segments = draw_segments(jax.random.fold_in(arg_keys[18], 71), 0)
    position_table = centred(arg_keys[3], (D, PATCHES), 0.5, 3.0, ((0, 32),))
    input_weight = centred(arg_keys[4], (D, 3 * D), D ** -0.5, 0.21875, ((0, 32),))
    query_bias = centred(arg_keys[5], (D,), 0.3, 1.796875, ((0, 32),))
    value_bias = centred(arg_keys[6], (D,), 0.5, 3.0, ((0, 32),))
    output_weight = centred(arg_keys[7], (D, D), (D // 64) ** -0.5, 1.75, ((0, 32),))
    output_bias = centred(arg_keys[8], (D,), 0.3, 1.796875, ((0, 32),))
    first_gain = jnp.clip(1.0 + 0.1 * jax.random.normal(arg_keys[9], (D,), jnp.float32), 0.5, 1.5).astype(jnp.bfloat16)
    first_shift = centred(arg_keys[10], (D,), 0.3, 1.796875, ((0, 32),))
    up_weight = centred(arg_keys[11], (D, FF), D ** -0.5, 0.21875, ((0, 32),))
    up_bias = centred(arg_keys[12], (FF,), 0.5, 3.0, ((0, 32),))
    down_weight = centred(arg_keys[13], (FF, D), FF ** -0.5, 0.109375, ((0, 32),))
    down_bias = centred(arg_keys[14], (D,), 0.3, 1.796875, ((0, 32),))
    second_gain = jnp.clip(1.0 + 0.1 * jax.random.normal(arg_keys[15], (D,), jnp.float32), 0.5, 1.5).astype(jnp.bfloat16)
    second_shift = centred(arg_keys[16], (D,), 0.3, 1.796875, ((0, 32),))
    cotangent = centred(arg_keys[17], (SEQS, SEQ, D), 1.0, 6.0, ((0, 8), (1, 4)))
    return dict(tokens=tokens, positions=positions, segments=segments, position_table=position_table, input_weight=input_weight, query_bias=query_bias, value_bias=value_bias, output_weight=output_weight, output_bias=output_bias, first_gain=first_gain, first_shift=first_shift, up_weight=up_weight, up_bias=up_bias, down_weight=down_weight, down_bias=down_bias, second_gain=second_gain, second_shift=second_shift, cotangent=cotangent)


epsilon = 1e-05
masked_score = -1e+30
highest = lax.Precision.HIGHEST

@jax.custom_vjp
def low(v):
    return lax.optimization_barrier(v.astype(jnp.bfloat16)).astype(jnp.float32)

@jax.custom_vjp
def low_back(v):
    return v

def low_keep(v):
    return (low(v), None)

def low_pass(kept, grad):
    return (grad,)

def back_keep(v):
    return (v, None)

def back_low(kept, grad):
    return (low(grad),)
low.defvjp(low_keep, low_pass)
low_back.defvjp(back_keep, back_low)

def layer_norm(values, gain_row, shift_row):
    average = lax.optimization_barrier(jnp.mean(values, axis=-1, keepdims=True))
    centered = values - average
    variance = lax.optimization_barrier(jnp.mean(centered * centered, axis=-1, keepdims=True))
    return centered * lax.rsqrt(variance + epsilon) * gain_row + shift_row

def matmul(left, right):
    return jnp.dot(left, right, precision=highest, preferred_element_type=jnp.float32)

def sequence_attention(query, key_rows, value_rows, segment_ids):
    length = query.shape[0]
    block_rows = min(2048, length)
    key_heads = key_rows.reshape(length, HEADS, HEAD_DIM)
    value_heads = value_rows.reshape(length, HEADS, HEAD_DIM)
    key_places = jnp.arange(length, dtype=jnp.int32)

    @jax.checkpoint
    def one_block(pieces):
        query_block, block_start = pieces
        places = block_start + jnp.arange(block_rows, dtype=jnp.int32)
        segment_rows = lax.dynamic_slice_in_dim(segment_ids, block_start, block_rows)
        allowed = (key_places[None, :] <= places[:, None]) & (segment_ids[None, :] == segment_rows[:, None])
        query_heads = query_block.reshape(block_rows, HEADS, HEAD_DIM)
        scores = jnp.einsum('qhd,khd->hqk', query_heads, key_heads, precision=highest) * HEAD_DIM ** (-0.5)
        scores = jnp.where(allowed[None], low_back(scores), masked_score)
        probabilities = low(jax.nn.softmax(scores, axis=-1))
        mixed = jnp.einsum('hqk,khd->qhd', probabilities, value_heads, precision=highest)
        return mixed.reshape(block_rows, HEADS * HEAD_DIM)
    starts = (jnp.arange(length // block_rows, dtype=jnp.int32) * block_rows).astype(jnp.int32)
    result = lax.map(one_block, (query.reshape(length // block_rows, block_rows, -1), starts))
    return result.reshape(length, -1)

@jax.checkpoint
def sequence_step(pieces):
    return sequence_attention(pieces[0], pieces[1], pieces[2], pieces[3])

def forward(tokens, position_table, input_weight, query_bias, value_bias, output_weight, output_bias, first_gain, first_shift, up_weight, up_bias, down_weight, down_bias, second_gain, second_shift, positions, segments):
    start = tokens + position_table[:, positions].T
    normed_one = low(layer_norm(start, first_gain, first_shift))
    projected = matmul(normed_one, input_weight)
    query = low_back(low(projected[:, :D] + query_bias))
    keys = low_back(low(projected[:, D:2 * D]))
    values = low_back(low(projected[:, 2 * D:] + value_bias))
    attended = lax.map(sequence_step, (query.reshape(SEQS, SEQ, D), keys.reshape(SEQS, SEQ, D), values.reshape(SEQS, SEQ, D), segments.reshape(SEQS, SEQ)))
    attended = low_back(low(attended.reshape(TOKENS, D)))
    middle = start + low_back(matmul(attended, output_weight) + output_bias)
    normed_two = low(layer_norm(middle, second_gain, second_shift))
    hidden = low_back(matmul(normed_two, up_weight) + up_bias)
    activated = low(jax.nn.gelu(hidden, approximate=True))
    return middle + low_back(matmul(activated, down_weight) + down_bias)

def reference(tokens, positions, segments, position_table, input_weight, query_bias, value_bias, output_weight, output_bias, first_gain, first_shift, up_weight, up_bias, down_weight, down_bias, second_gain, second_shift, cotangent):
    flat_tokens = tokens.reshape(TOKENS, D)
    floats = tuple((argument.astype(jnp.float32) for argument in (flat_tokens, position_table, input_weight, query_bias, value_bias, output_weight, output_bias, first_gain, first_shift, up_weight, up_bias, down_weight, down_bias, second_gain, second_shift)))
    flat_positions = positions.reshape(TOKENS).astype(jnp.int32)

    def closed(*params):
        return forward(*params, flat_positions, segments)
    result, pullback = jax.vjp(closed, *floats)
    grads = pullback(cotangent.reshape(TOKENS, D).astype(jnp.float32))
    return (result.reshape(SEQS, SEQ, D).astype(jnp.bfloat16), grads[0].reshape(SEQS, SEQ, D).astype(jnp.bfloat16), grads[1], grads[2], grads[3], grads[4], grads[5], grads[6], grads[7], grads[8], grads[9], grads[10], grads[11], grads[12], grads[13], grads[14])
```

```python
import jax
import jax.numpy as jnp
from jax import lax
from jax.sharding import PartitionSpec as P

HEADS = 12
PLACES = 4
epsilon = 1e-05
masked_score = -1e30

f32 = jnp.float32
bf16 = jnp.bfloat16


def layer_norm(values, gain_row, shift_row):
    average = jnp.mean(values, axis=-1, keepdims=True)
    centered = values - average
    variance = jnp.mean(centered * centered, axis=-1, keepdims=True)
    return centered * lax.rsqrt(variance + epsilon) * gain_row + shift_row


def gelu_tanh(values):
    return jax.nn.gelu(values, approximate=True)


def product(left, right):
    return jnp.dot(left, right, preferred_element_type=f32)


def product_left(left, right):
    return lax.dot_general(left, right, (((0,), (0,)), ((), ())), preferred_element_type=f32)


def product_right(left, right):
    return lax.dot_general(left, right, (((1,), (1,)), ((), ())), preferred_element_type=f32)


def swap(values, axis, bits):
    size = lax.axis_size(axis)
    return lax.ppermute(values, axis, [(i, i ^ bits) for i in range(size)])


def wide_bits():
    size, bits, bit = lax.axis_size("wide"), [], 1
    while bit < size:
        bits.append(bit)
        bit *= 2
    return bits


def spread_perm(turn):
    pairs = []
    for w in range(lax.axis_size("wide")):
        for z in range(PLACES):
            core = (0, 1, 1, 0)[z]
            which = turn ^ (z // 2)
            there = (w - w % 2 + core, 2 * (w % 2) + which)
            pairs.append((w * PLACES + z, there[0] * PLACES + there[1]))
    return pairs


def spread(values, place):
    late = place // 2
    got = [
        lax.ppermute(
            lax.dynamic_index_in_dim(values, turn ^ late, 0, keepdims=False),
            ("wide", "narrow"),
            spread_perm(turn),
        )
        for turn in range(2)
    ]
    odd = (place % 2) == 1
    return jnp.where(odd, got[1], got[0]), jnp.where(odd, got[0], got[1])


def unspread(low, high, place):
    odd = (place % 2) == 1
    sent = (jnp.where(odd, high, low), jnp.where(odd, low, high))
    got = [
        lax.ppermute(sent[turn], ("wide", "narrow"), [(b, a) for a, b in spread_perm(turn)])
        for turn in range(2)
    ]
    late = place >= 2
    return jnp.stack([jnp.where(late, got[1], got[0]), jnp.where(late, got[0], got[1])])


def doubling(piece, bits):
    held = {0: piece}
    for bit in bits:
        more = {}
        for index, part in held.items():
            more[index ^ bit] = swap(part, "wide", bit)
        held.update(more)
    return held


def gather(shard, cut, wide, place):
    rows, columns = shard.shape
    pieces = jnp.stack([shard] + [swap(shard, "narrow", k) for k in range(1, PLACES)])
    order = jnp.arange(PLACES) ^ place
    column = jnp.take(pieces, order, axis=0).reshape(PLACES * rows, columns)
    bits = wide_bits()
    halves = []
    for part, way in ((column[:, :cut], bits[1:]), (column[:, cut:], bits[:0:-1])):
        held = doubling(part, list(way))
        held = jnp.stack([held[2 * i] for i in range(len(held))])
        both = jnp.stack([held, swap(held, "wide", 1)], axis=1)
        halves.append(both.reshape((-1,) + part.shape))
    whole = jnp.concatenate(halves, axis=2)
    ranks = jnp.arange(whole.shape[0]) ^ wide
    return jnp.take(whole, ranks, axis=0).reshape(-1, columns)


def scatter(values, cut, wide, place, kind=bf16):
    size = lax.axis_size("wide")
    rows, columns = values.shape
    blocks = values.astype(kind).reshape(size, rows // size, columns)
    blocks = jnp.take(blocks, jnp.arange(size) ^ wide, axis=0)
    blocks = blocks.reshape(size // 2, 2, rows // size, columns)
    kept = blocks[:, 0].astype(f32) + swap(blocks[:, 1], "wide", 1).astype(f32)
    kept = kept.astype(kind)
    bits = wide_bits()
    halves = []
    for part, way in ((kept[:, :, :cut], bits[:0:-1]), (kept[:, :, cut:], bits[1:])):
        held = {2 * i: part[i] for i in range(size // 2)}
        for bit in way:
            keep = {}
            for index, piece in held.items():
                if not index & bit:
                    there = swap(held[index ^ bit], "wide", bit)
                    keep[index] = (piece.astype(f32) + there.astype(f32)).astype(kind)
            held = keep
        halves.append(held[0])
    column = jnp.concatenate(halves, axis=1)
    pieces = column.reshape(PLACES, -1, columns)
    pieces = jnp.take(pieces, jnp.arange(PLACES) ^ place, axis=0)
    total = pieces[0].astype(f32)
    for k in range(1, PLACES):
        total = total + swap(pieces[k], "narrow", k).astype(f32)
    return total


def local(
    tokens,
    positions,
    segments,
    position_table,
    input_weight,
    query_bias,
    value_bias,
    output_weight,
    output_bias,
    first_gain,
    first_shift,
    up_weight,
    up_bias,
    down_weight,
    down_bias,
    second_gain,
    second_shift,
    cotangent,
):
    seq_count, local_rows, width = tokens.shape
    hidden_width = up_weight.shape[1]
    patches = position_table.shape[1]
    full = segments.shape[1]
    head_width = width // HEADS
    scale = head_width ** (-0.5)
    wide = lax.axis_index("wide")
    place = lax.axis_index("narrow")
    core = wide % 2
    first_core = core == 0
    rows = 2 * local_rows

    vectors = (
        query_bias,
        value_bias,
        output_bias,
        first_gain,
        first_shift,
        down_bias,
        second_gain,
        second_shift,
    )
    spare = up_bias.shape[0] // query_bias.shape[0]
    small = jnp.concatenate(
        [position_table] + [v[:, None] for v in vectors] + [up_bias.reshape(-1, spare)], axis=1
    )
    small = jnp.pad(small, ((0, 0), (0, 128 - small.shape[1])))

    low, high = spread(tokens, place)
    mine = jnp.stack([low, high])
    others = swap(mine, "wide", 1)
    pos_low, pos_high = spread(positions, place)
    pos_mine = jnp.stack([pos_low, pos_high])
    pos_others = swap(pos_mine, "wide", 1)
    far = swap(segments, "wide", 1)
    segment = jnp.where((place // 2) == core, segments, far)
    segment = lax.dynamic_index_in_dim(segment, place % 2, 0, keepdims=False)

    def in_order(own, other):
        return jnp.where(
            first_core,
            jnp.concatenate([own[0], other[0], other[1], own[1]]),
            jnp.concatenate([other[0], own[0], own[1], other[1]]),
        )

    def of_core(values):
        blocks = values.reshape((4, local_rows) + values.shape[1:])
        return jnp.where(
            first_core,
            jnp.concatenate([blocks[0], blocks[3]]),
            jnp.concatenate([blocks[1], blocks[2]]),
        )

    def of_other(values):
        blocks = values.reshape((4, local_rows) + values.shape[1:])
        return jnp.where(
            first_core,
            jnp.concatenate([blocks[1], blocks[2]]),
            jnp.concatenate([blocks[0], blocks[3]]),
        )

    cot_low, cot_high = spread(cotangent, place)
    cotangent_rows = jnp.concatenate([cot_low, cot_high])

    in_full = gather(jnp.concatenate([small, input_weight], axis=1), 1280, wide, place)
    small_full, in_full = in_full[:, :128], in_full[:, 128:]
    out_up = gather(
        jnp.concatenate([output_weight, up_weight], axis=1), (width + hidden_width) // 2, wide, place
    )
    out_full, up_full = out_up[:, :width], out_up[:, width:]
    down_full = gather(down_weight, width // 2, wide, place)

    vector_full = small_full[:, patches:].astype(f32)
    (qb, vb, ob, g1, s1, db, g2, s2) = (vector_full[:, i] for i in range(8))
    ub = vector_full[:, 8 : 8 + spare].reshape(hidden_width)
    table_full = small_full[:, :patches]

    tokens_all = in_order(mine, others)
    pos_all = in_order(pos_mine, pos_others)
    one_hot_all = (pos_all[:, None] == jnp.arange(patches, dtype=jnp.int32)[None, :]).astype(bf16)
    start_all = tokens_all.astype(f32) + product_right(one_hot_all, table_full)
    normed_all = layer_norm(start_all, g1, s1).astype(bf16)
    start = of_core(start_all)
    one_hot = of_core(one_hot_all)
    normed_one = of_core(normed_all)
    query = (product(normed_one, in_full[:, :width]) + qb).astype(bf16)
    projected = product(normed_all, in_full[:, width:])
    keys = projected[:, :width].astype(bf16)
    values = (projected[:, width:] + vb).astype(bf16)

    places = of_core(jnp.arange(full, dtype=jnp.int32))
    allowed = (jnp.arange(full)[None, :] <= places[:, None]) & (
        segment[None, :] == of_core(segment)[:, None]
    )
    query_heads = query.reshape(rows, HEADS, head_width)
    key_heads = keys.reshape(full, HEADS, head_width)
    value_heads = values.reshape(full, HEADS, head_width)
    scores = jnp.einsum("qhd,khd->hqk", query_heads, key_heads, preferred_element_type=f32) * scale
    scores = jnp.where(allowed[None], scores, masked_score)
    probabilities = jax.nn.softmax(scores, axis=-1)
    probs_low = probabilities.astype(bf16)
    attended = jnp.einsum("hqk,khd->qhd", probs_low, value_heads, preferred_element_type=f32)
    attended_low = attended.reshape(rows, width).astype(bf16)

    middle = start + product(attended_low, out_full) + ob
    normed_float_two, norm_two_pull = jax.vjp(layer_norm, middle, g2, s2)
    normed_two = normed_float_two.astype(bf16)
    hidden = product(normed_two, up_full) + ub
    activated, gelu_pull = jax.vjp(gelu_tanh, hidden)
    activated_low = activated.astype(bf16)
    outputs = (middle + product(activated_low, down_full) + db).astype(bf16)
    outputs_back = unspread(outputs[:local_rows], outputs[local_rows:], place)

    grad_outputs = cotangent_rows.astype(f32)
    grad_down = product_left(activated_low, cotangent_rows)
    grad_down_bias = jnp.sum(grad_outputs, axis=0)
    grad_hidden = gelu_pull(product_right(cotangent_rows, down_full))[0].astype(bf16)
    grad_up = product_left(normed_two, grad_hidden)
    grad_up_bias = jnp.sum(grad_hidden.astype(f32), axis=0)
    grad_middle_norm, grad_gain_two, grad_shift_two = norm_two_pull(
        product_right(grad_hidden, up_full)
    )
    grad_middle = grad_outputs + grad_middle_norm
    grad_branch = grad_middle.astype(bf16)
    grad_output = product_left(attended_low, grad_branch)
    grad_output_bias = jnp.sum(grad_branch.astype(f32), axis=0)
    grad_attended = product_right(grad_branch, out_full).astype(bf16)
    down_share = scatter(grad_down, width // 2, wide, place)
    out_up_share = scatter(
        jnp.concatenate([grad_output, grad_up], axis=1), (width + hidden_width) // 2, wide, place
    )

    grad_heads = grad_attended.reshape(rows, HEADS, head_width)
    grad_probs = jnp.einsum("qhd,khd->hqk", grad_heads, value_heads, preferred_element_type=f32)
    inner = jnp.sum(probabilities * grad_probs, axis=-1, keepdims=True)
    grad_scores = (probabilities * (grad_probs - inner)).astype(bf16)
    grad_query = (
        jnp.einsum("hqk,khd->qhd", grad_scores, key_heads, preferred_element_type=f32) * scale
    )
    key_sums = (
        jnp.einsum("hqk,qhd->khd", grad_scores, query_heads, preferred_element_type=f32) * scale
    )
    value_sums = jnp.einsum("hqk,qhd->khd", probs_low, grad_heads, preferred_element_type=f32)
    sums = jnp.concatenate(
        [key_sums.reshape(full, width), value_sums.reshape(full, width)], axis=1
    )
    got = swap(of_other(sums).astype(bf16), "wide", 1)
    grad_key_value = (of_core(sums) + got.astype(f32)).astype(bf16)
    grad_query_low = grad_query.reshape(rows, width).astype(bf16)
    grad_projected = jnp.concatenate([grad_query_low, grad_key_value], axis=1)
    grad_input = product_left(normed_one, grad_projected)
    grad_bias = jnp.sum(grad_projected.astype(f32), axis=0)
    _, norm_one_pull = jax.vjp(layer_norm, start, g1, s1)
    grad_start_norm, grad_gain_one, grad_shift_one = norm_one_pull(
        product_right(grad_projected, in_full)
    )
    grad_start = grad_middle + grad_start_norm
    grad_low = grad_start.astype(bf16)
    grad_tokens = unspread(grad_low[:local_rows], grad_low[local_rows:], place)
    grad_table = product_left(grad_low, one_hot)

    in_share = scatter(grad_input, 1152, wide, place)
    small_grads = jnp.concatenate(
        [grad_table]
        + [
            v[:, None]
            for v in (
                grad_bias[:width],
                grad_bias[2 * width :],
                grad_output_bias,
                grad_gain_one,
                grad_shift_one,
                grad_down_bias,
                grad_gain_two,
                grad_shift_two,
            )
        ]
        + [grad_up_bias.reshape(width, spare)],
        axis=1,
    )
    small_share = scatter(small_grads, 64, wide, place, f32)
    tail = [small_share[:, patches + i] for i in range(8)]
    return (
        outputs_back,
        grad_tokens,
        small_share[:, :patches],
        in_share,
        tail[0],
        tail[1],
        out_up_share[:, :width],
        tail[2],
        tail[3],
        tail[4],
        out_up_share[:, width:],
        small_share[:, patches + 8 : patches + 8 + spare].reshape(-1),
        down_share,
        tail[5],
        tail[6],
        tail[7],
    )


def solution(mesh):
    both = ("wide", "narrow")
    matrix = P(both, None)
    vector = P(both)
    block = P("wide", "narrow", None)
    return jax.shard_map(
        local,
        mesh=mesh,
        in_specs=(
            block,
            P("wide", "narrow"),
            P("wide", None),
            matrix,
            matrix,
            vector,
            vector,
            matrix,
            vector,
            vector,
            vector,
            matrix,
            vector,
            matrix,
            vector,
            vector,
            vector,
            block,
        ),
        out_specs=(
            block,
            block,
            matrix,
            matrix,
            vector,
            vector,
            matrix,
            vector,
            vector,
            vector,
            matrix,
            vector,
            matrix,
            vector,
            vector,
            vector,
        ),
        check_vma=False,
    )
```

```python
import functools

import jax
import jax.numpy as jnp
from jax import lax
from jax.experimental import pallas as pl
from jax.experimental.pallas import tpu as pltpu
from jax.sharding import PartitionSpec as P

HEADS = 12
PLACES = 4
epsilon = 1e-05
masked_score = -1e30

f32 = jnp.float32
bf16 = jnp.bfloat16
MIB = 1 << 20
QUERY_BIAS, VALUE_BIAS, OUTPUT_BIAS, GAIN_ONE, SHIFT_ONE, DOWN_BIAS, GAIN_TWO, SHIFT_TWO = range(8)
SMALL = 128


def dot(left, right):
    return jnp.dot(left, right, preferred_element_type=f32)


def dot_left(left, right):
    return lax.dot_general(left, right, (((0,), (0,)), ((), ())), preferred_element_type=f32)


def dot_right(left, right):
    return lax.dot_general(left, right, (((1,), (1,)), ((), ())), preferred_element_type=f32)


def call(kernel, outs, ins, args, scratch=(), grid=None, limit=48, cost=None):
    return pl.pallas_call(
        kernel,
        out_shape=[shape for shape, _ in outs],
        in_specs=[pl.BlockSpec(memory_space=pltpu.SMEM)] + list(ins),
        out_specs=[spec for _, spec in outs],
        scratch_shapes=list(scratch),
        **({"grid": grid} if grid else {}),
        compiler_params=pltpu.CompilerParams(vmem_limit_bytes=limit * MIB),
        cost_estimate=pl.CostEstimate(
            flops=int(cost[0]), bytes_accessed=int(cost[1]), transcendentals=0
        ),
    )(*args)


def shaped(shape, kind):
    return jax.ShapeDtypeStruct(shape, kind)


def vmem():
    return pl.BlockSpec(memory_space=pltpu.VMEM)


def anywhere():
    return pl.BlockSpec(memory_space=pl.ANY)


def normalise(values):
    average = jnp.mean(values, axis=-1, keepdims=True)
    centered = values - average
    variance = jnp.mean(centered * centered, axis=-1, keepdims=True)
    scale = lax.rsqrt(variance + epsilon)
    return centered * scale, scale


def norm_back(normal, scale, gain, grad):
    inner = grad * gain
    return scale * (
        inner
        - jnp.mean(inner, axis=-1, keepdims=True)
        - normal * jnp.mean(inner * normal, axis=-1, keepdims=True)
    )


def run_copies(copies):
    for copy in copies:
        copy.start()
    for copy in copies:
        copy.wait()


def arrange_kernel(info, a, b, c, d, out):
    place = info[2]
    for k, ref in enumerate((a, b, c, d)):
        out[:, k ^ place] = ref[...]


def arrange(info, pieces):
    two, rows, columns = pieces[0].shape
    return call(
        arrange_kernel,
        [(shaped((two, PLACES, rows, columns), bf16), vmem())],
        [vmem()] * PLACES,
        [info] + list(pieces),
        limit=16,
        cost=(0, 8 * two * rows * columns * 2),
    )[0]


def front_kernel(blocks, patches, info, *refs):
    tokens_in, refs = refs[:4], refs[4:]
    weights_in, refs = refs[:blocks], refs[blocks:]
    (q_out, k_out, v_out, start_out, normed_out, small_out, turned_out, seg_out, spot_out) = refs[:9]
    held, weight, sem = refs[9:]
    core, chip, place = info[0], info[1], info[2]
    block, columns = held.shape[1] - 16, weight.shape[1] - SMALL
    part = columns // 3
    rows = weight.shape[0] // blocks
    copies = []
    for i in range(4):
        side = core if i < 2 else 1 - core
        there = 2 * side + ((i % 2) ^ (place % 2))
        copies.append(pltpu.make_async_copy(tokens_in[i], held.at[there], sem.at[i]))
    for r in range(blocks):
        there = pl.ds(pl.multiple_of((r ^ chip) * rows, rows), rows)
        copies.append(pltpu.make_async_copy(weights_in[r], weight.at[there], sem.at[4 + r]))
    run_copies(copies)
    small = weight[:, columns:]
    small_out[...] = small
    turned_out[...] = small.astype(f32).T
    vector = lambda i: turned_out[patches + i : patches + i + 1, :]
    half = pl.ds(pl.multiple_of(core * part, 128), part)
    query_bias = turned_out[patches + QUERY_BIAS : patches + QUERY_BIAS + 1, half]
    value_bias = turned_out[patches + VALUE_BIAS : patches + VALUE_BIAS + 1, half]
    gain, shift = vector(GAIN_ONE), vector(SHIFT_ONE)
    extra = held[0, block : block + 16, :].astype(f32)
    width = extra.shape[1]
    segment = jnp.concatenate([extra[1:2, :], extra[2:3, : 4 * block - width]], axis=1)
    seg_out[...] = jnp.broadcast_to(segment, seg_out.shape)
    ids = lax.broadcasted_iota(jnp.int32, (SMALL, block), 0).astype(f32)
    for b in range(4):
        here = slice(b * block, (b + 1) * block)
        spot = held[b, block : block + 16, :].astype(f32)[0:1, :block]
        spot_out[:, here] = jnp.broadcast_to(spot, (8, block))
        one_hot = jnp.where(ids == spot, 1.0, 0.0).astype(bf16)
        embedded = lax.dot_general(
            one_hot, small, (((0,), (1,)), ((), ())), preferred_element_type=f32
        )
        start = held[b, :block, :].astype(f32) + embedded
        start_out[here, :] = start
        normal, _ = normalise(start)
        normed = (normal * gain + shift).astype(bf16)
        normed_out[here, :] = normed
        projected = dot(normed, weight[:, :columns])
        query = (projected[:, :part] + query_bias).astype(bf16).astype(f32) * 0.125
        q_out[here, :] = query.astype(bf16)
        k_out[here, :] = projected[:, part : 2 * part].astype(bf16)
        v_out[here, :] = (projected[:, 2 * part :] + value_bias).astype(bf16)


def front(info, tokens, weights, patches):
    blocks = len(weights)
    block, width = tokens[0].shape[0] - 16, tokens[0].shape[1]
    columns = weights[0].shape[1]
    part = (columns - SMALL) // 3
    rows = 4 * block
    return call(
        functools.partial(front_kernel, blocks, patches),
        [
            (shaped((rows, part), bf16), vmem()),
            (shaped((rows, part), bf16), vmem()),
            (shaped((rows, part), bf16), vmem()),
            (shaped((rows, width), f32), vmem()),
            (shaped((rows, width), bf16), vmem()),
            (shaped((width, SMALL), bf16), vmem()),
            (shaped((SMALL, width), f32), vmem()),
            (shaped((8, rows), f32), vmem()),
            (shaped((8, rows), f32), vmem()),
        ],
        [anywhere()] * (4 + blocks),
        [info] + list(tokens) + list(weights),
        scratch=[
            pltpu.VMEM((4, block + 16, width), bf16),
            pltpu.VMEM((width, columns), bf16),
            pltpu.SemaphoreType.DMA((4 + blocks,)),
        ],
        cost=(2 * rows * width * columns, 12 * MIB),
    )


def fill_bias(bias, seg):
    block = bias.shape[1]
    wide = seg[...]
    tall = jnp.broadcast_to(wide[0:1, :], (128, wide.shape[1])).T[:, 0:1]
    base = 0
    for b in range(4):
        many = (b + 1) * block
        key = lax.broadcasted_iota(jnp.int32, (many, block), 0)
        ask = lax.broadcasted_iota(jnp.int32, (many, block), 1) + b * block
        same = tall[:many] == wide[0:1, b * block : (b + 1) * block]
        bias[base : base + many, :] = jnp.where((key <= ask) & same, 0.0, masked_score)
        base += many


def turn(values):
    return values.astype(f32).T.astype(bf16)


def attend_kernel(info, q, k, v, seg, out, total, bias):
    block = bias.shape[1]

    @pl.when(pl.program_id(0) == 0)
    def _():
        fill_bias(bias, seg)

    turned_q, turned_v = turn(q[...]), turn(v[...])
    side = lax.broadcasted_iota(jnp.int32, (128, block), 0) // 64
    base = 0
    for b in range(4):
        many = (b + 1) * block
        here = slice(b * block, (b + 1) * block)
        mixed = []
        for h in range(2):
            ask = jnp.where(side == h, turned_q[:, here].astype(f32), 0.0).astype(bf16)
            scores = dot(k[:many, :], ask) + bias[base : base + many, :]
            top = jnp.max(scores, axis=0, keepdims=True)
            raised = jnp.exp(scores - top)
            mass = jnp.sum(raised, axis=0, keepdims=True)
            total[0, h : h + 1, here] = top + jnp.log(mass)
            part = dot(turned_v[64 * h : 64 * h + 64, :many], raised.astype(bf16))
            mixed.append(part * (1.0 / mass))
        out[here, :] = jnp.concatenate(mixed, axis=0).T.astype(bf16)
        base += many


def attend(info, q, k, v, seg):
    rows, part = q.shape
    pairs = part // 128
    column = pl.BlockSpec((rows, 128), lambda i: (0, i))
    whole = pl.BlockSpec(seg.shape, lambda i: (0, 0))
    return call(
        attend_kernel,
        [
            (shaped((rows, part), bf16), column),
            (shaped((pairs, 8, rows), f32), pl.BlockSpec((1, 8, rows), lambda i: (i, 0, 0))),
        ],
        [column, column, column, whole],
        [info, q, k, v, seg],
        scratch=[pltpu.VMEM((10 * rows // 4, rows // 4), f32)],
        grid=(pairs,),
        cost=(6 * rows * rows * part, 4 * MIB),
    )


def attend_back_kernel(info, q, k, v, o, g, total, seg, dq, dk, dv, bias, dk_sum, dv_sum):
    block = bias.shape[1]

    @pl.when(pl.program_id(0) == 0)
    def _():
        fill_bias(bias, seg)

    wide_g = g[...].astype(f32).T
    product = wide_g * o[...].astype(f32).T
    inner = [jnp.sum(product[64 * h : 64 * h + 64], axis=0, keepdims=True) for h in range(2)]
    turned_q, turned_k = turn(q[...]), turn(k[...])
    turned_g = wide_g.astype(bf16)
    side = lax.broadcasted_iota(jnp.int32, (128, block), 0) // 64
    flat = lax.broadcasted_iota(jnp.int32, (block, 128), 1) // 64
    dk_sum[...] = jnp.zeros_like(dk_sum)
    dv_sum[...] = jnp.zeros_like(dv_sum)
    base = 0
    for b in range(4):
        many = (b + 1) * block
        here = slice(b * block, (b + 1) * block)
        grads = []
        for h in range(2):
            ask = jnp.where(side == h, turned_q[:, here].astype(f32), 0.0).astype(bf16)
            ask_g = jnp.where(side == h, turned_g[:, here].astype(f32), 0.0).astype(bf16)
            scores = dot(k[:many, :], ask) + bias[base : base + many, :]
            probs = jnp.exp(scores - total[0, h : h + 1, here])
            grad_probs = dot(v[:many, :], ask_g)
            grad_scores = (probs * (grad_probs - inner[h][:, here])).astype(bf16)
            own_q = jnp.where(flat == h, q[here, :].astype(f32), 0.0).astype(bf16)
            own_g = jnp.where(flat == h, g[here, :].astype(f32), 0.0).astype(bf16)
            dv_sum[:many, :] += dot(probs.astype(bf16), own_g)
            dk_sum[:many, :] += dot(grad_scores, own_q)
            grads.append(dot(turned_k[64 * h : 64 * h + 64, :many], grad_scores))
        dq[here, :] = (jnp.concatenate(grads, axis=0).T * 0.125).astype(bf16)
        base += many
    dk[...] = dk_sum[...].astype(bf16)
    dv[...] = dv_sum[...].astype(bf16)


def attend_back(info, q, k, v, o, g, total, seg):
    rows, part = q.shape
    pairs = part // 128
    column = pl.BlockSpec((rows, 128), lambda i: (0, i))
    whole = pl.BlockSpec(seg.shape, lambda i: (0, 0))
    out = (shaped((rows, part), bf16), column)
    return call(
        attend_back_kernel,
        [out, out, out],
        [column] * 5 + [pl.BlockSpec((1, 8, rows), lambda i: (i, 0, 0)), whole],
        [info, q, k, v, o, g, total, seg],
        scratch=[
            pltpu.VMEM((10 * rows // 4, rows // 4), f32),
            pltpu.VMEM((rows, 128), f32),
            pltpu.VMEM((rows, 128), f32),
        ],
        grid=(pairs,),
        cost=(15 * rows * rows * part, 6 * MIB),
    )


def cotangent_copies(info, pieces, held, sems):
    core, place = info[0], info[2]
    copies = []
    for i in range(4):
        side = core if i < 2 else 1 - core
        there = 2 * side + ((i % 2) ^ (place % 2))
        copies.append(pltpu.make_async_copy(pieces[i], held.at[there], sems[i]))
    return copies


def gelu_parts(values):
    scale = 0.7978845608028654
    square = values * values
    slope = jnp.tanh(values * (scale + (scale * 0.044715) * square))
    half = 0.5 * (1.0 + slope)
    grad = half + 0.5 * values * (1.0 - slope * slope) * (
        scale + (3.0 * scale * 0.044715) * square
    )
    return values * half, grad


def feed_kernel(blocks, patches, info, *refs):
    att, att_far, start, turned, up_bias, refs = refs[0], refs[1], refs[2], refs[3], refs[4], refs[5:]
    cot_in, refs = refs[:4], refs[4:]
    up_in, refs = refs[:blocks], refs[blocks:]
    down_in, refs = refs[:blocks], refs[blocks:]
    keep_out, send_out, back_out, back_low, middle_out, bias_out, refs = (
        refs[0], refs[1], refs[2], refs[3], refs[4], refs[5], refs[6:],
    )
    up_grads, refs = refs[:blocks], refs[blocks:]
    down_grads, refs = refs[:blocks], refs[blocks:]
    cot, up, down, normed, act, back, out_sum, up_grad, down_grad, sem = refs
    core, chip, place = info[0], info[1], info[2]
    rows, width = start.shape
    tile = rows // 4
    chunk = act.shape[1]
    up_rows = width // blocks
    half_rows = rows // 2
    hidden = 4 * chunk
    copies = cotangent_copies(info, cot_in, cot, [sem.at[i] for i in range(4)])
    count = 4
    for r in range(blocks):
        there = pl.ds(pl.multiple_of((r ^ chip) * up_rows, up_rows), up_rows)
        copies.append(pltpu.make_async_copy(up_in[r], up.at[there], sem.at[count]))
        count += 1
    later = []
    for r in range(blocks):
        if blocks == 4:
            for k in range(PLACES):
                later.append(
                    pltpu.make_async_copy(
                        down_in[r].at[k], down.at[r ^ chip, k ^ place], sem.at[count]
                    )
                )
                count += 1
        else:
            later.append(pltpu.make_async_copy(down_in[r], down, sem.at[count]))
            count += 1
    for copy in copies + later:
        copy.start()
    for copy in copies:
        copy.wait()
    part = width // 2
    vector = lambda i: turned[patches + i : patches + i + 1, :]
    own_rows = pl.ds(pl.multiple_of(core * part, 128), part)
    far_rows = pl.ds(pl.multiple_of((1 - core) * part, 128), part)
    gain, shift, out_bias = vector(GAIN_TWO), vector(SHIFT_TWO), vector(OUTPUT_BIAS)
    for t in range(4):
        here = slice(t * tile, (t + 1) * tile)
        middle = (
            start[here, :]
            + dot(att[here, :], up[own_rows, hidden:])
            + dot(att_far[here, :], up[far_rows, hidden:])
            + out_bias
        )
        middle_out[here, :] = middle
        normal, _ = normalise(middle)
        normed[here, :] = (normal * gain + shift).astype(bf16)
    out_sum[...] = jnp.zeros_like(out_sum)
    back_out[...] = jnp.zeros_like(back_out)
    for copy in later:
        copy.wait()

    def one_chunk(q, carry):
        lanes = pl.ds(pl.multiple_of(q * chunk, 128), chunk)
        down_part = down[q].reshape(chunk, width)
        bias_sum = jnp.zeros((1, chunk), f32)
        for t in range(4):
            here = slice(t * tile, (t + 1) * tile)
            value, slope = gelu_parts(dot(normed[here, :], up[:, lanes]) + up_bias[:, lanes])
            value = value.astype(bf16)
            act[here, :] = value
            out_sum[here, :] += dot(value, down_part)
            grad = (dot_right(cot[t], down_part) * slope).astype(bf16)
            back[here, :] = grad
            bias_sum += jnp.sum(grad.astype(f32), axis=0, keepdims=True)
            back_out[here, :] += dot_right(grad, up[:, lanes])
        bias_out[:, lanes] = jnp.broadcast_to(bias_sum, (8, chunk))
        flat = cot[...].reshape(rows, width)
        down_grad[q] = dot_left(act[...], flat).astype(bf16).reshape(PLACES, chunk // PLACES, width)
        up_grad[:, lanes] = dot_left(normed[...], back[...]).astype(bf16)
        return carry

    lax.fori_loop(0, 4, one_chunk, 0)
    back_low[...] = back_out[...].astype(bf16)
    own = pl.ds(pl.multiple_of(core * half_rows, half_rows), half_rows)
    far = pl.ds(pl.multiple_of((1 - core) * half_rows, half_rows), half_rows)
    keep_out[...] = middle_out[own, :] + out_sum[own, :] + vector(DOWN_BIAS)
    send_out[...] = out_sum[far, :].astype(bf16)
    outs = []
    for r in range(blocks):
        there = pl.ds(pl.multiple_of((r ^ chip) * up_rows, up_rows), up_rows)
        outs.append(pltpu.make_async_copy(up_grad.at[there], up_grads[r], sem.at[r]))
        source = down_grad.at[r ^ chip] if blocks == 4 else down_grad
        outs.append(pltpu.make_async_copy(source, down_grads[r], sem.at[blocks + r]))
    run_copies(outs)


def feed(info, att, att_far, start, turned, up_bias, cots, ups, downs, patches):
    blocks = len(ups)
    rows, width = start.shape
    hidden = up_bias.shape[1]
    chunk = hidden // 4
    down_shape = (4, PLACES, chunk // PLACES, width)
    up_rows = width // blocks
    one = down_shape[1:] if blocks == 4 else down_shape
    return call(
        functools.partial(feed_kernel, blocks, patches),
        [
            (shaped((rows // 2, width), f32), vmem()),
            (shaped((rows // 2, width), bf16), vmem()),
            (shaped((rows, width), f32), vmem()),
            (shaped((rows, width), bf16), vmem()),
            (shaped((rows, width), f32), vmem()),
            (shaped((8, hidden), f32), vmem()),
        ]
        + [(shaped((up_rows, hidden), bf16), anywhere())] * blocks
        + [(shaped(one, bf16), anywhere())] * blocks,
        [vmem()] * 5 + [anywhere()] * (4 + 2 * blocks),
        [info, att, att_far, start, turned, up_bias] + list(cots) + list(ups) + list(downs),
        scratch=[
            pltpu.VMEM((4, rows // 4, width), bf16),
            pltpu.VMEM((width, hidden + width), bf16),
            pltpu.VMEM(down_shape, bf16),
            pltpu.VMEM((rows, width), bf16),
            pltpu.VMEM((rows, chunk), bf16),
            pltpu.VMEM((rows, chunk), bf16),
            pltpu.VMEM((rows, width), f32),
            pltpu.VMEM((width, hidden), bf16),
            pltpu.VMEM(down_shape, bf16),
            pltpu.SemaphoreType.DMA((4 + 5 * blocks,)),
        ],
        limit=56,
        cost=(12 * rows * width * hidden, 30 * MIB),
    )


def middle_kernel(blocks, patches, info, *refs):
    back, back_far, middle, turned, att, refs = refs[0], refs[1], refs[2], refs[3], refs[4], refs[5:]
    cot_in, refs = refs[:4], refs[4:]
    up_in, refs = refs[:blocks], refs[blocks:]
    grad_out, attended_out, keep_out, send_out, sums_out, cot, weight, branch, sem = refs
    core, chip = info[0], info[1]
    rows, width = middle.shape
    tile = rows // 4
    part = width // 2
    up_rows = width // blocks
    hidden = up_in[0].shape[1] - width
    copies = cotangent_copies(info, cot_in, cot, [sem.at[i] for i in range(4)])
    for r in range(blocks):
        there = pl.ds(pl.multiple_of((r ^ chip) * up_rows, up_rows), up_rows)
        copies.append(
            pltpu.make_async_copy(up_in[r].at[:, hidden:], weight.at[there], sem.at[4 + r])
        )
    run_copies(copies)
    gain = turned[patches + GAIN_TWO : patches + GAIN_TWO + 1, :]
    own_rows = pl.ds(pl.multiple_of(core * part, 128), part)
    for t in range(4):
        here = slice(t * tile, (t + 1) * tile)
        grad_normed = back[here, :] + back_far[here, :].astype(f32)
        normal, scale = normalise(middle[here, :])
        grad_outputs = cot[t].astype(f32)
        grad = grad_outputs + norm_back(normal, scale, gain, grad_normed)
        low = grad.astype(bf16)
        branch[here, :] = low
        attended_out[here, :] = dot_right(low, weight[own_rows, :]).astype(bf16)

        @pl.when(core == t // 2)
        def _():
            grad_out[(t % 2) * tile : (t % 2 + 1) * tile, :] = grad
            sums = jnp.concatenate(
                [
                    jnp.sum(low.astype(f32), axis=0, keepdims=True),
                    jnp.sum(grad_outputs, axis=0, keepdims=True),
                    jnp.sum(grad_normed * normal, axis=0, keepdims=True),
                    jnp.sum(grad_normed, axis=0, keepdims=True),
                    jnp.zeros((4, width), f32),
                ],
                axis=0,
            )
            sums_out[...] = sums if t % 2 == 0 else sums_out[...] + sums

    weight_grad = dot_left(att[...], branch[...]).astype(bf16)
    shape = send_out.shape[:1] + (2,) + send_out.shape[1:]
    sorted_grad = weight_grad.reshape(shape) if blocks == 4 else None
    if blocks == 4:
        for c in range(2):

            @pl.when(core == c)
            def _():
                keep_out[...] = sorted_grad[:, c]
                send_out[...] = sorted_grad[:, 1 - c]

    else:
        keep_out[...] = weight_grad
        send_out[...] = weight_grad


def middle_back(info, back, back_far, middle, turned, att, cots, ups, patches):
    blocks = len(ups)
    rows, width = middle.shape
    part = width // 2
    slab = (2, part // 4, width) if blocks == 4 else (part, width)
    return call(
        functools.partial(middle_kernel, blocks, patches),
        [
            (shaped((rows // 2, width), f32), vmem()),
            (shaped((rows, part), bf16), vmem()),
            (shaped(slab, bf16), vmem()),
            (shaped(slab, bf16), vmem()),
            (shaped((8, width), f32), vmem()),
        ],
        [vmem()] * 5 + [anywhere()] * (4 + blocks),
        [info, back, back_far, middle, turned, att] + list(cots) + list(ups),
        scratch=[
            pltpu.VMEM((4, rows // 4, width), bf16),
            pltpu.VMEM((width, width), bf16),
            pltpu.VMEM((rows, width), bf16),
            pltpu.SemaphoreType.DMA((4 + blocks,)),
        ],
        cost=(4 * rows * width * part, 14 * MIB),
    )


def project_kernel(blocks, info, *refs):
    dq, dk, dv, refs = refs[0], refs[1], refs[2], refs[3:]
    weights_in, refs = refs[:blocks], refs[blocks:]
    keep_out, send_out, weight, sem = refs
    core, chip = info[0], info[1]
    rows, part = dq.shape
    width = weight.shape[0]
    up_rows = width // blocks
    half_rows = rows // 2
    copies = []
    for r in range(blocks):
        there = pl.ds(pl.multiple_of((r ^ chip) * up_rows, up_rows), up_rows)
        copies.append(
            pltpu.make_async_copy(
                weights_in[r].at[:, : 3 * part], weight.at[there], sem.at[r]
            )
        )
    run_copies(copies)

    def product(first):
        here = pl.ds(pl.multiple_of(first, 128), half_rows)
        return (
            dot_right(dq[here, :], weight[:, :part])
            + dot_right(dk[here, :], weight[:, part : 2 * part])
            + dot_right(dv[here, :], weight[:, 2 * part :])
        )

    send_out[...] = product((1 - core) * half_rows).astype(bf16)
    keep_out[...] = product(core * half_rows)


def project_back(info, dq, dk, dv, weights, width):
    blocks = len(weights)
    rows, part = dq.shape
    return call(
        functools.partial(project_kernel, blocks),
        [
            (shaped((rows // 2, width), f32), vmem()),
            (shaped((rows // 2, width), bf16), vmem()),
        ],
        [vmem()] * 3 + [anywhere()] * blocks,
        [info, dq, dk, dv] + list(weights),
        scratch=[
            pltpu.VMEM((width, 3 * part), bf16),
            pltpu.SemaphoreType.DMA((blocks,)),
        ],
        cost=(6 * rows * width * part, 8 * MIB),
    )


def start_kernel(blocks, patches, info, *refs):
    (keep, far, start, grad_middle, turned, sums, up_bias_rows, spots, normed, dq, dk, dv) = refs[:12]
    refs = refs[12:]
    low_out, refs = refs[0], refs[1:]
    grads, refs = refs[:blocks], refs[blocks:]
    held, rows_held, sem = refs
    core, chip = info[0], info[1]
    rows, part = dq.shape
    half_rows, width = keep.shape
    up_rows = width // blocks
    columns = 3 * part
    for i, ref in enumerate((dq, dk, dv)):
        held[:, i * part : (i + 1) * part] = dot_left(normed[...], ref[...]).astype(bf16)
    gain = turned[patches + GAIN_ONE : patches + GAIN_ONE + 1, :]
    own = pl.ds(pl.multiple_of(core * half_rows, half_rows), half_rows)
    grad_normed = keep[...] + far[...].astype(f32)
    normal, scale = normalise(start[own, :])
    grad = grad_middle[...] + norm_back(normal, scale, gain, grad_normed)
    low = grad.astype(bf16)
    low_out[...] = low
    ids = lax.broadcasted_iota(jnp.int32, (SMALL, half_rows), 0).astype(f32)
    mine = spots[0:1, pl.ds(pl.multiple_of(core * half_rows, 128), half_rows)]
    one_hot = jnp.where(ids == mine, 1.0, 0.0).astype(bf16)
    rows_held[...] = dot(one_hot, low)
    half = pl.ds(pl.multiple_of(core * part, 128), part)
    rows_held[patches : patches + 8, :] = jnp.zeros((8, width), f32)

    def put(i, row):
        rows_held[patches + i : patches + i + 1, :] = row

    rows_held[patches + QUERY_BIAS : patches + QUERY_BIAS + 1, half] = jnp.sum(
        dq[...].astype(f32), axis=0, keepdims=True
    )
    rows_held[patches + VALUE_BIAS : patches + VALUE_BIAS + 1, half] = jnp.sum(
        dv[...].astype(f32), axis=0, keepdims=True
    )
    put(OUTPUT_BIAS, sums[0:1, :])
    put(DOWN_BIAS, sums[1:2, :])
    put(GAIN_TWO, sums[2:3, :])
    put(SHIFT_TWO, sums[3:4, :])
    put(GAIN_ONE, jnp.sum(grad_normed * normal, axis=0, keepdims=True))
    put(SHIFT_ONE, jnp.sum(grad_normed, axis=0, keepdims=True))
    spare = up_bias_rows.shape[0]
    rows_held[patches + 8 : patches + 8 + spare, :] = up_bias_rows[...]
    held[:, columns:] = rows_held[...].T.astype(bf16)
    copies = []
    for r in range(blocks):
        there = pl.ds(pl.multiple_of((r ^ chip) * up_rows, up_rows), up_rows)
        copies.append(pltpu.make_async_copy(held.at[there], grads[r], sem.at[r]))
    run_copies(copies)


def start_back(
    info, blocks, keep, far, start, grad_middle, turned, sums, up_bias_rows, spots, normed, dq, dk, dv, patches
):
    half_rows, width = keep.shape
    rows, part = dq.shape
    columns = 3 * part + SMALL
    return call(
        functools.partial(start_kernel, blocks, patches),
        [(shaped((half_rows, width), bf16), vmem())]
        + [(shaped((width // blocks, columns), bf16), anywhere())] * blocks,
        [vmem()] * 12,
        [info, keep, far, start, grad_middle, turned, sums, up_bias_rows, spots, normed, dq, dk, dv],
        scratch=[
            pltpu.VMEM((width, columns), bf16),
            pltpu.VMEM((SMALL, width), f32),
            pltpu.SemaphoreType.DMA((blocks,)),
        ],
        cost=(6 * rows * width * part, 14 * MIB),
    )


def split_kernel(groups, info, *refs):
    place = info[2]
    inputs, outs = refs[: sum(groups)], refs[sum(groups) :]
    base, column = 0, 0
    for count in groups:
        total = inputs[base][...].astype(f32)
        for ref in inputs[base + 1 : base + count]:
            total = total + ref[...].astype(f32)
        base += count
        lanes = total.shape[-1]
        outs[PLACES][:, :, :, column : column + lanes] = total
        column += lanes
    for k in range(PLACES):
        outs[k][...] = outs[PLACES][:, k ^ place].astype(outs[k].dtype)


def split(info, groups):
    two, places, rows, _ = groups[0][0].shape
    columns = sum(group[0].shape[3] for group in groups)
    one = (two, rows, columns)
    outs = [(shaped(one, f32 if k == 0 else bf16), vmem()) for k in range(places)]
    outs.append((shaped((two, places, rows, columns), f32), vmem()))
    arrays = [array for group in groups for array in group]
    return call(
        functools.partial(split_kernel, [len(group) for group in groups]),
        outs,
        [vmem()] * len(arrays),
        [info] + arrays,
        limit=32,
        cost=(0, 8 * two * places * rows * columns),
    )[:places]


def swap(values, axis, bits):
    size = lax.axis_size(axis)
    return lax.ppermute(values, axis, [(i, i ^ bits) for i in range(size)])


def spread_perm(turn):
    pairs = []
    for w in range(lax.axis_size("wide")):
        for z in range(PLACES):
            there = (w - w % 2 + z // 2, 2 * (w % 2) + (turn ^ (z % 2)))
            pairs.append((w * PLACES + z, there[0] * PLACES + there[1]))
    return pairs


def spread(values, place):
    mine = [
        lax.ppermute(
            lax.dynamic_index_in_dim(values, turn ^ (place % 2), 0, keepdims=False),
            ("wide", "narrow"),
            spread_perm(turn),
        )
        for turn in range(2)
    ]
    return mine + [swap(part, "wide", 1) for part in mine]


def unspread(blocks, place):
    got = [
        lax.ppermute(
            lax.dynamic_index_in_dim(blocks, turn ^ (place % 2), 0, keepdims=False),
            ("wide", "narrow"),
            [(b, a) for a, b in spread_perm(turn)],
        )
        for turn in range(2)
    ]
    odd = (place % 2) == 1
    return jnp.stack([jnp.where(odd, got[1], got[0]), jnp.where(odd, got[0], got[1])])


def along(piece, bits):
    held = {0: piece}
    for bit in bits:
        held.update({index ^ (bit // 2): swap(part, "wide", bit) for index, part in list(held.items())})
    return [held[index] for index in range(len(held))]


def direct(piece, chips):
    return [piece] + [swap(piece, "wide", 2 * index) for index in range(1, chips)]


def fold(pieces, bits):
    held = dict(enumerate(pieces))
    for number, bit in enumerate(bits):
        step = bit // 2
        got = {i: swap(held[i ^ step], "wide", bit) for i in held if not i & step}
        if number == len(bits) - 1:
            return [held[0], got[0]]
        held = {i: (held[i].astype(f32) + got[i].astype(f32)).astype(bf16) for i in got}
    return [held[0]]


def after(values, *others):
    return lax.optimization_barrier((values,) + others)[0]


def local(
    tokens,
    positions,
    segments,
    position_table,
    input_weight,
    query_bias,
    value_bias,
    output_weight,
    output_bias,
    first_gain,
    first_shift,
    up_weight,
    up_bias,
    down_weight,
    down_bias,
    second_gain,
    second_shift,
    cotangent,
):
    size = lax.axis_size("wide")
    chips = size // 2
    bits = [2**i for i in range(1, size.bit_length() - 1)]
    seq_count, block, width = tokens.shape
    hidden = up_weight.shape[1]
    patches = position_table.shape[1]
    full = segments.shape[1]
    rows = width // (size * PLACES)
    part = width // 2
    own_hidden = hidden // 2
    wide, place = lax.axis_index("wide"), lax.axis_index("narrow")
    core, chip = wide % 2, wide // 2
    first_core = core == 0
    blocks = 4 if chips == 4 else 1
    info = jnp.stack([core, chip if blocks == 4 else 0 * chip, place, chip]).astype(jnp.int32)

    def pick(values, index, axis=0):
        return lax.dynamic_index_in_dim(values, index, axis, keepdims=False)

    def by_chip(pieces):
        flat = [piece.reshape((-1,) + piece.shape[-1:]) for piece in pieces]
        if blocks == 4:
            return flat
        whole = jnp.take(jnp.stack(flat), jnp.arange(chips) ^ chip, axis=0)
        return [whole.reshape((-1,) + flat[0].shape[1:])]

    def by_distance(outs, shape):
        if blocks == 4:
            return [out.reshape(shape) for out in outs]
        whole = outs[0].reshape((chips,) + shape)
        return [pick(whole, index ^ chip) for index in range(chips)]

    relative = (segments - segments[:, :1]).astype(bf16)
    extra = [
        jnp.pad(positions.astype(bf16), ((0, 0), (0, width - block)))[:, None],
        relative[:, None, :width],
        jnp.pad(relative[:, width:], ((0, 0), (0, 2 * width - full)))[:, None],
        jnp.zeros((seq_count, 13, width), bf16),
    ]
    packed = jnp.concatenate([tokens] + extra, axis=1)

    vectors = (
        query_bias,
        value_bias,
        output_bias,
        first_gain,
        first_shift,
        down_bias,
        second_gain,
        second_shift,
    )
    spare = up_bias.shape[0] // rows
    small = jnp.concatenate(
        [position_table] + [v[:, None] for v in vectors] + [up_bias.reshape(rows, spare)], axis=1
    )
    small = jnp.pad(small, ((0, 0), (0, SMALL - small.shape[1])))

    def pair(keep, send):
        got = swap(send, "wide", 1)
        return jnp.where(first_core, jnp.stack([keep, got]), jnp.stack([got, keep]))

    def in_halves(index):
        cut = pick(input_weight.reshape(rows, 3, 2, part), index, 2).reshape(rows, 3 * part)
        return jnp.concatenate([cut, small], axis=1)

    def up_halves(index):
        cut = pick(up_weight.reshape(rows, chips, 2, -1), index, 2).reshape(rows, own_hidden)
        return jnp.concatenate([cut, output_weight], axis=1)

    def narrow_pieces(piece):
        return [piece] + [swap(piece, "narrow", k) for k in range(1, PLACES)]

    in_pair = pair(in_halves(core), in_halves(1 - core))
    in_piece = arrange(info, narrow_pieces(in_pair))
    in_chips = direct(in_piece, chips) if blocks == 4 else along(in_piece, bits)
    in_blocks = by_chip(in_chips)
    token_blocks = spread(packed, place)

    up_pair = pair(up_halves(core), up_halves(1 - core))
    up_pair = after(up_pair, in_piece)
    up_piece = arrange(info, narrow_pieces(up_pair))
    up_blocks = by_chip(along(up_piece, bits[::-1]))
    down_pieces = jnp.stack(narrow_pieces(after(down_weight, up_piece)))
    if blocks == 4:
        down_blocks = along(down_pieces, bits)
    else:
        down_pieces = jnp.take(down_pieces, jnp.arange(PLACES) ^ place, axis=0)
        down_blocks = by_chip(along(down_pieces, bits))
        down_blocks = [down_blocks[0].reshape(4, PLACES, -1, width)]
    cots = spread(cotangent, place)

    q, k, v, start, normed, small_full, turned, seg, spots = front(
        info, token_blocks, in_blocks, patches
    )
    att, total = attend(info, q, k, v, seg)
    att_far = swap(att, "wide", 1)
    bias = small_full[:, patches + 8 : patches + 8 + spare]
    up_bias_own = pick(bias.reshape(chips, 2, -1), core, 1).reshape(1, own_hidden).astype(f32)
    fed = feed(
        info, att, att_far, start, turned, up_bias_own, cots, up_blocks, down_blocks, patches
    )
    keep, send, back, back_low, middle, bias_grad = fed[:6]
    up_grads, down_grads = fed[6 : 6 + blocks], fed[6 + blocks :]
    back_far = swap(back_low, "wide", 1)
    out_far = swap(send, "wide", 1)
    outputs = (keep + out_far.astype(f32)).astype(bf16).reshape(2, block, width)
    outputs = unspread(outputs, place)

    down_sum = fold(
        by_distance(down_grads, (1, PLACES, own_hidden // (chips * PLACES), width)), bits[::-1]
    )
    down_cut = split(info, [down_sum])
    down_share = down_cut[0][0]
    for index in range(1, PLACES):
        down_share = down_share + swap(down_cut[index], "narrow", index)[0].astype(f32)

    grad_middle, grad_att, out_keep, out_send, sums = middle_back(
        info, back, back_far, middle, turned, att, cots, up_blocks, patches
    )
    if blocks == 1:
        shape = (chips // 2, 2, PLACES * rows, width)
        out_keep = pick(out_keep.reshape(shape), core, 1)
        out_send = pick(out_send.reshape(shape), 1 - core, 1)
    out_got = swap(out_send, "wide", 1)
    out_grad = jnp.where(
        first_core,
        jnp.concatenate([out_keep, out_got]),
        jnp.concatenate([out_got, out_keep]),
    ).reshape(chips, PLACES, rows, 2, part)
    out_grad = jnp.swapaxes(jnp.swapaxes(out_grad, 2, 3), 1, 2)
    out_pieces = [pick(out_grad, index ^ chip) for index in range(chips)]
    up_pieces = by_distance(up_grads, (2, PLACES, rows, own_hidden))
    up_cut = split(info, [fold(up_pieces, bits), fold(out_pieces, bits)])

    def narrow_sum(cut):
        whole = cut[0]
        for index in range(1, PLACES):
            whole = whole + swap(cut[index], "narrow", index).astype(f32)
        return whole

    up_total = narrow_sum(up_cut)
    up_keep = pick(up_total[:, :, :own_hidden], core)
    up_got = swap(pick(up_total[:, :, :own_hidden], 1 - core).astype(bf16), "wide", 1).astype(f32)
    up_both = [up_keep.reshape(rows, chips, 1, -1), up_got.reshape(rows, chips, 1, -1)]
    up_share = jnp.where(
        first_core, jnp.concatenate(up_both, axis=2), jnp.concatenate(up_both[::-1], axis=2)
    ).reshape(rows, hidden)
    out_share = jnp.concatenate([up_total[0, :, own_hidden:], up_total[1, :, own_hidden:]], axis=1)

    dq, dk, dv = attend_back(info, q, k, v, att, grad_att, total, seg)
    start_keep, start_send = project_back(info, dq, dk, dv, in_blocks, width)
    start_far = swap(start_send, "wide", 1)
    bias_rows = bias_grad[0].reshape(chips, 1, rows * PLACES, spare)
    mine = (jnp.arange(2) == core)[None, :, None, None]
    bias_rows = jnp.where(mine, bias_rows, 0.0).reshape(width, spare).T
    started = start_back(
        info, blocks, start_keep, start_far, start, grad_middle, turned, sums, bias_rows,
        spots, normed, dq, dk, dv, patches,
    )
    grad_tokens = unspread(started[0].reshape(2, block, width), place)
    columns = 3 * part + SMALL
    in_pieces = by_distance(started[1:], (2, PLACES, rows, columns))
    if blocks == 4:
        in_sum = [in_pieces[0]] + [swap(in_pieces[i], "wide", 2 * i) for i in range(1, chips)]
    else:
        in_sum = fold(in_pieces, bits)
    in_total = narrow_sum(split(info, [in_sum]))
    in_keep = pick(in_total, core)
    in_got = swap(pick(in_total, 1 - core).astype(bf16), "wide", 1).astype(f32)
    in_both = [
        in_keep[:, : 3 * part].reshape(rows, 3, 1, part),
        in_got[:, : 3 * part].reshape(rows, 3, 1, part),
    ]
    in_share = jnp.where(
        first_core, jnp.concatenate(in_both, axis=2), jnp.concatenate(in_both[::-1], axis=2)
    ).reshape(rows, 3 * width)
    small_share = in_keep[:, 3 * part :] + in_got[:, 3 * part :]
    tail = [small_share[:, patches + i] for i in range(8)]
    return (
        outputs,
        grad_tokens,
        small_share[:, :patches],
        in_share,
        tail[QUERY_BIAS],
        tail[VALUE_BIAS],
        out_share,
        tail[OUTPUT_BIAS],
        tail[GAIN_ONE],
        tail[SHIFT_ONE],
        up_share,
        small_share[:, patches + 8 : patches + 8 + spare].reshape(-1),
        down_share,
        tail[DOWN_BIAS],
        tail[GAIN_TWO],
        tail[SHIFT_TWO],
    )


def solution(mesh):
    both = ("wide", "narrow")
    matrix = P(both, None)
    vector = P(both)
    block = P("wide", "narrow", None)
    gains = [matrix, matrix] + [vector] * 2 + [matrix] + [vector] * 3 + [matrix, vector, matrix]
    gains += [vector] * 3
    return jax.shard_map(
        local,
        mesh=mesh,
        in_specs=tuple([block, P("wide", "narrow"), P("wide", None)] + gains + [block]),
        out_specs=tuple([block, block] + gains),
        check_vma=False,
    )
```

```python
import functools

import jax
import jax.numpy as jnp
from jax import lax
from jax.experimental import pallas as pl
from jax.experimental.pallas import tpu as pltpu
from jax.sharding import PartitionSpec as P

HEADS = 12
PLACES = 4
epsilon = 1e-05
masked_score = -1e30

f32 = jnp.float32
bf16 = jnp.bfloat16
MIB = 1 << 20
LOAD, HELD = "load", "held"
QUERY_BIAS, VALUE_BIAS, OUTPUT_BIAS, GAIN_ONE, SHIFT_ONE, DOWN_BIAS, GAIN_TWO, SHIFT_TWO = range(8)
SMALL = 128


def dot(left, right):
    return jnp.dot(left, right, preferred_element_type=f32)


def dot_left(left, right):
    return lax.dot_general(left, right, (((0,), (0,)), ((), ())), preferred_element_type=f32)


def dot_right(left, right):
    return lax.dot_general(left, right, (((1,), (1,)), ((), ())), preferred_element_type=f32)


def call(kernel, outs, ins, args, scratch=(), grid=None, limit=14, cost=None):
    loads = []
    specs = [pl.BlockSpec(memory_space=pltpu.SMEM)]
    for index, (spec, array) in enumerate(zip(ins, args[1:], strict=True)):
        if spec == LOAD:
            whole = False
            spec = pl.BlockSpec(memory_space=pl.ANY if whole else pltpu.VMEM)
            if whole:
                loads.append(index)
        elif spec == HELD:
            spec = pl.BlockSpec(memory_space=pl.ANY)
        specs.append(spec)
    count, news = len(ins), len(loads)

    def loaded(info, *refs):
        refs, held, sem = list(refs[: -1 - news]), refs[-1 - news : -1], refs[-1]
        copies = []
        for i, index in enumerate(loads):
            copies.append(pltpu.make_async_copy(refs[index], held[i], sem.at[i]))
            refs[index] = held[i]
        run_copies(copies)
        kernel(info, *refs)

    extra = [pltpu.VMEM(args[1 + i].shape, args[1 + i].dtype) for i in loads]
    if loads:
        extra.append(pltpu.SemaphoreType.DMA((news,)))
    return pl.pallas_call(
        loaded if loads else kernel,
        out_shape=[shape for shape, _ in outs],
        in_specs=specs,
        out_specs=[spec for _, spec in outs],
        scratch_shapes=list(scratch) + extra,
        **({"grid": grid} if grid else {}),
        compiler_params=pltpu.CompilerParams(vmem_limit_bytes=limit * MIB),
        cost_estimate=pl.CostEstimate(
            flops=int(cost[0]), bytes_accessed=int(cost[1]), transcendentals=0
        ),
    )(*args)


def shaped(shape, kind):
    return jax.ShapeDtypeStruct(shape, kind)


def vmem():
    return pl.BlockSpec(memory_space=pltpu.VMEM)


def anywhere():
    return pl.BlockSpec(memory_space=pl.ANY)


def normalise(values):
    average = jnp.mean(values, axis=-1, keepdims=True)
    centered = values - average
    variance = jnp.mean(centered * centered, axis=-1, keepdims=True)
    scale = lax.rsqrt(variance + epsilon)
    return centered * scale, scale


def norm_back(normal, scale, gain, grad):
    inner = grad * gain
    return scale * (
        inner
        - jnp.mean(inner, axis=-1, keepdims=True)
        - normal * jnp.mean(inner * normal, axis=-1, keepdims=True)
    )


def run_copies(copies):
    for copy in copies:
        copy.start()
    for copy in copies:
        copy.wait()


def pack_kernel(patches, info, weight, table, rows_in, spare_in, up, out_weight, ins_keep, ins_send, ups_keep, ups_send):
    core = info[0]
    part = weight.shape[1] // 6
    small = jnp.zeros((weight.shape[0], SMALL), f32)
    turned = rows_in[...].astype(f32).T
    count = patches + turned.shape[1]
    small = jnp.concatenate(
        [
            table[...].astype(f32),
            turned,
            spare_in[...].astype(f32),
            small[:, count + spare_in.shape[1] :],
        ],
        axis=1,
    ).astype(bf16)
    columns = 3 * part
    own = ups_keep.shape[1] - out_weight.shape[1]
    for ref, up_ref, side in ((ins_keep, ups_keep, core), (ins_send, ups_send, 1 - core)):
        for i in range(3):
            there = pl.ds(pl.multiple_of((2 * i + side) * part, 128), part)
            ref[:, i * part : (i + 1) * part] = weight[:, there]
        ref[:, columns:] = small
        if up is not None:
            step = own // 4
            for q in range(4):
                there = pl.ds(pl.multiple_of((2 * q + side) * step, 128), step)
                up_ref[:, q * step : (q + 1) * step] = up[:, there]
        up_ref[:, own:] = out_weight[...]


def pack(info, weight, table, rows_in, spare_in, up, out_weight, patches):
    rows, columns = weight.shape[0], weight.shape[1] // 2 + SMALL
    own = up.shape[1] // 2 + out_weight.shape[1]
    return call(
        functools.partial(pack_kernel, patches),
        [(shaped((rows, columns), bf16), vmem())] * 2 + [(shaped((rows, own), bf16), vmem())] * 2,
        [vmem()] * 6,
        [info, weight, table, rows_in, spare_in, up, out_weight],
        limit=8,
        cost=(0, MIB),
    )


def sent_kernel(info, tokens, positions, segments, first, second, extra):
    place = info[2]
    block, width = tokens.shape[1], tokens.shape[2]
    full = segments.shape[1]
    extra[...] = jnp.zeros_like(extra)
    for k, out in enumerate((first, second)):
        index = k ^ (place % 2)
        row = segments[pl.ds(index, 1), :]
        row = (row - row[:, 0:1]).astype(f32)
        extra[0:1, :block] = positions[pl.ds(index, 1), :].astype(f32)
        extra[1:2, :] = row[:, :width]
        extra[2:3, : full - width] = row[:, width:]
        out[:block, :] = tokens[index]
        out[block:, :] = extra[...].astype(bf16)


def sent(info, tokens, positions, segments):
    _, block, width = tokens.shape
    one = (shaped((block + 16, width), bf16), vmem())
    return call(
        sent_kernel,
        [one, one],
        [vmem()] * 3,
        [info, tokens, positions, segments],
        scratch=[pltpu.VMEM((16, width), f32)],
        limit=8,
        cost=(0, 2 * MIB),
    )


def arrange_kernel(slot, shift, info, *refs):
    ins, out = refs[:-1], refs[-1]
    lead = len(out.shape) - 3
    place = lax.rem(info[slot] >> shift, len(ins))
    for k, ref in enumerate(ins):
        out[(slice(None),) * lead + (k ^ place,)] = ref[...]


def arrange(info, pieces, shift=0, slot=2):
    shape = pieces[0].shape
    shape = shape[:-2] + (len(pieces),) + shape[-2:]
    total = 1
    for extent in shape:
        total *= extent
    return call(
        functools.partial(arrange_kernel, slot, shift),
        [(shaped(shape, bf16), vmem())],
        [vmem()] * len(pieces),
        [info] + list(pieces),
        limit=8,
        cost=(0, 4 * total),
    )[0]


def cut_kernel(info, x, y, first, second):
    half = first.shape[0]
    first[...] = y[:half]
    second[...] = x[half:]


def cut(info, x, y):
    one = shaped((x.shape[0] // 2,) + x.shape[1:], bf16)
    return call(cut_kernel, [(one, vmem())] * 2, [LOAD] * 2, [info, x, y], limit=8, cost=(0, MIB))


def add_kernel(info, a, b, c, d, first, second):
    first[...] = (a[...].astype(f32) + b[...].astype(f32)).astype(bf16)
    second[...] = (c[...].astype(f32) + d[...].astype(f32)).astype(bf16)


def add_pairs(info, a, b, c, d):
    out = (shaped(a.shape, bf16), vmem())
    return call(add_kernel, [out] * 2, [LOAD] * 4, [info, a, b, c, d], limit=8, cost=(0, MIB))


def pick_kernel(info, blocks, first, second):
    odd = lax.rem(info[2], 2)
    first[...] = blocks[odd]
    second[...] = blocks[1 - odd]


def pick_turns(info, blocks):
    out = (shaped(blocks.shape[1:], bf16), vmem())
    return call(pick_kernel, [out] * 2, [LOAD], [info, blocks], limit=8, cost=(0, MIB))


def output_kernel(patches, info, middle, keep, far, turned, first, second):
    core, odd = info[0], lax.rem(info[2], 2)
    half = keep.shape[0]
    block = half // 2
    bias = turned[patches + DOWN_BIAS : patches + DOWN_BIAS + 1, :]
    for ref, which in ((first, odd), (second, 1 - odd)):
        here = pl.ds(pl.multiple_of(which * block, block), block)
        there = pl.ds(pl.multiple_of(core * half + which * block, block), block)
        ref[...] = (middle[there, :] + keep[here, :] + far[here, :].astype(f32) + bias).astype(bf16)


def output_turns(info, middle, keep, far, turned, patches):
    out = (shaped((keep.shape[0] // 2, keep.shape[1]), bf16), vmem())
    return call(
        functools.partial(output_kernel, patches),
        [out] * 2,
        [LOAD] * 4,
        [info, middle, keep, far, turned],
        limit=8,
        cost=(0, 6 * MIB),
    )


def front_kernel(blocks, patches, info, *refs):
    tokens_in, refs = refs[:4], refs[4:]
    weights_in, refs = refs[:blocks], refs[blocks:]
    (q_out, k_out, v_out, start_out, normed_out, small_out, turned_out, seg_out, spot_out) = refs[:9]
    held, weight, sem = refs[9:]
    core, chip, place = info[0], info[1], info[2]
    block, columns = held.shape[1] - 16, weight.shape[1] - SMALL
    part = columns // 3
    rows = weight.shape[0] // blocks
    copies = []
    for i in range(4):
        side = core if i < 2 else 1 - core
        there = 2 * side + ((i % 2) ^ (place % 2))
        copies.append(pltpu.make_async_copy(tokens_in[i], held.at[there], sem.at[i]))
    for r in range(blocks):
        there = pl.ds(pl.multiple_of((r ^ chip) * rows, rows), rows)
        copies.append(pltpu.make_async_copy(weights_in[r], weight.at[there], sem.at[4 + r]))
    run_copies(copies)
    small = weight[:, columns:]
    small_out[...] = small
    turned_out[...] = small.astype(f32).T
    vector = lambda i: turned_out[patches + i : patches + i + 1, :]
    half = pl.ds(pl.multiple_of(core * part, 128), part)
    query_bias = turned_out[patches + QUERY_BIAS : patches + QUERY_BIAS + 1, half]
    value_bias = turned_out[patches + VALUE_BIAS : patches + VALUE_BIAS + 1, half]
    gain, shift = vector(GAIN_ONE), vector(SHIFT_ONE)
    extra = held[0, block : block + 16, :].astype(f32)
    width = extra.shape[1]
    segment = jnp.concatenate([extra[1:2, :], extra[2:3, : 4 * block - width]], axis=1)
    seg_out[...] = jnp.broadcast_to(segment, seg_out.shape)
    ids = lax.broadcasted_iota(jnp.int32, (SMALL, block), 0).astype(f32)
    for b in range(4):
        here = slice(b * block, (b + 1) * block)
        spot = held[b, block : block + 16, :].astype(f32)[0:1, :block]
        spot_out[:, here] = jnp.broadcast_to(spot, (8, block))
        one_hot = jnp.where(ids == spot, 1.0, 0.0).astype(bf16)
        embedded = lax.dot_general(
            one_hot, small, (((0,), (1,)), ((), ())), preferred_element_type=f32
        )
        start = held[b, :block, :].astype(f32) + embedded
        start_out[here, :] = start
        normal, _ = normalise(start)
        normed = (normal * gain + shift).astype(bf16)
        normed_out[here, :] = normed
        projected = dot(normed, weight[:, :columns])
        query = (projected[:, :part] + query_bias).astype(bf16).astype(f32) * 0.125
        q_out[here, :] = query.astype(bf16)
        k_out[here, :] = projected[:, part : 2 * part].astype(bf16)
        v_out[here, :] = (projected[:, 2 * part :] + value_bias).astype(bf16)


def front(info, tokens, weights, patches):
    blocks = len(weights)
    block, width = tokens[0].shape[0] - 16, tokens[0].shape[1]
    columns = weights[0].shape[1]
    part = (columns - SMALL) // 3
    rows = 4 * block
    return call(
        functools.partial(front_kernel, blocks, patches),
        [
            (shaped((rows, part), bf16), vmem()),
            (shaped((rows, part), bf16), vmem()),
            (shaped((rows, part), bf16), vmem()),
            (shaped((rows, width), f32), vmem()),
            (shaped((rows, width), bf16), vmem()),
            (shaped((width, SMALL), bf16), vmem()),
            (shaped((SMALL, width), f32), vmem()),
            (shaped((8, rows), f32), vmem()),
            (shaped((8, rows), f32), vmem()),
        ],
        [HELD] * (4 + blocks),
        [info] + list(tokens) + list(weights),
        scratch=[
            pltpu.VMEM((4, block + 16, width), bf16),
            pltpu.VMEM((width, columns), bf16),
            pltpu.SemaphoreType.DMA((4 + blocks,)),
        ],
        cost=(2 * rows * width * columns, 12 * MIB),
    )


def fill_bias(bias, seg):
    block = bias.shape[1]
    wide = seg[...]
    tall = jnp.broadcast_to(wide[0:1, :], (128, wide.shape[1])).T[:, 0:1]
    base = 0
    for b in range(4):
        many = (b + 1) * block
        key = lax.broadcasted_iota(jnp.int32, (many, block), 0)
        ask = lax.broadcasted_iota(jnp.int32, (many, block), 1) + b * block
        same = tall[:many] == wide[0:1, b * block : (b + 1) * block]
        bias[base : base + many, :] = jnp.where((key <= ask) & same, 0.0, masked_score)
        base += many


def turn(values):
    return values.astype(f32).T.astype(bf16)


def attend_kernel(info, q, k, v, seg, out, total, bias):
    block = bias.shape[1]

    @pl.when(pl.program_id(0) == 0)
    def _():
        fill_bias(bias, seg)

    turned_q, turned_v = turn(q[...]), turn(v[...])
    side = lax.broadcasted_iota(jnp.int32, (128, block), 0) // 64
    base = 0
    for b in range(4):
        many = (b + 1) * block
        here = slice(b * block, (b + 1) * block)
        mixed = []
        for h in range(2):
            ask = jnp.where(side == h, turned_q[:, here].astype(f32), 0.0).astype(bf16)
            scores = dot(k[:many, :], ask) + bias[base : base + many, :]
            top = jnp.max(scores, axis=0, keepdims=True)
            raised = jnp.exp(scores - top)
            mass = jnp.sum(raised, axis=0, keepdims=True)
            total[0, h : h + 1, here] = top + jnp.log(mass)
            part = dot(turned_v[64 * h : 64 * h + 64, :many], raised.astype(bf16))
            mixed.append(part * (1.0 / mass))
        out[here, :] = jnp.concatenate(mixed, axis=0).T.astype(bf16)
        base += many


def attend(info, q, k, v, seg):
    rows, part = q.shape
    pairs = part // 128
    column = pl.BlockSpec((rows, 128), lambda i: (0, i))
    whole = pl.BlockSpec(seg.shape, lambda i: (0, 0))
    return call(
        attend_kernel,
        [
            (shaped((rows, part), bf16), column),
            (shaped((pairs, 8, rows), f32), pl.BlockSpec((1, 8, rows), lambda i: (i, 0, 0))),
        ],
        [column, column, column, whole],
        [info, q, k, v, seg],
        scratch=[pltpu.VMEM((10 * rows // 4, rows // 4), f32)],
        grid=(pairs,),
        cost=(6 * rows * rows * part, 4 * MIB),
    )


def attend_back_kernel(info, q, k, v, o, g, total, seg, dq, dk, dv, bias, dk_sum, dv_sum):
    block = bias.shape[1]

    @pl.when(pl.program_id(0) == 0)
    def _():
        fill_bias(bias, seg)

    wide_g = g[...].astype(f32).T
    product = wide_g * o[...].astype(f32).T
    inner = [jnp.sum(product[64 * h : 64 * h + 64], axis=0, keepdims=True) for h in range(2)]
    turned_q, turned_k = turn(q[...]), turn(k[...])
    turned_g = wide_g.astype(bf16)
    side = lax.broadcasted_iota(jnp.int32, (128, block), 0) // 64
    flat = lax.broadcasted_iota(jnp.int32, (block, 128), 1) // 64
    dk_sum[...] = jnp.zeros_like(dk_sum)
    dv_sum[...] = jnp.zeros_like(dv_sum)
    base = 0
    for b in range(4):
        many = (b + 1) * block
        here = slice(b * block, (b + 1) * block)
        grads = []
        for h in range(2):
            ask = jnp.where(side == h, turned_q[:, here].astype(f32), 0.0).astype(bf16)
            ask_g = jnp.where(side == h, turned_g[:, here].astype(f32), 0.0).astype(bf16)
            scores = dot(k[:many, :], ask) + bias[base : base + many, :]
            probs = jnp.exp(scores - total[0, h : h + 1, here])
            grad_probs = dot(v[:many, :], ask_g)
            grad_scores = (probs * (grad_probs - inner[h][:, here])).astype(bf16)
            own_q = jnp.where(flat == h, q[here, :].astype(f32), 0.0).astype(bf16)
            own_g = jnp.where(flat == h, g[here, :].astype(f32), 0.0).astype(bf16)
            dv_sum[:many, :] += dot(probs.astype(bf16), own_g)
            dk_sum[:many, :] += dot(grad_scores, own_q)
            grads.append(dot(turned_k[64 * h : 64 * h + 64, :many], grad_scores))
        dq[here, :] = (jnp.concatenate(grads, axis=0).T * 0.125).astype(bf16)
        base += many
    dk[...] = dk_sum[...].astype(bf16)
    dv[...] = dv_sum[...].astype(bf16)


def attend_back(info, q, k, v, o, g, total, seg):
    rows, part = q.shape
    pairs = part // 128
    column = pl.BlockSpec((rows, 128), lambda i: (0, i))
    whole = pl.BlockSpec(seg.shape, lambda i: (0, 0))
    out = (shaped((rows, part), bf16), column)
    return call(
        attend_back_kernel,
        [out, out, out],
        [column] * 5 + [pl.BlockSpec((1, 8, rows), lambda i: (i, 0, 0)), whole],
        [info, q, k, v, o, g, total, seg],
        scratch=[
            pltpu.VMEM((10 * rows // 4, rows // 4), f32),
            pltpu.VMEM((rows, 128), f32),
            pltpu.VMEM((rows, 128), f32),
        ],
        grid=(pairs,),
        cost=(15 * rows * rows * part, 6 * MIB),
    )


def cotangent_copies(info, pieces, held, sems):
    core, place = info[0], info[2]
    copies = []
    for i in range(4):
        side = core if i < 2 else 1 - core
        there = 2 * side + ((i % 2) ^ (place % 2))
        copies.append(pltpu.make_async_copy(pieces[i], held.at[there], sems[i]))
    return copies


def gelu_parts(values):
    scale = 0.7978845608028654
    square = values * values
    slope = jnp.tanh(values * (scale + (scale * 0.044715) * square))
    half = 0.5 * (1.0 + slope)
    grad = half + 0.5 * values * (1.0 - slope * slope) * (
        scale + (3.0 * scale * 0.044715) * square
    )
    return values * half, grad


def piece_copies(pieces, target, info, sem, lanes=None):
    chip = info[1]
    rows = pieces[0].shape[0]
    copies, base = [], 0
    for i, ref in enumerate(pieces):
        distance = min(i, 3)
        begin = pl.multiple_of((distance ^ chip) * rows, rows)
        if i == 4:
            begin = pl.multiple_of(begin + rows // 2, rows // 2)
        source = ref if lanes is None else ref.at[:, lanes]
        there = target.at[pl.ds(begin, ref.shape[0])]
        copies.append(pltpu.make_async_copy(source, there, sem.at[i]))
    return copies


def hidden_places(core, hidden, width, chips):
    spare = 2 * hidden // width
    share = hidden // chips
    unit = lax.broadcasted_iota(jnp.int32, (hidden, 1), 0)
    chip, rest = unit // share, lax.rem(unit, share)
    row = (2 * chip + core) * (share // spare) + rest // spare
    lane = lax.broadcasted_iota(jnp.int32, (hidden, width), 1)
    return jnp.where(lane == row, 1.0, 0.0).astype(bf16)


def middle_kernel(count, patches, chips, info, att, att_far, start, turned, *refs):
    up_in, refs = refs[:count], refs[count:]
    middle_out, normed_out, bias_out, weight, sem = refs
    core = info[0]
    rows, width = start.shape
    part, tile = width // 2, rows // 4
    hidden = up_in[0].shape[1] - width
    copies = piece_copies(up_in, weight, info, sem, slice(hidden, hidden + width))
    for copy in copies:
        copy.start()
    spare = 2 * hidden // width
    biases = turned[patches + 8 : patches + 8 + spare, :].astype(bf16)
    spread_out = dot_right(biases, hidden_places(core, hidden, width, chips))
    turns = lax.rem(lax.broadcasted_iota(jnp.int32, (spare, hidden), 1), spare)
    ranks = lax.broadcasted_iota(jnp.int32, (spare, hidden), 0)
    bias = jnp.sum(jnp.where(turns == ranks, spread_out, 0.0), axis=0, keepdims=True)
    bias_out[...] = jnp.broadcast_to(bias, bias_out.shape)
    for copy in copies:
        copy.wait()
    vector = lambda i: turned[patches + i : patches + i + 1, :]
    own = pl.ds(pl.multiple_of(core * part, 128), part)
    far = pl.ds(pl.multiple_of((1 - core) * part, 128), part)
    gain, shift, out_bias = vector(GAIN_TWO), vector(SHIFT_TWO), vector(OUTPUT_BIAS)
    for t in range(4):
        here = slice(t * tile, (t + 1) * tile)
        mixed = dot(att[here, :], weight[own, :]) + dot(att_far[here, :], weight[far, :])
        middle = start[here, :] + mixed + out_bias
        middle_out[here, :] = middle
        normal, _ = normalise(middle)
        normed_out[here, :] = (normal * gain + shift).astype(bf16)


def middle_front(info, att, att_far, start, turned, ups, patches, chips):
    rows, width = start.shape
    count = len(ups)
    return call(
        functools.partial(middle_kernel, count, patches, chips),
        [
            (shaped((rows, width), f32), vmem()),
            (shaped((rows, width), bf16), vmem()),
            (shaped((8, ups[0].shape[1] - width), f32), vmem()),
        ],
        [LOAD] * 4 + [HELD] * count,
        [info, att, att_far, start, turned] + list(ups),
        scratch=[pltpu.VMEM((width, width), bf16), pltpu.SemaphoreType.DMA((count,))],
        cost=(2 * rows * width * width, 12 * MIB),
    )


def feed_front_kernel(ups, downs, blocks, info, normed, up_bias, *refs):
    cot_in, refs = refs[:4], refs[4:]
    up_in, refs = refs[:ups], refs[ups:]
    down_in, refs = refs[:downs], refs[downs:]
    keep_out, send_out, slope_out, refs = refs[0], refs[1], refs[2], refs[3:]
    cut = 2 if blocks == 4 else 1
    down_grads, refs = refs[: cut * blocks], refs[cut * blocks :]
    cot, up, down, out_sum, down_grad, cot_sem, up_sem, down_sem = refs
    core, chip = info[0], info[1]
    rows, width = normed.shape
    hidden = up.shape[1]
    chunk = hidden // 4
    early = piece_copies(up_in, up, info, up_sem, slice(0, hidden))
    late = cotangent_copies(info, cot_in, cot, [cot_sem.at[i] for i in range(4)])
    late += piece_copies(down_in, down, info, down_sem)
    for copy in early + late:
        copy.start()
    for copy in early + late:
        copy.wait()
    out_sum[...] = jnp.zeros_like(out_sum)

    def one_chunk(q, carry):
        lanes = pl.ds(pl.multiple_of(q * chunk, 128), chunk)
        down_part = down[pl.ds(q * PLACES, PLACES)].reshape(chunk, width)
        value, slope = gelu_parts(dot(normed[...], up[:, lanes]) + up_bias[0:1, lanes])
        value = value.astype(bf16)
        slope_out[:, lanes] = slope.astype(bf16)
        out_sum[...] += dot(value, down_part)
        flat = cot[...].reshape(rows, width)
        grad = dot_left(value, flat).astype(bf16)
        down_grad[pl.ds(q * PLACES, PLACES)] = grad.reshape(PLACES, chunk // PLACES, width)
        return carry

    lax.fori_loop(0, 4, one_chunk, 0)
    outs = []
    if blocks == 4:
        for r in range(blocks):
            for h in range(2):
                there = pl.ds((r ^ chip) * PLACES + 2 * h, 2)
                i = 2 * r + h
                outs.append(pltpu.make_async_copy(down_grad.at[there], down_grads[i], down_sem.at[i]))
    else:
        outs.append(pltpu.make_async_copy(down_grad, down_grads[0], down_sem.at[0]))
    for copy in outs:
        copy.start()
    half = rows // 2
    own = pl.ds(pl.multiple_of(core * half, half), half)
    far = pl.ds(pl.multiple_of((1 - core) * half, half), half)
    keep_out[...] = out_sum[own, :]
    send_out[...] = out_sum[far, :].astype(bf16)
    for copy in outs:
        copy.wait()


def feed_front(info, normed, up_bias, cots, ups, downs, blocks):
    rows, width = normed.shape
    hidden = up_bias.shape[1]
    whole = (4 * PLACES, hidden // (4 * PLACES), width)
    grads = [(2,) + whole[1:]] * 8 if blocks == 4 else [whole]
    return call(
        functools.partial(feed_front_kernel, len(ups), len(downs), blocks),
        [
            (shaped((rows // 2, width), f32), vmem()),
            (shaped((rows // 2, width), bf16), vmem()),
            (shaped((rows, hidden), bf16), vmem()),
        ]
        + [(shaped(one, bf16), anywhere()) for one in grads],
        [LOAD] * 2 + [HELD] * (4 + len(ups) + len(downs)),
        [info, normed, up_bias] + list(cots) + list(ups) + list(downs),
        scratch=[
            pltpu.VMEM((4, rows // 4, width), bf16),
            pltpu.VMEM((width, hidden), bf16),
            pltpu.VMEM(whole, bf16),
            pltpu.VMEM((rows, width), f32),
            pltpu.VMEM(whole, bf16),
            pltpu.SemaphoreType.DMA((4,)),
            pltpu.SemaphoreType.DMA((len(ups),)),
            pltpu.SemaphoreType.DMA((8,)),
        ],
        limit=20,
        cost=(6 * rows * width * hidden, 24 * MIB),
    )


def feed_back_kernel(ups, downs, info, slope, *refs):
    cot_in, refs = refs[:4], refs[4:]
    up_in, refs = refs[:ups], refs[ups:]
    down_in, refs = refs[:downs], refs[downs:]
    back_out, low_out, grad_out, bias_out, cot, up, down, cot_sem, up_sem, down_sem = refs
    rows, hidden = slope.shape
    width = up.shape[0]
    chunk = hidden // 4
    copies = cotangent_copies(info, cot_in, cot, [cot_sem.at[i] for i in range(4)])
    copies += piece_copies(down_in, down, info, down_sem)
    copies += piece_copies(up_in, up, info, up_sem, slice(0, hidden))
    run_copies(copies)
    back_out[...] = jnp.zeros_like(back_out)

    def one_chunk(q, carry):
        lanes = pl.ds(pl.multiple_of(q * chunk, 128), chunk)
        down_part = down[pl.ds(q * PLACES, PLACES)].reshape(chunk, width)
        flat = cot[...].reshape(rows, width)
        grad = (dot_right(flat, down_part) * slope[:, lanes].astype(f32)).astype(bf16)
        grad_out[:, lanes] = grad
        bias_out[:, lanes] = jnp.broadcast_to(
            jnp.sum(grad.astype(f32), axis=0, keepdims=True), (8, chunk)
        )
        back_out[...] += dot_right(grad, up[:, lanes])
        return carry

    lax.fori_loop(0, 4, one_chunk, 0)
    low_out[...] = back_out[...].astype(bf16)


def feed_back(info, slope, cots, ups, downs, width):
    rows, hidden = slope.shape
    whole = (4 * PLACES, hidden // (4 * PLACES), width)
    return call(
        functools.partial(feed_back_kernel, len(ups), len(downs)),
        [
            (shaped((rows, width), f32), vmem()),
            (shaped((rows, width), bf16), vmem()),
            (shaped((rows, hidden), bf16), vmem()),
            (shaped((8, hidden), f32), vmem()),
        ],
        [LOAD] + [HELD] * (4 + len(ups) + len(downs)),
        [info, slope] + list(cots) + list(ups) + list(downs),
        scratch=[
            pltpu.VMEM((4, rows // 4, width), bf16),
            pltpu.VMEM((width, hidden), bf16),
            pltpu.VMEM(whole, bf16),
            pltpu.SemaphoreType.DMA((4,)),
            pltpu.SemaphoreType.DMA((len(ups),)),
            pltpu.SemaphoreType.DMA((len(downs),)),
        ],
        limit=20,
        cost=(4 * rows * width * hidden, 24 * MIB),
    )


def weight_kernel(pieces, cut, count, info, left, *refs):
    parts, outs = refs[:count], refs[count : count + pieces * cut]
    held, sem = refs[count + pieces * cut :][:2]
    chip = info[1]
    width = left.shape[1]
    base = 0
    for ref in parts:
        for begin in range(0, ref.shape[1], 384):
            size = min(384, ref.shape[1] - begin)
            product = dot_left(left[...], ref[:, begin : begin + size]).astype(bf16)
            held[:, base : base + size] = product
            base += size
    copies = []
    rows = width // (pieces * cut)
    for r in range(pieces):
        for h in range(cut):
            there = pl.ds(pl.multiple_of(((r ^ chip) * cut + h) * rows, rows), rows)
            i = cut * r + h
            copies.append(pltpu.make_async_copy(held.at[there], outs[i], sem.at[i]))
    run_copies(copies)


def weight_grad(info, left, parts, pieces, cut=1):
    rows, width = left.shape
    columns = sum(part.shape[1] for part in parts)
    count = pieces * cut
    return call(
        functools.partial(weight_kernel, pieces, cut, len(parts)),
        [(shaped((width // count, columns), bf16), anywhere())] * count,
        [LOAD] * (1 + len(parts)),
        [info, left] + list(parts),
        scratch=[pltpu.VMEM((width, columns), bf16), pltpu.SemaphoreType.DMA((count,))],
        cost=(2 * rows * width * columns, 8 * MIB),
    )


def middle_back_kernel(count, blocks, patches, info, *refs):
    back, back_far, middle, turned, att, refs = refs[0], refs[1], refs[2], refs[3], refs[4], refs[5:]
    cot_in, refs = refs[:4], refs[4:]
    up_in, refs = refs[:count], refs[count:]
    grad_out, attended_out, keep_out, send_out, sums_out, cot, weight, branch, sem, up_sem = refs
    core, chip = info[0], info[1]
    rows, width = middle.shape
    tile = rows // 4
    part = width // 2
    hidden = up_in[0].shape[1] - width
    copies = cotangent_copies(info, cot_in, cot, [sem.at[i] for i in range(4)])
    copies += piece_copies(up_in, weight, info, up_sem, slice(hidden, hidden + width))
    run_copies(copies)
    gain = turned[patches + GAIN_TWO : patches + GAIN_TWO + 1, :]
    own_rows = pl.ds(pl.multiple_of(core * part, 128), part)
    for t in range(4):
        here = slice(t * tile, (t + 1) * tile)
        grad_normed = back[here, :] + back_far[here, :].astype(f32)
        normal, scale = normalise(middle[here, :])
        grad_outputs = cot[t].astype(f32)
        grad = grad_outputs + norm_back(normal, scale, gain, grad_normed)
        low = grad.astype(bf16)
        branch[here, :] = low
        attended_out[here, :] = dot_right(low, weight[own_rows, :]).astype(bf16)

        @pl.when(core == t // 2)
        def _():
            grad_out[(t % 2) * tile : (t % 2 + 1) * tile, :] = grad
            sums = jnp.concatenate(
                [
                    jnp.sum(low.astype(f32), axis=0, keepdims=True),
                    jnp.sum(grad_outputs, axis=0, keepdims=True),
                    jnp.sum(grad_normed * normal, axis=0, keepdims=True),
                    jnp.sum(grad_normed, axis=0, keepdims=True),
                    jnp.zeros((4, width), f32),
                ],
                axis=0,
            )
            sums_out[...] = sums if t % 2 == 0 else sums_out[...] + sums

    weight_grad = dot_left(att[...], branch[...]).astype(bf16)
    shape = send_out.shape[:1] + (2,) + send_out.shape[1:]
    sorted_grad = weight_grad.reshape(shape) if blocks == 4 else None
    if blocks == 4:
        for c in range(2):

            @pl.when(core == c)
            def _():
                keep_out[...] = sorted_grad[:, c]
                send_out[...] = sorted_grad[:, 1 - c]

    else:
        keep_out[...] = weight_grad
        send_out[...] = weight_grad


def middle_back(info, back, back_far, middle, turned, att, cots, ups, patches, blocks):
    count = len(ups)
    rows, width = middle.shape
    part = width // 2
    slab = (2, part // 4, width) if blocks == 4 else (part, width)
    return call(
        functools.partial(middle_back_kernel, count, blocks, patches),
        [
            (shaped((rows // 2, width), f32), vmem()),
            (shaped((rows, part), bf16), vmem()),
            (shaped(slab, bf16), vmem()),
            (shaped(slab, bf16), vmem()),
            (shaped((8, width), f32), vmem()),
        ],
        [LOAD] * 5 + [HELD] * (4 + count),
        [info, back, back_far, middle, turned, att] + list(cots) + list(ups),
        scratch=[
            pltpu.VMEM((4, rows // 4, width), bf16),
            pltpu.VMEM((width, width), bf16),
            pltpu.VMEM((rows, width), bf16),
            pltpu.SemaphoreType.DMA((4,)),
            pltpu.SemaphoreType.DMA((count,)),
        ],
        cost=(4 * rows * width * part, 14 * MIB),
    )


def project_kernel(blocks, info, *refs):
    dq, dk, dv, refs = refs[0], refs[1], refs[2], refs[3:]
    weights_in, refs = refs[:blocks], refs[blocks:]
    keep_out, send_out, weight, sem = refs
    core, chip = info[0], info[1]
    rows, part = dq.shape
    width = weight.shape[0]
    up_rows = width // blocks
    half_rows = rows // 2
    copies = []
    for r in range(blocks):
        there = pl.ds(pl.multiple_of((r ^ chip) * up_rows, up_rows), up_rows)
        copies.append(
            pltpu.make_async_copy(
                weights_in[r].at[:, : 3 * part], weight.at[there], sem.at[r]
            )
        )
    run_copies(copies)

    def product(first):
        here = pl.ds(pl.multiple_of(first, 128), half_rows)
        return (
            dot_right(dq[here, :], weight[:, :part])
            + dot_right(dk[here, :], weight[:, part : 2 * part])
            + dot_right(dv[here, :], weight[:, 2 * part :])
        )

    send_out[...] = product((1 - core) * half_rows).astype(bf16)
    keep_out[...] = product(core * half_rows)


def project_back(info, dq, dk, dv, weights, width):
    blocks = len(weights)
    rows, part = dq.shape
    return call(
        functools.partial(project_kernel, blocks),
        [
            (shaped((rows // 2, width), f32), vmem()),
            (shaped((rows // 2, width), bf16), vmem()),
        ],
        [LOAD] * 3 + [HELD] * blocks,
        [info, dq, dk, dv] + list(weights),
        scratch=[
            pltpu.VMEM((width, 3 * part), bf16),
            pltpu.SemaphoreType.DMA((blocks,)),
        ],
        cost=(6 * rows * width * part, 8 * MIB),
    )


def start_kernel(blocks, patches, chips, info, *refs):
    (keep, far, start, grad_middle, turned, sums, bias_grad, spots, dq, dv, out_keep, out_got) = refs[:12]
    refs = refs[12:]
    low_out, refs = refs[0], refs[1:]
    grads, refs = refs[:blocks], refs[blocks:]
    held, rows_held, sem = refs
    core, chip = info[0], info[1]
    rows, part = dq.shape
    half_rows, width = keep.shape
    up_rows = width // blocks
    gain = turned[patches + GAIN_ONE : patches + GAIN_ONE + 1, :]
    own = pl.ds(pl.multiple_of(core * half_rows, half_rows), half_rows)
    grad_normed = keep[...] + far[...].astype(f32)
    normal, scale = normalise(start[own, :])
    grad = grad_middle[...] + norm_back(normal, scale, gain, grad_normed)
    low = grad.astype(bf16)
    low_out[...] = low
    ids = lax.broadcasted_iota(jnp.int32, (SMALL, half_rows), 0).astype(f32)
    mine = spots[0:1, pl.ds(pl.multiple_of(core * half_rows, 128), half_rows)]
    one_hot = jnp.where(ids == mine, 1.0, 0.0).astype(bf16)
    rows_held[...] = dot(one_hot, low)
    half = pl.ds(pl.multiple_of(core * part, 128), part)
    rows_held[patches : patches + 8, :] = jnp.zeros((8, width), f32)

    def put(i, row):
        rows_held[patches + i : patches + i + 1, :] = row

    rows_held[patches + QUERY_BIAS : patches + QUERY_BIAS + 1, half] = jnp.sum(
        dq[...].astype(f32), axis=0, keepdims=True
    )
    rows_held[patches + VALUE_BIAS : patches + VALUE_BIAS + 1, half] = jnp.sum(
        dv[...].astype(f32), axis=0, keepdims=True
    )
    put(OUTPUT_BIAS, sums[0:1, :])
    put(DOWN_BIAS, sums[1:2, :])
    put(GAIN_TWO, sums[2:3, :])
    put(SHIFT_TWO, sums[3:4, :])
    put(GAIN_ONE, jnp.sum(grad_normed * normal, axis=0, keepdims=True))
    put(SHIFT_ONE, jnp.sum(grad_normed, axis=0, keepdims=True))
    hidden = bias_grad.shape[1]
    spare = 2 * hidden // width
    turns = lax.rem(lax.broadcasted_iota(jnp.int32, (spare, hidden), 1), spare)
    ranks = lax.broadcasted_iota(jnp.int32, (spare, hidden), 0)
    biases = jnp.where(turns == ranks, bias_grad[0:1, :], 0.0)
    high = biases.astype(bf16)
    both = jnp.concatenate([high.astype(f32), biases - high.astype(f32)]).astype(bf16)
    placed = dot(both, hidden_places(core, hidden, width, chips))
    rows_held[patches + 8 : patches + 8 + spare, :] = placed[:spare] + placed[spare:]
    held[:, :SMALL] = rows_held[...].T.astype(bf16)
    if blocks == 4:
        slab = up_rows // 2
        for x in range(2):
            for side, ref in ((core, out_keep), (1 - core, out_got)):
                begin = pl.multiple_of((2 * side + x) * up_rows, up_rows)
                held[pl.ds(begin, slab), SMALL:] = ref[x, :, : width // 2]
                held[pl.ds(begin + slab, slab), SMALL:] = ref[x, :, width // 2 :]
    copies = []
    for r in range(blocks):
        there = pl.ds(pl.multiple_of((r ^ chip) * up_rows, up_rows), up_rows)
        copies.append(pltpu.make_async_copy(held.at[there], grads[r], sem.at[r]))
    run_copies(copies)


def start_back(info, blocks, args, patches, chips):
    half_rows, width = args[0].shape
    columns = SMALL + width // 2 if blocks == 4 else SMALL
    return call(
        functools.partial(start_kernel, blocks, patches, chips),
        [(shaped((half_rows, width), bf16), vmem())]
        + [(shaped((width // blocks, columns), bf16), anywhere())] * blocks,
        [LOAD] * len(args),
        [info] + list(args),
        scratch=[
            pltpu.VMEM((width, columns), bf16),
            pltpu.VMEM((SMALL, width), f32),
            pltpu.SemaphoreType.DMA((blocks,)),
        ],
        cost=(2 * half_rows * width * SMALL, 10 * MIB),
    )


def split_kernel(terms, parts, shift, count, info, *refs):
    place = lax.rem(info[2] >> shift, count)
    outs, held = refs[terms * parts : terms * parts + count], refs[terms * parts + count]
    totals = []
    for part in range(parts):
        total = refs[part * terms][...].astype(f32)
        for ref in refs[part * terms + 1 : (part + 1) * terms]:
            total = total + ref[...].astype(f32)
        totals.append(total)
    held[...] = (totals[0] if parts == 1 else jnp.concatenate(totals)).reshape(held.shape)
    lead = (slice(None),) * (len(held.shape) - 3)
    for k in range(count):
        outs[k][...] = held[lead + (k ^ place,)].astype(outs[k].dtype)


def split(info, parts, shape, shift=0):
    columns = parts[0][0].shape[-1]
    count = shape[-2]
    outs = [
        (shaped(shape[:-2] + (shape[-1], columns), f32 if k == 0 else bf16), vmem())
        for k in range(count)
    ]
    arrays = [array.reshape(-1, columns) for part in parts for array in part]
    total = 1
    for extent in shape + (columns,):
        total *= extent
    return call(
        functools.partial(split_kernel, len(parts[0]), len(parts), shift, count),
        outs,
        [LOAD] * len(arrays),
        [info] + arrays,
        scratch=[pltpu.VMEM(shape + (columns,), f32)],
        limit=16,
        cost=(0, 8 * total),
    )


def swap(values, axis, bits):
    size = lax.axis_size(axis)
    return lax.ppermute(values, axis, [(i, i ^ bits) for i in range(size)])


def spread_perm(turn):
    pairs = []
    for w in range(lax.axis_size("wide")):
        for z in range(PLACES):
            there = (w - w % 2 + z // 2, 2 * (w % 2) + (turn ^ (z % 2)))
            pairs.append((w * PLACES + z, there[0] * PLACES + there[1]))
    return pairs


def unspread(turns):
    return [
        lax.ppermute(part, ("wide", "narrow"), [(b, a) for a, b in spread_perm(turn)])
        for turn, part in enumerate(turns)
    ]


def unspread_join(got, place):
    odd = (place % 2) == 1
    return jnp.stack([jnp.where(odd, got[1], got[0]), jnp.where(odd, got[0], got[1])])


def along(piece, bits):
    held = {0: piece}
    for bit in bits:
        held.update({index ^ (bit // 2): swap(part, "wide", bit) for index, part in list(held.items())})
    return [held[index] for index in range(len(held))]


def direct(piece, chips):
    return [piece] + [swap(piece, "wide", 2 * index) for index in range(1, chips)]


def fold(pieces, bits):
    held = dict(enumerate(pieces))
    for number, bit in enumerate(bits):
        step = bit // 2
        got = {i: swap(held[i ^ step], "wide", bit) for i in held if not i & step}
        if number == len(bits) - 1:
            return [held[0], got[0]]
        held = {i: (held[i].astype(f32) + got[i].astype(f32)).astype(bf16) for i in got}
    return [held[0]]


def after(values, *others):
    return lax.optimization_barrier((values,) + others)[0]


def together(*values):
    return lax.optimization_barrier(values)


class Fold:
    def __init__(self, info, pieces, bits):
        self.info, self.pieces, self.bits = info, pieces, bits
        if len(pieces[0]) == 2:
            own, x, y, d = pieces
            self.near = [swap(d[0], "wide", 2), swap(x[0], "wide", 2), swap(d[1], "wide", 4), swap(y[1], "wide", 4)]

    def second(self, *values):
        if len(self.pieces[0]) == 2:
            own, x, y, d = self.pieces
            count = len(values)
            values = together(*values, *self.near)
            values, self.near = values[:count], values[count:]
            first, second = add_pairs(self.info, y[0], self.near[0], x[1], self.near[2])
            self.far = [swap(first, "wide", 4), swap(second, "wide", 2)]
        return values

    def last(self, *values):
        if len(self.pieces[0]) == 1:
            self.parts = [fold([piece[0] for piece in self.pieces], self.bits)]
            return values
        count = len(values)
        *values, one, two = together(*values, *self.far)
        own = self.pieces[0]
        self.parts = [[own[0], self.near[1], one], [own[1], self.near[3], two]]
        return values


def local(
    tokens,
    positions,
    segments,
    position_table,
    input_weight,
    query_bias,
    value_bias,
    output_weight,
    output_bias,
    first_gain,
    first_shift,
    up_weight,
    up_bias,
    down_weight,
    down_bias,
    second_gain,
    second_shift,
    cotangent,
):
    size = lax.axis_size("wide")
    chips = size // 2
    bits = [2**i for i in range(1, size.bit_length() - 1)]
    seq_count, block, width = tokens.shape
    hidden = up_weight.shape[1]
    patches = position_table.shape[1]
    full = segments.shape[1]
    rows = width // (size * PLACES)
    part = width // 2
    own_hidden = hidden // 2
    wide, place = lax.axis_index("wide"), lax.axis_index("narrow")
    core, chip = wide % 2, wide // 2
    first_core = core == 0
    blocks = 4 if chips == 4 else 1
    info = jnp.stack([core, chip if blocks == 4 else 0 * chip, place, chip]).astype(jnp.int32)

    def pick(values, index, axis=0):
        return lax.dynamic_index_in_dim(values, index, axis, keepdims=False)

    def by_chip(pieces):
        flat = [piece.reshape((-1,) + piece.shape[-1:]) for piece in pieces]
        if blocks == 4:
            return flat
        whole = jnp.take(jnp.stack(flat), jnp.arange(chips) ^ chip, axis=0)
        return [whole.reshape((-1,) + flat[0].shape[1:])]

    def by_distance(outs, shape):
        if blocks == 4:
            return [out.reshape(shape) for out in outs]
        whole = outs[0].reshape((chips,) + shape)
        return [pick(whole, index ^ chip) for index in range(chips)]

    vectors = (
        query_bias,
        value_bias,
        output_bias,
        first_gain,
        first_shift,
        down_bias,
        second_gain,
        second_shift,
    )
    spare = up_bias.shape[0] // rows
    if blocks == 4:
        up_sorted = up_weight
    else:
        up_sorted = up_weight.reshape(rows, 4, chips // 4, 2, -1)
        up_sorted = jnp.swapaxes(up_sorted, 2, 3).reshape(rows, hidden)
    in_keep, in_send, up_keep, up_send = pack(
        info,
        input_weight,
        position_table,
        jnp.stack(vectors),
        up_bias.reshape(rows, spare),
        up_sorted,
        output_weight,
        patches,
    )

    def cross_one(piece):
        if blocks == 4:
            return [piece, swap(piece, "wide", 2), swap(piece, "wide", 4)]
        return along(piece, bits)

    def cross_two(pieces):
        if blocks == 4:
            own, x, y = pieces
            first, second = cut(info, x, y)
            return [own, x, y, swap(first, "wide", 2), swap(second, "wide", 4)]
        return pieces

    def gather_sum(pieces):
        if blocks == 4:
            return [pieces[0]] + [swap(pieces[i], "wide", 2 * i) for i in range(1, chips)]
        return fold(pieces, bits)

    def pair(keep, send):
        return arrange(info, [keep, swap(send, "wide", 1)], 0, 0)

    def narrow_pieces(piece):
        return [piece] + [swap(piece, "narrow", k) for k in range(1, PLACES)]

    def place_axis(piece):
        return piece.reshape(piece.shape[:-4] + (PLACES,) + piece.shape[-2:])

    def halves(outs, shape):
        if blocks == 4:
            shape = (shape[0] // 2,) + shape[1:]
            return [[out.reshape(shape) for out in outs[2 * r : 2 * r + 2]] for r in range(4)]
        whole = outs[0].reshape((chips,) + shape)
        return [[pick(whole, index ^ chip)] for index in range(chips)]

    in_pair = pair(in_keep, in_send)
    up_pair = pair(up_keep, up_send)
    in_piece = arrange(info, narrow_pieces(in_pair))
    in_chips = direct(in_piece, chips) if blocks == 4 else along(in_piece, bits)
    in_blocks = by_chip(in_chips)
    plane = blocks == 4
    first, second = sent(info, tokens, positions, segments)
    down_half = arrange(info, [down_weight, swap(down_weight, "narrow", 2)], 1)
    in_got = [in_pair] + [swap(in_pair, "narrow", k) for k in range(1, PLACES)]
    down_got = swap(down_half, "narrow", 1)
    in_piece, down_got, up_pair, first = together(arrange(info, in_got), down_got, up_pair, first)
    in_chips = direct(in_piece, chips) if plane else along(in_piece, bits)
    up_got = swap(up_pair, "narrow", 2)
    low = lax.ppermute(first, ("wide", "narrow"), spread_perm(0))
    down_piece = place_axis(arrange(info, [down_half, down_got]))
    up_half = arrange(info, [up_pair, up_got], 1)
    down_piece, second, up_half, low, *in_chips = together(
        down_piece, second, up_half, low, *in_chips
    )
    up_got = swap(up_half, "narrow", 1)
    in_blocks = by_chip(in_chips)
    plane = blocks == 4
    first, second = sent(info, tokens, positions, segments)
    in_got = [in_pair] + [swap(in_pair, "narrow", k) for k in range(1, PLACES)]
    down_half = [down_weight, swap(down_weight, "narrow", 2)]
    in_piece, down_half, up_pair = together(
        arrange(info, in_got), arrange(info, down_half, 1), up_pair
    )
    in_chips = direct(in_piece, chips) if plane else along(in_piece, bits)
    up_got, down_got, first = together(
        swap(up_pair, "narrow", 2), swap(down_half, "narrow", 1), first
    )
    low = lax.ppermute(first, ("wide", "narrow"), spread_perm(0))
    up_half = arrange(info, [up_pair, up_got], 1)
    up_got = swap(up_half, "narrow", 1)
    down_piece = place_axis(arrange(info, [down_half, down_got]))
    down_piece, second, *in_chips = together(down_piece, second, *in_chips)
    in_blocks = by_chip(in_chips)
    down_chips = cross_one(down_piece)
    high = lax.ppermute(second, ("wide", "narrow"), spread_perm(1))
    low, high, up_got, *down_chips = together(low, high, up_got, *down_chips)
    token_blocks = [low, high, swap(low, "wide", 1), swap(high, "wide", 1)]
    up_piece = place_axis(arrange(info, [up_half, up_got]))
    up_chips = cross_one(up_piece)
    down_chips = cross_two(down_chips)
    q, k, v, start, normed, small_full, turned, seg, spots = front(
        info, token_blocks, in_blocks, patches
    )
    q, k, v, seg, cotangent, *down_chips = together(q, k, v, seg, cotangent, *down_chips)
    cot_low, cot_high = (
        lax.ppermute(block, ("wide", "narrow"), spread_perm(turn))
        for turn, block in enumerate(pick_turns(info, cotangent))
    )
    att, total = attend(info, q, k, v, seg)
    att, cot_low, cot_high, *up_chips = together(att, cot_low, cot_high, *up_chips)
    att_far = swap(att, "wide", 1)
    up_chips = cross_two(up_chips)
    cots = [cot_low, cot_high, swap(cot_low, "wide", 1), swap(cot_high, "wide", 1)]
    if plane:
        up_blocks = [part.reshape((-1,) + part.shape[-1:]) for part in up_chips]
        down_blocks = down_chips
    else:
        up_blocks = by_chip(up_chips)
        down_blocks = [by_chip(down_chips)[0].reshape(4 * PLACES, -1, width)]
    middle, normed_two, up_bias_own = middle_front(
        info, att, att_far, start, turned, up_blocks, patches, chips
    )
    keep, send, slope, *down_grads = feed_front(
        info, normed_two, up_bias_own, cots, up_blocks, down_blocks, blocks
    )
    down_rows = own_hidden // (chips * PLACES)
    down_fold = Fold(info, halves(down_grads, (PLACES, down_rows, width)), bits)
    fed = feed_back(info, slope, cots, up_blocks, down_blocks, width)
    back, back_low, grad_hidden, bias_grad, send, normed_two = down_fold.second(
        *fed, send, normed_two
    )
    back_far = swap(back_low, "wide", 1)
    out_far = swap(send, "wide", 1)
    up_grads = weight_grad(info, normed_two, [grad_hidden], blocks, 2 if plane else 1)
    back_far, out_far, *up_grads = down_fold.last(back_far, out_far, *up_grads)
    up_fold = Fold(info, halves(up_grads, (2, PLACES, rows, own_hidden)), bits)
    down_keep, down_send = split(info, down_fold.parts, (2, 2, down_rows))
    down_got = swap(down_send, "narrow", 1)
    grad_middle, grad_att, out_keep, out_send, sums = middle_back(
        info, back, back_far, middle, turned, att, cots, up_blocks, patches, blocks
    )
    if blocks == 1:
        shape = (chips // 2, 2, PLACES * rows, width)
        out_keep = pick(out_keep.reshape(shape), core, 1)
        out_send = pick(out_send.reshape(shape), 1 - core, 1)
    grad_att, out_send, out_far, down_got = up_fold.second(grad_att, out_send, out_far, down_got)
    out_got = swap(out_send, "wide", 1)
    out_turns = unspread(output_turns(info, middle, keep, out_far, turned, patches))
    dq, dk, dv = attend_back(info, q, k, v, att, grad_att, total, seg)
    dq, dk, dv, out_got, normed, *out_turns = up_fold.last(
        dq, dk, dv, out_got, normed, *out_turns
    )
    outputs = unspread_join(out_turns, place)
    down_keep, down_send = split(info, [[down_keep, down_got]], (2, down_rows), 1)
    down_got = swap(down_send, "narrow", 2)
    up_keep, up_send = split(info, up_fold.parts, (2, 2, 2, rows))
    up_got = swap(up_send, "narrow", 1)
    start_keep, start_send = project_back(info, dq, dk, dv, in_blocks, width)
    start_send, down_got, up_got = together(start_send, down_got, up_got)
    start_far = swap(start_send, "wide", 1)
    up_keep, up_send = split(info, [[up_keep, up_got]], (2, 2, rows), 1)
    up_got = swap(up_send, "narrow", 2)
    in_grads = weight_grad(info, normed, [dq, dk, dv], blocks)
    start_far, up_got, *in_grads = together(start_far, up_got, *in_grads)
    in_sum = gather_sum(by_distance(in_grads, (2, PLACES, rows, 3 * part)))
    args = [start_keep, start_far, start, grad_middle, turned, sums, bias_grad, spots, dq, dv]
    started = start_back(info, blocks, args + [out_keep, out_got], patches, chips)
    grad_blocks, *small_grads = started
    grad_turns = unspread(pick_turns(info, grad_blocks.reshape(2, block, width)))
    down_got, up_got, *rest = together(down_got, up_got, *grad_turns, *in_sum[1:], *small_grads)
    grad_tokens = unspread_join(rest[:2], place)
    in_sum, small_grads = [in_sum[0], *rest[2 : 1 + len(in_sum)]], rest[1 + len(in_sum) :]
    if plane:
        small_sum = gather_sum(by_distance(small_grads, (2, PLACES, rows, SMALL + part)))
    else:
        out_grad = jnp.where(
            first_core,
            jnp.concatenate([out_keep, out_got]),
            jnp.concatenate([out_got, out_keep]),
        ).reshape(chips, PLACES, rows, 2, part)
        out_grad = jnp.transpose(out_grad, (0, 3, 1, 2, 4)).reshape(width, part)
        small_grads = jnp.concatenate([small_grads[0], out_grad], axis=1)
        small_sum = gather_sum(by_distance([small_grads], (2, PLACES, rows, SMALL + part)))

    def narrow_sum(parts):
        cut = split(info, [parts], (2, PLACES, rows))
        whole = cut[0]
        for index in range(1, PLACES):
            whole = whole + swap(cut[index], "narrow", index).astype(f32)
        return whole

    down_share = down_keep + down_got.astype(f32)
    up_total = up_keep + up_got.astype(f32)
    up_keep = pick(up_total, core)
    up_got = swap(pick(up_total, 1 - core).astype(bf16), "wide", 1).astype(f32)
    up_both = [up_keep.reshape(rows, chips, 1, -1), up_got.reshape(rows, chips, 1, -1)]
    up_share = jnp.where(
        first_core, jnp.concatenate(up_both, axis=2), jnp.concatenate(up_both[::-1], axis=2)
    ).reshape(rows, hidden)
    in_total = narrow_sum(in_sum)
    small_total = narrow_sum(small_sum)
    in_keep = pick(in_total, core)
    in_got = swap(pick(in_total, 1 - core).astype(bf16), "wide", 1).astype(f32)
    small_far = swap(pick(small_total, 1 - core)[:, :SMALL].astype(bf16), "wide", 1)
    small_share = pick(small_total, core)[:, :SMALL] + small_far.astype(f32)
    out_share = jnp.concatenate([small_total[0, :, SMALL:], small_total[1, :, SMALL:]], axis=1)
    in_both = [
        in_keep.reshape(rows, 3, 1, part),
        in_got.reshape(rows, 3, 1, part),
    ]
    in_share = jnp.where(
        first_core, jnp.concatenate(in_both, axis=2), jnp.concatenate(in_both[::-1], axis=2)
    ).reshape(rows, 3 * width)
    tail = [small_share[:, patches + i] for i in range(8)]
    return (
        outputs,
        grad_tokens,
        small_share[:, :patches],
        in_share,
        tail[QUERY_BIAS],
        tail[VALUE_BIAS],
        out_share,
        tail[OUTPUT_BIAS],
        tail[GAIN_ONE],
        tail[SHIFT_ONE],
        up_share,
        small_share[:, patches + 8 : patches + 8 + spare].reshape(-1),
        down_share,
        tail[DOWN_BIAS],
        tail[GAIN_TWO],
        tail[SHIFT_TWO],
    )


def solution(mesh):
    both = ("wide", "narrow")
    matrix = P(both, None)
    vector = P(both)
    block = P("wide", "narrow", None)
    gains = [matrix, matrix] + [vector] * 2 + [matrix] + [vector] * 3 + [matrix, vector, matrix]
    gains += [vector] * 3
    return jax.shard_map(
        local,
        mesh=mesh,
        in_specs=tuple([block, P("wide", "narrow"), P("wide", None)] + gains + [block]),
        out_specs=tuple([block, block] + gains),
        check_vma=False,
    )
```

```python
import functools

import jax
import jax.numpy as jnp
from jax import lax
from jax.experimental import pallas as pl
from jax.experimental.pallas import tpu as pltpu
from jax.sharding import PartitionSpec as P

HEADS = 12
PLACES = 4
epsilon = 1e-05
masked_score = -1e30

f32 = jnp.float32
bf16 = jnp.bfloat16
MIB = 1 << 20
LOAD, HELD = "load", "held"
QUERY_BIAS, VALUE_BIAS, OUTPUT_BIAS, GAIN_ONE, SHIFT_ONE, DOWN_BIAS, GAIN_TWO, SHIFT_TWO = range(8)
SMALL = 128


def dot(left, right):
    return jnp.dot(left, right, preferred_element_type=f32)


def dot_left(left, right):
    return lax.dot_general(left, right, (((0,), (0,)), ((), ())), preferred_element_type=f32)


def dot_right(left, right):
    return lax.dot_general(left, right, (((1,), (1,)), ((), ())), preferred_element_type=f32)


def call(kernel, outs, ins, args, scratch=(), grid=None, limit=14, cost=None):
    loads = []
    specs = [pl.BlockSpec(memory_space=pltpu.SMEM)]
    for index, (spec, array) in enumerate(zip(ins, args[1:], strict=True)):
        if spec == LOAD:
            whole = False
            spec = pl.BlockSpec(memory_space=pl.ANY if whole else pltpu.VMEM)
            if whole:
                loads.append(index)
        elif spec == HELD:
            spec = pl.BlockSpec(memory_space=pl.ANY)
        specs.append(spec)
    count, news = len(ins), len(loads)

    def loaded(info, *refs):
        refs, held, sem = list(refs[: -1 - news]), refs[-1 - news : -1], refs[-1]
        copies = []
        for i, index in enumerate(loads):
            copies.append(pltpu.make_async_copy(refs[index], held[i], sem.at[i]))
            refs[index] = held[i]
        run_copies(copies)
        kernel(info, *refs)

    extra = [pltpu.VMEM(args[1 + i].shape, args[1 + i].dtype) for i in loads]
    if loads:
        extra.append(pltpu.SemaphoreType.DMA((news,)))
    return pl.pallas_call(
        loaded if loads else kernel,
        out_shape=[shape for shape, _ in outs],
        in_specs=specs,
        out_specs=[spec for _, spec in outs],
        scratch_shapes=list(scratch) + extra,
        **({"grid": grid} if grid else {}),
        compiler_params=pltpu.CompilerParams(vmem_limit_bytes=limit * MIB),
        cost_estimate=pl.CostEstimate(
            flops=int(cost[0]), bytes_accessed=int(cost[1]), transcendentals=0
        ),
    )(*args)


def shaped(shape, kind):
    return jax.ShapeDtypeStruct(shape, kind)


def vmem():
    return pl.BlockSpec(memory_space=pltpu.VMEM)


def anywhere():
    return pl.BlockSpec(memory_space=pl.ANY)


def normalise(values):
    average = jnp.mean(values, axis=-1, keepdims=True)
    centered = values - average
    variance = jnp.mean(centered * centered, axis=-1, keepdims=True)
    scale = lax.rsqrt(variance + epsilon)
    return centered * scale, scale


def norm_back(normal, scale, gain, grad):
    inner = grad * gain
    return scale * (
        inner
        - jnp.mean(inner, axis=-1, keepdims=True)
        - normal * jnp.mean(inner * normal, axis=-1, keepdims=True)
    )


def run_copies(copies):
    for copy in copies:
        copy.start()
    for copy in copies:
        copy.wait()


def pack_in_kernel(patches, info, weight, table, rows_in, keep, send):
    core = info[0]
    part = weight.shape[1] // 6
    turned = rows_in[...].astype(f32).T
    empty = jnp.zeros((weight.shape[0], SMALL - patches - turned.shape[1]), f32)
    small = jnp.concatenate([table[...].astype(f32), turned, empty], axis=1).astype(bf16)
    for ref, side in ((keep, core), (send, 1 - core)):
        for i in range(3):
            there = pl.ds(pl.multiple_of((2 * i + side) * part, 128), part)
            ref[:, i * part : (i + 1) * part] = weight[:, there]
        ref[:, 3 * part :] = small


def pack_in(info, weight, table, rows_in):
    rows, columns = weight.shape[0], weight.shape[1] // 2 + SMALL
    return call(
        functools.partial(pack_in_kernel, table.shape[1]),
        [(shaped((rows, columns), bf16), vmem())] * 2,
        [vmem()] * 3,
        [info, weight, table, rows_in],
        limit=8,
        cost=(0, MIB),
    )


def pack_up_kernel(info, up, keep, send):
    step = keep.shape[1] // 4
    for ref, side in ((keep, info[0]), (send, 1 - info[0])):
        for q in range(4):
            there = pl.ds(pl.multiple_of((2 * q + side) * step, 128), step)
            ref[:, q * step : (q + 1) * step] = up[:, there]


def pack_up(info, up):
    out = (shaped((up.shape[0], up.shape[1] // 2), bf16), vmem())
    return call(pack_up_kernel, [out] * 2, [vmem()], [info, up], limit=8, cost=(0, MIB))


def sent_kernel(info, tokens, positions, segments, first, second, extra):
    place = info[2]
    block, width = tokens.shape[1], tokens.shape[2]
    full = segments.shape[1]
    extra[...] = jnp.zeros_like(extra)
    for k, out in enumerate((first, second)):
        index = k ^ (place % 2)
        row = segments[pl.ds(index, 1), :]
        row = (row - row[:, 0:1]).astype(f32)
        extra[0:1, :block] = positions[pl.ds(index, 1), :].astype(f32)
        extra[1:2, :] = row[:, :width]
        extra[2:3, : full - width] = row[:, width:]
        out[:block, :] = tokens[index]
        out[block:, :] = extra[...].astype(bf16)


def sent(info, tokens, positions, segments):
    _, block, width = tokens.shape
    one = (shaped((block + 16, width), bf16), vmem())
    return call(
        sent_kernel,
        [one, one],
        [vmem()] * 3,
        [info, tokens, positions, segments],
        scratch=[pltpu.VMEM((16, width), f32)],
        limit=8,
        cost=(0, 2 * MIB),
    )


def arrange_kernel(slot, shift, info, *refs):
    ins, out = refs[:-1], refs[-1]
    lead = len(out.shape) - 3
    place = lax.rem(info[slot] >> shift, len(ins))
    for k, ref in enumerate(ins):
        out[(slice(None),) * lead + (k ^ place,)] = ref[...]


def arrange(info, pieces, shift=0, slot=2):
    shape = pieces[0].shape
    shape = shape[:-2] + (len(pieces),) + shape[-2:]
    total = 1
    for extent in shape:
        total *= extent
    return call(
        functools.partial(arrange_kernel, slot, shift),
        [(shaped(shape, bf16), vmem())],
        [vmem()] * len(pieces),
        [info] + list(pieces),
        limit=8,
        cost=(0, 4 * total),
    )[0]


def settle_kernel(info, own, far, out):
    odd = lax.rem(info[2], 2)
    block = out.shape[1]
    rows = own.shape[1] - block
    for k, ref in enumerate((own, far)):
        for high in range(2):
            out[2 * high + (k ^ odd)] = ref[high, :block, :]
    both = (own, far)
    for high in range(2):
        pair = [ref[high, block:, :].astype(f32) for ref in both]
        for low in range(2):
            row = jnp.where(odd == low, pair[0], pair[1]).astype(bf16)
            begin = (2 * high + low) * rows
            out[PLACES, begin : begin + rows, :] = row


def settle(info, own, far):
    _, rows, width = own.shape
    block = rows * PLACES // (PLACES + 1)
    return call(
        settle_kernel,
        [(shaped((PLACES + 1, block, width), bf16), vmem())],
        [vmem()] * 2,
        [info, own, far],
        limit=8,
        cost=(0, 2 * MIB),
    )[0]


def last_kernel(info, own, x, y, d, out):
    for distance, ref in enumerate((own, x, y, d)):
        out[distance ^ info[1]] = ref[ref.shape[0] - 1]


def last_blocks(info, own, x, y, d):
    return call(
        last_kernel,
        [(shaped((4,) + own.shape[1:], bf16), vmem())],
        [vmem()] * 4,
        [info, own, x, y, d],
        limit=8,
        cost=(0, MIB),
    )[0]


def cut_kernel(info, x, y, first, second):
    half = first.shape[0]
    first[...] = y[:half]
    second[...] = x[half:]


def cut(info, x, y):
    half = x.shape[0] // 2
    outs = [
        (shaped((half,) + x.shape[1:], bf16), vmem()),
        (shaped((x.shape[0] - half,) + x.shape[1:], bf16), vmem()),
    ]
    return call(cut_kernel, outs, [LOAD] * 2, [info, x, y], limit=8, cost=(0, MIB))


def add_kernel(info, a, b, c, d, first, second):
    first[...] = (a[...].astype(f32) + b[...].astype(f32)).astype(bf16)
    second[...] = (c[...].astype(f32) + d[...].astype(f32)).astype(bf16)


def add_pairs(info, a, b, c, d):
    out = (shaped(a.shape, bf16), vmem())
    return call(add_kernel, [out] * 2, [LOAD] * 4, [info, a, b, c, d], limit=8, cost=(0, MIB))


def pick_kernel(info, blocks, first, second):
    odd = lax.rem(info[2], 2)
    first[...] = blocks[odd]
    second[...] = blocks[1 - odd]


def pick_turns(info, blocks):
    out = (shaped(blocks.shape[1:], bf16), vmem())
    return call(pick_kernel, [out] * 2, [LOAD], [info, blocks], limit=8, cost=(0, MIB))


def output_kernel(patches, info, middle, keep, far, turned, first, second):
    core, odd = info[0], lax.rem(info[2], 2)
    half = keep.shape[0]
    block = half // 2
    bias = turned[patches + DOWN_BIAS : patches + DOWN_BIAS + 1, :]
    for ref, which in ((first, odd), (second, 1 - odd)):
        here = pl.ds(pl.multiple_of(which * block, block), block)
        there = pl.ds(pl.multiple_of(core * half + which * block, block), block)
        ref[...] = (middle[there, :] + keep[here, :] + far[here, :].astype(f32) + bias).astype(bf16)


def output_turns(info, middle, keep, far, turned, patches):
    out = (shaped((keep.shape[0] // 2, keep.shape[1]), bf16), vmem())
    return call(
        functools.partial(output_kernel, patches),
        [out] * 2,
        [LOAD] * 4,
        [info, middle, keep, far, turned],
        limit=8,
        cost=(0, 6 * MIB),
    )


def front_kernel(blocks, patches, info, *refs):
    tokens_in, refs = refs[:4], refs[4:]
    weights_in, refs = refs[:blocks], refs[blocks:]
    (q_out, k_out, v_out, start_out, normed_out, small_out, turned_out, seg_out, spot_out) = refs[:9]
    held, weight, sem = refs[9:]
    core, chip, place = info[0], info[1], info[2]
    block, columns = held.shape[1] - 16, weight.shape[1] - SMALL
    part = columns // 3
    rows = weight.shape[0] // blocks
    copies = []
    for i in range(4):
        side = core if i < 2 else 1 - core
        there = 2 * side + ((i % 2) ^ (place % 2))
        copies.append(pltpu.make_async_copy(tokens_in[i], held.at[there], sem.at[i]))
    for r in range(blocks):
        there = pl.ds(pl.multiple_of((r ^ chip) * rows, rows), rows)
        copies.append(pltpu.make_async_copy(weights_in[r], weight.at[there], sem.at[4 + r]))
    run_copies(copies)
    small = weight[:, columns:]
    small_out[...] = small
    turned_out[...] = small.astype(f32).T
    vector = lambda i: turned_out[patches + i : patches + i + 1, :]
    half = pl.ds(pl.multiple_of(core * part, 128), part)
    query_bias = turned_out[patches + QUERY_BIAS : patches + QUERY_BIAS + 1, half]
    value_bias = turned_out[patches + VALUE_BIAS : patches + VALUE_BIAS + 1, half]
    gain, shift = vector(GAIN_ONE), vector(SHIFT_ONE)
    extra = held[0, block : block + 16, :].astype(f32)
    width = extra.shape[1]
    segment = jnp.concatenate([extra[1:2, :], extra[2:3, : 4 * block - width]], axis=1)
    seg_out[...] = jnp.broadcast_to(segment, seg_out.shape)
    ids = lax.broadcasted_iota(jnp.int32, (SMALL, block), 0).astype(f32)
    for b in range(4):
        here = slice(b * block, (b + 1) * block)
        spot = held[b, block : block + 16, :].astype(f32)[0:1, :block]
        spot_out[:, here] = jnp.broadcast_to(spot, (8, block))
        one_hot = jnp.where(ids == spot, 1.0, 0.0).astype(bf16)
        embedded = lax.dot_general(
            one_hot, small, (((0,), (1,)), ((), ())), preferred_element_type=f32
        )
        start = held[b, :block, :].astype(f32) + embedded
        start_out[here, :] = start
        normal, _ = normalise(start)
        normed = (normal * gain + shift).astype(bf16)
        normed_out[here, :] = normed
        projected = dot(normed, weight[:, :columns])
        query = (projected[:, :part] + query_bias).astype(bf16).astype(f32) * 0.125
        q_out[here, :] = query.astype(bf16)
        k_out[here, :] = projected[:, part : 2 * part].astype(bf16)
        v_out[here, :] = (projected[:, 2 * part :] + value_bias).astype(bf16)


def front(info, tokens, weights, patches):
    blocks = len(weights)
    block, width = tokens[0].shape[0] - 16, tokens[0].shape[1]
    columns = weights[0].shape[1]
    part = (columns - SMALL) // 3
    rows = 4 * block
    return call(
        functools.partial(front_kernel, blocks, patches),
        [
            (shaped((rows, part), bf16), vmem()),
            (shaped((rows, part), bf16), vmem()),
            (shaped((rows, part), bf16), vmem()),
            (shaped((rows, width), f32), vmem()),
            (shaped((rows, width), bf16), vmem()),
            (shaped((width, SMALL), bf16), vmem()),
            (shaped((SMALL, width), f32), vmem()),
            (shaped((8, rows), f32), vmem()),
            (shaped((8, rows), f32), vmem()),
        ],
        [HELD] * (4 + blocks),
        [info] + list(tokens) + list(weights),
        scratch=[
            pltpu.VMEM((4, block + 16, width), bf16),
            pltpu.VMEM((width, columns), bf16),
            pltpu.SemaphoreType.DMA((4 + blocks,)),
        ],
        cost=(2 * rows * width * columns, 12 * MIB),
    )


def fill_bias(bias, seg):
    block = bias.shape[1]
    wide = seg[...]
    tall = jnp.broadcast_to(wide[0:1, :], (128, wide.shape[1])).T[:, 0:1]
    base = 0
    for b in range(4):
        many = (b + 1) * block
        key = lax.broadcasted_iota(jnp.int32, (many, block), 0)
        ask = lax.broadcasted_iota(jnp.int32, (many, block), 1) + b * block
        same = tall[:many] == wide[0:1, b * block : (b + 1) * block]
        bias[base : base + many, :] = jnp.where((key <= ask) & same, 0.0, masked_score)
        base += many


def turn(values):
    return values.astype(f32).T.astype(bf16)


def attend_kernel(info, q, k, v, seg, out, total, bias):
    block = bias.shape[1]

    @pl.when(pl.program_id(0) == 0)
    def _():
        fill_bias(bias, seg)

    turned_q, turned_v = turn(q[...]), turn(v[...])
    side = lax.broadcasted_iota(jnp.int32, (128, block), 0) // 64
    base = 0
    for b in range(4):
        many = (b + 1) * block
        here = slice(b * block, (b + 1) * block)
        mixed = []
        for h in range(2):
            ask = jnp.where(side == h, turned_q[:, here].astype(f32), 0.0).astype(bf16)
            scores = dot(k[:many, :], ask) + bias[base : base + many, :]
            top = jnp.max(scores, axis=0, keepdims=True)
            raised = jnp.exp(scores - top)
            mass = jnp.sum(raised, axis=0, keepdims=True)
            total[0, h : h + 1, here] = top + jnp.log(mass)
            part = dot(turned_v[64 * h : 64 * h + 64, :many], raised.astype(bf16))
            mixed.append(part * (1.0 / mass))
        out[here, :] = jnp.concatenate(mixed, axis=0).T.astype(bf16)
        base += many


def attend(info, q, k, v, seg):
    rows, part = q.shape
    pairs = part // 128
    column = pl.BlockSpec((rows, 128), lambda i: (0, i))
    whole = pl.BlockSpec(seg.shape, lambda i: (0, 0))
    return call(
        attend_kernel,
        [
            (shaped((rows, part), bf16), column),
            (shaped((pairs, 8, rows), f32), pl.BlockSpec((1, 8, rows), lambda i: (i, 0, 0))),
        ],
        [column, column, column, whole],
        [info, q, k, v, seg],
        scratch=[pltpu.VMEM((10 * rows // 4, rows // 4), f32)],
        grid=(pairs,),
        cost=(6 * rows * rows * part, 4 * MIB),
    )


def attend_back_kernel(info, q, k, v, o, g, total, seg, dq, dk, dv, bias, dk_sum, dv_sum):
    block = bias.shape[1]

    @pl.when(pl.program_id(0) == 0)
    def _():
        fill_bias(bias, seg)

    wide_g = g[...].astype(f32).T
    product = wide_g * o[...].astype(f32).T
    inner = [jnp.sum(product[64 * h : 64 * h + 64], axis=0, keepdims=True) for h in range(2)]
    turned_q, turned_k = turn(q[...]), turn(k[...])
    turned_g = wide_g.astype(bf16)
    side = lax.broadcasted_iota(jnp.int32, (128, block), 0) // 64
    flat = lax.broadcasted_iota(jnp.int32, (block, 128), 1) // 64
    dk_sum[...] = jnp.zeros_like(dk_sum)
    dv_sum[...] = jnp.zeros_like(dv_sum)
    base = 0
    for b in range(4):
        many = (b + 1) * block
        here = slice(b * block, (b + 1) * block)
        grads = []
        for h in range(2):
            ask = jnp.where(side == h, turned_q[:, here].astype(f32), 0.0).astype(bf16)
            ask_g = jnp.where(side == h, turned_g[:, here].astype(f32), 0.0).astype(bf16)
            scores = dot(k[:many, :], ask) + bias[base : base + many, :]
            probs = jnp.exp(scores - total[0, h : h + 1, here])
            grad_probs = dot(v[:many, :], ask_g)
            grad_scores = (probs * (grad_probs - inner[h][:, here])).astype(bf16)
            own_q = jnp.where(flat == h, q[here, :].astype(f32), 0.0).astype(bf16)
            own_g = jnp.where(flat == h, g[here, :].astype(f32), 0.0).astype(bf16)
            dv_sum[:many, :] += dot(probs.astype(bf16), own_g)
            dk_sum[:many, :] += dot(grad_scores, own_q)
            grads.append(dot(turned_k[64 * h : 64 * h + 64, :many], grad_scores))
        dq[here, :] = (jnp.concatenate(grads, axis=0).T * 0.125).astype(bf16)
        base += many
    dk[...] = dk_sum[...].astype(bf16)
    dv[...] = dv_sum[...].astype(bf16)


def attend_back(info, q, k, v, o, g, total, seg):
    rows, part = q.shape
    pairs = part // 128
    column = pl.BlockSpec((rows, 128), lambda i: (0, i))
    whole = pl.BlockSpec(seg.shape, lambda i: (0, 0))
    out = (shaped((rows, part), bf16), column)
    return call(
        attend_back_kernel,
        [out, out, out],
        [column] * 5 + [pl.BlockSpec((1, 8, rows), lambda i: (i, 0, 0)), whole],
        [info, q, k, v, o, g, total, seg],
        scratch=[
            pltpu.VMEM((10 * rows // 4, rows // 4), f32),
            pltpu.VMEM((rows, 128), f32),
            pltpu.VMEM((rows, 128), f32),
        ],
        grid=(pairs,),
        cost=(15 * rows * rows * part, 6 * MIB),
    )


def cotangent_copies(info, pieces, held, sems):
    core, place = info[0], info[2]
    copies = []
    for i in range(4):
        side = core if i < 2 else 1 - core
        there = 2 * side + ((i % 2) ^ (place % 2))
        copies.append(pltpu.make_async_copy(pieces[i], held.at[there], sems[i]))
    return copies


def gelu_parts(values):
    scale = 0.7978845608028654
    square = values * values
    slope = jnp.tanh(values * (scale + (scale * 0.044715) * square))
    half = 0.5 * (1.0 + slope)
    grad = half + 0.5 * values * (1.0 - slope * slope) * (
        scale + (3.0 * scale * 0.044715) * square
    )
    return values * half, grad


def piece_copies(pieces, target, info, sem, lanes=None):
    chip = info[1]
    rows = pieces[0].shape[0]
    copies, base = [], 0
    for i, ref in enumerate(pieces):
        distance = min(i, 3)
        begin = pl.multiple_of((distance ^ chip) * rows, rows)
        if i == 4:
            begin = pl.multiple_of(begin + rows // 2, rows // 2)
        source = ref if lanes is None else ref.at[:, lanes]
        there = target.at[pl.ds(begin, ref.shape[0])]
        copies.append(pltpu.make_async_copy(source, there, sem.at[i]))
    return copies


def block_copies(pieces, target, info, sem):
    if len(pieces) == 1:
        return [pltpu.make_async_copy(pieces[0], target, sem.at[0])]
    copies = []
    for i, ref in enumerate(pieces):
        begin = (min(i, 3) ^ info[1]) * PLACES + (2 if i == 4 else 0)
        count = 2 if i >= 3 else PLACES
        copies.append(
            pltpu.make_async_copy(ref.at[pl.ds(0, count)], target.at[pl.ds(begin, count)], sem.at[i])
        )
    return copies


def hidden_places(core, hidden, width, chips):
    spare = 2 * hidden // width
    share = hidden // chips
    device = share // PLACES
    rows = device // spare
    unit = lax.broadcasted_iota(jnp.int32, (hidden, 1), 0)
    rest = lax.rem(unit, share)
    row = ((2 * (unit // share) + core) * PLACES + rest // device) * rows + lax.rem(rest, rows)
    lane = lax.broadcasted_iota(jnp.int32, (hidden, width), 1)
    return jnp.where(lane == row, 1.0, 0.0).astype(bf16)


def hidden_turns(spare, hidden, chips):
    device = hidden // (chips * PLACES)
    unit = lax.broadcasted_iota(jnp.int32, (spare, hidden), 1)
    return lax.rem(unit, device) // (device // spare) == lax.broadcasted_iota(
        jnp.int32, (spare, hidden), 0
    )


def middle_kernel(patches, chips, hidden, info, att, att_far, start, turned, *refs):
    weights, refs = refs[:-4], refs[-4:]
    middle_out, normed_out, bias_out, weight_out = refs
    core = info[0]
    rows, width = start.shape
    part, tile = width // 2, rows // 4
    if len(weights) == 2:
        block = weights[0].shape[1]
        for side, ref in ((core, weights[0]), (1 - core, weights[1])):
            for q in range(4):
                begin = pl.multiple_of((2 * q + side) * block, block)
                weight_out[pl.ds(begin, block), :] = ref[q]
    else:
        weight_out[...] = weights[0][...]
    spare = 2 * hidden // width
    biases = turned[patches + 8 : patches + 8 + spare, :].astype(bf16)
    spread_out = dot_right(biases, hidden_places(core, hidden, width, chips))
    bias = jnp.sum(
        jnp.where(hidden_turns(spare, hidden, chips), spread_out, 0.0), axis=0, keepdims=True
    )
    bias_out[...] = jnp.broadcast_to(bias, bias_out.shape)
    vector = lambda i: turned[patches + i : patches + i + 1, :]
    own = pl.ds(pl.multiple_of(core * part, 128), part)
    far = pl.ds(pl.multiple_of((1 - core) * part, 128), part)
    gain, shift, out_bias = vector(GAIN_TWO), vector(SHIFT_TWO), vector(OUTPUT_BIAS)
    for t in range(4):
        here = slice(t * tile, (t + 1) * tile)
        mixed = dot(att[here, :], weight_out[own, :]) + dot(att_far[here, :], weight_out[far, :])
        middle = start[here, :] + mixed + out_bias
        middle_out[here, :] = middle
        normal, _ = normalise(middle)
        normed_out[here, :] = (normal * gain + shift).astype(bf16)


def middle_front(info, att, att_far, start, turned, weights, hidden, patches, chips):
    rows, width = start.shape
    return call(
        functools.partial(middle_kernel, patches, chips, hidden),
        [
            (shaped((rows, width), f32), vmem()),
            (shaped((rows, width), bf16), vmem()),
            (shaped((8, hidden), f32), vmem()),
            (shaped((width, width), bf16), vmem()),
        ],
        [LOAD] * (4 + len(weights)),
        [info, att, att_far, start, turned] + list(weights),
        cost=(2 * rows * width * width, 12 * MIB),
    )


def feed_front_kernel(ups, downs, blocks, info, normed, up_bias, *refs):
    cot_in, refs = refs[:4], refs[4:]
    up_in, refs = refs[:ups], refs[ups:]
    down_in, refs = refs[:downs], refs[downs:]
    keep_out, send_out, slope_out, refs = refs[0], refs[1], refs[2], refs[3:]
    cut = 2 if blocks == 4 else 1
    down_grads, refs = refs[: cut * blocks], refs[cut * blocks :]
    cot, up, down, out_sum, down_grad, cot_sem, up_sem, down_sem = refs
    core, chip = info[0], info[1]
    rows, width = normed.shape
    hidden = up.shape[1]
    chunk = hidden // 4
    early = piece_copies(up_in, up, info, up_sem)
    late = cotangent_copies(info, cot_in, cot, [cot_sem.at[i] for i in range(4)])
    late += block_copies(down_in, down, info, down_sem)
    for copy in early + late:
        copy.start()
    for copy in early + late:
        copy.wait()
    out_sum[...] = jnp.zeros_like(out_sum)

    def one_chunk(q, carry):
        lanes = pl.ds(pl.multiple_of(q * chunk, 128), chunk)
        down_part = down[pl.ds(q * PLACES, PLACES)].reshape(chunk, width)
        value, slope = gelu_parts(dot(normed[...], up[:, lanes]) + up_bias[0:1, lanes])
        value = value.astype(bf16)
        slope_out[:, lanes] = slope.astype(bf16)
        out_sum[...] += dot(value, down_part)
        flat = cot[...].reshape(rows, width)
        grad = dot_left(value, flat).astype(bf16)
        down_grad[pl.ds(q * PLACES, PLACES)] = grad.reshape(PLACES, chunk // PLACES, width)
        return carry

    lax.fori_loop(0, 4, one_chunk, 0)
    outs = []
    if blocks == 4:
        for r in range(blocks):
            for h in range(2):
                there = pl.ds((r ^ chip) * PLACES + 2 * h, 2)
                i = 2 * r + h
                outs.append(pltpu.make_async_copy(down_grad.at[there], down_grads[i], down_sem.at[i]))
    else:
        outs.append(pltpu.make_async_copy(down_grad, down_grads[0], down_sem.at[0]))
    for copy in outs:
        copy.start()
    half = rows // 2
    own = pl.ds(pl.multiple_of(core * half, half), half)
    far = pl.ds(pl.multiple_of((1 - core) * half, half), half)
    keep_out[...] = out_sum[own, :]
    send_out[...] = out_sum[far, :].astype(bf16)
    for copy in outs:
        copy.wait()


def feed_front(info, normed, up_bias, cots, ups, downs, blocks):
    rows, width = normed.shape
    hidden = up_bias.shape[1]
    whole = (4 * PLACES, hidden // (4 * PLACES), width)
    grads = [(2,) + whole[1:]] * 8 if blocks == 4 else [whole]
    return call(
        functools.partial(feed_front_kernel, len(ups), len(downs), blocks),
        [
            (shaped((rows // 2, width), f32), vmem()),
            (shaped((rows // 2, width), bf16), vmem()),
            (shaped((rows, hidden), bf16), vmem()),
        ]
        + [(shaped(one, bf16), anywhere()) for one in grads],
        [LOAD] * 2 + [HELD] * (4 + len(ups) + len(downs)),
        [info, normed, up_bias] + list(cots) + list(ups) + list(downs),
        scratch=[
            pltpu.VMEM((4, rows // 4, width), bf16),
            pltpu.VMEM((width, hidden), bf16),
            pltpu.VMEM(whole, bf16),
            pltpu.VMEM((rows, width), f32),
            pltpu.VMEM(whole, bf16),
            pltpu.SemaphoreType.DMA((4,)),
            pltpu.SemaphoreType.DMA((len(ups),)),
            pltpu.SemaphoreType.DMA((8,)),
        ],
        limit=20,
        cost=(6 * rows * width * hidden, 24 * MIB),
    )


def feed_back_kernel(ups, downs, info, slope, *refs):
    cot_in, refs = refs[:4], refs[4:]
    up_in, refs = refs[:ups], refs[ups:]
    down_in, refs = refs[:downs], refs[downs:]
    back_out, low_out, grad_out, bias_out, cot, up, down, cot_sem, up_sem, down_sem = refs
    rows, hidden = slope.shape
    width = up.shape[0]
    chunk = hidden // 4
    copies = cotangent_copies(info, cot_in, cot, [cot_sem.at[i] for i in range(4)])
    copies += block_copies(down_in, down, info, down_sem)
    copies += piece_copies(up_in, up, info, up_sem)
    run_copies(copies)
    back_out[...] = jnp.zeros_like(back_out)

    def one_chunk(q, carry):
        lanes = pl.ds(pl.multiple_of(q * chunk, 128), chunk)
        down_part = down[pl.ds(q * PLACES, PLACES)].reshape(chunk, width)
        flat = cot[...].reshape(rows, width)
        grad = (dot_right(flat, down_part) * slope[:, lanes].astype(f32)).astype(bf16)
        grad_out[:, lanes] = grad
        bias_out[:, lanes] = jnp.broadcast_to(
            jnp.sum(grad.astype(f32), axis=0, keepdims=True), (8, chunk)
        )
        back_out[...] += dot_right(grad, up[:, lanes])
        return carry

    lax.fori_loop(0, 4, one_chunk, 0)
    low_out[...] = back_out[...].astype(bf16)


def feed_back(info, slope, cots, ups, downs, width):
    rows, hidden = slope.shape
    whole = (4 * PLACES, hidden // (4 * PLACES), width)
    return call(
        functools.partial(feed_back_kernel, len(ups), len(downs)),
        [
            (shaped((rows, width), f32), vmem()),
            (shaped((rows, width), bf16), vmem()),
            (shaped((rows, hidden), bf16), vmem()),
            (shaped((8, hidden), f32), vmem()),
        ],
        [LOAD] + [HELD] * (4 + len(ups) + len(downs)),
        [info, slope] + list(cots) + list(ups) + list(downs),
        scratch=[
            pltpu.VMEM((4, rows // 4, width), bf16),
            pltpu.VMEM((width, hidden), bf16),
            pltpu.VMEM(whole, bf16),
            pltpu.SemaphoreType.DMA((4,)),
            pltpu.SemaphoreType.DMA((len(ups),)),
            pltpu.SemaphoreType.DMA((len(downs),)),
        ],
        limit=20,
        cost=(4 * rows * width * hidden, 24 * MIB),
    )


def weight_kernel(pieces, cut, count, info, left, *refs):
    parts, outs = refs[:count], refs[count : count + pieces * cut]
    held, sem = refs[count + pieces * cut :][:2]
    chip = info[1]
    width = left.shape[1]
    base = 0
    for ref in parts:
        for begin in range(0, ref.shape[1], 384):
            size = min(384, ref.shape[1] - begin)
            product = dot_left(left[...], ref[:, begin : begin + size]).astype(bf16)
            held[:, base : base + size] = product
            base += size
    copies = []
    rows = width // (pieces * cut)
    for r in range(pieces):
        for h in range(cut):
            there = pl.ds(pl.multiple_of(((r ^ chip) * cut + h) * rows, rows), rows)
            i = cut * r + h
            copies.append(pltpu.make_async_copy(held.at[there], outs[i], sem.at[i]))
    run_copies(copies)


def weight_grad(info, left, parts, pieces, cut=1):
    rows, width = left.shape
    columns = sum(part.shape[1] for part in parts)
    count = pieces * cut
    return call(
        functools.partial(weight_kernel, pieces, cut, len(parts)),
        [(shaped((width // count, columns), bf16), anywhere())] * count,
        [LOAD] * (1 + len(parts)),
        [info, left] + list(parts),
        scratch=[pltpu.VMEM((width, columns), bf16), pltpu.SemaphoreType.DMA((count,))],
        cost=(2 * rows * width * columns, 8 * MIB),
    )


def middle_back_kernel(blocks, patches, info, back, back_far, middle, turned, att, weight, *refs):
    cot_in, refs = refs[:4], refs[4:]
    grad_out, attended_out, keep_out, send_out, sums_out, cot, branch, sem = refs
    core = info[0]
    rows, width = middle.shape
    tile = rows // 4
    part = width // 2
    run_copies(cotangent_copies(info, cot_in, cot, [sem.at[i] for i in range(4)]))
    gain = turned[patches + GAIN_TWO : patches + GAIN_TWO + 1, :]
    own_rows = pl.ds(pl.multiple_of(core * part, 128), part)
    for t in range(4):
        here = slice(t * tile, (t + 1) * tile)
        grad_normed = back[here, :] + back_far[here, :].astype(f32)
        normal, scale = normalise(middle[here, :])
        grad_outputs = cot[t].astype(f32)
        grad = grad_outputs + norm_back(normal, scale, gain, grad_normed)
        low = grad.astype(bf16)
        branch[here, :] = low
        attended_out[here, :] = dot_right(low, weight[own_rows, :]).astype(bf16)

        @pl.when(core == t // 2)
        def _():
            grad_out[(t % 2) * tile : (t % 2 + 1) * tile, :] = grad
            sums = jnp.concatenate(
                [
                    jnp.sum(low.astype(f32), axis=0, keepdims=True),
                    jnp.sum(grad_outputs, axis=0, keepdims=True),
                    jnp.sum(grad_normed * normal, axis=0, keepdims=True),
                    jnp.sum(grad_normed, axis=0, keepdims=True),
                    jnp.zeros((4, width), f32),
                ],
                axis=0,
            )
            sums_out[...] = sums if t % 2 == 0 else sums_out[...] + sums

    weight_grad = dot_left(att[...], branch[...]).astype(bf16)
    shape = send_out.shape[:1] + (2,) + send_out.shape[1:]
    sorted_grad = weight_grad.reshape(shape) if blocks == 4 else None
    if blocks == 4:
        for c in range(2):

            @pl.when(core == c)
            def _():
                keep_out[...] = sorted_grad[:, c]
                send_out[...] = sorted_grad[:, 1 - c]

    else:
        keep_out[...] = weight_grad
        send_out[...] = weight_grad


def middle_back(info, back, back_far, middle, turned, att, weight, cots, patches, blocks):
    rows, width = middle.shape
    part = width // 2
    slab = (2, part // 4, width) if blocks == 4 else (part, width)
    return call(
        functools.partial(middle_back_kernel, blocks, patches),
        [
            (shaped((rows // 2, width), f32), vmem()),
            (shaped((rows, part), bf16), vmem()),
            (shaped(slab, bf16), vmem()),
            (shaped(slab, bf16), vmem()),
            (shaped((8, width), f32), vmem()),
        ],
        [LOAD] * 6 + [HELD] * 4,
        [info, back, back_far, middle, turned, att, weight] + list(cots),
        scratch=[
            pltpu.VMEM((4, rows // 4, width), bf16),
            pltpu.VMEM((rows, width), bf16),
            pltpu.SemaphoreType.DMA((4,)),
        ],
        cost=(4 * rows * width * part, 14 * MIB),
    )


def project_kernel(blocks, info, *refs):
    dq, dk, dv, refs = refs[0], refs[1], refs[2], refs[3:]
    weights_in, refs = refs[:blocks], refs[blocks:]
    keep_out, send_out, weight, sem = refs
    core, chip = info[0], info[1]
    rows, part = dq.shape
    width = weight.shape[0]
    up_rows = width // blocks
    half_rows = rows // 2
    copies = []
    for r in range(blocks):
        there = pl.ds(pl.multiple_of((r ^ chip) * up_rows, up_rows), up_rows)
        copies.append(
            pltpu.make_async_copy(
                weights_in[r].at[:, : 3 * part], weight.at[there], sem.at[r]
            )
        )
    run_copies(copies)

    def product(first):
        here = pl.ds(pl.multiple_of(first, 128), half_rows)
        return (
            dot_right(dq[here, :], weight[:, :part])
            + dot_right(dk[here, :], weight[:, part : 2 * part])
            + dot_right(dv[here, :], weight[:, 2 * part :])
        )

    send_out[...] = product((1 - core) * half_rows).astype(bf16)
    keep_out[...] = product(core * half_rows)


def project_back(info, dq, dk, dv, weights, width):
    blocks = len(weights)
    rows, part = dq.shape
    return call(
        functools.partial(project_kernel, blocks),
        [
            (shaped((rows // 2, width), f32), vmem()),
            (shaped((rows // 2, width), bf16), vmem()),
        ],
        [LOAD] * 3 + [HELD] * blocks,
        [info, dq, dk, dv] + list(weights),
        scratch=[
            pltpu.VMEM((width, 3 * part), bf16),
            pltpu.SemaphoreType.DMA((blocks,)),
        ],
        cost=(6 * rows * width * part, 8 * MIB),
    )


def start_kernel(blocks, patches, chips, info, *refs):
    (keep, far, start, grad_middle, turned, sums, bias_grad, spots, dq, dv, out_keep, out_got) = refs[:12]
    refs = refs[12:]
    low_out, refs = refs[0], refs[1:]
    grads, refs = refs[:blocks], refs[blocks:]
    held, rows_held, sem = refs
    core, chip = info[0], info[1]
    rows, part = dq.shape
    half_rows, width = keep.shape
    up_rows = width // blocks
    gain = turned[patches + GAIN_ONE : patches + GAIN_ONE + 1, :]
    own = pl.ds(pl.multiple_of(core * half_rows, half_rows), half_rows)
    grad_normed = keep[...] + far[...].astype(f32)
    normal, scale = normalise(start[own, :])
    grad = grad_middle[...] + norm_back(normal, scale, gain, grad_normed)
    low = grad.astype(bf16)
    low_out[...] = low
    ids = lax.broadcasted_iota(jnp.int32, (SMALL, half_rows), 0).astype(f32)
    mine = spots[0:1, pl.ds(pl.multiple_of(core * half_rows, 128), half_rows)]
    one_hot = jnp.where(ids == mine, 1.0, 0.0).astype(bf16)
    rows_held[...] = dot(one_hot, low)
    half = pl.ds(pl.multiple_of(core * part, 128), part)
    rows_held[patches : patches + 8, :] = jnp.zeros((8, width), f32)

    def put(i, row):
        rows_held[patches + i : patches + i + 1, :] = row

    rows_held[patches + QUERY_BIAS : patches + QUERY_BIAS + 1, half] = jnp.sum(
        dq[...].astype(f32), axis=0, keepdims=True
    )
    rows_held[patches + VALUE_BIAS : patches + VALUE_BIAS + 1, half] = jnp.sum(
        dv[...].astype(f32), axis=0, keepdims=True
    )
    put(OUTPUT_BIAS, sums[0:1, :])
    put(DOWN_BIAS, sums[1:2, :])
    put(GAIN_TWO, sums[2:3, :])
    put(SHIFT_TWO, sums[3:4, :])
    put(GAIN_ONE, jnp.sum(grad_normed * normal, axis=0, keepdims=True))
    put(SHIFT_ONE, jnp.sum(grad_normed, axis=0, keepdims=True))
    hidden = bias_grad.shape[1]
    spare = 2 * hidden // width
    biases = jnp.where(hidden_turns(spare, hidden, chips), bias_grad[0:1, :], 0.0)
    high = biases.astype(bf16)
    both = jnp.concatenate([high.astype(f32), biases - high.astype(f32)]).astype(bf16)
    placed = dot(both, hidden_places(core, hidden, width, chips))
    rows_held[patches + 8 : patches + 8 + spare, :] = placed[:spare] + placed[spare:]
    held[:, :SMALL] = rows_held[...].T.astype(bf16)
    if blocks == 4:
        slab = up_rows // 2
        for x in range(2):
            for side, ref in ((core, out_keep), (1 - core, out_got)):
                begin = pl.multiple_of((2 * side + x) * up_rows, up_rows)
                held[pl.ds(begin, slab), SMALL:] = ref[x, :, : width // 2]
                held[pl.ds(begin + slab, slab), SMALL:] = ref[x, :, width // 2 :]
    copies = []
    for r in range(blocks):
        there = pl.ds(pl.multiple_of((r ^ chip) * up_rows, up_rows), up_rows)
        copies.append(pltpu.make_async_copy(held.at[there], grads[r], sem.at[r]))
    run_copies(copies)


def start_back(info, blocks, args, patches, chips):
    half_rows, width = args[0].shape
    columns = SMALL + width // 2 if blocks == 4 else SMALL
    return call(
        functools.partial(start_kernel, blocks, patches, chips),
        [(shaped((half_rows, width), bf16), vmem())]
        + [(shaped((width // blocks, columns), bf16), anywhere())] * blocks,
        [LOAD] * len(args),
        [info] + list(args),
        scratch=[
            pltpu.VMEM((width, columns), bf16),
            pltpu.VMEM((SMALL, width), f32),
            pltpu.SemaphoreType.DMA((blocks,)),
        ],
        cost=(2 * half_rows * width * SMALL, 10 * MIB),
    )


def split_kernel(terms, parts, shift, count, info, *refs):
    place = lax.rem(info[2] >> shift, count)
    outs, held = refs[terms * parts : terms * parts + count], refs[terms * parts + count]
    totals = []
    for part in range(parts):
        total = refs[part * terms][...].astype(f32)
        for ref in refs[part * terms + 1 : (part + 1) * terms]:
            total = total + ref[...].astype(f32)
        totals.append(total)
    held[...] = (totals[0] if parts == 1 else jnp.concatenate(totals)).reshape(held.shape)
    lead = (slice(None),) * (len(held.shape) - 3)
    for k in range(count):
        outs[k][...] = held[lead + (k ^ place,)].astype(outs[k].dtype)


def split(info, parts, shape, shift=0):
    columns = parts[0][0].shape[-1]
    count = shape[-2]
    outs = [
        (shaped(shape[:-2] + (shape[-1], columns), f32 if k == 0 else bf16), vmem())
        for k in range(count)
    ]
    arrays = [array.reshape(-1, columns) for part in parts for array in part]
    total = 1
    for extent in shape + (columns,):
        total *= extent
    return call(
        functools.partial(split_kernel, len(parts[0]), len(parts), shift, count),
        outs,
        [LOAD] * len(arrays),
        [info] + arrays,
        scratch=[pltpu.VMEM(shape + (columns,), f32)],
        limit=16,
        cost=(0, 8 * total),
    )


def swap(values, axis, bits):
    size = lax.axis_size(axis)
    return lax.ppermute(values, axis, [(i, i ^ bits) for i in range(size)])


def spread_perm(turn):
    pairs = []
    for w in range(lax.axis_size("wide")):
        for z in range(PLACES):
            there = (w - w % 2 + z // 2, 2 * (w % 2) + (turn ^ (z % 2)))
            pairs.append((w * PLACES + z, there[0] * PLACES + there[1]))
    return pairs


def unspread_turn(part, turn):
    return lax.ppermute(part, ("wide", "narrow"), [(b, a) for a, b in spread_perm(turn)])


def unspread_join(got, place):
    odd = (place % 2) == 1
    return jnp.stack([jnp.where(odd, got[1], got[0]), jnp.where(odd, got[0], got[1])])


def along(piece, bits):
    held = {0: piece}
    for bit in bits:
        held.update({index ^ (bit // 2): swap(part, "wide", bit) for index, part in list(held.items())})
    return [held[index] for index in range(len(held))]


def direct(piece, chips):
    return [piece] + [swap(piece, "wide", 2 * index) for index in range(1, chips)]


def fold(pieces, bits):
    held = dict(enumerate(pieces))
    for number, bit in enumerate(bits):
        step = bit // 2
        got = {i: swap(held[i ^ step], "wide", bit) for i in held if not i & step}
        if number == len(bits) - 1:
            return [held[0], got[0]]
        held = {i: (held[i].astype(f32) + got[i].astype(f32)).astype(bf16) for i in got}
    return [held[0]]


def after(values, *others):
    return lax.optimization_barrier((values,) + others)[0]


def together(*values):
    return lax.optimization_barrier(values)


class Fold:
    def __init__(self, info, pieces, bits):
        self.info, self.pieces, self.bits = info, pieces, bits
        if len(pieces[0]) == 2:
            own, x, y, d = pieces
            self.near = [swap(d[0], "wide", 2), swap(x[0], "wide", 2), swap(d[1], "wide", 4), swap(y[1], "wide", 4)]

    def second(self, *values):
        if len(self.pieces[0]) == 2:
            own, x, y, d = self.pieces
            count = len(values)
            values = together(*values, *self.near)
            values, self.near = values[:count], values[count:]
            first, second = add_pairs(self.info, y[0], self.near[0], x[1], self.near[2])
            self.far = [swap(first, "wide", 4), swap(second, "wide", 2)]
        return values

    def last(self, *values):
        if len(self.pieces[0]) == 1:
            self.parts = [fold([piece[0] for piece in self.pieces], self.bits)]
            return values
        count = len(values)
        *values, one, two = together(*values, *self.far)
        own = self.pieces[0]
        self.parts = [[own[0], self.near[1], one], [own[1], self.near[3], two]]
        return values


def local(
    tokens,
    positions,
    segments,
    position_table,
    input_weight,
    query_bias,
    value_bias,
    output_weight,
    output_bias,
    first_gain,
    first_shift,
    up_weight,
    up_bias,
    down_weight,
    down_bias,
    second_gain,
    second_shift,
    cotangent,
):
    size = lax.axis_size("wide")
    chips = size // 2
    bits = [2**i for i in range(1, size.bit_length() - 1)]
    seq_count, block, width = tokens.shape
    hidden = up_weight.shape[1]
    patches = position_table.shape[1]
    full = segments.shape[1]
    rows = width // (size * PLACES)
    part = width // 2
    own_hidden = hidden // 2
    wide, place = lax.axis_index("wide"), lax.axis_index("narrow")
    core, chip = wide % 2, wide // 2
    first_core = core == 0
    blocks = 4 if chips == 4 else 1
    info = jnp.stack([core, chip if blocks == 4 else 0 * chip, place, chip]).astype(jnp.int32)

    def pick(values, index, axis=0):
        return lax.dynamic_index_in_dim(values, index, axis, keepdims=False)

    def by_chip(pieces):
        flat = [piece.reshape((-1,) + piece.shape[-1:]) for piece in pieces]
        if blocks == 4:
            return flat
        whole = jnp.take(jnp.stack(flat), jnp.arange(chips) ^ chip, axis=0)
        return [whole.reshape((-1,) + flat[0].shape[1:])]

    def by_distance(outs, shape):
        if blocks == 4:
            return [out.reshape(shape) for out in outs]
        whole = outs[0].reshape((chips,) + shape)
        return [pick(whole, index ^ chip) for index in range(chips)]

    vectors = (
        query_bias,
        value_bias,
        output_bias,
        first_gain,
        first_shift,
        down_bias,
        second_gain,
        second_shift,
    )
    spare = up_bias.shape[0] // rows
    plane = blocks == 4
    up_sorted = up_weight
    if not plane:
        up_sorted = up_weight.reshape(rows, 4, chips // 4, 2, -1)
        up_sorted = jnp.swapaxes(up_sorted, 2, 3).reshape(rows, hidden)

    def cross_one(piece):
        if blocks == 4:
            return [piece, swap(piece, "wide", 2), swap(piece, "wide", 4)]
        return along(piece, bits)

    def cross_two(pieces):
        if blocks == 4:
            own, x, y = pieces
            first, second = cut(info, x, y)
            return [own, x, y, swap(first, "wide", 2), swap(second, "wide", 4)]
        return pieces

    def gather_sum(pieces):
        if blocks == 4:
            return [pieces[0]] + [swap(pieces[i], "wide", 2 * i) for i in range(1, chips)]
        return fold(pieces, bits)

    def place_axis(piece):
        return piece.reshape(piece.shape[:-4] + (PLACES,) + piece.shape[-2:])

    def halves(outs, shape):
        if blocks == 4:
            shape = (shape[0] // 2,) + shape[1:]
            return [[out.reshape(shape) for out in outs[2 * r : 2 * r + 2]] for r in range(4)]
        whole = outs[0].reshape((chips,) + shape)
        return [[pick(whole, index ^ chip)] for index in range(chips)]

    rows_in = jnp.concatenate([jnp.stack(vectors), up_bias.reshape(spare, rows)])
    in_keep, in_send = pack_in(info, input_weight, position_table, rows_in)
    in_far = swap(in_send, "wide", 1)
    raw_parts = together(down_weight, output_weight, up_sorted, tokens, in_keep)
    raw = jnp.concatenate(raw_parts[:2]) if plane else raw_parts[0]
    up_keep, up_send = pack_up(info, raw_parts[2])
    first, second = sent(info, raw_parts[3], positions, segments)
    in_far, raw, up_send, first = together(in_far, raw, up_send, first)

    in_pair = arrange(info, [in_keep, in_far], 0, 0)
    in_got = [in_pair] + [swap(in_pair, "narrow", k) for k in range(1, PLACES)]
    raw_far = swap(raw, "narrow", 2)
    up_far = swap(up_send, "wide", 1)
    up_far, raw_far, first, *in_got = together(up_far, raw_far, first, *in_got)

    in_piece = arrange(info, in_got)
    in_chips = direct(in_piece, chips) if plane else along(in_piece, bits)
    raw_half = arrange(info, [raw, raw_far], 1)
    raw_far = swap(raw_half, "narrow", 1)
    low = lax.ppermute(first, ("wide", "narrow"), spread_perm(0))
    up_pair = arrange(info, [up_keep, up_far], 0, 0)
    low, raw_far, up_pair, second = together(low, raw_far, up_pair, second)

    up_far = swap(up_pair, "narrow", 2)
    high = lax.ppermute(second, ("wide", "narrow"), spread_perm(1))
    if plane:
        raw_far, *in_chips = together(settle(info, raw_half, raw_far), *in_chips)
        down_chips = cross_one(raw_far)
    else:
        down_chips = along(place_axis(arrange(info, [raw_half, raw_far])), bits)
    high, up_far = together(high, up_far)

    up_half = arrange(info, [up_pair, up_far], 1)
    up_far = swap(up_half, "narrow", 1)
    low_far, high_far = swap(low, "wide", 1), swap(high, "wide", 1)
    low_far, high_far, cotangent = together(low_far, high_far, cotangent)
    token_blocks = [low, high, low_far, high_far]
    cot_first, cot_second = pick_turns(info, cotangent)
    cot_low = lax.ppermute(cot_first, ("wide", "narrow"), spread_perm(0))
    in_blocks = by_chip(in_chips)
    q, k, v, start, normed, small_full, turned, seg, spots = front(
        info, token_blocks, in_blocks, patches
    )
    q, k, v, seg, cot_second, up_far, *down_chips = together(
        q, k, v, seg, cot_second, up_far, *down_chips
    )

    up_chips = cross_one(place_axis(arrange(info, [up_half, up_far])))
    cot_high = lax.ppermute(cot_second, ("wide", "narrow"), spread_perm(1))
    if plane:
        down_chips = cross_two(down_chips)
    att, total = attend(info, q, k, v, seg)
    count = len(down_chips)
    att, cot_low, cot_high, *rest = together(att, cot_low, cot_high, *down_chips, *up_chips)
    down_chips, up_chips = rest[:count], rest[count:]

    att_far = swap(att, "wide", 1)
    if plane:
        out_rows = last_blocks(info, *down_chips[:3], down_chips[4])
        out_weights = [out_rows, swap(out_rows, "wide", 1)]
    else:
        out_weights = [lax.all_gather(output_weight, ("wide", "narrow"), axis=0, tiled=True)]
    if plane:
        up_chips = cross_two(up_chips)
    cots = [cot_low, cot_high, swap(cot_low, "wide", 1), swap(cot_high, "wide", 1)]
    if plane:
        up_blocks = [part.reshape((-1,) + part.shape[-1:]) for part in up_chips]
        down_blocks = down_chips
    else:
        up_blocks = by_chip(up_chips)
        down_blocks = [by_chip(down_chips)[0].reshape(4 * PLACES, -1, width)]
    middle, normed_two, up_bias_own, out_full = middle_front(
        info, att, att_far, start, turned, out_weights, own_hidden, patches, chips
    )
    keep, send, slope, *down_grads = feed_front(
        info, normed_two, up_bias_own, cots, up_blocks, down_blocks, blocks
    )
    down_rows = own_hidden // (chips * PLACES)
    down_fold = Fold(info, halves(down_grads, (PLACES, down_rows, width)), bits)
    fed = feed_back(info, slope, cots, up_blocks, down_blocks, width)
    back, back_low, grad_hidden, bias_grad, send, normed_two = down_fold.second(
        *fed, send, normed_two
    )
    back_far = swap(back_low, "wide", 1)
    out_far = swap(send, "wide", 1)
    up_grads = weight_grad(info, normed_two, [grad_hidden], blocks, 2 if plane else 1)
    back_far, out_far, *up_grads = down_fold.last(back_far, out_far, *up_grads)
    up_fold = Fold(info, halves(up_grads, (2, PLACES, rows, own_hidden)), bits)
    down_keep, down_send = split(info, down_fold.parts, (2, 2, down_rows))
    down_got = swap(down_send, "narrow", 1)
    grad_middle, grad_att, out_keep, out_send, sums = middle_back(
        info, back, back_far, middle, turned, att, out_full, cots, patches, blocks
    )
    if blocks == 1:
        shape = (chips // 2, 2, PLACES * rows, width)
        out_keep = pick(out_keep.reshape(shape), core, 1)
        out_send = pick(out_send.reshape(shape), 1 - core, 1)
    grad_att, out_send, out_far, down_got = up_fold.second(grad_att, out_send, out_far, down_got)
    out_got = swap(out_send, "wide", 1)
    out_turns = output_turns(info, middle, keep, out_far, turned, patches)
    out_turns = [unspread_turn(part, turn) for turn, part in enumerate(out_turns)]
    dq, dk, dv = attend_back(info, q, k, v, att, grad_att, total, seg)
    dq, dk, dv, out_got, normed, *out_turns = up_fold.last(
        dq, dk, dv, out_got, normed, *out_turns
    )
    start_keep, start_send = project_back(info, dq, dk, dv, in_blocks, width)
    start_far = swap(start_send, "wide", 1)
    normed, start_keep = together(normed, start_keep)
    in_grads = weight_grad(info, normed, [dq, dk, dv], blocks)
    start_far, *in_grads = together(start_far, *in_grads)
    in_sum = gather_sum(by_distance(in_grads, (2, PLACES, rows, 3 * part)))
    down_keep, down_send = split(info, [[down_keep, down_got]], (2, down_rows), 1)
    up_keep, up_send = split(info, up_fold.parts, (2, 2, 2, rows))
    start_far, down_send, up_send = together(start_far, down_send, up_send)
    down_got = swap(down_send, "narrow", 2)
    up_got = swap(up_send, "narrow", 1)
    args = [start_keep, start_far, start, grad_middle, turned, sums, bias_grad, spots, dq, dv]
    started = start_back(info, blocks, args + [out_keep, out_got], patches, chips)
    down_got, up_got, grad_blocks, *small_grads = together(down_got, up_got, *started)
    up_keep, up_send = split(info, [[up_keep, up_got]], (2, 2, rows), 1)
    up_got = swap(up_send, "narrow", 2)
    grad_first, grad_second = pick_turns(info, grad_blocks.reshape(2, block, width))
    grad_first = unspread_turn(grad_first, 0)
    up_got, grad_second, *rest = together(up_got, grad_second, *in_sum[1:], *small_grads)
    in_sum, small_grads = [in_sum[0], *rest[: len(in_sum) - 1]], rest[len(in_sum) - 1 :]
    if plane:
        small_sum = gather_sum(by_distance(small_grads, (2, PLACES, rows, SMALL + part)))
    else:
        out_grad = jnp.where(
            first_core,
            jnp.concatenate([out_keep, out_got]),
            jnp.concatenate([out_got, out_keep]),
        ).reshape(chips, PLACES, rows, 2, part)
        out_grad = jnp.transpose(out_grad, (0, 3, 1, 2, 4)).reshape(width, part)
        small_grads = jnp.concatenate([small_grads[0], out_grad], axis=1)
        small_sum = gather_sum(by_distance([small_grads], (2, PLACES, rows, SMALL + part)))

    def narrow_sum(cut):
        whole = cut[0]
        for index in range(1, PLACES):
            whole = whole + swap(cut[index], "narrow", index).astype(f32)
        return whole

    in_cut = split(info, [in_sum], (2, PLACES, rows))
    down_keep, up_keep, grad_first, *rest = together(
        down_keep, up_keep, grad_first, *out_turns, *in_cut
    )
    out_turns, in_cut = rest[:2], rest[2:]
    outputs = unspread_join(out_turns, place)
    grad_tokens = unspread_join([grad_first, unspread_turn(grad_second, 1)], place)
    down_share = down_keep + down_got.astype(f32)
    up_total = up_keep + up_got.astype(f32)
    up_keep = pick(up_total, core)
    up_got = swap(pick(up_total, 1 - core).astype(bf16), "wide", 1).astype(f32)
    up_both = [up_keep.reshape(rows, chips, 1, -1), up_got.reshape(rows, chips, 1, -1)]
    up_share = jnp.where(
        first_core, jnp.concatenate(up_both, axis=2), jnp.concatenate(up_both[::-1], axis=2)
    ).reshape(rows, hidden)
    in_total = narrow_sum(in_cut)
    small_total = narrow_sum(split(info, [small_sum], (2, PLACES, rows)))
    in_keep = pick(in_total, core)
    in_got = swap(pick(in_total, 1 - core).astype(bf16), "wide", 1).astype(f32)
    small_far = swap(pick(small_total, 1 - core)[:, :SMALL].astype(bf16), "wide", 1)
    small_share = pick(small_total, core)[:, :SMALL] + small_far.astype(f32)
    out_share = jnp.concatenate([small_total[0, :, SMALL:], small_total[1, :, SMALL:]], axis=1)
    in_both = [
        in_keep.reshape(rows, 3, 1, part),
        in_got.reshape(rows, 3, 1, part),
    ]
    in_share = jnp.where(
        first_core, jnp.concatenate(in_both, axis=2), jnp.concatenate(in_both[::-1], axis=2)
    ).reshape(rows, 3 * width)
    tail = [small_share[:, patches + i] for i in range(8)]
    return (
        outputs,
        grad_tokens,
        small_share[:, :patches],
        in_share,
        tail[QUERY_BIAS],
        tail[VALUE_BIAS],
        out_share,
        tail[OUTPUT_BIAS],
        tail[GAIN_ONE],
        tail[SHIFT_ONE],
        up_share,
        small_share[:, patches + 8 : patches + 8 + spare].T.reshape(-1),
        down_share,
        tail[DOWN_BIAS],
        tail[GAIN_TWO],
        tail[SHIFT_TWO],
    )


def solution(mesh):
    both = ("wide", "narrow")
    matrix = P(both, None)
    vector = P(both)
    block = P("wide", "narrow", None)
    gains = [matrix, matrix] + [vector] * 2 + [matrix] + [vector] * 3 + [matrix, vector, matrix]
    gains += [vector] * 3
    return jax.shard_map(
        local,
        mesh=mesh,
        in_specs=tuple([block, P("wide", "narrow"), P("wide", None)] + gains + [block]),
        out_specs=tuple([block, block] + gains),
        check_vma=False,
    )
```

```python
import functools

import jax
import jax.numpy as jnp
from jax import lax
from jax.experimental import pallas as pl
from jax.experimental.pallas import tpu as pltpu
from jax.sharding import PartitionSpec as P

HEADS = 12
PLACES = 4
epsilon = 1e-05
masked_score = -1e30

f32 = jnp.float32
bf16 = jnp.bfloat16
MIB = 1 << 20
LOAD, HELD = "load", "held"
QUERY_BIAS, VALUE_BIAS, OUTPUT_BIAS, GAIN_ONE, SHIFT_ONE, DOWN_BIAS, GAIN_TWO, SHIFT_TWO = range(8)
SMALL = 128


def dot(left, right):
    return jnp.dot(left, right, preferred_element_type=f32)


def dot_left(left, right):
    return lax.dot_general(left, right, (((0,), (0,)), ((), ())), preferred_element_type=f32)


def dot_right(left, right):
    return lax.dot_general(left, right, (((1,), (1,)), ((), ())), preferred_element_type=f32)


def call(kernel, outs, ins, args, scratch=(), grid=None, limit=14, cost=None):
    loads = []
    specs = [pl.BlockSpec(memory_space=pltpu.SMEM)]
    for index, (spec, array) in enumerate(zip(ins, args[1:], strict=True)):
        if spec == LOAD:
            whole = False
            spec = pl.BlockSpec(memory_space=pl.ANY if whole else pltpu.VMEM)
            if whole:
                loads.append(index)
        elif spec == HELD:
            spec = pl.BlockSpec(memory_space=pl.ANY)
        specs.append(spec)
    count, news = len(ins), len(loads)

    def loaded(info, *refs):
        refs, held, sem = list(refs[: -1 - news]), refs[-1 - news : -1], refs[-1]
        copies = []
        for i, index in enumerate(loads):
            copies.append(pltpu.make_async_copy(refs[index], held[i], sem.at[i]))
            refs[index] = held[i]
        run_copies(copies)
        kernel(info, *refs)

    extra = [pltpu.VMEM(args[1 + i].shape, args[1 + i].dtype) for i in loads]
    if loads:
        extra.append(pltpu.SemaphoreType.DMA((news,)))
    return pl.pallas_call(
        loaded if loads else kernel,
        out_shape=[shape for shape, _ in outs],
        in_specs=specs,
        out_specs=[spec for _, spec in outs],
        scratch_shapes=list(scratch) + extra,
        **({"grid": grid} if grid else {}),
        compiler_params=pltpu.CompilerParams(vmem_limit_bytes=limit * MIB),
        cost_estimate=pl.CostEstimate(
            flops=int(cost[0]), bytes_accessed=int(cost[1]), transcendentals=0
        ),
    )(*args)


def shaped(shape, kind):
    return jax.ShapeDtypeStruct(shape, kind)


def vmem():
    return pl.BlockSpec(memory_space=pltpu.VMEM)


def anywhere():
    return pl.BlockSpec(memory_space=pl.ANY)


def normalise(values):
    average = jnp.mean(values, axis=-1, keepdims=True)
    centered = values - average
    variance = jnp.mean(centered * centered, axis=-1, keepdims=True)
    scale = lax.rsqrt(variance + epsilon)
    return centered * scale, scale


def norm_back(normal, scale, gain, grad):
    inner = grad * gain
    return scale * (
        inner
        - jnp.mean(inner, axis=-1, keepdims=True)
        - normal * jnp.mean(inner * normal, axis=-1, keepdims=True)
    )


def fold_shapes(rows, rest):
    return [shaped((count,) + rest, bf16) for count in (rows, rows, rows, rows // 2, rows // 2)]


def fold_copies(held, outs, chip, sem):
    rows = outs[0].shape[0]
    half = rows // 2
    at = lambda distance, second: pl.ds(
        pl.multiple_of((distance ^ chip) * rows + second * half, half), half
    )
    whole = pl.ds(pl.multiple_of(chip * rows, rows), rows)
    first, second = pl.ds(0, half), pl.ds(half, half)
    own, to_x, to_y, y_left, x_left = outs
    pairs = [
        (0, held.at[whole], own),
        (3, held.at[at(3, 0)], to_x.at[first]),
        (1, held.at[at(1, 0)], to_x.at[second]),
        (3, held.at[at(3, 1)], to_y.at[first]),
        (2, held.at[at(2, 1)], to_y.at[second]),
        (2, held.at[at(2, 0)], y_left),
        (1, held.at[at(1, 1)], x_left),
    ]
    return [
        (pltpu.make_async_copy(a, b, sem.at[i]), distance)
        for i, (distance, a, b) in enumerate(pairs)
    ]


def run_copies(copies):
    for copy in copies:
        copy.start()
    for copy in copies:
        copy.wait()


def pack_in_kernel(patches, info, weight, table, rows_in, keep, send):
    core = info[0]
    part = weight.shape[1] // 6
    turned = rows_in[...].astype(f32).T
    empty = jnp.zeros((weight.shape[0], SMALL - patches - turned.shape[1]), f32)
    small = jnp.concatenate([table[...].astype(f32), turned, empty], axis=1).astype(bf16)
    for ref, side in ((keep, core), (send, 1 - core)):
        for i in range(3):
            there = pl.ds(pl.multiple_of((2 * i + side) * part, 128), part)
            ref[:, i * part : (i + 1) * part] = weight[:, there]
        ref[:, 3 * part :] = small


def pack_in(info, weight, table, rows_in):
    rows, columns = weight.shape[0], weight.shape[1] // 2 + SMALL
    return call(
        functools.partial(pack_in_kernel, table.shape[1]),
        [(shaped((rows, columns), bf16), vmem())] * 2,
        [vmem()] * 3,
        [info, weight, table, rows_in],
        limit=8,
        cost=(0, MIB),
    )


def pack_up_kernel(info, up, keep, send):
    step = keep.shape[1] // 4
    for ref, side in ((keep, info[0]), (send, 1 - info[0])):
        for q in range(4):
            there = pl.ds(pl.multiple_of((2 * q + side) * step, 128), step)
            ref[:, q * step : (q + 1) * step] = up[:, there]


def pack_up(info, up):
    out = (shaped((up.shape[0], up.shape[1] // 2), bf16), vmem())
    return call(pack_up_kernel, [out] * 2, [vmem()], [info, up], limit=8, cost=(0, MIB))


def sent_kernel(info, tokens, positions, segments, first, second, extra):
    place = info[2]
    block, width = tokens.shape[1], tokens.shape[2]
    full = segments.shape[1]
    extra[...] = jnp.zeros_like(extra)
    for k, out in enumerate((first, second)):
        index = k ^ (place % 2)
        row = segments[pl.ds(index, 1), :]
        row = (row - row[:, 0:1]).astype(f32)
        extra[0:1, :block] = positions[pl.ds(index, 1), :].astype(f32)
        extra[1:2, :] = row[:, :width]
        extra[2:3, : full - width] = row[:, width:]
        out[:block, :] = tokens[index]
        out[block:, :] = extra[...].astype(bf16)


def sent(info, tokens, positions, segments):
    _, block, width = tokens.shape
    one = (shaped((block + 16, width), bf16), vmem())
    return call(
        sent_kernel,
        [one, one],
        [vmem()] * 3,
        [info, tokens, positions, segments],
        scratch=[pltpu.VMEM((16, width), f32)],
        limit=8,
        cost=(0, 2 * MIB),
    )


def arrange_kernel(slot, shift, info, *refs):
    ins, out = refs[:-1], refs[-1]
    lead = len(out.shape) - 3
    place = lax.rem(info[slot] >> shift, len(ins))
    for k, ref in enumerate(ins):
        out[(slice(None),) * lead + (k ^ place,)] = ref[...]


def arrange(info, pieces, shift=0, slot=2):
    shape = pieces[0].shape
    shape = shape[:-2] + (len(pieces),) + shape[-2:]
    total = 1
    for extent in shape:
        total *= extent
    return call(
        functools.partial(arrange_kernel, slot, shift),
        [(shaped(shape, bf16), vmem())],
        [vmem()] * len(pieces),
        [info] + list(pieces),
        limit=8,
        cost=(0, 4 * total),
    )[0]


def settle_kernel(info, own, far, out):
    odd = lax.rem(info[2], 2)
    block = out.shape[1]
    rows = own.shape[1] - block
    for k, ref in enumerate((own, far)):
        for high in range(2):
            out[2 * high + (k ^ odd)] = ref[high, :block, :]
    both = (own, far)
    for high in range(2):
        pair = [ref[high, block:, :].astype(f32) for ref in both]
        for low in range(2):
            row = jnp.where(odd == low, pair[0], pair[1]).astype(bf16)
            begin = (2 * high + low) * rows
            out[PLACES, begin : begin + rows, :] = row


def settle(info, own, far):
    _, rows, width = own.shape
    block = rows * PLACES // (PLACES + 1)
    return call(
        settle_kernel,
        [(shaped((PLACES + 1, block, width), bf16), vmem())],
        [vmem()] * 2,
        [info, own, far],
        limit=8,
        cost=(0, 2 * MIB),
    )[0]


def last_kernel(info, own, x, y, d, out):
    for distance, ref in enumerate((own, x, y, d)):
        out[distance ^ info[1]] = ref[ref.shape[0] - 1]


def last_blocks(info, own, x, y, d):
    return call(
        last_kernel,
        [(shaped((4,) + own.shape[1:], bf16), vmem())],
        [vmem()] * 4,
        [info, own, x, y, d],
        limit=8,
        cost=(0, MIB),
    )[0]


def cut_kernel(info, x, y, first, second):
    half = first.shape[0]
    first[...] = y[:half]
    second[...] = x[half:]


def cut(info, x, y):
    half = x.shape[0] // 2
    outs = [
        (shaped((half,) + x.shape[1:], bf16), vmem()),
        (shaped((x.shape[0] - half,) + x.shape[1:], bf16), vmem()),
    ]
    return call(cut_kernel, outs, [LOAD] * 2, [info, x, y], limit=8, cost=(0, MIB))


def add_kernel(info, *refs):
    for i in range(0, len(refs), 3):
        a, b, out = refs[i : i + 3]
        out[...] = (a[...].astype(f32) + b[: out.shape[0]].astype(f32)).astype(bf16)


def add_firsts(info, pairs):
    def kernel(info, *refs):
        outs = refs[2 * len(pairs) :]
        add_kernel(info, *[ref for i, out in enumerate(outs) for ref in (*refs[2 * i : 2 * i + 2], out)])

    return call(
        kernel,
        [(shaped(a.shape, bf16), vmem()) for a, _ in pairs],
        [LOAD] * (2 * len(pairs)),
        [info] + [array for pair in pairs for array in pair],
        limit=8,
        cost=(0, MIB),
    )


def pick_kernel(info, blocks, first, second):
    odd = lax.rem(info[2], 2)
    first[...] = blocks[odd]
    second[...] = blocks[1 - odd]


def pick_turns(info, blocks):
    out = (shaped(blocks.shape[1:], bf16), vmem())
    return call(pick_kernel, [out] * 2, [LOAD], [info, blocks], limit=8, cost=(0, MIB))


def output_kernel(patches, info, middle, keep, far, turned, first, second):
    core, odd = info[0], lax.rem(info[2], 2)
    half = keep.shape[0]
    block = half // 2
    bias = turned[patches + DOWN_BIAS : patches + DOWN_BIAS + 1, :]
    for ref, which in ((first, odd), (second, 1 - odd)):
        here = pl.ds(pl.multiple_of(which * block, block), block)
        there = pl.ds(pl.multiple_of(core * half + which * block, block), block)
        ref[...] = (middle[there, :] + keep[here, :] + far[here, :].astype(f32) + bias).astype(bf16)


def output_turns(info, middle, keep, far, turned, patches):
    out = (shaped((keep.shape[0] // 2, keep.shape[1]), bf16), vmem())
    return call(
        functools.partial(output_kernel, patches),
        [out] * 2,
        [LOAD] * 4,
        [info, middle, keep, far, turned],
        limit=8,
        cost=(0, 6 * MIB),
    )


def front_kernel(blocks, patches, info, *refs):
    tokens_in, refs = refs[:4], refs[4:]
    weights_in, refs = refs[:blocks], refs[blocks:]
    q_out, k_out, v_out, start_out, normed_out, weight, turned_out, seg_out, spot_out = refs[:9]
    held, sem, weight_sem = refs[9:]
    core, chip, place = info[0], info[1], info[2]
    block, columns = held.shape[1] - 16, weight.shape[1] - SMALL
    part = columns // 3
    copies = []
    for i in range(4):
        side = core if i < 2 else 1 - core
        there = 2 * side + ((i % 2) ^ (place % 2))
        copies.append(pltpu.make_async_copy(tokens_in[i], held.at[there], sem.at[i]))
    copies += piece_copies(weights_in, weight, info, weight_sem)
    run_copies(copies)
    small = weight[:, columns:]
    turned_out[...] = small.astype(f32).T
    vector = lambda i: turned_out[patches + i : patches + i + 1, :]
    half = pl.ds(pl.multiple_of(core * part, 128), part)
    query_bias = turned_out[patches + QUERY_BIAS : patches + QUERY_BIAS + 1, half]
    value_bias = turned_out[patches + VALUE_BIAS : patches + VALUE_BIAS + 1, half]
    gain, shift = vector(GAIN_ONE), vector(SHIFT_ONE)
    extra = held[0, block : block + 16, :].astype(f32)
    width = extra.shape[1]
    segment = jnp.concatenate([extra[1:2, :], extra[2:3, : 4 * block - width]], axis=1)
    seg_out[...] = jnp.broadcast_to(segment, seg_out.shape)
    ids = lax.broadcasted_iota(jnp.int32, (SMALL, block), 0).astype(f32)
    for b in range(4):
        here = slice(b * block, (b + 1) * block)
        spot = held[b, block : block + 16, :].astype(f32)[0:1, :block]
        spot_out[:, here] = jnp.broadcast_to(spot, (8, block))
        one_hot = jnp.where(ids == spot, 1.0, 0.0).astype(bf16)
        embedded = lax.dot_general(
            one_hot, small, (((0,), (1,)), ((), ())), preferred_element_type=f32
        )
        start = held[b, :block, :].astype(f32) + embedded
        start_out[here, :] = start
        normal, _ = normalise(start)
        normed = (normal * gain + shift).astype(bf16)
        normed_out[here, :] = normed
        projected = dot(normed, weight[:, :columns])
        query = (projected[:, :part] + query_bias).astype(bf16).astype(f32) * 0.125
        q_out[here, :] = query.astype(bf16)
        k_out[here, :] = projected[:, part : 2 * part].astype(bf16)
        v_out[here, :] = (projected[:, 2 * part :] + value_bias).astype(bf16)


def front(info, tokens, weights, patches):
    blocks = len(weights)
    block, width = tokens[0].shape[0] - 16, tokens[0].shape[1]
    columns = weights[0].shape[1]
    part = (columns - SMALL) // 3
    rows = 4 * block
    return call(
        functools.partial(front_kernel, blocks, patches),
        [
            (shaped((rows, part), bf16), vmem()),
            (shaped((rows, part), bf16), vmem()),
            (shaped((rows, part), bf16), vmem()),
            (shaped((rows, width), f32), vmem()),
            (shaped((rows, width), bf16), vmem()),
            (shaped((width, columns), bf16), vmem()),
            (shaped((SMALL, width), f32), vmem()),
            (shaped((8, rows), f32), vmem()),
            (shaped((8, rows), f32), vmem()),
        ],
        [HELD] * (4 + blocks),
        [info] + list(tokens) + list(weights),
        scratch=[
            pltpu.VMEM((4, block + 16, width), bf16),
            pltpu.SemaphoreType.DMA((4,)),
            pltpu.SemaphoreType.DMA((blocks,)),
        ],
        cost=(2 * rows * width * columns, 12 * MIB),
    )


def fill_bias(bias, seg):
    block = bias.shape[1]
    wide = seg[...]
    tall = jnp.broadcast_to(wide[0:1, :], (128, wide.shape[1])).T[:, 0:1]
    base = 0
    for b in range(4):
        many = (b + 1) * block
        key = lax.broadcasted_iota(jnp.int32, (many, block), 0)
        ask = lax.broadcasted_iota(jnp.int32, (many, block), 1) + b * block
        same = tall[:many] == wide[0:1, b * block : (b + 1) * block]
        bias[base : base + many, :] = jnp.where((key <= ask) & same, 0.0, masked_score)
        base += many


def turn(values):
    return values.astype(f32).T.astype(bf16)


def attend_kernel(info, q, k, v, seg, out, total, bias):
    block = bias.shape[1]

    @pl.when(pl.program_id(0) == 0)
    def _():
        fill_bias(bias, seg)

    turned_q, turned_v = turn(q[...]), turn(v[...])
    side = lax.broadcasted_iota(jnp.int32, (128, block), 0) // 64
    base = 0
    for b in range(4):
        many = (b + 1) * block
        here = slice(b * block, (b + 1) * block)
        mixed = []
        for h in range(2):
            ask = jnp.where(side == h, turned_q[:, here].astype(f32), 0.0).astype(bf16)
            scores = dot(k[:many, :], ask) + bias[base : base + many, :]
            top = jnp.max(scores, axis=0, keepdims=True)
            raised = jnp.exp(scores - top)
            mass = jnp.sum(raised, axis=0, keepdims=True)
            total[0, h : h + 1, here] = top + jnp.log(mass)
            part = dot(turned_v[64 * h : 64 * h + 64, :many], raised.astype(bf16))
            mixed.append(part * (1.0 / mass))
        out[here, :] = jnp.concatenate(mixed, axis=0).T.astype(bf16)
        base += many


def attend(info, q, k, v, seg):
    rows, part = q.shape
    pairs = part // 128
    column = pl.BlockSpec((rows, 128), lambda i: (0, i))
    whole = pl.BlockSpec(seg.shape, lambda i: (0, 0))
    return call(
        attend_kernel,
        [
            (shaped((rows, part), bf16), column),
            (shaped((pairs, 8, rows), f32), pl.BlockSpec((1, 8, rows), lambda i: (i, 0, 0))),
        ],
        [column, column, column, whole],
        [info, q, k, v, seg],
        scratch=[pltpu.VMEM((10 * rows // 4, rows // 4), f32)],
        grid=(pairs,),
        cost=(6 * rows * rows * part, 4 * MIB),
    )


def attend_back_kernel(info, q, k, v, o, g, total, seg, dq, dk, dv, bias, dk_sum, dv_sum):
    block = bias.shape[1]

    @pl.when(pl.program_id(0) == 0)
    def _():
        fill_bias(bias, seg)

    wide_g = g[...].astype(f32).T
    product = wide_g * o[...].astype(f32).T
    inner = [jnp.sum(product[64 * h : 64 * h + 64], axis=0, keepdims=True) for h in range(2)]
    turned_q, turned_k = turn(q[...]), turn(k[...])
    turned_g = wide_g.astype(bf16)
    side = lax.broadcasted_iota(jnp.int32, (128, block), 0) // 64
    flat = lax.broadcasted_iota(jnp.int32, (block, 128), 1) // 64
    dk_sum[...] = jnp.zeros_like(dk_sum)
    dv_sum[...] = jnp.zeros_like(dv_sum)
    base = 0
    for b in range(4):
        many = (b + 1) * block
        here = slice(b * block, (b + 1) * block)
        grads = []
        for h in range(2):
            ask = jnp.where(side == h, turned_q[:, here].astype(f32), 0.0).astype(bf16)
            ask_g = jnp.where(side == h, turned_g[:, here].astype(f32), 0.0).astype(bf16)
            scores = dot(k[:many, :], ask) + bias[base : base + many, :]
            probs = jnp.exp(scores - total[0, h : h + 1, here])
            grad_probs = dot(v[:many, :], ask_g)
            grad_scores = (probs * (grad_probs - inner[h][:, here])).astype(bf16)
            own_q = jnp.where(flat == h, q[here, :].astype(f32), 0.0).astype(bf16)
            own_g = jnp.where(flat == h, g[here, :].astype(f32), 0.0).astype(bf16)
            dv_sum[:many, :] += dot(probs.astype(bf16), own_g)
            dk_sum[:many, :] += dot(grad_scores, own_q)
            grads.append(dot(turned_k[64 * h : 64 * h + 64, :many], grad_scores))
        dq[here, :] = (jnp.concatenate(grads, axis=0).T * 0.125).astype(bf16)
        base += many
    dk[...] = dk_sum[...].astype(bf16)
    dv[...] = dv_sum[...].astype(bf16)


def attend_back(info, q, k, v, o, g, total, seg):
    rows, part = q.shape
    pairs = part // 128
    column = pl.BlockSpec((rows, 128), lambda i: (0, i))
    whole = pl.BlockSpec(seg.shape, lambda i: (0, 0))
    out = (shaped((rows, part), bf16), column)
    return call(
        attend_back_kernel,
        [out, out, out],
        [column] * 5 + [pl.BlockSpec((1, 8, rows), lambda i: (i, 0, 0)), whole],
        [info, q, k, v, o, g, total, seg],
        scratch=[
            pltpu.VMEM((10 * rows // 4, rows // 4), f32),
            pltpu.VMEM((rows, 128), f32),
            pltpu.VMEM((rows, 128), f32),
        ],
        grid=(pairs,),
        cost=(15 * rows * rows * part, 6 * MIB),
    )


def cotangent_copies(info, pieces, held, sems):
    core, place = info[0], info[2]
    copies = []
    for i in range(4):
        side = core if i < 2 else 1 - core
        there = 2 * side + ((i % 2) ^ (place % 2))
        copies.append(pltpu.make_async_copy(pieces[i], held.at[there], sems[i]))
    return copies


def gelu_parts(values):
    scale = 0.7978845608028654
    square = values * values
    slope = jnp.tanh(values * (scale + (scale * 0.044715) * square))
    half = 0.5 * (1.0 + slope)
    grad = half + 0.5 * values * (1.0 - slope * slope) * (
        scale + (3.0 * scale * 0.044715) * square
    )
    return values * half, grad


def piece_copies(pieces, target, info, sem, lanes=None):
    chip = info[1]
    rows = pieces[0].shape[0]
    copies, base = [], 0
    for i, ref in enumerate(pieces):
        distance = min(i, 3)
        begin = pl.multiple_of((distance ^ chip) * rows, rows)
        if i == 4:
            begin = pl.multiple_of(begin + rows // 2, rows // 2)
        source = ref if lanes is None else ref.at[:, lanes]
        there = target.at[pl.ds(begin, ref.shape[0])]
        copies.append(pltpu.make_async_copy(source, there, sem.at[i]))
    return copies


def block_copies(pieces, target, info, sem):
    if len(pieces) == 1:
        return [pltpu.make_async_copy(pieces[0], target, sem.at[0])]
    copies = []
    for i, ref in enumerate(pieces):
        begin = (min(i, 3) ^ info[1]) * PLACES + (2 if i == 4 else 0)
        count = 2 if i >= 3 else PLACES
        copies.append(
            pltpu.make_async_copy(ref.at[pl.ds(0, count)], target.at[pl.ds(begin, count)], sem.at[i])
        )
    return copies


def hidden_places(core, hidden, width, chips):
    spare = 2 * hidden // width
    share = hidden // chips
    device = share // PLACES
    rows = device // spare
    unit = lax.broadcasted_iota(jnp.int32, (hidden, 1), 0)
    rest = lax.rem(unit, share)
    row = ((2 * (unit // share) + core) * PLACES + rest // device) * rows + lax.rem(rest, rows)
    lane = lax.broadcasted_iota(jnp.int32, (hidden, width), 1)
    return jnp.where(lane == row, 1.0, 0.0).astype(bf16)


def hidden_turns(spare, hidden, chips):
    device = hidden // (chips * PLACES)
    unit = lax.broadcasted_iota(jnp.int32, (spare, hidden), 1)
    return lax.rem(unit, device) // (device // spare) == lax.broadcasted_iota(
        jnp.int32, (spare, hidden), 0
    )


def middle_kernel(patches, chips, hidden, info, att, att_far, start, turned, *refs):
    weights, refs = refs[:-4], refs[-4:]
    middle_out, normed_out, bias_out, weight_out = refs
    core = info[0]
    rows, width = start.shape
    part, tile = width // 2, rows // 4
    if len(weights) == 2:
        block = weights[0].shape[1]
        for side, ref in ((core, weights[0]), (1 - core, weights[1])):
            for q in range(4):
                begin = pl.multiple_of((2 * q + side) * block, block)
                weight_out[pl.ds(begin, block), :] = ref[q]
    else:
        weight_out[...] = weights[0][...]
    spare = 2 * hidden // width
    biases = turned[patches + 8 : patches + 8 + spare, :].astype(bf16)
    spread_out = dot_right(biases, hidden_places(core, hidden, width, chips))
    bias = jnp.sum(
        jnp.where(hidden_turns(spare, hidden, chips), spread_out, 0.0), axis=0, keepdims=True
    )
    bias_out[...] = jnp.broadcast_to(bias, bias_out.shape)
    vector = lambda i: turned[patches + i : patches + i + 1, :]
    own = pl.ds(pl.multiple_of(core * part, 128), part)
    far = pl.ds(pl.multiple_of((1 - core) * part, 128), part)
    gain, shift, out_bias = vector(GAIN_TWO), vector(SHIFT_TWO), vector(OUTPUT_BIAS)
    for t in range(4):
        here = slice(t * tile, (t + 1) * tile)
        mixed = dot(att[here, :], weight_out[own, :]) + dot(att_far[here, :], weight_out[far, :])
        middle = start[here, :] + mixed + out_bias
        middle_out[here, :] = middle
        normal, _ = normalise(middle)
        normed_out[here, :] = (normal * gain + shift).astype(bf16)


def middle_front(info, att, att_far, start, turned, weights, hidden, patches, chips):
    rows, width = start.shape
    return call(
        functools.partial(middle_kernel, patches, chips, hidden),
        [
            (shaped((rows, width), f32), vmem()),
            (shaped((rows, width), bf16), vmem()),
            (shaped((8, hidden), f32), vmem()),
            (shaped((width, width), bf16), vmem()),
        ],
        [LOAD] * (4 + len(weights)),
        [info, att, att_far, start, turned] + list(weights),
        cost=(2 * rows * width * width, 12 * MIB),
    )


def feed_front_kernel(ups, downs, blocks, info, normed, up_bias, *refs):
    cot_in, refs = refs[:4], refs[4:]
    up_in, refs = refs[:ups], refs[ups:]
    down_in, refs = refs[:downs], refs[downs:]
    keep_out, send_out, slope_out, up, down, cot, refs = *refs[:6], refs[6:]
    down_grads, (act, far_sum, down_grad, cot_sem, up_sem, down_sem) = refs[:-6], refs[-6:]
    core, chip = info[0], info[1]
    rows, width = normed.shape
    hidden = up.shape[1]
    chunk = hidden // 4
    half = rows // 2
    early = piece_copies(up_in, up, info, up_sem)
    late = block_copies(down_in, down, info, down_sem)
    late += cotangent_copies(info, cot_in, cot, [cot_sem.at[i] for i in range(4)])
    for copy in early + late:
        copy.start()
    for copy in early:
        copy.wait()
    own = pl.ds(pl.multiple_of(core * half, half), half)
    far = pl.ds(pl.multiple_of((1 - core) * half, half), half)
    outs, flat = [], None
    for step, distance in enumerate((3, 1, 2, 0)):
        q = distance ^ chip
        lanes = pl.ds(pl.multiple_of(q * chunk, 128), chunk)
        value, slope = gelu_parts(dot(normed[...], up[:, lanes]) + up_bias[0:1, lanes])
        value = value.astype(bf16)
        act[...] = value
        slope_out[:, lanes] = slope.astype(bf16)
        if step == 0:
            for copy in late:
                copy.wait()
            flat = cot[...].reshape(rows, width)
        blocks_here = pl.ds(pl.multiple_of(q * PLACES, PLACES), PLACES)
        grad = dot_left(value, flat).astype(bf16)
        down_grad[blocks_here] = grad.reshape(PLACES, chunk // PLACES, width)
        if blocks == 4:
            outs += [
                copy
                for copy, where in fold_copies(down_grad, down_grads, chip, down_sem)
                if where == distance
            ]
            for copy in outs[-2 if distance else -1 :]:
                copy.start()
        down_part = down[blocks_here].reshape(chunk, width)
        keep, send = dot(act[own, :], down_part), dot(act[far, :], down_part)
        keep_out[...] = keep if step == 0 else keep_out[...] + keep
        if step < 3:
            far_sum[...] = send if step == 0 else far_sum[...] + send
        else:
            send_out[...] = (far_sum[...] + send).astype(bf16)
    if blocks != 4:
        outs.append(pltpu.make_async_copy(down_grad, down_grads[0], down_sem.at[0]))
        outs[0].start()
    for copy in outs:
        copy.wait()


def feed_front(info, normed, up_bias, cots, ups, downs, blocks):
    rows, width = normed.shape
    hidden = up_bias.shape[1]
    whole = (4 * PLACES, hidden // (4 * PLACES), width)
    grads = fold_shapes(PLACES, whole[1:]) if blocks == 4 else [shaped(whole, bf16)]
    return call(
        functools.partial(feed_front_kernel, len(ups), len(downs), blocks),
        [
            (shaped((rows // 2, width), f32), vmem()),
            (shaped((rows // 2, width), bf16), vmem()),
            (shaped((rows, hidden), bf16), vmem()),
            (shaped((width, hidden), bf16), vmem()),
            (shaped(whole, bf16), vmem()),
            (shaped((4, rows // 4, width), bf16), vmem()),
        ]
        + [(one, anywhere()) for one in grads],
        [LOAD] * 2 + [HELD] * (4 + len(ups) + len(downs)),
        [info, normed, up_bias] + list(cots) + list(ups) + list(downs),
        scratch=[
            pltpu.VMEM((rows, hidden // 4), bf16),
            pltpu.VMEM((rows // 2, width), f32),
            pltpu.VMEM(whole, bf16),
            pltpu.SemaphoreType.DMA((4,)),
            pltpu.SemaphoreType.DMA((len(ups),)),
            pltpu.SemaphoreType.DMA((8,)),
        ],
        limit=14,
        cost=(6 * rows * width * hidden, 24 * MIB),
    )


def feed_back_kernel(info, slope, cot, up, down, back_out, low_out, grad_out, bias_out):
    rows, hidden = slope.shape
    width = up.shape[0]
    chunk = hidden // 4
    flat = cot[...].reshape(rows, width)
    for q in range(4):
        lanes = slice(q * chunk, (q + 1) * chunk)
        down_part = down[q * PLACES : (q + 1) * PLACES].reshape(chunk, width)
        grad = (dot_right(flat, down_part) * slope[:, lanes].astype(f32)).astype(bf16)
        grad_out[:, lanes] = grad
        bias_out[:, lanes] = jnp.broadcast_to(
            jnp.sum(grad.astype(f32), axis=0, keepdims=True), (8, chunk)
        )
        back = dot_right(grad, up[:, lanes])
        if q == 0:
            back_out[...] = back
        elif q < 3:
            back_out[...] += back
        else:
            back = back_out[...] + back
            back_out[...] = back
            low_out[...] = back.astype(bf16)


def feed_back(info, slope, cot, up, down):
    rows, hidden = slope.shape
    width = up.shape[0]
    return call(
        feed_back_kernel,
        [
            (shaped((rows, width), f32), vmem()),
            (shaped((rows, width), bf16), vmem()),
            (shaped((rows, hidden), bf16), vmem()),
            (shaped((8, hidden), f32), vmem()),
        ],
        [LOAD] * 4,
        [info, slope, cot, up, down],
        limit=10,
        cost=(4 * rows * width * hidden, 24 * MIB),
    )


def weight_kernel(blocks, count, info, left, *refs):
    parts, outs, held, sem = refs[:count], refs[count:-2], refs[-2], refs[-1]
    base = 0
    for ref in parts:
        for begin in range(0, ref.shape[1], 384):
            size = min(384, ref.shape[1] - begin)
            product = dot_left(left[...], ref[:, begin : begin + size]).astype(bf16)
            held[:, base : base + size] = product
            base += size
    if blocks == 4:
        run_copies([copy for copy, _ in fold_copies(held, outs, info[1], sem)])
    else:
        run_copies([pltpu.make_async_copy(held, outs[0], sem.at[0])])


def weight_grad(info, left, parts, blocks):
    rows, width = left.shape
    columns = sum(part.shape[1] for part in parts)
    outs = [shaped((width, columns), bf16)]
    if blocks == 4:
        outs = fold_shapes(width // 4, (columns,))
    return call(
        functools.partial(weight_kernel, blocks, len(parts)),
        [(one, anywhere()) for one in outs],
        [LOAD] * (1 + len(parts)),
        [info, left] + list(parts),
        scratch=[pltpu.VMEM((width, columns), bf16), pltpu.SemaphoreType.DMA((8,))],
        cost=(2 * rows * width * columns, 8 * MIB),
    )


def middle_back_kernel(blocks, patches, info, back, back_far, middle, turned, att, weight, cot, *refs):
    grad_out, attended_out, keep_out, send_out, sums_out, branch = refs
    core = info[0]
    rows, width = middle.shape
    tile = rows // 4
    part = width // 2
    gain = turned[patches + GAIN_TWO : patches + GAIN_TWO + 1, :]
    own_rows = pl.ds(pl.multiple_of(core * part, 128), part)
    for t in range(4):
        here = slice(t * tile, (t + 1) * tile)
        grad_normed = back[here, :] + back_far[here, :].astype(f32)
        normal, scale = normalise(middle[here, :])
        grad_outputs = cot[t].astype(f32)
        grad = grad_outputs + norm_back(normal, scale, gain, grad_normed)
        low = grad.astype(bf16)
        branch[here, :] = low
        attended_out[here, :] = dot_right(low, weight[own_rows, :]).astype(bf16)

        @pl.when(core == t // 2)
        def _():
            grad_out[(t % 2) * tile : (t % 2 + 1) * tile, :] = grad
            sums = jnp.concatenate(
                [
                    jnp.sum(low.astype(f32), axis=0, keepdims=True),
                    jnp.sum(grad_outputs, axis=0, keepdims=True),
                    jnp.sum(grad_normed * normal, axis=0, keepdims=True),
                    jnp.sum(grad_normed, axis=0, keepdims=True),
                    jnp.zeros((4, width), f32),
                ],
                axis=0,
            )
            sums_out[...] = sums if t % 2 == 0 else sums_out[...] + sums

    weight_grad = dot_left(att[...], branch[...]).astype(bf16)
    shape = send_out.shape[:1] + (2,) + send_out.shape[1:]
    sorted_grad = weight_grad.reshape(shape) if blocks == 4 else None
    if blocks == 4:
        for c in range(2):

            @pl.when(core == c)
            def _():
                keep_out[...] = sorted_grad[:, c]
                send_out[...] = sorted_grad[:, 1 - c]

    else:
        keep_out[...] = weight_grad
        send_out[...] = weight_grad


def middle_back(info, back, back_far, middle, turned, att, weight, cot, patches, blocks):
    rows, width = middle.shape
    part = width // 2
    slab = (2, part // 4, width) if blocks == 4 else (part, width)
    return call(
        functools.partial(middle_back_kernel, blocks, patches),
        [
            (shaped((rows // 2, width), f32), vmem()),
            (shaped((rows, part), bf16), vmem()),
            (shaped(slab, bf16), vmem()),
            (shaped(slab, bf16), vmem()),
            (shaped((8, width), f32), vmem()),
        ],
        [LOAD] * 7,
        [info, back, back_far, middle, turned, att, weight, cot],
        scratch=[pltpu.VMEM((rows, width), bf16)],
        cost=(4 * rows * width * part, 14 * MIB),
    )


def project_kernel(info, dq, dk, dv, weight, keep_out, send_out):
    core = info[0]
    rows, part = dq.shape
    half_rows = rows // 2

    def product(first):
        here = pl.ds(pl.multiple_of(first, 128), half_rows)
        return (
            dot_right(dq[here, :], weight[:, :part])
            + dot_right(dk[here, :], weight[:, part : 2 * part])
            + dot_right(dv[here, :], weight[:, 2 * part : 3 * part])
        )

    send_out[...] = product((1 - core) * half_rows).astype(bf16)
    keep_out[...] = product(core * half_rows)


def project_back(info, dq, dk, dv, weight):
    rows, part = dq.shape
    width = weight.shape[0]
    return call(
        project_kernel,
        [
            (shaped((rows // 2, width), f32), vmem()),
            (shaped((rows // 2, width), bf16), vmem()),
        ],
        [LOAD] * 4,
        [info, dq, dk, dv, weight],
        cost=(6 * rows * width * part, 8 * MIB),
    )


def start_kernel(blocks, patches, chips, info, *refs):
    (keep, far, start, grad_middle, turned, sums, bias_grad, spots, dq, dv, out_keep, out_got) = refs[:12]
    refs = refs[12:]
    low_out, refs = refs[0], refs[1:]
    grads, refs = refs[:-3], refs[-3:]
    held, rows_held, sem = refs
    core, chip = info[0], info[1]
    rows, part = dq.shape
    half_rows, width = keep.shape
    up_rows = width // blocks
    gain = turned[patches + GAIN_ONE : patches + GAIN_ONE + 1, :]
    own = pl.ds(pl.multiple_of(core * half_rows, half_rows), half_rows)
    grad_normed = keep[...] + far[...].astype(f32)
    normal, scale = normalise(start[own, :])
    grad = grad_middle[...] + norm_back(normal, scale, gain, grad_normed)
    low = grad.astype(bf16)
    low_out[...] = low
    ids = lax.broadcasted_iota(jnp.int32, (SMALL, half_rows), 0).astype(f32)
    mine = spots[0:1, pl.ds(pl.multiple_of(core * half_rows, 128), half_rows)]
    one_hot = jnp.where(ids == mine, 1.0, 0.0).astype(bf16)
    rows_held[...] = dot(one_hot, low)
    half = pl.ds(pl.multiple_of(core * part, 128), part)
    rows_held[patches : patches + 8, :] = jnp.zeros((8, width), f32)

    def put(i, row):
        rows_held[patches + i : patches + i + 1, :] = row

    rows_held[patches + QUERY_BIAS : patches + QUERY_BIAS + 1, half] = jnp.sum(
        dq[...].astype(f32), axis=0, keepdims=True
    )
    rows_held[patches + VALUE_BIAS : patches + VALUE_BIAS + 1, half] = jnp.sum(
        dv[...].astype(f32), axis=0, keepdims=True
    )
    put(OUTPUT_BIAS, sums[0:1, :])
    put(DOWN_BIAS, sums[1:2, :])
    put(GAIN_TWO, sums[2:3, :])
    put(SHIFT_TWO, sums[3:4, :])
    put(GAIN_ONE, jnp.sum(grad_normed * normal, axis=0, keepdims=True))
    put(SHIFT_ONE, jnp.sum(grad_normed, axis=0, keepdims=True))
    hidden = bias_grad.shape[1]
    spare = 2 * hidden // width
    biases = jnp.where(hidden_turns(spare, hidden, chips), bias_grad[0:1, :], 0.0)
    high = biases.astype(bf16)
    both = jnp.concatenate([high.astype(f32), biases - high.astype(f32)]).astype(bf16)
    placed = dot(both, hidden_places(core, hidden, width, chips))
    rows_held[patches + 8 : patches + 8 + spare, :] = placed[:spare] + placed[spare:]
    held[:, :SMALL] = rows_held[...].T.astype(bf16)
    if blocks == 4:
        slab = up_rows // 2
        for x in range(2):
            for side, ref in ((core, out_keep), (1 - core, out_got)):
                begin = pl.multiple_of((2 * side + x) * up_rows, up_rows)
                held[pl.ds(begin, slab), SMALL:] = ref[x, :, : width // 2]
                held[pl.ds(begin + slab, slab), SMALL:] = ref[x, :, width // 2 :]
    if blocks == 4:
        run_copies([copy for copy, _ in fold_copies(held, grads, chip, sem)])
    else:
        run_copies([pltpu.make_async_copy(held, grads[0], sem.at[0])])


def start_back(info, blocks, args, patches, chips):
    half_rows, width = args[0].shape
    columns = SMALL + width // 2 if blocks == 4 else SMALL
    outs = [shaped((width, columns), bf16)]
    if blocks == 4:
        outs = fold_shapes(width // 4, (columns,))
    return call(
        functools.partial(start_kernel, blocks, patches, chips),
        [(shaped((half_rows, width), bf16), vmem())]
        + [(one, anywhere()) for one in outs],
        [LOAD] * len(args),
        [info] + list(args),
        scratch=[
            pltpu.VMEM((width, columns), bf16),
            pltpu.VMEM((SMALL, width), f32),
            pltpu.SemaphoreType.DMA((8,)),
        ],
        cost=(2 * half_rows * width * SMALL, 10 * MIB),
    )


def split_kernel(plan, count, shift, info, *refs):
    place = lax.rem(info[2] >> shift, count)
    inputs, held = refs[: -1 - count], refs[-1]
    outs = refs[-1 - count : -1]
    column = 0
    for parts in plan:
        totals = []
        for terms in parts:
            total = 0.0
            for index, begin, rows in terms:
                total = total + inputs[index][begin : begin + rows, :].astype(f32)
            totals.append(total)
        whole = totals[0] if len(totals) == 1 else jnp.concatenate(totals)
        lanes = whole.shape[-1]
        held[..., column : column + lanes] = whole.reshape(held.shape[:-1] + (lanes,))
        column += lanes
    lead = (slice(None),) * (len(held.shape) - 3)
    for k in range(count):
        outs[k][...] = held[lead + (k ^ place,)].astype(outs[k].dtype)


def split(info, groups, shape, shift=0):
    arrays, plan, columns = [], [], 0
    for group in groups:
        base = len(arrays)
        parts = group.parts if isinstance(group, Fold) else [[(i, 0, None) for i in range(len(group))]]
        terms = group.terms if isinstance(group, Fold) else group
        flat = [array.reshape((-1,) + array.shape[-1:]) for array in terms]
        half = flat[0].shape[0] // 2
        plan.append(
            [
                [
                    (base + i, 0, flat[i].shape[0]) if begin is None else (base + i, begin * half, half)
                    for i, begin, _ in [(i, None if size is None else begin, size) for i, begin, size in part]
                ]
                for part in parts
            ]
        )
        arrays += flat
        columns += flat[0].shape[-1]
    count, total = shape[-2], columns
    for extent in shape:
        total *= extent
    one = shape[:-2] + (shape[-1], columns)
    return call(
        functools.partial(split_kernel, plan, count, shift),
        [(shaped(one, f32 if k == 0 else bf16), vmem()) for k in range(count)],
        [LOAD] * len(arrays),
        [info] + arrays,
        scratch=[pltpu.VMEM(shape + (columns,), f32)],
        limit=20,
        cost=(0, 8 * total),
    )


def swap(values, axis, bits):
    size = lax.axis_size(axis)
    return lax.ppermute(values, axis, [(i, i ^ bits) for i in range(size)])


def spread_perm(turn):
    pairs = []
    for w in range(lax.axis_size("wide")):
        for z in range(PLACES):
            there = (w - w % 2 + z // 2, 2 * (w % 2) + (turn ^ (z % 2)))
            pairs.append((w * PLACES + z, there[0] * PLACES + there[1]))
    return pairs


def unspread_turn(part, turn):
    return lax.ppermute(part, ("wide", "narrow"), [(b, a) for a, b in spread_perm(turn)])


def unspread_join(got, place):
    odd = (place % 2) == 1
    return jnp.stack([jnp.where(odd, got[1], got[0]), jnp.where(odd, got[0], got[1])])


def along(piece, bits):
    held = {0: piece}
    for bit in bits:
        held.update({index ^ (bit // 2): swap(part, "wide", bit) for index, part in list(held.items())})
    return [held[index] for index in range(len(held))]


def direct(piece, chips):
    return [piece] + [swap(piece, "wide", 2 * index) for index in range(1, chips)]


def fold(pieces, bits):
    held = dict(enumerate(pieces))
    for number, bit in enumerate(bits):
        step = bit // 2
        got = {i: swap(held[i ^ step], "wide", bit) for i in held if not i & step}
        if number == len(bits) - 1:
            return [held[0], got[0]]
        held = {i: (held[i].astype(f32) + got[i].astype(f32)).astype(bf16) for i in got}
    return [held[0]]


def after(values, *others):
    return lax.optimization_barrier((values,) + others)[0]


def together(*values):
    return lax.optimization_barrier(values)


class Fold:
    def __init__(self, outs, bits):
        self.outs, self.bits = list(outs), bits
        self.plane = len(outs) == 5
        if self.plane:
            self.near = [swap(outs[1], "wide", 2), swap(outs[2], "wide", 4)]

    def pairs(self):
        return [(self.outs[3], self.near[0]), (self.outs[4], self.near[1])] if self.plane else []

    def cross(self, sums):
        if self.plane:
            self.far = [swap(sums[0], "wide", 4), swap(sums[1], "wide", 2)]
            self.terms = [self.outs[0], *self.near, *self.far]
            first = [(0, 0, 1), (1, 1, 1), (3, 0, 1)]
            self.parts = [first, [(0, 1, 1), (2, 1, 1), (4, 0, 1)]]
        else:
            self.terms = fold(self.outs, self.bits)
            self.parts = [[(i, 0, None) for i in range(len(self.terms))]]


def local(
    tokens,
    positions,
    segments,
    position_table,
    input_weight,
    query_bias,
    value_bias,
    output_weight,
    output_bias,
    first_gain,
    first_shift,
    up_weight,
    up_bias,
    down_weight,
    down_bias,
    second_gain,
    second_shift,
    cotangent,
):
    size = lax.axis_size("wide")
    chips = size // 2
    bits = [2**i for i in range(1, size.bit_length() - 1)]
    seq_count, block, width = tokens.shape
    hidden = up_weight.shape[1]
    patches = position_table.shape[1]
    full = segments.shape[1]
    rows = width // (size * PLACES)
    part = width // 2
    own_hidden = hidden // 2
    wide, place = lax.axis_index("wide"), lax.axis_index("narrow")
    core, chip = wide % 2, wide // 2
    first_core = core == 0
    blocks = 4 if chips == 4 else 1
    info = jnp.stack([core, chip if blocks == 4 else 0 * chip, place, chip]).astype(jnp.int32)

    def pick(values, index, axis=0):
        return lax.dynamic_index_in_dim(values, index, axis, keepdims=False)

    def by_chip(pieces):
        flat = [piece.reshape((-1,) + piece.shape[-1:]) for piece in pieces]
        if blocks == 4:
            return flat
        whole = jnp.take(jnp.stack(flat), jnp.arange(chips) ^ chip, axis=0)
        return [whole.reshape((-1,) + flat[0].shape[1:])]

    def by_distance(outs, shape):
        if blocks == 4:
            return [out.reshape(shape) for out in outs]
        whole = outs[0].reshape((chips,) + shape)
        return [pick(whole, index ^ chip) for index in range(chips)]

    vectors = (
        query_bias,
        value_bias,
        output_bias,
        first_gain,
        first_shift,
        down_bias,
        second_gain,
        second_shift,
    )
    spare = up_bias.shape[0] // rows
    plane = blocks == 4
    up_sorted = up_weight
    if not plane:
        up_sorted = up_weight.reshape(rows, 4, chips // 4, 2, -1)
        up_sorted = jnp.swapaxes(up_sorted, 2, 3).reshape(rows, hidden)

    def cross_one(piece):
        if blocks == 4:
            return [piece, swap(piece, "wide", 2), swap(piece, "wide", 4)]
        return along(piece, bits)

    def cross_two(pieces):
        if blocks == 4:
            own, x, y = pieces
            first, second = cut(info, x, y)
            return [own, x, y, swap(first, "wide", 2), swap(second, "wide", 4)]
        return pieces

    def place_axis(piece):
        return piece.reshape(piece.shape[:-4] + (PLACES,) + piece.shape[-2:])

    def folded(outs, shape):
        if plane:
            return Fold(outs, bits)
        whole = outs[0].reshape((chips,) + shape)
        return Fold([pick(whole, index ^ chip) for index in range(chips)], bits)

    def crossed(folds, *values):
        count = len(values)
        near = [array for one in folds if one.plane for array in one.near]
        values = together(*values, *near)
        values, near = values[:count], list(values[count:])
        if plane:
            for one in folds:
                one.near, near = near[:2], near[2:]
            sums = add_firsts(info, [pair for one in folds for pair in one.pairs()])
        for i, one in enumerate(folds):
            one.cross(sums[2 * i : 2 * i + 2] if plane else None)
        return values

    def arrived(folds, *values):
        if not plane:
            return values
        count = len(values)
        far = [array for one in folds for array in one.far]
        values = together(*values, *far)
        values, far = values[:count], list(values[count:])
        for one in folds:
            one.far, far = far[:2], far[2:]
            one.terms = [*one.terms[:3], *one.far]
        return values

    rows_in = jnp.concatenate([jnp.stack(vectors), up_bias.reshape(spare, rows)])
    in_keep, in_send = pack_in(info, input_weight, position_table, rows_in)
    in_far = swap(in_send, "wide", 1)
    raw_parts = together(down_weight, output_weight, up_sorted, tokens, in_keep)
    raw = jnp.concatenate(raw_parts[:2]) if plane else raw_parts[0]
    up_keep, up_send = pack_up(info, raw_parts[2])
    first, second = sent(info, raw_parts[3], positions, segments)
    in_far, raw, up_send = together(in_far, raw, up_send)

    in_pair = arrange(info, [in_keep, in_far], 0, 0)
    in_got = [in_pair] + [swap(in_pair, "narrow", k) for k in range(1, PLACES)]
    raw_far = swap(raw, "narrow", 2)
    up_far = swap(up_send, "wide", 1)
    up_far, raw_far, first, *in_got = together(up_far, raw_far, first, *in_got)

    in_piece = arrange(info, in_got)
    in_chips = direct(in_piece, chips) if plane else along(in_piece, bits)
    raw_half = arrange(info, [raw, raw_far], 1)
    raw_far = swap(raw_half, "narrow", 1)
    low = lax.ppermute(first, ("wide", "narrow"), spread_perm(0))
    up_pair = arrange(info, [up_keep, up_far], 0, 0)
    low, raw_far, up_pair, second = together(low, raw_far, up_pair, second)

    up_far = swap(up_pair, "narrow", 2)
    high = lax.ppermute(second, ("wide", "narrow"), spread_perm(1))
    if plane:
        raw_far, *in_chips = together(settle(info, raw_half, raw_far), *in_chips)
        down_chips = cross_one(raw_far)
    else:
        down_chips = along(place_axis(arrange(info, [raw_half, raw_far])), bits)
    high, up_far = together(high, up_far)

    up_half = arrange(info, [up_pair, up_far], 1)
    up_far = swap(up_half, "narrow", 1)
    low_far, high_far = swap(low, "wide", 1), swap(high, "wide", 1)
    low_far, high_far, cotangent = together(low_far, high_far, cotangent)
    token_blocks = [low, high, low_far, high_far]
    cot_first, cot_second = pick_turns(info, cotangent)
    cot_low = lax.ppermute(cot_first, ("wide", "narrow"), spread_perm(0))
    in_blocks = by_chip(in_chips)
    q, k, v, start, normed, in_full, turned, seg, spots = front(
        info, token_blocks, in_blocks, patches
    )
    q, k, v, seg, cot_second, up_far, *down_chips = together(
        q, k, v, seg, cot_second, up_far, *down_chips
    )

    up_chips = cross_one(place_axis(arrange(info, [up_half, up_far])))
    cot_high = lax.ppermute(cot_second, ("wide", "narrow"), spread_perm(1))
    if plane:
        down_chips = cross_two(down_chips)
    att, total = attend(info, q, k, v, seg)
    count = len(down_chips)
    att, cot_low, cot_high, *rest = together(att, cot_low, cot_high, *down_chips, *up_chips)
    down_chips, up_chips = rest[:count], rest[count:]

    att_far = swap(att, "wide", 1)
    if plane:
        out_rows = last_blocks(info, *down_chips[:3], down_chips[4])
        out_weights = [out_rows, swap(out_rows, "wide", 1)]
    else:
        out_weights = [lax.all_gather(output_weight, ("wide", "narrow"), axis=0, tiled=True)]
    if plane:
        up_chips = cross_two(up_chips)
    cots = [cot_low, cot_high, swap(cot_low, "wide", 1), swap(cot_high, "wide", 1)]
    if plane:
        up_blocks = [part.reshape((-1,) + part.shape[-1:]) for part in up_chips]
        down_blocks = down_chips
    else:
        up_blocks = by_chip(up_chips)
        down_blocks = [by_chip(down_chips)[0].reshape(4 * PLACES, -1, width)]
    middle, normed_two, up_bias_own, out_full = middle_front(
        info, att, att_far, start, turned, out_weights, own_hidden, patches, chips
    )
    keep, send, slope, up_full, down_full, cot, *down_grads = feed_front(
        info, normed_two, up_bias_own, cots, up_blocks, down_blocks, blocks
    )
    down_rows = own_hidden // (chips * PLACES)
    down_fold = folded(down_grads, (PLACES, down_rows, width))
    fed = feed_back(info, slope, cot, up_full, down_full)
    back, back_low, grad_hidden, bias_grad, send, normed_two = crossed(
        [down_fold], *fed, send, normed_two
    )
    back_far = swap(back_low, "wide", 1)
    out_far = swap(send, "wide", 1)
    up_grads = weight_grad(info, normed_two, [grad_hidden], blocks)
    back_far, out_far, *up_grads = arrived([down_fold], back_far, out_far, *up_grads)
    up_fold = folded(up_grads, (2, PLACES, rows, own_hidden))
    down_keep, down_send = split(info, [down_fold], (2, 2, down_rows))
    down_got = swap(down_send, "narrow", 1)
    grad_middle, grad_att, out_keep, out_send, sums = middle_back(
        info, back, back_far, middle, turned, att, out_full, cot, patches, blocks
    )
    out_far, grad_att = together(out_far, grad_att)
    out_turns = output_turns(info, middle, keep, out_far, turned, patches)
    out_turns = [unspread_turn(part, turn) for turn, part in enumerate(out_turns)]
    if blocks == 1:
        shape = (chips // 2, 2, PLACES * rows, width)
        out_keep = pick(out_keep.reshape(shape), core, 1)
        out_send = pick(out_send.reshape(shape), 1 - core, 1)
    grad_att, down_got = crossed([up_fold], grad_att, down_got)
    dq, dk, dv = attend_back(info, q, k, v, att, grad_att, total, seg)
    dq, dk, dv, out_send, normed, *out_turns = arrived(
        [up_fold], dq, dk, dv, out_send, normed, *out_turns
    )
    start_keep, start_send = project_back(info, dq, dk, dv, in_full)
    start_far, out_got = swap(start_send, "wide", 1), swap(out_send, "wide", 1)
    up_keep, up_send = split(info, [up_fold], (2, 2, 2, rows))
    down_keep, down_send = split(info, [[down_keep, down_got]], (2, down_rows), 1)
    normed, start_keep, up_send, down_send = together(normed, start_keep, up_send, down_send)
    up_got = swap(up_send, "narrow", 1)
    down_got = swap(down_send, "narrow", 2)
    in_grads = weight_grad(info, normed, [dq, dk, dv], blocks)
    start_far, out_got, up_got, down_got, *in_grads = together(
        start_far, out_got, up_got, down_got, *in_grads
    )
    in_fold = folded(in_grads, (2, PLACES, rows, 3 * part))
    up_keep, up_send = split(info, [[up_keep, up_got]], (2, 2, rows), 1)
    start_far, up_send = together(start_far, up_send)
    up_got = swap(up_send, "narrow", 2)
    args = [start_keep, start_far, start, grad_middle, turned, sums, bias_grad, spots, dq, dv]
    started = start_back(info, blocks, args + [out_keep, out_got], patches, chips)
    if not plane:
        out_grad = jnp.where(
            first_core,
            jnp.concatenate([out_keep, out_got]),
            jnp.concatenate([out_got, out_keep]),
        ).reshape(chips, PLACES, rows, 2, part)
        out_grad = jnp.transpose(out_grad, (0, 3, 1, 2, 4)).reshape(width, part)
        started = [started[0], jnp.concatenate([started[1], out_grad], axis=1)]
    up_got, grad_blocks, *small_grads = crossed([in_fold], up_got, *started)
    small_fold = folded(small_grads, (2, PLACES, rows, SMALL + part))
    grad_first, grad_second = pick_turns(info, grad_blocks.reshape(2, block, width))
    grad_first = unspread_turn(grad_first, 0)
    (grad_second,) = crossed([small_fold], *arrived([in_fold], grad_second))
    grad_second = unspread_turn(grad_second, 1)
    (grad_first,) = arrived([small_fold], grad_first)
    in_cut = split(info, [in_fold, small_fold], (2, PLACES, rows))
    in_got = [swap(in_cut[index], "narrow", index) for index in range(1, PLACES)]
    in_keep, down_keep, up_keep, up_got, grad_first, grad_second, *out_turns = together(
        in_cut[0], down_keep, up_keep, up_got, grad_first, grad_second, *out_turns
    )
    outputs = unspread_join(out_turns, place)
    grad_tokens = unspread_join([grad_first, grad_second], place)
    down_share = down_keep + down_got.astype(f32)
    up_total = up_keep + up_got.astype(f32)
    up_keep = pick(up_total, core)
    up_got = swap(pick(up_total, 1 - core).astype(bf16), "wide", 1).astype(f32)
    up_both = [up_keep.reshape(rows, chips, 1, -1), up_got.reshape(rows, chips, 1, -1)]
    up_share = jnp.where(
        first_core, jnp.concatenate(up_both, axis=2), jnp.concatenate(up_both[::-1], axis=2)
    ).reshape(rows, hidden)
    outputs, grad_tokens, down_share, up_share, *in_got = together(
        outputs, grad_tokens, down_share, up_share, *in_got
    )
    in_total = in_keep
    for array in in_got:
        in_total = in_total + array.astype(f32)
    sent_columns = 3 * part + SMALL
    in_keep = pick(in_total, core)
    in_far = pick(in_total, 1 - core)[:, :sent_columns].astype(bf16)
    in_far = swap(in_far, "wide", 1).astype(f32)
    in_both = [in_keep[:, : 3 * part].reshape(rows, 3, 1, part), in_far[:, : 3 * part].reshape(rows, 3, 1, part)]
    in_share = jnp.where(
        first_core, jnp.concatenate(in_both, axis=2), jnp.concatenate(in_both[::-1], axis=2)
    ).reshape(rows, 3 * width)
    small_share = in_keep[:, 3 * part : sent_columns] + in_far[:, 3 * part :]
    out_share = jnp.concatenate([in_total[0, :, sent_columns:], in_total[1, :, sent_columns:]], axis=1)
    tail = [small_share[:, patches + i] for i in range(8)]
    return (
        outputs,
        grad_tokens,
        small_share[:, :patches],
        in_share,
        tail[QUERY_BIAS],
        tail[VALUE_BIAS],
        out_share,
        tail[OUTPUT_BIAS],
        tail[GAIN_ONE],
        tail[SHIFT_ONE],
        up_share,
        small_share[:, patches + 8 : patches + 8 + spare].T.reshape(-1),
        down_share,
        tail[DOWN_BIAS],
        tail[GAIN_TWO],
        tail[SHIFT_TWO],
    )


def solution(mesh):
    both = ("wide", "narrow")
    matrix = P(both, None)
    vector = P(both)
    block = P("wide", "narrow", None)
    gains = [matrix, matrix] + [vector] * 2 + [matrix] + [vector] * 3 + [matrix, vector, matrix]
    gains += [vector] * 3
    return jax.shard_map(
        local,
        mesh=mesh,
        in_specs=tuple([block, P("wide", "narrow"), P("wide", None)] + gains + [block]),
        out_specs=tuple([block, block] + gains),
        check_vma=False,
    )
```

```python
import functools

import jax
import jax.numpy as jnp
from jax import lax
from jax.experimental import pallas as pl
from jax.experimental.pallas import tpu as pltpu
from jax.sharding import PartitionSpec as P

HEADS = 12
PLACES = 4
epsilon = 1e-05
masked_score = -1e30

f32 = jnp.float32
bf16 = jnp.bfloat16
MIB = 1 << 20
LOAD, HELD = "load", "held"
QUERY_BIAS, VALUE_BIAS, OUTPUT_BIAS, GAIN_ONE, SHIFT_ONE, DOWN_BIAS, GAIN_TWO, SHIFT_TWO = range(8)
SMALL = 128


def dot(left, right):
    return jnp.dot(left, right, preferred_element_type=f32)


def dot_left(left, right):
    return lax.dot_general(left, right, (((0,), (0,)), ((), ())), preferred_element_type=f32)


def dot_right(left, right):
    return lax.dot_general(left, right, (((1,), (1,)), ((), ())), preferred_element_type=f32)


def call(kernel, outs, ins, args, scratch=(), grid=None, limit=14, cost=None):
    loads = []
    specs = [pl.BlockSpec(memory_space=pltpu.SMEM)]
    for index, (spec, array) in enumerate(zip(ins, args[1:], strict=True)):
        if spec == LOAD:
            whole = False
            spec = pl.BlockSpec(memory_space=pl.ANY if whole else pltpu.VMEM)
            if whole:
                loads.append(index)
        elif spec == HELD:
            spec = pl.BlockSpec(memory_space=pl.ANY)
        specs.append(spec)
    count, news = len(ins), len(loads)

    def loaded(info, *refs):
        refs, held, sem = list(refs[: -1 - news]), refs[-1 - news : -1], refs[-1]
        copies = []
        for i, index in enumerate(loads):
            copies.append(pltpu.make_async_copy(refs[index], held[i], sem.at[i]))
            refs[index] = held[i]
        run_copies(copies)
        kernel(info, *refs)

    extra = [pltpu.VMEM(args[1 + i].shape, args[1 + i].dtype) for i in loads]
    if loads:
        extra.append(pltpu.SemaphoreType.DMA((news,)))
    return pl.pallas_call(
        loaded if loads else kernel,
        out_shape=[shape for shape, _ in outs],
        in_specs=specs,
        out_specs=[spec for _, spec in outs],
        scratch_shapes=list(scratch) + extra,
        **({"grid": grid} if grid else {}),
        compiler_params=pltpu.CompilerParams(vmem_limit_bytes=limit * MIB),
        cost_estimate=pl.CostEstimate(
            flops=int(cost[0]), bytes_accessed=int(cost[1]), transcendentals=0
        ),
    )(*args)


def shaped(shape, kind):
    return jax.ShapeDtypeStruct(shape, kind)


def vmem():
    return pl.BlockSpec(memory_space=pltpu.VMEM)


def anywhere():
    return pl.BlockSpec(memory_space=pl.ANY)


def normalise(values):
    average = jnp.mean(values, axis=-1, keepdims=True)
    centered = values - average
    variance = jnp.mean(centered * centered, axis=-1, keepdims=True)
    scale = lax.rsqrt(variance + epsilon)
    return centered * scale, scale


def norm_back(normal, scale, gain, grad):
    inner = grad * gain
    return scale * (
        inner
        - jnp.mean(inner, axis=-1, keepdims=True)
        - normal * jnp.mean(inner * normal, axis=-1, keepdims=True)
    )


def fold_shapes(rows, rest):
    return [shaped((count,) + rest, bf16) for count in (rows, rows, rows, rows // 2, rows // 2)]


def fold_copies(held, outs, chip, sem):
    rows = outs[0].shape[0]
    half = rows // 2
    at = lambda distance, second: pl.ds(
        pl.multiple_of((distance ^ chip) * rows + second * half, half), half
    )
    whole = pl.ds(pl.multiple_of(chip * rows, rows), rows)
    first, second = pl.ds(0, half), pl.ds(half, half)
    own, to_x, to_y, y_left, x_left = outs
    pairs = [
        (0, held.at[whole], own),
        (3, held.at[at(3, 0)], to_x.at[first]),
        (1, held.at[at(1, 0)], to_x.at[second]),
        (3, held.at[at(3, 1)], to_y.at[first]),
        (2, held.at[at(2, 1)], to_y.at[second]),
        (2, held.at[at(2, 0)], y_left),
        (1, held.at[at(1, 1)], x_left),
    ]
    return [
        (pltpu.make_async_copy(a, b, sem.at[i]), distance)
        for i, (distance, a, b) in enumerate(pairs)
    ]


def run_copies(copies):
    for copy in copies:
        copy.start()
    for copy in copies:
        copy.wait()


def pack_in_kernel(patches, info, weight, table, rows_in, keep, send):
    core = info[0]
    part = weight.shape[1] // 6
    turned = rows_in[...].astype(f32).T
    empty = jnp.zeros((weight.shape[0], SMALL - patches - turned.shape[1]), f32)
    small = jnp.concatenate([table[...].astype(f32), turned, empty], axis=1).astype(bf16)
    for ref, side in ((keep, core), (send, 1 - core)):
        for i in range(3):
            there = pl.ds(pl.multiple_of((2 * i + side) * part, 128), part)
            ref[:, i * part : (i + 1) * part] = weight[:, there]
        ref[:, 3 * part :] = small


def pack_in(info, weight, table, rows_in):
    rows, columns = weight.shape[0], weight.shape[1] // 2 + SMALL
    return call(
        functools.partial(pack_in_kernel, table.shape[1]),
        [(shaped((rows, columns), bf16), vmem())] * 2,
        [vmem()] * 3,
        [info, weight, table, rows_in],
        limit=8,
        cost=(0, MIB),
    )


def pack_up_kernel(info, up, keep, send):
    step = keep.shape[1] // 4
    for ref, side in ((keep, info[0]), (send, 1 - info[0])):
        for q in range(4):
            there = pl.ds(pl.multiple_of((2 * q + side) * step, 128), step)
            ref[:, q * step : (q + 1) * step] = up[:, there]


def pack_up(info, up):
    out = (shaped((up.shape[0], up.shape[1] // 2), bf16), vmem())
    return call(pack_up_kernel, [out] * 2, [vmem()], [info, up], limit=8, cost=(0, MIB))


def sent_kernel(info, tokens, positions, segments, first, second, extra):
    place = info[2]
    block, width = tokens.shape[1], tokens.shape[2]
    full = segments.shape[1]
    extra[...] = jnp.zeros_like(extra)
    for k, out in enumerate((first, second)):
        index = k ^ (place % 2)
        row = segments[pl.ds(index, 1), :]
        row = (row - row[:, 0:1]).astype(f32)
        extra[0:1, :block] = positions[pl.ds(index, 1), :].astype(f32)
        extra[1:2, :] = row[:, :width]
        extra[2:3, : full - width] = row[:, width:]
        out[:block, :] = tokens[index]
        out[block:, :] = extra[...].astype(bf16)


def sent(info, tokens, positions, segments):
    _, block, width = tokens.shape
    one = (shaped((block + 16, width), bf16), vmem())
    return call(
        sent_kernel,
        [one, one],
        [vmem()] * 3,
        [info, tokens, positions, segments],
        scratch=[pltpu.VMEM((16, width), f32)],
        limit=8,
        cost=(0, 2 * MIB),
    )


def arrange_kernel(slot, shift, info, *refs):
    ins, out = refs[:-1], refs[-1]
    lead = len(out.shape) - 3
    place = lax.rem(info[slot] >> shift, len(ins))
    for k, ref in enumerate(ins):
        out[(slice(None),) * lead + (k ^ place,)] = ref[...]


def arrange(info, pieces, shift=0, slot=2):
    shape = pieces[0].shape
    shape = shape[:-2] + (len(pieces),) + shape[-2:]
    total = 1
    for extent in shape:
        total *= extent
    return call(
        functools.partial(arrange_kernel, slot, shift),
        [(shaped(shape, bf16), vmem())],
        [vmem()] * len(pieces),
        [info] + list(pieces),
        limit=8,
        cost=(0, 4 * total),
    )[0]


def settle_kernel(info, own, far, out):
    odd = lax.rem(info[2], 2)
    block = out.shape[1]
    rows = own.shape[1] - block
    for k, ref in enumerate((own, far)):
        for high in range(2):
            out[2 * high + (k ^ odd)] = ref[high, :block, :]
    both = (own, far)
    for high in range(2):
        pair = [ref[high, block:, :].astype(f32) for ref in both]
        for low in range(2):
            row = jnp.where(odd == low, pair[0], pair[1]).astype(bf16)
            begin = (2 * high + low) * rows
            out[PLACES, begin : begin + rows, :] = row


def settle(info, own, far):
    _, rows, width = own.shape
    block = rows * PLACES // (PLACES + 1)
    return call(
        settle_kernel,
        [(shaped((PLACES + 1, block, width), bf16), vmem())],
        [vmem()] * 2,
        [info, own, far],
        limit=8,
        cost=(0, 2 * MIB),
    )[0]


def last_kernel(info, own, x, y, d, out):
    for distance, ref in enumerate((own, x, y, d)):
        out[distance ^ info[1]] = ref[ref.shape[0] - 1]


def last_blocks(info, own, x, y, d):
    return call(
        last_kernel,
        [(shaped((4,) + own.shape[1:], bf16), vmem())],
        [vmem()] * 4,
        [info, own, x, y, d],
        limit=8,
        cost=(0, MIB),
    )[0]


def cut_kernel(info, x, y, first, second):
    half = first.shape[0]
    first[...] = y[:half]
    second[...] = x[half:]


def cut(info, x, y):
    half = x.shape[0] // 2
    outs = [
        (shaped((half,) + x.shape[1:], bf16), vmem()),
        (shaped((x.shape[0] - half,) + x.shape[1:], bf16), vmem()),
    ]
    return call(cut_kernel, outs, [LOAD] * 2, [info, x, y], limit=8, cost=(0, MIB))


def add_kernel(info, *refs):
    for i in range(0, len(refs), 3):
        a, b, out = refs[i : i + 3]
        out[...] = (a[...].astype(f32) + b[: out.shape[0]].astype(f32)).astype(bf16)


def add_firsts(info, pairs):
    def kernel(info, *refs):
        outs = refs[2 * len(pairs) :]
        add_kernel(info, *[ref for i, out in enumerate(outs) for ref in (*refs[2 * i : 2 * i + 2], out)])

    return call(
        kernel,
        [(shaped(a.shape, bf16), vmem()) for a, _ in pairs],
        [LOAD] * (2 * len(pairs)),
        [info] + [array for pair in pairs for array in pair],
        limit=8,
        cost=(0, MIB),
    )


def pick_kernel(info, blocks, first, second):
    odd = lax.rem(info[2], 2)
    first[...] = blocks[odd]
    second[...] = blocks[1 - odd]


def pick_turns(info, blocks):
    out = (shaped(blocks.shape[1:], bf16), vmem())
    return call(pick_kernel, [out] * 2, [LOAD], [info, blocks], limit=8, cost=(0, MIB))


def output_kernel(patches, info, middle, keep, far, turned, first, second):
    core, odd = info[0], lax.rem(info[2], 2)
    half = keep.shape[0]
    block = half // 2
    bias = turned[patches + DOWN_BIAS : patches + DOWN_BIAS + 1, :]
    for ref, which in ((first, odd), (second, 1 - odd)):
        here = pl.ds(pl.multiple_of(which * block, block), block)
        there = pl.ds(pl.multiple_of(core * half + which * block, block), block)
        ref[...] = (middle[there, :] + keep[here, :] + far[here, :].astype(f32) + bias).astype(bf16)


def output_turns(info, middle, keep, far, turned, patches):
    out = (shaped((keep.shape[0] // 2, keep.shape[1]), bf16), vmem())
    return call(
        functools.partial(output_kernel, patches),
        [out] * 2,
        [LOAD] * 4,
        [info, middle, keep, far, turned],
        limit=8,
        cost=(0, 6 * MIB),
    )


def front_kernel(blocks, patches, info, *refs):
    tokens_in, refs = refs[:4], refs[4:]
    weights_in, refs = refs[:blocks], refs[blocks:]
    q_out, k_out, v_out, start_out, normed_out, weight, turned_out, seg_out, spot_out = refs[:9]
    held, sem, weight_sem = refs[9:]
    core, chip, place = info[0], info[1], info[2]
    block, columns = held.shape[1] - 16, weight.shape[1] - SMALL
    part = columns // 3
    copies = []
    for i in range(4):
        side = core if i < 2 else 1 - core
        there = 2 * side + ((i % 2) ^ (place % 2))
        copies.append(pltpu.make_async_copy(tokens_in[i], held.at[there], sem.at[i]))
    copies += piece_copies(weights_in, weight, info, weight_sem)
    run_copies(copies)
    small = weight[:, columns:]
    turned_out[...] = small.astype(f32).T
    vector = lambda i: turned_out[patches + i : patches + i + 1, :]
    half = pl.ds(pl.multiple_of(core * part, 128), part)
    query_bias = turned_out[patches + QUERY_BIAS : patches + QUERY_BIAS + 1, half]
    value_bias = turned_out[patches + VALUE_BIAS : patches + VALUE_BIAS + 1, half]
    gain, shift = vector(GAIN_ONE), vector(SHIFT_ONE)
    extra = held[0, block : block + 16, :].astype(f32)
    width = extra.shape[1]
    segment = jnp.concatenate([extra[1:2, :], extra[2:3, : 4 * block - width]], axis=1)
    seg_out[...] = jnp.broadcast_to(segment, seg_out.shape)
    ids = lax.broadcasted_iota(jnp.int32, (SMALL, block), 0).astype(f32)
    for b in range(4):
        here = slice(b * block, (b + 1) * block)
        spot = held[b, block : block + 16, :].astype(f32)[0:1, :block]
        spot_out[:, here] = jnp.broadcast_to(spot, (8, block))
        one_hot = jnp.where(ids == spot, 1.0, 0.0).astype(bf16)
        embedded = lax.dot_general(
            one_hot, small, (((0,), (1,)), ((), ())), preferred_element_type=f32
        )
        start = held[b, :block, :].astype(f32) + embedded
        start_out[here, :] = start
        normal, _ = normalise(start)
        normed = (normal * gain + shift).astype(bf16)
        normed_out[here, :] = normed
        projected = dot(normed, weight[:, :columns])
        query = (projected[:, :part] + query_bias).astype(bf16).astype(f32) * 0.125
        q_out[here, :] = query.astype(bf16)
        k_out[here, :] = projected[:, part : 2 * part].astype(bf16)
        v_out[here, :] = (projected[:, 2 * part :] + value_bias).astype(bf16)


def front(info, tokens, weights, patches):
    blocks = len(weights)
    block, width = tokens[0].shape[0] - 16, tokens[0].shape[1]
    columns = weights[0].shape[1]
    part = (columns - SMALL) // 3
    rows = 4 * block
    return call(
        functools.partial(front_kernel, blocks, patches),
        [
            (shaped((rows, part), bf16), vmem()),
            (shaped((rows, part), bf16), vmem()),
            (shaped((rows, part), bf16), vmem()),
            (shaped((rows, width), f32), vmem()),
            (shaped((rows, width), bf16), vmem()),
            (shaped((width, columns), bf16), vmem()),
            (shaped((SMALL, width), f32), vmem()),
            (shaped((8, rows), f32), vmem()),
            (shaped((8, rows), f32), vmem()),
        ],
        [HELD] * (4 + blocks),
        [info] + list(tokens) + list(weights),
        scratch=[
            pltpu.VMEM((4, block + 16, width), bf16),
            pltpu.SemaphoreType.DMA((4,)),
            pltpu.SemaphoreType.DMA((blocks,)),
        ],
        cost=(2 * rows * width * columns, 12 * MIB),
    )


def fill_bias(bias, seg):
    block = bias.shape[1]
    wide = seg[...]
    tall = jnp.broadcast_to(wide[0:1, :], (128, wide.shape[1])).T[:, 0:1]
    base = 0
    for b in range(4):
        many = (b + 1) * block
        key = lax.broadcasted_iota(jnp.int32, (many, block), 0)
        ask = lax.broadcasted_iota(jnp.int32, (many, block), 1) + b * block
        same = tall[:many] == wide[0:1, b * block : (b + 1) * block]
        bias[base : base + many, :] = jnp.where((key <= ask) & same, 0.0, masked_score)
        base += many


def turn(values):
    return values.astype(f32).T.astype(bf16)


def attend_kernel(info, q, k, v, seg, out, total, bias):
    block = bias.shape[1]

    @pl.when(pl.program_id(0) == 0)
    def _():
        fill_bias(bias, seg)

    turned_q, turned_v = turn(q[...]), turn(v[...])
    side = lax.broadcasted_iota(jnp.int32, (128, block), 0) // 64
    base = 0
    for b in range(4):
        many = (b + 1) * block
        here = slice(b * block, (b + 1) * block)
        mixed = []
        for h in range(2):
            ask = jnp.where(side == h, turned_q[:, here].astype(f32), 0.0).astype(bf16)
            scores = dot(k[:many, :], ask) + bias[base : base + many, :]
            top = jnp.max(scores, axis=0, keepdims=True)
            raised = jnp.exp(scores - top)
            mass = jnp.sum(raised, axis=0, keepdims=True)
            total[0, h : h + 1, here] = top + jnp.log(mass)
            part = dot(turned_v[64 * h : 64 * h + 64, :many], raised.astype(bf16))
            mixed.append(part * (1.0 / mass))
        out[here, :] = jnp.concatenate(mixed, axis=0).T.astype(bf16)
        base += many


def attend(info, q, k, v, seg):
    rows, part = q.shape
    pairs = part // 128
    column = pl.BlockSpec((rows, 128), lambda i: (0, i))
    whole = pl.BlockSpec(seg.shape, lambda i: (0, 0))
    return call(
        attend_kernel,
        [
            (shaped((rows, part), bf16), column),
            (shaped((pairs, 8, rows), f32), pl.BlockSpec((1, 8, rows), lambda i: (i, 0, 0))),
        ],
        [column, column, column, whole],
        [info, q, k, v, seg],
        scratch=[pltpu.VMEM((10 * rows // 4, rows // 4), f32)],
        grid=(pairs,),
        cost=(6 * rows * rows * part, 4 * MIB),
    )


def attend_back_kernel(info, q, k, v, o, g, total, seg, dq, dk, dv, bias, dk_sum, dv_sum):
    block = bias.shape[1]

    @pl.when(pl.program_id(0) == 0)
    def _():
        fill_bias(bias, seg)

    wide_g = g[...].astype(f32).T
    product = wide_g * o[...].astype(f32).T
    inner = [jnp.sum(product[64 * h : 64 * h + 64], axis=0, keepdims=True) for h in range(2)]
    turned_q, turned_k = turn(q[...]), turn(k[...])
    turned_g = wide_g.astype(bf16)
    side = lax.broadcasted_iota(jnp.int32, (128, block), 0) // 64
    flat = lax.broadcasted_iota(jnp.int32, (block, 128), 1) // 64
    dk_sum[...] = jnp.zeros_like(dk_sum)
    dv_sum[...] = jnp.zeros_like(dv_sum)
    base = 0
    for b in range(4):
        many = (b + 1) * block
        here = slice(b * block, (b + 1) * block)
        grads = []
        for h in range(2):
            ask = jnp.where(side == h, turned_q[:, here].astype(f32), 0.0).astype(bf16)
            ask_g = jnp.where(side == h, turned_g[:, here].astype(f32), 0.0).astype(bf16)
            scores = dot(k[:many, :], ask) + bias[base : base + many, :]
            probs = jnp.exp(scores - total[0, h : h + 1, here])
            grad_probs = dot(v[:many, :], ask_g)
            grad_scores = (probs * (grad_probs - inner[h][:, here])).astype(bf16)
            own_q = jnp.where(flat == h, q[here, :].astype(f32), 0.0).astype(bf16)
            own_g = jnp.where(flat == h, g[here, :].astype(f32), 0.0).astype(bf16)
            dv_sum[:many, :] += dot(probs.astype(bf16), own_g)
            dk_sum[:many, :] += dot(grad_scores, own_q)
            grads.append(dot(turned_k[64 * h : 64 * h + 64, :many], grad_scores))
        dq[here, :] = (jnp.concatenate(grads, axis=0).T * 0.125).astype(bf16)
        base += many
    dk[...] = dk_sum[...].astype(bf16)
    dv[...] = dv_sum[...].astype(bf16)


def attend_back(info, q, k, v, o, g, total, seg):
    rows, part = q.shape
    pairs = part // 128
    column = pl.BlockSpec((rows, 128), lambda i: (0, i))
    whole = pl.BlockSpec(seg.shape, lambda i: (0, 0))
    out = (shaped((rows, part), bf16), column)
    return call(
        attend_back_kernel,
        [out, out, out],
        [column] * 5 + [pl.BlockSpec((1, 8, rows), lambda i: (i, 0, 0)), whole],
        [info, q, k, v, o, g, total, seg],
        scratch=[
            pltpu.VMEM((10 * rows // 4, rows // 4), f32),
            pltpu.VMEM((rows, 128), f32),
            pltpu.VMEM((rows, 128), f32),
        ],
        grid=(pairs,),
        cost=(15 * rows * rows * part, 6 * MIB),
    )


def cotangent_copies(info, pieces, held, sems):
    core, place = info[0], info[2]
    copies = []
    for i in range(4):
        side = core if i < 2 else 1 - core
        there = 2 * side + ((i % 2) ^ (place % 2))
        copies.append(pltpu.make_async_copy(pieces[i], held.at[there], sems[i]))
    return copies


def gelu_parts(values):
    scale = 0.7978845608028654
    square = values * values
    slope = jnp.tanh(values * (scale + (scale * 0.044715) * square))
    half = 0.5 * (1.0 + slope)
    grad = half + 0.5 * values * (1.0 - slope * slope) * (
        scale + (3.0 * scale * 0.044715) * square
    )
    return values * half, grad


def piece_copies(pieces, target, info, sem, lanes=None):
    chip = info[1]
    rows = pieces[0].shape[0]
    copies, base = [], 0
    for i, ref in enumerate(pieces):
        distance = min(i, 3)
        begin = pl.multiple_of((distance ^ chip) * rows, rows)
        if i == 4:
            begin = pl.multiple_of(begin + rows // 2, rows // 2)
        source = ref if lanes is None else ref.at[:, lanes]
        there = target.at[pl.ds(begin, ref.shape[0])]
        copies.append(pltpu.make_async_copy(source, there, sem.at[i]))
    return copies


def block_copies(pieces, target, info, sem):
    if len(pieces) == 1:
        return [pltpu.make_async_copy(pieces[0], target, sem.at[0])]
    copies = []
    for i, ref in enumerate(pieces):
        begin = (min(i, 3) ^ info[1]) * PLACES + (2 if i == 4 else 0)
        count = 2 if i >= 3 else PLACES
        copies.append(
            pltpu.make_async_copy(ref.at[pl.ds(0, count)], target.at[pl.ds(begin, count)], sem.at[i])
        )
    return copies


def hidden_places(core, hidden, width, chips):
    spare = 2 * hidden // width
    share = hidden // chips
    device = share // PLACES
    rows = device // spare
    unit = lax.broadcasted_iota(jnp.int32, (hidden, 1), 0)
    rest = lax.rem(unit, share)
    row = ((2 * (unit // share) + core) * PLACES + rest // device) * rows + lax.rem(rest, rows)
    lane = lax.broadcasted_iota(jnp.int32, (hidden, width), 1)
    return jnp.where(lane == row, 1.0, 0.0).astype(bf16)


def hidden_turns(spare, hidden, chips):
    device = hidden // (chips * PLACES)
    unit = lax.broadcasted_iota(jnp.int32, (spare, hidden), 1)
    return lax.rem(unit, device) // (device // spare) == lax.broadcasted_iota(
        jnp.int32, (spare, hidden), 0
    )


def middle_kernel(patches, chips, hidden, info, att, att_far, start, turned, *refs):
    weights, refs = refs[:-4], refs[-4:]
    middle_out, normed_out, bias_out, weight_out = refs
    core = info[0]
    rows, width = start.shape
    part, tile = width // 2, rows // 4
    if len(weights) == 2:
        block = weights[0].shape[1]
        for side, ref in ((core, weights[0]), (1 - core, weights[1])):
            for q in range(4):
                begin = pl.multiple_of((2 * q + side) * block, block)
                weight_out[pl.ds(begin, block), :] = ref[q]
    else:
        weight_out[...] = weights[0][...]
    spare = 2 * hidden // width
    biases = turned[patches + 8 : patches + 8 + spare, :].astype(bf16)
    spread_out = dot_right(biases, hidden_places(core, hidden, width, chips))
    bias = jnp.sum(
        jnp.where(hidden_turns(spare, hidden, chips), spread_out, 0.0), axis=0, keepdims=True
    )
    bias_out[...] = jnp.broadcast_to(bias, bias_out.shape)
    vector = lambda i: turned[patches + i : patches + i + 1, :]
    own = pl.ds(pl.multiple_of(core * part, 128), part)
    far = pl.ds(pl.multiple_of((1 - core) * part, 128), part)
    gain, shift, out_bias = vector(GAIN_TWO), vector(SHIFT_TWO), vector(OUTPUT_BIAS)
    for t in range(4):
        here = slice(t * tile, (t + 1) * tile)
        mixed = dot(att[here, :], weight_out[own, :]) + dot(att_far[here, :], weight_out[far, :])
        middle = start[here, :] + mixed + out_bias
        middle_out[here, :] = middle
        normal, _ = normalise(middle)
        normed_out[here, :] = (normal * gain + shift).astype(bf16)


def middle_front(info, att, att_far, start, turned, weights, hidden, patches, chips):
    rows, width = start.shape
    return call(
        functools.partial(middle_kernel, patches, chips, hidden),
        [
            (shaped((rows, width), f32), vmem()),
            (shaped((rows, width), bf16), vmem()),
            (shaped((8, hidden), f32), vmem()),
            (shaped((width, width), bf16), vmem()),
        ],
        [LOAD] * (4 + len(weights)),
        [info, att, att_far, start, turned] + list(weights),
        cost=(2 * rows * width * width, 12 * MIB),
    )


def feed_front_kernel(ups, downs, blocks, info, normed, up_bias, *refs):
    cot_in, refs = refs[:4], refs[4:]
    up_in, refs = refs[:ups], refs[ups:]
    down_in, refs = refs[:downs], refs[downs:]
    keep_out, send_out, slope_out, up, down, cot, refs = *refs[:6], refs[6:]
    down_grads, (act, far_sum, down_grad, cot_sem, up_sem, down_sem) = refs[:-6], refs[-6:]
    core, chip = info[0], info[1]
    rows, width = normed.shape
    hidden = up.shape[1]
    chunk = hidden // 4
    half = rows // 2
    early = piece_copies(up_in, up, info, up_sem)
    late = block_copies(down_in, down, info, down_sem)
    late += cotangent_copies(info, cot_in, cot, [cot_sem.at[i] for i in range(4)])
    for copy in early + late:
        copy.start()
    for copy in early:
        copy.wait()
    own = pl.ds(pl.multiple_of(core * half, half), half)
    far = pl.ds(pl.multiple_of((1 - core) * half, half), half)
    outs = []
    pair = 2 * chunk
    for step, distances in enumerate(((3, 2), (1, 0))):
        which = (1 - step) ^ (chip // 2)
        lanes = pl.ds(pl.multiple_of(which * pair, 128), pair)
        blocks_here = pl.ds(pl.multiple_of(which * 2 * PLACES, 2 * PLACES), 2 * PLACES)
        for side, here in enumerate((own, far)):
            value, slope = gelu_parts(dot(normed[here, :], up[:, lanes]) + up_bias[0:1, lanes])
            value = value.astype(bf16)
            act[here, :] = value
            slope_out[here, lanes] = slope.astype(bf16)
            if step == 0 and side == 0:
                for copy in late:
                    copy.wait()
            part = dot(value, down[blocks_here].reshape(pair, width))
            if side == 0:
                keep_out[...] = part if step == 0 else keep_out[...] + part
            elif step == 0:
                far_sum[...] = part
            else:
                send_out[...] = (far_sum[...] + part).astype(bf16)
        grad = dot_left(act[...], cot[...].reshape(rows, width)).astype(bf16)
        down_grad[blocks_here] = grad.reshape(2 * PLACES, chunk // PLACES, width)
        if blocks == 4:
            ready = [
                copy
                for copy, where in fold_copies(down_grad, down_grads, chip, down_sem)
                if where in distances
            ]
            for copy in ready:
                copy.start()
            outs += ready
    if blocks != 4:
        outs.append(pltpu.make_async_copy(down_grad, down_grads[0], down_sem.at[0]))
        outs[0].start()
    for copy in outs:
        copy.wait()


def feed_front(info, normed, up_bias, cots, ups, downs, blocks):
    rows, width = normed.shape
    hidden = up_bias.shape[1]
    whole = (4 * PLACES, hidden // (4 * PLACES), width)
    grads = fold_shapes(PLACES, whole[1:]) if blocks == 4 else [shaped(whole, bf16)]
    return call(
        functools.partial(feed_front_kernel, len(ups), len(downs), blocks),
        [
            (shaped((rows // 2, width), f32), vmem()),
            (shaped((rows // 2, width), bf16), vmem()),
            (shaped((rows, hidden), bf16), vmem()),
            (shaped((width, hidden), bf16), vmem()),
            (shaped(whole, bf16), vmem()),
            (shaped((4, rows // 4, width), bf16), vmem()),
        ]
        + [(one, anywhere()) for one in grads],
        [LOAD] * 2 + [HELD] * (4 + len(ups) + len(downs)),
        [info, normed, up_bias] + list(cots) + list(ups) + list(downs),
        scratch=[
            pltpu.VMEM((rows, hidden // 2), bf16),
            pltpu.VMEM((rows // 2, width), f32),
            pltpu.VMEM(whole, bf16),
            pltpu.SemaphoreType.DMA((4,)),
            pltpu.SemaphoreType.DMA((len(ups),)),
            pltpu.SemaphoreType.DMA((8,)),
        ],
        limit=16,
        cost=(6 * rows * width * hidden, 24 * MIB),
    )


def feed_back_kernel(info, slope, cot, up, down, back_out, low_out, grad_out, bias_out):
    rows, hidden = slope.shape
    width = up.shape[0]
    chunk = hidden // 2
    flat = cot[...].reshape(rows, width)
    for q in range(2):
        lanes = slice(q * chunk, (q + 1) * chunk)
        down_part = down[2 * q * PLACES : 2 * (q + 1) * PLACES].reshape(chunk, width)
        grad = (dot_right(flat, down_part) * slope[:, lanes].astype(f32)).astype(bf16)
        grad_out[:, lanes] = grad
        bias_out[:, lanes] = jnp.broadcast_to(
            jnp.sum(grad.astype(f32), axis=0, keepdims=True), (8, chunk)
        )
        back = dot_right(grad, up[:, lanes])
        if q == 0:
            back_out[...] = back
        else:
            back = back_out[...] + back
            back_out[...] = back
            low_out[...] = back.astype(bf16)


def feed_back(info, slope, cot, up, down):
    rows, hidden = slope.shape
    width = up.shape[0]
    return call(
        feed_back_kernel,
        [
            (shaped((rows, width), f32), vmem()),
            (shaped((rows, width), bf16), vmem()),
            (shaped((rows, hidden), bf16), vmem()),
            (shaped((8, hidden), f32), vmem()),
        ],
        [LOAD] * 4,
        [info, slope, cot, up, down],
        limit=12,
        cost=(4 * rows * width * hidden, 24 * MIB),
    )


def weight_kernel(blocks, count, info, left, *refs):
    parts, outs, held, sem = refs[:count], refs[count:-2], refs[-2], refs[-1]
    if count > 1:
        right = jnp.concatenate([ref[...] for ref in parts], axis=1)
        held[...] = dot_left(left[...], right).astype(bf16)
    else:
        for begin in range(0, held.shape[1], 768):
            lanes = slice(begin, begin + 768)
            held[:, lanes] = dot_left(left[...], parts[0][:, lanes]).astype(bf16)
    if blocks == 4:
        run_copies([copy for copy, _ in fold_copies(held, outs, info[1], sem)])
    else:
        run_copies([pltpu.make_async_copy(held, outs[0], sem.at[0])])


def weight_grad(info, left, parts, blocks):
    rows, width = left.shape
    columns = sum(part.shape[1] for part in parts)
    outs = [shaped((width, columns), bf16)]
    if blocks == 4:
        outs = fold_shapes(width // 4, (columns,))
    return call(
        functools.partial(weight_kernel, blocks, len(parts)),
        [(one, anywhere()) for one in outs],
        [LOAD] * (1 + len(parts)),
        [info, left] + list(parts),
        scratch=[pltpu.VMEM((width, columns), bf16), pltpu.SemaphoreType.DMA((8,))],
        cost=(2 * rows * width * columns, 8 * MIB),
    )


def middle_back_kernel(blocks, patches, info, back, back_far, middle, turned, att, weight, cot, *refs):
    grad_out, attended_out, keep_out, send_out, sums_out, branch = refs
    core = info[0]
    rows, width = middle.shape
    tile = rows // 4
    part = width // 2
    gain = turned[patches + GAIN_TWO : patches + GAIN_TWO + 1, :]
    own_rows = pl.ds(pl.multiple_of(core * part, 128), part)
    for t in range(4):
        here = slice(t * tile, (t + 1) * tile)
        grad_normed = back[here, :] + back_far[here, :].astype(f32)
        normal, scale = normalise(middle[here, :])
        grad_outputs = cot[t].astype(f32)
        grad = grad_outputs + norm_back(normal, scale, gain, grad_normed)
        low = grad.astype(bf16)
        branch[here, :] = low
        attended_out[here, :] = dot_right(low, weight[own_rows, :]).astype(bf16)

        @pl.when(core == t // 2)
        def _():
            grad_out[(t % 2) * tile : (t % 2 + 1) * tile, :] = grad
            sums = jnp.concatenate(
                [
                    jnp.sum(low.astype(f32), axis=0, keepdims=True),
                    jnp.sum(grad_outputs, axis=0, keepdims=True),
                    jnp.sum(grad_normed * normal, axis=0, keepdims=True),
                    jnp.sum(grad_normed, axis=0, keepdims=True),
                    jnp.zeros((4, width), f32),
                ],
                axis=0,
            )
            sums_out[...] = sums if t % 2 == 0 else sums_out[...] + sums

    weight_grad = dot_left(att[...], branch[...]).astype(bf16)
    shape = send_out.shape[:1] + (2,) + send_out.shape[1:]
    sorted_grad = weight_grad.reshape(shape) if blocks == 4 else None
    if blocks == 4:
        for c in range(2):

            @pl.when(core == c)
            def _():
                keep_out[...] = sorted_grad[:, c]
                send_out[...] = sorted_grad[:, 1 - c]

    else:
        keep_out[...] = weight_grad
        send_out[...] = weight_grad


def middle_back(info, back, back_far, middle, turned, att, weight, cot, patches, blocks):
    rows, width = middle.shape
    part = width // 2
    slab = (2, part // 4, width) if blocks == 4 else (part, width)
    return call(
        functools.partial(middle_back_kernel, blocks, patches),
        [
            (shaped((rows // 2, width), f32), vmem()),
            (shaped((rows, part), bf16), vmem()),
            (shaped(slab, bf16), vmem()),
            (shaped(slab, bf16), vmem()),
            (shaped((8, width), f32), vmem()),
        ],
        [LOAD] * 7,
        [info, back, back_far, middle, turned, att, weight, cot],
        scratch=[pltpu.VMEM((rows, width), bf16)],
        cost=(4 * rows * width * part, 14 * MIB),
    )


def project_kernel(info, dq, dk, dv, weight, keep_out, send_out):
    core = info[0]
    rows, part = dq.shape
    half_rows = rows // 2

    def product(first):
        here = pl.ds(pl.multiple_of(first, 128), half_rows)
        return (
            dot_right(dq[here, :], weight[:, :part])
            + dot_right(dk[here, :], weight[:, part : 2 * part])
            + dot_right(dv[here, :], weight[:, 2 * part : 3 * part])
        )

    send_out[...] = product((1 - core) * half_rows).astype(bf16)
    keep_out[...] = product(core * half_rows)


def project_back(info, dq, dk, dv, weight):
    rows, part = dq.shape
    width = weight.shape[0]
    return call(
        project_kernel,
        [
            (shaped((rows // 2, width), f32), vmem()),
            (shaped((rows // 2, width), bf16), vmem()),
        ],
        [LOAD] * 4,
        [info, dq, dk, dv, weight],
        cost=(6 * rows * width * part, 8 * MIB),
    )


def start_kernel(blocks, patches, chips, info, *refs):
    (keep, far, start, grad_middle, turned, sums, bias_grad, spots, dq, dv, out_keep, out_got) = refs[:12]
    refs = refs[12:]
    low_out, refs = refs[0], refs[1:]
    grads, refs = refs[:-3], refs[-3:]
    held, rows_held, sem = refs
    core, chip = info[0], info[1]
    rows, part = dq.shape
    half_rows, width = keep.shape
    up_rows = width // blocks
    gain = turned[patches + GAIN_ONE : patches + GAIN_ONE + 1, :]
    own = pl.ds(pl.multiple_of(core * half_rows, half_rows), half_rows)
    grad_normed = keep[...] + far[...].astype(f32)
    normal, scale = normalise(start[own, :])
    grad = grad_middle[...] + norm_back(normal, scale, gain, grad_normed)
    low = grad.astype(bf16)
    low_out[...] = low
    ids = lax.broadcasted_iota(jnp.int32, (SMALL, half_rows), 0).astype(f32)
    mine = spots[0:1, pl.ds(pl.multiple_of(core * half_rows, 128), half_rows)]
    one_hot = jnp.where(ids == mine, 1.0, 0.0).astype(bf16)
    rows_held[...] = dot(one_hot, low)
    half = pl.ds(pl.multiple_of(core * part, 128), part)
    rows_held[patches : patches + 8, :] = jnp.zeros((8, width), f32)

    def put(i, row):
        rows_held[patches + i : patches + i + 1, :] = row

    rows_held[patches + QUERY_BIAS : patches + QUERY_BIAS + 1, half] = jnp.sum(
        dq[...].astype(f32), axis=0, keepdims=True
    )
    rows_held[patches + VALUE_BIAS : patches + VALUE_BIAS + 1, half] = jnp.sum(
        dv[...].astype(f32), axis=0, keepdims=True
    )
    put(OUTPUT_BIAS, sums[0:1, :])
    put(DOWN_BIAS, sums[1:2, :])
    put(GAIN_TWO, sums[2:3, :])
    put(SHIFT_TWO, sums[3:4, :])
    put(GAIN_ONE, jnp.sum(grad_normed * normal, axis=0, keepdims=True))
    put(SHIFT_ONE, jnp.sum(grad_normed, axis=0, keepdims=True))
    hidden = bias_grad.shape[1]
    spare = 2 * hidden // width
    biases = jnp.where(hidden_turns(spare, hidden, chips), bias_grad[0:1, :], 0.0)
    high = biases.astype(bf16)
    both = jnp.concatenate([high.astype(f32), biases - high.astype(f32)]).astype(bf16)
    placed = dot(both, hidden_places(core, hidden, width, chips))
    rows_held[patches + 8 : patches + 8 + spare, :] = placed[:spare] + placed[spare:]
    held[:, :SMALL] = rows_held[...].T.astype(bf16)
    if blocks == 4:
        slab = up_rows // 2
        for x in range(2):
            for side, ref in ((core, out_keep), (1 - core, out_got)):
                begin = pl.multiple_of((2 * side + x) * up_rows, up_rows)
                held[pl.ds(begin, slab), SMALL:] = ref[x, :, : width // 2]
                held[pl.ds(begin + slab, slab), SMALL:] = ref[x, :, width // 2 :]
    if blocks == 4:
        run_copies([copy for copy, _ in fold_copies(held, grads, chip, sem)])
    else:
        run_copies([pltpu.make_async_copy(held, grads[0], sem.at[0])])


def start_back(info, blocks, args, patches, chips):
    half_rows, width = args[0].shape
    columns = SMALL + width // 2 if blocks == 4 else SMALL
    outs = [shaped((width, columns), bf16)]
    if blocks == 4:
        outs = fold_shapes(width // 4, (columns,))
    return call(
        functools.partial(start_kernel, blocks, patches, chips),
        [(shaped((half_rows, width), bf16), vmem())]
        + [(one, anywhere()) for one in outs],
        [LOAD] * len(args),
        [info] + list(args),
        scratch=[
            pltpu.VMEM((width, columns), bf16),
            pltpu.VMEM((SMALL, width), f32),
            pltpu.SemaphoreType.DMA((8,)),
        ],
        cost=(2 * half_rows * width * SMALL, 10 * MIB),
    )


def split_kernel(plan, count, shift, info, *refs):
    place = lax.rem(info[2] >> shift, count)
    inputs, held = refs[: -1 - count], refs[-1]
    outs = refs[-1 - count : -1]
    column = 0
    for parts in plan:
        totals = []
        for terms in parts:
            total = 0.0
            for index, begin, rows in terms:
                total = total + inputs[index][begin : begin + rows, :].astype(f32)
            totals.append(total)
        whole = totals[0] if len(totals) == 1 else jnp.concatenate(totals)
        lanes = whole.shape[-1]
        held[..., column : column + lanes] = whole.reshape(held.shape[:-1] + (lanes,))
        column += lanes
    lead = (slice(None),) * (len(held.shape) - 3)
    for k in range(count):
        outs[k][...] = held[lead + (k ^ place,)].astype(outs[k].dtype)


def split(info, groups, shape, shift=0):
    arrays, plan, columns = [], [], 0
    for group in groups:
        base = len(arrays)
        parts = group.parts if isinstance(group, Fold) else [[(i, 0, None) for i in range(len(group))]]
        terms = group.terms if isinstance(group, Fold) else group
        flat = [array.reshape((-1,) + array.shape[-1:]) for array in terms]
        half = flat[0].shape[0] // 2
        plan.append(
            [
                [
                    (base + i, 0, flat[i].shape[0]) if begin is None else (base + i, begin * half, half)
                    for i, begin, _ in [(i, None if size is None else begin, size) for i, begin, size in part]
                ]
                for part in parts
            ]
        )
        arrays += flat
        columns += flat[0].shape[-1]
    count, total = shape[-2], columns
    for extent in shape:
        total *= extent
    one = shape[:-2] + (shape[-1], columns)
    return call(
        functools.partial(split_kernel, plan, count, shift),
        [(shaped(one, f32 if k == 0 else bf16), vmem()) for k in range(count)],
        [LOAD] * len(arrays),
        [info] + arrays,
        scratch=[pltpu.VMEM(shape + (columns,), f32)],
        limit=20,
        cost=(0, 8 * total),
    )


def swap(values, axis, bits):
    size = lax.axis_size(axis)
    return lax.ppermute(values, axis, [(i, i ^ bits) for i in range(size)])


def spread_perm(turn):
    pairs = []
    for w in range(lax.axis_size("wide")):
        for z in range(PLACES):
            there = (w - w % 2 + z // 2, 2 * (w % 2) + (turn ^ (z % 2)))
            pairs.append((w * PLACES + z, there[0] * PLACES + there[1]))
    return pairs


def unspread_turn(part, turn):
    return lax.ppermute(part, ("wide", "narrow"), [(b, a) for a, b in spread_perm(turn)])


def unspread_join(got, place):
    odd = (place % 2) == 1
    return jnp.stack([jnp.where(odd, got[1], got[0]), jnp.where(odd, got[0], got[1])])


def along(piece, bits):
    held = {0: piece}
    for bit in bits:
        held.update({index ^ (bit // 2): swap(part, "wide", bit) for index, part in list(held.items())})
    return [held[index] for index in range(len(held))]


def direct(piece, chips):
    return [piece] + [swap(piece, "wide", 2 * index) for index in range(1, chips)]


def fold(pieces, bits):
    held = dict(enumerate(pieces))
    for number, bit in enumerate(bits):
        step = bit // 2
        got = {i: swap(held[i ^ step], "wide", bit) for i in held if not i & step}
        if number == len(bits) - 1:
            return [held[0], got[0]]
        held = {i: (held[i].astype(f32) + got[i].astype(f32)).astype(bf16) for i in got}
    return [held[0]]


def after(values, *others):
    return lax.optimization_barrier((values,) + others)[0]


def together(*values):
    return lax.optimization_barrier(values)


class Fold:
    def __init__(self, outs, bits):
        self.outs, self.bits = list(outs), bits
        self.plane = len(outs) == 5
        if self.plane:
            self.near = [swap(outs[1], "wide", 2), swap(outs[2], "wide", 4)]

    def pairs(self):
        return [(self.outs[3], self.near[0]), (self.outs[4], self.near[1])] if self.plane else []

    def cross(self, sums):
        if self.plane:
            self.far = [swap(sums[0], "wide", 4), swap(sums[1], "wide", 2)]
            self.terms = [self.outs[0], *self.near, *self.far]
            first = [(0, 0, 1), (1, 1, 1), (3, 0, 1)]
            self.parts = [first, [(0, 1, 1), (2, 1, 1), (4, 0, 1)]]
        else:
            self.terms = fold(self.outs, self.bits)
            self.parts = [[(i, 0, None) for i in range(len(self.terms))]]


def local(
    tokens,
    positions,
    segments,
    position_table,
    input_weight,
    query_bias,
    value_bias,
    output_weight,
    output_bias,
    first_gain,
    first_shift,
    up_weight,
    up_bias,
    down_weight,
    down_bias,
    second_gain,
    second_shift,
    cotangent,
):
    size = lax.axis_size("wide")
    chips = size // 2
    bits = [2**i for i in range(1, size.bit_length() - 1)]
    seq_count, block, width = tokens.shape
    hidden = up_weight.shape[1]
    patches = position_table.shape[1]
    full = segments.shape[1]
    rows = width // (size * PLACES)
    part = width // 2
    own_hidden = hidden // 2
    wide, place = lax.axis_index("wide"), lax.axis_index("narrow")
    core, chip = wide % 2, wide // 2
    first_core = core == 0
    blocks = 4 if chips == 4 else 1
    info = jnp.stack([core, chip if blocks == 4 else 0 * chip, place, chip]).astype(jnp.int32)

    def pick(values, index, axis=0):
        return lax.dynamic_index_in_dim(values, index, axis, keepdims=False)

    def by_chip(pieces):
        flat = [piece.reshape((-1,) + piece.shape[-1:]) for piece in pieces]
        if blocks == 4:
            return flat
        whole = jnp.take(jnp.stack(flat), jnp.arange(chips) ^ chip, axis=0)
        return [whole.reshape((-1,) + flat[0].shape[1:])]

    def by_distance(outs, shape):
        if blocks == 4:
            return [out.reshape(shape) for out in outs]
        whole = outs[0].reshape((chips,) + shape)
        return [pick(whole, index ^ chip) for index in range(chips)]

    vectors = (
        query_bias,
        value_bias,
        output_bias,
        first_gain,
        first_shift,
        down_bias,
        second_gain,
        second_shift,
    )
    spare = up_bias.shape[0] // rows
    plane = blocks == 4
    up_sorted = up_weight
    if not plane:
        up_sorted = up_weight.reshape(rows, 4, chips // 4, 2, -1)
        up_sorted = jnp.swapaxes(up_sorted, 2, 3).reshape(rows, hidden)

    def cross_one(piece):
        if blocks == 4:
            return [piece, swap(piece, "wide", 2), swap(piece, "wide", 4)]
        return along(piece, bits)

    def cross_two(pieces):
        if blocks == 4:
            own, x, y = pieces
            first, second = cut(info, x, y)
            return [own, x, y, swap(first, "wide", 2), swap(second, "wide", 4)]
        return pieces

    def place_axis(piece):
        return piece.reshape(piece.shape[:-4] + (PLACES,) + piece.shape[-2:])

    def folded(outs, shape):
        if plane:
            return Fold(outs, bits)
        whole = outs[0].reshape((chips,) + shape)
        return Fold([pick(whole, index ^ chip) for index in range(chips)], bits)

    def crossed(folds, *values):
        count = len(values)
        near = [array for one in folds if one.plane for array in one.near]
        values = together(*values, *near)
        values, near = values[:count], list(values[count:])
        if plane:
            for one in folds:
                one.near, near = near[:2], near[2:]
            sums = add_firsts(info, [pair for one in folds for pair in one.pairs()])
        for i, one in enumerate(folds):
            one.cross(sums[2 * i : 2 * i + 2] if plane else None)
        return values

    def arrived(folds, *values):
        if not plane:
            return values
        count = len(values)
        far = [array for one in folds for array in one.far]
        values = together(*values, *far)
        values, far = values[:count], list(values[count:])
        for one in folds:
            one.far, far = far[:2], far[2:]
            one.terms = [*one.terms[:3], *one.far]
        return values

    rows_in = jnp.concatenate([jnp.stack(vectors), up_bias.reshape(spare, rows)])
    in_keep, in_send = pack_in(info, input_weight, position_table, rows_in)
    in_far = swap(in_send, "wide", 1)
    raw_parts = together(down_weight, output_weight, up_sorted, tokens, in_keep)
    raw = jnp.concatenate(raw_parts[:2]) if plane else raw_parts[0]
    up_keep, up_send = pack_up(info, raw_parts[2])
    first, second = sent(info, raw_parts[3], positions, segments)
    in_far, raw, up_send = together(in_far, raw, up_send)

    in_pair = arrange(info, [in_keep, in_far], 0, 0)
    in_got = [in_pair] + [swap(in_pair, "narrow", k) for k in range(1, PLACES)]
    raw_far = swap(raw, "narrow", 2)
    up_far = swap(up_send, "wide", 1)
    up_far, raw_far, first, *in_got = together(up_far, raw_far, first, *in_got)

    in_piece = arrange(info, in_got)
    in_chips = direct(in_piece, chips) if plane else along(in_piece, bits)
    raw_half = arrange(info, [raw, raw_far], 1)
    raw_far = swap(raw_half, "narrow", 1)
    low = lax.ppermute(first, ("wide", "narrow"), spread_perm(0))
    up_pair = arrange(info, [up_keep, up_far], 0, 0)
    low, raw_far, up_pair, second = together(low, raw_far, up_pair, second)

    up_far = swap(up_pair, "narrow", 2)
    high = lax.ppermute(second, ("wide", "narrow"), spread_perm(1))
    if plane:
        raw_far, *in_chips = together(settle(info, raw_half, raw_far), *in_chips)
        down_chips = cross_one(raw_far)
    else:
        down_chips = along(place_axis(arrange(info, [raw_half, raw_far])), bits)
    high, up_far = together(high, up_far)

    up_half = arrange(info, [up_pair, up_far], 1)
    up_far = swap(up_half, "narrow", 1)
    low_far, high_far = swap(low, "wide", 1), swap(high, "wide", 1)
    low_far, high_far, cotangent = together(low_far, high_far, cotangent)
    token_blocks = [low, high, low_far, high_far]
    cot_first, cot_second = pick_turns(info, cotangent)
    cot_low = lax.ppermute(cot_first, ("wide", "narrow"), spread_perm(0))
    in_blocks = by_chip(in_chips)
    q, k, v, start, normed, in_full, turned, seg, spots = front(
        info, token_blocks, in_blocks, patches
    )
    q, k, v, seg, cot_second, up_far, *down_chips = together(
        q, k, v, seg, cot_second, up_far, *down_chips
    )

    up_chips = cross_one(place_axis(arrange(info, [up_half, up_far])))
    cot_high = lax.ppermute(cot_second, ("wide", "narrow"), spread_perm(1))
    if plane:
        down_chips = cross_two(down_chips)
    att, total = attend(info, q, k, v, seg)
    count = len(down_chips)
    att, cot_low, cot_high, *rest = together(att, cot_low, cot_high, *down_chips, *up_chips)
    down_chips, up_chips = rest[:count], rest[count:]

    att_far = swap(att, "wide", 1)
    if plane:
        out_rows = last_blocks(info, *down_chips[:3], down_chips[4])
        out_weights = [out_rows, swap(out_rows, "wide", 1)]
    else:
        out_weights = [lax.all_gather(output_weight, ("wide", "narrow"), axis=0, tiled=True)]
    if plane:
        up_chips = cross_two(up_chips)
    cots = [cot_low, cot_high, swap(cot_low, "wide", 1), swap(cot_high, "wide", 1)]
    if plane:
        up_blocks = [part.reshape((-1,) + part.shape[-1:]) for part in up_chips]
        down_blocks = down_chips
    else:
        up_blocks = by_chip(up_chips)
        down_blocks = [by_chip(down_chips)[0].reshape(4 * PLACES, -1, width)]
    middle, normed_two, up_bias_own, out_full = middle_front(
        info, att, att_far, start, turned, out_weights, own_hidden, patches, chips
    )
    keep, send, slope, up_full, down_full, cot, *down_grads = feed_front(
        info, normed_two, up_bias_own, cots, up_blocks, down_blocks, blocks
    )
    down_rows = own_hidden // (chips * PLACES)
    down_fold = folded(down_grads, (PLACES, down_rows, width))
    fed = feed_back(info, slope, cot, up_full, down_full)
    back, back_low, grad_hidden, bias_grad, send, normed_two = crossed(
        [down_fold], *fed, send, normed_two
    )
    back_far = swap(back_low, "wide", 1)
    out_far = swap(send, "wide", 1)
    up_grads = weight_grad(info, normed_two, [grad_hidden], blocks)
    back_far, out_far, *up_grads = arrived([down_fold], back_far, out_far, *up_grads)
    up_fold = folded(up_grads, (2, PLACES, rows, own_hidden))
    down_keep, down_send = split(info, [down_fold], (2, 2, down_rows))
    down_got = swap(down_send, "narrow", 1)
    grad_middle, grad_att, out_keep, out_send, sums = middle_back(
        info, back, back_far, middle, turned, att, out_full, cot, patches, blocks
    )
    out_far, grad_att = together(out_far, grad_att)
    out_turns = output_turns(info, middle, keep, out_far, turned, patches)
    out_turns = [unspread_turn(part, turn) for turn, part in enumerate(out_turns)]
    if blocks == 1:
        shape = (chips // 2, 2, PLACES * rows, width)
        out_keep = pick(out_keep.reshape(shape), core, 1)
        out_send = pick(out_send.reshape(shape), 1 - core, 1)
    grad_att, down_got = crossed([up_fold], grad_att, down_got)
    dq, dk, dv = attend_back(info, q, k, v, att, grad_att, total, seg)
    dq, dk, dv, out_send, normed, *out_turns = arrived(
        [up_fold], dq, dk, dv, out_send, normed, *out_turns
    )
    start_keep, start_send = project_back(info, dq, dk, dv, in_full)
    start_far, out_got = swap(start_send, "wide", 1), swap(out_send, "wide", 1)
    down_keep, down_send = split(info, [[down_keep, down_got]], (2, down_rows), 1)
    up_keep, up_send = split(info, [up_fold], (2, 2, 2, rows))
    start_far, out_got, up_send, down_send = together(start_far, out_got, up_send, down_send)
    up_got = swap(up_send, "narrow", 1)
    down_got = swap(down_send, "narrow", 2)
    args = [start_keep, start_far, start, grad_middle, turned, sums, bias_grad, spots, dq, dv]
    started = start_back(info, blocks, args + [out_keep, out_got], patches, chips)
    if not plane:
        out_grad = jnp.where(
            first_core,
            jnp.concatenate([out_keep, out_got]),
            jnp.concatenate([out_got, out_keep]),
        ).reshape(chips, PLACES, rows, 2, part)
        out_grad = jnp.transpose(out_grad, (0, 3, 1, 2, 4)).reshape(width, part)
        started = [started[0], jnp.concatenate([started[1], out_grad], axis=1)]
    normed, grad_blocks, *small_grads = together(normed, *started)
    small_fold = folded(small_grads, (2, PLACES, rows, SMALL + part))
    grad_first, grad_second = pick_turns(info, grad_blocks.reshape(2, block, width))
    grad_first = unspread_turn(grad_first, 0)
    in_grads = weight_grad(info, normed, [dq, dk, dv], blocks)
    up_got, down_got, *in_grads = crossed([small_fold], up_got, down_got, *in_grads)
    in_fold = folded(in_grads, (2, PLACES, rows, 3 * part))
    up_keep, up_send = split(info, [[up_keep, up_got]], (2, 2, rows), 1)
    grad_first, grad_second, up_send = crossed(
        [in_fold], *arrived([small_fold], grad_first, grad_second, up_send)
    )
    grad_second = unspread_turn(grad_second, 1)
    up_got = swap(up_send, "narrow", 2)
    (down_keep,) = arrived([in_fold], down_keep)
    in_cut = split(info, [in_fold, small_fold], (2, PLACES, rows))
    in_got = [swap(in_cut[index], "narrow", index) for index in range(1, PLACES)]
    in_keep, down_keep, up_keep, up_got, grad_first, grad_second, *out_turns = together(
        in_cut[0], down_keep, up_keep, up_got, grad_first, grad_second, *out_turns
    )
    outputs = unspread_join(out_turns, place)
    grad_tokens = unspread_join([grad_first, grad_second], place)
    down_share = down_keep + down_got.astype(f32)
    up_total = up_keep + up_got.astype(f32)
    up_keep = pick(up_total, core)
    up_got = swap(pick(up_total, 1 - core).astype(bf16), "wide", 1).astype(f32)
    up_both = [up_keep.reshape(rows, chips, 1, -1), up_got.reshape(rows, chips, 1, -1)]
    up_share = jnp.where(
        first_core, jnp.concatenate(up_both, axis=2), jnp.concatenate(up_both[::-1], axis=2)
    ).reshape(rows, hidden)
    outputs, grad_tokens, down_share, up_share, *in_got = together(
        outputs, grad_tokens, down_share, up_share, *in_got
    )
    in_total = in_keep
    for array in in_got:
        in_total = in_total + array.astype(f32)
    sent_columns = 3 * part + SMALL
    in_keep = pick(in_total, core)
    in_far = pick(in_total, 1 - core)[:, :sent_columns].astype(bf16)
    in_far = swap(in_far, "wide", 1).astype(f32)
    in_both = [in_keep[:, : 3 * part].reshape(rows, 3, 1, part), in_far[:, : 3 * part].reshape(rows, 3, 1, part)]
    in_share = jnp.where(
        first_core, jnp.concatenate(in_both, axis=2), jnp.concatenate(in_both[::-1], axis=2)
    ).reshape(rows, 3 * width)
    small_share = in_keep[:, 3 * part : sent_columns] + in_far[:, 3 * part :]
    out_share = jnp.concatenate([in_total[0, :, sent_columns:], in_total[1, :, sent_columns:]], axis=1)
    tail = [small_share[:, patches + i] for i in range(8)]
    return (
        outputs,
        grad_tokens,
        small_share[:, :patches],
        in_share,
        tail[QUERY_BIAS],
        tail[VALUE_BIAS],
        out_share,
        tail[OUTPUT_BIAS],
        tail[GAIN_ONE],
        tail[SHIFT_ONE],
        up_share,
        small_share[:, patches + 8 : patches + 8 + spare].T.reshape(-1),
        down_share,
        tail[DOWN_BIAS],
        tail[GAIN_TWO],
        tail[SHIFT_TWO],
    )


def solution(mesh):
    both = ("wide", "narrow")
    matrix = P(both, None)
    vector = P(both)
    block = P("wide", "narrow", None)
    gains = [matrix, matrix] + [vector] * 2 + [matrix] + [vector] * 3 + [matrix, vector, matrix]
    gains += [vector] * 3
    return jax.shard_map(
        local,
        mesh=mesh,
        in_specs=tuple([block, P("wide", "narrow"), P("wide", None)] + gains + [block]),
        out_specs=tuple([block, block] + gains),
        check_vma=False,
    )
```

```python
import functools

import jax
import jax.numpy as jnp
from jax import lax
from jax.experimental import pallas as pl
from jax.experimental.pallas import tpu as pltpu
from jax.sharding import PartitionSpec as P

HEADS = 12
PLACES = 4
epsilon = 1e-05
masked_score = -1e30

f32 = jnp.float32
bf16 = jnp.bfloat16
MIB = 1 << 20
LOAD, HELD = "load", "held"
QUERY_BIAS, VALUE_BIAS, OUTPUT_BIAS, GAIN_ONE, SHIFT_ONE, DOWN_BIAS, GAIN_TWO, SHIFT_TWO = range(8)
SMALL = 128


def dot(left, right):
    return jnp.dot(left, right, preferred_element_type=f32)


def dot_left(left, right):
    return lax.dot_general(left, right, (((0,), (0,)), ((), ())), preferred_element_type=f32)


def dot_right(left, right):
    return lax.dot_general(left, right, (((1,), (1,)), ((), ())), preferred_element_type=f32)


def call(kernel, outs, ins, args, scratch=(), grid=None, limit=14, cost=None):
    loads = []
    specs = [pl.BlockSpec(memory_space=pltpu.SMEM)]
    for index, (spec, array) in enumerate(zip(ins, args[1:], strict=True)):
        if spec == LOAD:
            whole = False
            spec = pl.BlockSpec(memory_space=pl.ANY if whole else pltpu.VMEM)
            if whole:
                loads.append(index)
        elif spec == HELD:
            spec = pl.BlockSpec(memory_space=pl.ANY)
        specs.append(spec)
    count, news = len(ins), len(loads)

    def loaded(info, *refs):
        refs, held, sem = list(refs[: -1 - news]), refs[-1 - news : -1], refs[-1]
        copies = []
        for i, index in enumerate(loads):
            copies.append(pltpu.make_async_copy(refs[index], held[i], sem.at[i]))
            refs[index] = held[i]
        run_copies(copies)
        kernel(info, *refs)

    extra = [pltpu.VMEM(args[1 + i].shape, args[1 + i].dtype) for i in loads]
    if loads:
        extra.append(pltpu.SemaphoreType.DMA((news,)))
    return pl.pallas_call(
        loaded if loads else kernel,
        out_shape=[shape for shape, _ in outs],
        in_specs=specs,
        out_specs=[spec for _, spec in outs],
        scratch_shapes=list(scratch) + extra,
        **({"grid": grid} if grid else {}),
        compiler_params=pltpu.CompilerParams(vmem_limit_bytes=limit * MIB),
        cost_estimate=pl.CostEstimate(
            flops=int(cost[0]), bytes_accessed=int(cost[1]), transcendentals=0
        ),
    )(*args)


def shaped(shape, kind):
    return jax.ShapeDtypeStruct(shape, kind)


def vmem():
    return pl.BlockSpec(memory_space=pltpu.VMEM)


def anywhere():
    return pl.BlockSpec(memory_space=pl.ANY)


def normalise(values):
    average = jnp.mean(values, axis=-1, keepdims=True)
    centered = values - average
    variance = jnp.mean(centered * centered, axis=-1, keepdims=True)
    scale = lax.rsqrt(variance + epsilon)
    return centered * scale, scale


def norm_back(normal, scale, gain, grad):
    inner = grad * gain
    return scale * (
        inner
        - jnp.mean(inner, axis=-1, keepdims=True)
        - normal * jnp.mean(inner * normal, axis=-1, keepdims=True)
    )


def fold_shapes(rows, rest):
    return [shaped((count,) + rest, bf16) for count in (rows, rows, rows, rows // 2, rows // 2)]


def fold_copies(held, outs, chip, sem):
    rows = outs[0].shape[0]
    half = rows // 2
    at = lambda distance, second: pl.ds(
        pl.multiple_of((distance ^ chip) * rows + second * half, half), half
    )
    whole = pl.ds(pl.multiple_of(chip * rows, rows), rows)
    first, second = pl.ds(0, half), pl.ds(half, half)
    own, to_x, to_y, y_left, x_left = outs
    pairs = [
        (0, held.at[whole], own),
        (3, held.at[at(3, 0)], to_x.at[first]),
        (1, held.at[at(1, 0)], to_x.at[second]),
        (3, held.at[at(3, 1)], to_y.at[first]),
        (2, held.at[at(2, 1)], to_y.at[second]),
        (2, held.at[at(2, 0)], y_left),
        (1, held.at[at(1, 1)], x_left),
    ]
    return [
        (pltpu.make_async_copy(a, b, sem.at[i]), distance)
        for i, (distance, a, b) in enumerate(pairs)
    ]


def run_copies(copies):
    for copy in copies:
        copy.start()
    for copy in copies:
        copy.wait()


def pack_in_kernel(patches, info, weight, table, rows_in, keep, send):
    core = info[0]
    part = weight.shape[1] // 6
    turned = rows_in[...].astype(f32).T
    empty = jnp.zeros((weight.shape[0], SMALL - patches - turned.shape[1]), f32)
    small = jnp.concatenate([table[...].astype(f32), turned, empty], axis=1).astype(bf16)
    for ref, side in ((keep, core), (send, 1 - core)):
        for i in range(3):
            there = pl.ds(pl.multiple_of((2 * i + side) * part, 128), part)
            ref[:, i * part : (i + 1) * part] = weight[:, there]
        ref[:, 3 * part :] = small


def pack_in(info, weight, table, rows_in):
    rows, columns = weight.shape[0], weight.shape[1] // 2 + SMALL
    return call(
        functools.partial(pack_in_kernel, table.shape[1]),
        [(shaped((rows, columns), bf16), vmem())] * 2,
        [vmem()] * 3,
        [info, weight, table, rows_in],
        limit=8,
        cost=(0, MIB),
    )


def pack_up_kernel(info, up, keep, send):
    step = keep.shape[1] // 4
    for ref, side in ((keep, info[0]), (send, 1 - info[0])):
        for q in range(4):
            there = pl.ds(pl.multiple_of((2 * q + side) * step, 128), step)
            ref[:, q * step : (q + 1) * step] = up[:, there]


def pack_up(info, up):
    out = (shaped((up.shape[0], up.shape[1] // 2), bf16), vmem())
    return call(pack_up_kernel, [out] * 2, [vmem()], [info, up], limit=8, cost=(0, MIB))


def sent_kernel(info, tokens, positions, segments, first, second, extra):
    place = info[2]
    block, width = tokens.shape[1], tokens.shape[2]
    full = segments.shape[1]
    extra[...] = jnp.zeros_like(extra)
    for k, out in enumerate((first, second)):
        index = k ^ (place % 2)
        row = segments[pl.ds(index, 1), :]
        row = (row - row[:, 0:1]).astype(f32)
        extra[0:1, :block] = positions[pl.ds(index, 1), :].astype(f32)
        extra[1:2, :] = row[:, :width]
        extra[2:3, : full - width] = row[:, width:]
        out[:block, :] = tokens[index]
        out[block:, :] = extra[...].astype(bf16)


def sent(info, tokens, positions, segments):
    _, block, width = tokens.shape
    one = (shaped((block + 16, width), bf16), vmem())
    return call(
        sent_kernel,
        [one, one],
        [vmem()] * 3,
        [info, tokens, positions, segments],
        scratch=[pltpu.VMEM((16, width), f32)],
        limit=8,
        cost=(0, 2 * MIB),
    )


def arrange_kernel(slot, shift, info, *refs):
    ins, out = refs[:-1], refs[-1]
    lead = len(out.shape) - 3
    place = lax.rem(info[slot] >> shift, len(ins))
    for k, ref in enumerate(ins):
        out[(slice(None),) * lead + (k ^ place,)] = ref[...]


def arrange(info, pieces, shift=0, slot=2):
    shape = pieces[0].shape
    shape = shape[:-2] + (len(pieces),) + shape[-2:]
    total = 1
    for extent in shape:
        total *= extent
    return call(
        functools.partial(arrange_kernel, slot, shift),
        [(shaped(shape, bf16), vmem())],
        [vmem()] * len(pieces),
        [info] + list(pieces),
        limit=8,
        cost=(0, 4 * total),
    )[0]


def settle_kernel(info, own, far, out):
    odd = lax.rem(info[2], 2)
    block = out.shape[1]
    rows = own.shape[1] - block
    for k, ref in enumerate((own, far)):
        for high in range(2):
            out[2 * high + (k ^ odd)] = ref[high, :block, :]
    both = (own, far)
    for high in range(2):
        pair = [ref[high, block:, :].astype(f32) for ref in both]
        for low in range(2):
            row = jnp.where(odd == low, pair[0], pair[1]).astype(bf16)
            begin = (2 * high + low) * rows
            out[PLACES, begin : begin + rows, :] = row


def settle(info, own, far):
    _, rows, width = own.shape
    block = rows * PLACES // (PLACES + 1)
    return call(
        settle_kernel,
        [(shaped((PLACES + 1, block, width), bf16), vmem())],
        [vmem()] * 2,
        [info, own, far],
        limit=8,
        cost=(0, 2 * MIB),
    )[0]


def last_kernel(info, own, x, y, d, out):
    for distance, ref in enumerate((own, x, y, d)):
        out[distance ^ info[1]] = ref[ref.shape[0] - 1]


def last_blocks(info, own, x, y, d):
    return call(
        last_kernel,
        [(shaped((4,) + own.shape[1:], bf16), vmem())],
        [vmem()] * 4,
        [info, own, x, y, d],
        limit=8,
        cost=(0, MIB),
    )[0]


def cut_kernel(info, x, y, first, second):
    half = first.shape[0]
    first[...] = y[:half]
    second[...] = x[half:]


def cut(info, x, y):
    half = x.shape[0] // 2
    outs = [
        (shaped((half,) + x.shape[1:], bf16), vmem()),
        (shaped((x.shape[0] - half,) + x.shape[1:], bf16), vmem()),
    ]
    return call(cut_kernel, outs, [LOAD] * 2, [info, x, y], limit=8, cost=(0, MIB))


def add_kernel(info, *refs):
    for i in range(0, len(refs), 3):
        a, b, out = refs[i : i + 3]
        out[...] = (a[...].astype(f32) + b[: out.shape[0]].astype(f32)).astype(bf16)


def add_firsts(info, pairs):
    def kernel(info, *refs):
        outs = refs[2 * len(pairs) :]
        add_kernel(info, *[ref for i, out in enumerate(outs) for ref in (*refs[2 * i : 2 * i + 2], out)])

    return call(
        kernel,
        [(shaped(a.shape, bf16), vmem()) for a, _ in pairs],
        [LOAD] * (2 * len(pairs)),
        [info] + [array for pair in pairs for array in pair],
        limit=8,
        cost=(0, MIB),
    )


def pick_kernel(info, blocks, first, second):
    odd = lax.rem(info[2], 2)
    first[...] = blocks[odd]
    second[...] = blocks[1 - odd]


def pick_turns(info, blocks):
    out = (shaped(blocks.shape[1:], bf16), vmem())
    return call(pick_kernel, [out] * 2, [LOAD], [info, blocks], limit=8, cost=(0, MIB))


def output_kernel(patches, info, middle, keep, far, turned, first, second):
    core, odd = info[0], lax.rem(info[2], 2)
    half = keep.shape[0]
    block = half // 2
    bias = turned[patches + DOWN_BIAS : patches + DOWN_BIAS + 1, :]
    for ref, which in ((first, odd), (second, 1 - odd)):
        here = pl.ds(pl.multiple_of(which * block, block), block)
        there = pl.ds(pl.multiple_of(core * half + which * block, block), block)
        ref[...] = (middle[there, :] + keep[here, :] + far[here, :].astype(f32) + bias).astype(bf16)


def output_turns(info, middle, keep, far, turned, patches):
    out = (shaped((keep.shape[0] // 2, keep.shape[1]), bf16), vmem())
    return call(
        functools.partial(output_kernel, patches),
        [out] * 2,
        [LOAD] * 4,
        [info, middle, keep, far, turned],
        limit=8,
        cost=(0, 6 * MIB),
    )


def front_kernel(blocks, patches, info, *refs):
    tokens_in, refs = refs[:4], refs[4:]
    weights_in, refs = refs[:blocks], refs[blocks:]
    q_out, k_out, v_out, start_out, normed_out, weight, turned_out, seg_out, spot_out = refs[:9]
    held, sem, weight_sem = refs[9:]
    core, chip, place = info[0], info[1], info[2]
    block, columns = held.shape[1] - 16, weight.shape[1] - SMALL
    part = columns // 3
    copies = []
    for i in range(4):
        side = core if i < 2 else 1 - core
        there = 2 * side + ((i % 2) ^ (place % 2))
        copies.append(pltpu.make_async_copy(tokens_in[i], held.at[there], sem.at[i]))
    copies += piece_copies(weights_in, weight, info, weight_sem)
    run_copies(copies)
    small = weight[:, columns:]
    turned_out[...] = small.astype(f32).T
    vector = lambda i: turned_out[patches + i : patches + i + 1, :]
    half = pl.ds(pl.multiple_of(core * part, 128), part)
    query_bias = turned_out[patches + QUERY_BIAS : patches + QUERY_BIAS + 1, half]
    value_bias = turned_out[patches + VALUE_BIAS : patches + VALUE_BIAS + 1, half]
    gain, shift = vector(GAIN_ONE), vector(SHIFT_ONE)
    extra = held[0, block : block + 16, :].astype(f32)
    width = extra.shape[1]
    segment = jnp.concatenate([extra[1:2, :], extra[2:3, : 4 * block - width]], axis=1)
    seg_out[...] = jnp.broadcast_to(segment, seg_out.shape)
    ids = lax.broadcasted_iota(jnp.int32, (SMALL, block), 0).astype(f32)
    for b in range(4):
        here = slice(b * block, (b + 1) * block)
        spot = held[b, block : block + 16, :].astype(f32)[0:1, :block]
        spot_out[:, here] = jnp.broadcast_to(spot, (8, block))
        one_hot = jnp.where(ids == spot, 1.0, 0.0).astype(bf16)
        embedded = lax.dot_general(
            one_hot, small, (((0,), (1,)), ((), ())), preferred_element_type=f32
        )
        start = held[b, :block, :].astype(f32) + embedded
        start_out[here, :] = start
        normal, _ = normalise(start)
        normed = (normal * gain + shift).astype(bf16)
        normed_out[here, :] = normed
        projected = dot(normed, weight[:, :columns])
        query = (projected[:, :part] + query_bias).astype(bf16).astype(f32) * 0.125
        q_out[here, :] = query.astype(bf16)
        k_out[here, :] = projected[:, part : 2 * part].astype(bf16)
        v_out[here, :] = (projected[:, 2 * part :] + value_bias).astype(bf16)


def front(info, tokens, weights, patches):
    blocks = len(weights)
    block, width = tokens[0].shape[0] - 16, tokens[0].shape[1]
    columns = weights[0].shape[1]
    part = (columns - SMALL) // 3
    rows = 4 * block
    return call(
        functools.partial(front_kernel, blocks, patches),
        [
            (shaped((rows, part), bf16), vmem()),
            (shaped((rows, part), bf16), vmem()),
            (shaped((rows, part), bf16), vmem()),
            (shaped((rows, width), f32), vmem()),
            (shaped((rows, width), bf16), vmem()),
            (shaped((width, columns), bf16), vmem()),
            (shaped((SMALL, width), f32), vmem()),
            (shaped((8, rows), f32), vmem()),
            (shaped((8, rows), f32), vmem()),
        ],
        [HELD] * (4 + blocks),
        [info] + list(tokens) + list(weights),
        scratch=[
            pltpu.VMEM((4, block + 16, width), bf16),
            pltpu.SemaphoreType.DMA((4,)),
            pltpu.SemaphoreType.DMA((blocks,)),
        ],
        cost=(2 * rows * width * columns, 12 * MIB),
    )


def fill_bias(bias, seg):
    block = bias.shape[1]
    wide = seg[...]
    tall = jnp.broadcast_to(wide[0:1, :], (128, wide.shape[1])).T[:, 0:1]
    base = 0
    for b in range(4):
        many = (b + 1) * block
        key = lax.broadcasted_iota(jnp.int32, (many, block), 0)
        ask = lax.broadcasted_iota(jnp.int32, (many, block), 1) + b * block
        same = tall[:many] == wide[0:1, b * block : (b + 1) * block]
        bias[base : base + many, :] = jnp.where((key <= ask) & same, 0.0, masked_score)
        base += many


def turn(values):
    return values.astype(f32).T.astype(bf16)


def attend_kernel(info, q, k, v, seg, out, total, bias):
    block = bias.shape[1]

    @pl.when(pl.program_id(0) == 0)
    def _():
        fill_bias(bias, seg)

    turned_q, turned_v = turn(q[...]), turn(v[...])
    side = lax.broadcasted_iota(jnp.int32, (128, block), 0) // 64
    base = 0
    for b in range(4):
        many = (b + 1) * block
        here = slice(b * block, (b + 1) * block)
        mixed = []
        for h in range(2):
            ask = jnp.where(side == h, turned_q[:, here].astype(f32), 0.0).astype(bf16)
            scores = dot(k[:many, :], ask) + bias[base : base + many, :]
            top = jnp.max(scores, axis=0, keepdims=True)
            raised = jnp.exp(scores - top)
            mass = jnp.sum(raised, axis=0, keepdims=True)
            total[0, h : h + 1, here] = top + jnp.log(mass)
            part = dot(turned_v[64 * h : 64 * h + 64, :many], raised.astype(bf16))
            mixed.append(part * (1.0 / mass))
        out[here, :] = jnp.concatenate(mixed, axis=0).T.astype(bf16)
        base += many


def attend(info, q, k, v, seg):
    rows, part = q.shape
    pairs = part // 128
    column = pl.BlockSpec((rows, 128), lambda i: (0, i))
    whole = pl.BlockSpec(seg.shape, lambda i: (0, 0))
    return call(
        attend_kernel,
        [
            (shaped((rows, part), bf16), column),
            (shaped((pairs, 8, rows), f32), pl.BlockSpec((1, 8, rows), lambda i: (i, 0, 0))),
        ],
        [column, column, column, whole],
        [info, q, k, v, seg],
        scratch=[pltpu.VMEM((10 * rows // 4, rows // 4), f32)],
        grid=(pairs,),
        cost=(6 * rows * rows * part, 4 * MIB),
    )


def attend_back_kernel(info, q, k, v, o, g, total, seg, dq, dk, dv, bias, dk_sum, dv_sum):
    block = bias.shape[1]

    @pl.when(pl.program_id(0) == 0)
    def _():
        fill_bias(bias, seg)

    wide_g = g[...].astype(f32).T
    product = wide_g * o[...].astype(f32).T
    inner = [jnp.sum(product[64 * h : 64 * h + 64], axis=0, keepdims=True) for h in range(2)]
    turned_q, turned_k = turn(q[...]), turn(k[...])
    turned_g = wide_g.astype(bf16)
    side = lax.broadcasted_iota(jnp.int32, (128, block), 0) // 64
    flat = lax.broadcasted_iota(jnp.int32, (block, 128), 1) // 64
    dk_sum[...] = jnp.zeros_like(dk_sum)
    dv_sum[...] = jnp.zeros_like(dv_sum)
    base = 0
    for b in range(4):
        many = (b + 1) * block
        here = slice(b * block, (b + 1) * block)
        low_probs, low_scores, own_qs, own_gs = [], [], [], []
        for h in range(2):
            ask = jnp.where(side == h, turned_q[:, here].astype(f32), 0.0).astype(bf16)
            ask_g = jnp.where(side == h, turned_g[:, here].astype(f32), 0.0).astype(bf16)
            scores = dot(k[:many, :], ask) + bias[base : base + many, :]
            probs = jnp.exp(scores - total[0, h : h + 1, here])
            grad_probs = dot(v[:many, :], ask_g)
            grad_scores = (probs * (grad_probs - inner[h][:, here])).astype(bf16)
            own_qs.append(jnp.where(flat == h, q[here, :].astype(f32), 0.0).astype(bf16))
            own_gs.append(jnp.where(flat == h, g[here, :].astype(f32), 0.0).astype(bf16))
            low_probs.append(probs.astype(bf16))
            low_scores.append(grad_scores)
        dv_sum[:many, :] += dot(jnp.concatenate(low_probs, axis=1), jnp.concatenate(own_gs))
        dk_sum[:many, :] += dot(jnp.concatenate(low_scores, axis=1), jnp.concatenate(own_qs))
        both = dot(turned_k[:, :many], jnp.concatenate(low_scores, axis=1))
        half = both.shape[1] // 2
        mixed = jnp.concatenate([both[:64, :half], both[64:, half:]], axis=0)
        dq[here, :] = (mixed.T * 0.125).astype(bf16)
        base += many
    dk[...] = dk_sum[...].astype(bf16)
    dv[...] = dv_sum[...].astype(bf16)


def attend_back(info, q, k, v, o, g, total, seg):
    rows, part = q.shape
    pairs = part // 128
    column = pl.BlockSpec((rows, 128), lambda i: (0, i))
    whole = pl.BlockSpec(seg.shape, lambda i: (0, 0))
    out = (shaped((rows, part), bf16), column)
    return call(
        attend_back_kernel,
        [out, out, out],
        [column] * 5 + [pl.BlockSpec((1, 8, rows), lambda i: (i, 0, 0)), whole],
        [info, q, k, v, o, g, total, seg],
        scratch=[
            pltpu.VMEM((10 * rows // 4, rows // 4), f32),
            pltpu.VMEM((rows, 128), f32),
            pltpu.VMEM((rows, 128), f32),
        ],
        grid=(pairs,),
        cost=(15 * rows * rows * part, 6 * MIB),
    )


def cotangent_copies(info, pieces, held, sems):
    core, place = info[0], info[2]
    copies = []
    for i in range(4):
        side = core if i < 2 else 1 - core
        there = 2 * side + ((i % 2) ^ (place % 2))
        copies.append(pltpu.make_async_copy(pieces[i], held.at[there], sems[i]))
    return copies


def gelu_parts(values):
    scale = 0.7978845608028654
    square = values * values
    slope = jnp.tanh(values * (scale + (scale * 0.044715) * square))
    half = 0.5 * (1.0 + slope)
    grad = half + 0.5 * values * (1.0 - slope * slope) * (
        scale + (3.0 * scale * 0.044715) * square
    )
    return values * half, grad


def piece_copies(pieces, target, info, sem, lanes=None):
    chip = info[1]
    rows = pieces[0].shape[0]
    copies, base = [], 0
    for i, ref in enumerate(pieces):
        distance = min(i, 3)
        begin = pl.multiple_of((distance ^ chip) * rows, rows)
        if i == 4:
            begin = pl.multiple_of(begin + rows // 2, rows // 2)
        source = ref if lanes is None else ref.at[:, lanes]
        there = target.at[pl.ds(begin, ref.shape[0])]
        copies.append(pltpu.make_async_copy(source, there, sem.at[i]))
    return copies


def block_copies(pieces, target, info, sem):
    if len(pieces) == 1:
        return [pltpu.make_async_copy(pieces[0], target, sem.at[0])]
    copies = []
    for i, ref in enumerate(pieces):
        begin = (min(i, 3) ^ info[1]) * PLACES + (2 if i == 4 else 0)
        count = 2 if i >= 3 else PLACES
        copies.append(
            pltpu.make_async_copy(ref.at[pl.ds(0, count)], target.at[pl.ds(begin, count)], sem.at[i])
        )
    return copies


def hidden_places(core, hidden, width, chips):
    spare = 2 * hidden // width
    share = hidden // chips
    device = share // PLACES
    rows = device // spare
    unit = lax.broadcasted_iota(jnp.int32, (hidden, 1), 0)
    rest = lax.rem(unit, share)
    row = ((2 * (unit // share) + core) * PLACES + rest // device) * rows + lax.rem(rest, rows)
    lane = lax.broadcasted_iota(jnp.int32, (hidden, width), 1)
    return jnp.where(lane == row, 1.0, 0.0).astype(bf16)


def hidden_turns(spare, hidden, chips):
    device = hidden // (chips * PLACES)
    unit = lax.broadcasted_iota(jnp.int32, (spare, hidden), 1)
    return lax.rem(unit, device) // (device // spare) == lax.broadcasted_iota(
        jnp.int32, (spare, hidden), 0
    )


def middle_kernel(patches, chips, hidden, info, att, att_far, start, turned, *refs):
    weights, refs = refs[:-4], refs[-4:]
    middle_out, normed_out, bias_out, weight_out = refs
    core = info[0]
    rows, width = start.shape
    part, tile = width // 2, rows // 4
    if len(weights) == 2:
        block = weights[0].shape[1]
        for side, ref in ((core, weights[0]), (1 - core, weights[1])):
            for q in range(4):
                begin = pl.multiple_of((2 * q + side) * block, block)
                weight_out[pl.ds(begin, block), :] = ref[q]
    else:
        weight_out[...] = weights[0][...]
    spare = 2 * hidden // width
    biases = turned[patches + 8 : patches + 8 + spare, :].astype(bf16)
    spread_out = dot_right(biases, hidden_places(core, hidden, width, chips))
    bias = jnp.sum(
        jnp.where(hidden_turns(spare, hidden, chips), spread_out, 0.0), axis=0, keepdims=True
    )
    bias_out[...] = jnp.broadcast_to(bias, bias_out.shape)
    vector = lambda i: turned[patches + i : patches + i + 1, :]
    own = pl.ds(pl.multiple_of(core * part, 128), part)
    far = pl.ds(pl.multiple_of((1 - core) * part, 128), part)
    gain, shift, out_bias = vector(GAIN_TWO), vector(SHIFT_TWO), vector(OUTPUT_BIAS)
    for t in range(4):
        here = slice(t * tile, (t + 1) * tile)
        mixed = dot(att[here, :], weight_out[own, :]) + dot(att_far[here, :], weight_out[far, :])
        middle = start[here, :] + mixed + out_bias
        middle_out[here, :] = middle
        normal, _ = normalise(middle)
        normed_out[here, :] = (normal * gain + shift).astype(bf16)


def middle_front(info, att, att_far, start, turned, weights, hidden, patches, chips):
    rows, width = start.shape
    return call(
        functools.partial(middle_kernel, patches, chips, hidden),
        [
            (shaped((rows, width), f32), vmem()),
            (shaped((rows, width), bf16), vmem()),
            (shaped((8, hidden), f32), vmem()),
            (shaped((width, width), bf16), vmem()),
        ],
        [LOAD] * (4 + len(weights)),
        [info, att, att_far, start, turned] + list(weights),
        cost=(2 * rows * width * width, 12 * MIB),
    )


def feed_front_kernel(ups, downs, blocks, info, normed, up_bias, *refs):
    cot_in, refs = refs[:4], refs[4:]
    up_in, refs = refs[:ups], refs[ups:]
    down_in, refs = refs[:downs], refs[downs:]
    keep_out, send_out, slope_out, up, down, cot, refs = *refs[:6], refs[6:]
    down_grads, (act, far_sum, down_grad, cot_sem, up_sem, down_sem) = refs[:-6], refs[-6:]
    core, chip = info[0], info[1]
    rows, width = normed.shape
    hidden = up.shape[1]
    chunk = hidden // 4
    half = rows // 2
    early = piece_copies(up_in, up, info, up_sem)
    late = block_copies(down_in, down, info, down_sem)
    late += cotangent_copies(info, cot_in, cot, [cot_sem.at[i] for i in range(4)])
    for copy in early + late:
        copy.start()
    for copy in early:
        copy.wait()
    own = pl.ds(pl.multiple_of(core * half, half), half)
    far = pl.ds(pl.multiple_of((1 - core) * half, half), half)
    outs = []
    pair = 2 * chunk
    for step, distances in enumerate(((3, 2), (1, 0))):
        which = (1 - step) ^ (chip // 2)
        lanes = pl.ds(pl.multiple_of(which * pair, 128), pair)
        blocks_here = pl.ds(pl.multiple_of(which * 2 * PLACES, 2 * PLACES), 2 * PLACES)
        for side, here in enumerate((own, far)):
            value, slope = gelu_parts(dot(normed[here, :], up[:, lanes]) + up_bias[0:1, lanes])
            value = value.astype(bf16)
            act[here, :] = value
            slope_out[here, lanes] = slope.astype(bf16)
            if step == 0 and side == 0:
                for copy in late:
                    copy.wait()
            part = dot(value, down[blocks_here].reshape(pair, width))
            if side == 0:
                keep_out[...] = part if step == 0 else keep_out[...] + part
            elif step == 0:
                far_sum[...] = part
            else:
                send_out[...] = (far_sum[...] + part).astype(bf16)
        grad = dot_left(act[...], cot[...].reshape(rows, width)).astype(bf16)
        down_grad[blocks_here] = grad.reshape(2 * PLACES, chunk // PLACES, width)
        if blocks == 4:
            ready = [
                copy
                for copy, where in fold_copies(down_grad, down_grads, chip, down_sem)
                if where in distances
            ]
            for copy in ready:
                copy.start()
            outs += ready
    if blocks != 4:
        outs.append(pltpu.make_async_copy(down_grad, down_grads[0], down_sem.at[0]))
        outs[0].start()
    for copy in outs:
        copy.wait()


def feed_front(info, normed, up_bias, cots, ups, downs, blocks):
    rows, width = normed.shape
    hidden = up_bias.shape[1]
    whole = (4 * PLACES, hidden // (4 * PLACES), width)
    grads = fold_shapes(PLACES, whole[1:]) if blocks == 4 else [shaped(whole, bf16)]
    return call(
        functools.partial(feed_front_kernel, len(ups), len(downs), blocks),
        [
            (shaped((rows // 2, width), f32), vmem()),
            (shaped((rows // 2, width), bf16), vmem()),
            (shaped((rows, hidden), bf16), vmem()),
            (shaped((width, hidden), bf16), vmem()),
            (shaped(whole, bf16), vmem()),
            (shaped((4, rows // 4, width), bf16), vmem()),
        ]
        + [(one, anywhere()) for one in grads],
        [LOAD] * 2 + [HELD] * (4 + len(ups) + len(downs)),
        [info, normed, up_bias] + list(cots) + list(ups) + list(downs),
        scratch=[
            pltpu.VMEM((rows, hidden // 2), bf16),
            pltpu.VMEM((rows // 2, width), f32),
            pltpu.VMEM(whole, bf16),
            pltpu.SemaphoreType.DMA((4,)),
            pltpu.SemaphoreType.DMA((len(ups),)),
            pltpu.SemaphoreType.DMA((8,)),
        ],
        limit=16,
        cost=(6 * rows * width * hidden, 24 * MIB),
    )


def feed_back_kernel(chips, info, slope, cot, up, down, back_out, low_out, grad_out, bias_out):
    rows, hidden = slope.shape
    width = up.shape[0]
    chunk = hidden // 2
    flat = cot[...].reshape(rows, width)
    sums = []
    for q in range(2):
        lanes = slice(q * chunk, (q + 1) * chunk)
        down_part = down[2 * q * PLACES : 2 * (q + 1) * PLACES].reshape(chunk, width)
        grad = (dot_right(flat, down_part) * slope[:, lanes].astype(f32)).astype(bf16)
        grad_out[:, lanes] = grad
        sums.append(jnp.sum(grad.astype(f32), axis=0, keepdims=True))
        back = dot_right(grad, up[:, lanes])
        if q == 0:
            back_out[...] = back
        else:
            back = back_out[...] + back
            back_out[...] = back
            low_out[...] = back.astype(bf16)
    spare = 2 * hidden // width
    turns = hidden_turns(spare, hidden, chips)
    biases = jnp.where(turns, jnp.concatenate(sums, axis=1), 0.0)
    high = biases.astype(bf16)
    both = jnp.concatenate([high.astype(f32), biases - high.astype(f32)]).astype(bf16)
    placed = dot(both, hidden_places(info[0], hidden, width, chips))
    bias_out[...] = jnp.zeros_like(bias_out)
    bias_out[:spare, :] = placed[:spare] + placed[spare:]


def feed_back(info, slope, cot, up, down, chips):
    rows, hidden = slope.shape
    width = up.shape[0]
    return call(
        functools.partial(feed_back_kernel, chips),
        [
            (shaped((rows, width), f32), vmem()),
            (shaped((rows, width), bf16), vmem()),
            (shaped((rows, hidden), bf16), vmem()),
            (shaped((8, width), f32), vmem()),
        ],
        [LOAD] * 4,
        [info, slope, cot, up, down],
        limit=12,
        cost=(4 * rows * width * hidden, 24 * MIB),
    )


def weight_kernel(blocks, count, info, left, *refs):
    parts, outs, held, sem = refs[:count], refs[count:-2], refs[-2], refs[-1]
    if count > 1:
        right = jnp.concatenate([ref[...] for ref in parts], axis=1)
        held[...] = dot_left(left[...], right).astype(bf16)
    else:
        for begin in range(0, held.shape[1], 768):
            lanes = slice(begin, begin + 768)
            held[:, lanes] = dot_left(left[...], parts[0][:, lanes]).astype(bf16)
    if blocks == 4:
        run_copies([copy for copy, _ in fold_copies(held, outs, info[1], sem)])
    else:
        run_copies([pltpu.make_async_copy(held, outs[0], sem.at[0])])


def weight_grad(info, left, parts, blocks):
    rows, width = left.shape
    columns = sum(part.shape[1] for part in parts)
    outs = [shaped((width, columns), bf16)]
    if blocks == 4:
        outs = fold_shapes(width // 4, (columns,))
    return call(
        functools.partial(weight_kernel, blocks, len(parts)),
        [(one, anywhere()) for one in outs],
        [LOAD] * (1 + len(parts)),
        [info, left] + list(parts),
        scratch=[pltpu.VMEM((width, columns), bf16), pltpu.SemaphoreType.DMA((8,))],
        cost=(2 * rows * width * columns, 8 * MIB),
    )


def middle_back_kernel(blocks, patches, info, back, back_far, middle, turned, att, weight, cot, *refs):
    grad_out, attended_out, keep_out, send_out, sums_out, branch = refs
    core = info[0]
    rows, width = middle.shape
    tile = rows // 4
    part = width // 2
    gain = turned[patches + GAIN_TWO : patches + GAIN_TWO + 1, :]
    own_rows = pl.ds(pl.multiple_of(core * part, 128), part)
    for t in range(4):
        here = slice(t * tile, (t + 1) * tile)
        grad_normed = back[here, :] + back_far[here, :].astype(f32)
        normal, scale = normalise(middle[here, :])
        grad_outputs = cot[t].astype(f32)
        grad = grad_outputs + norm_back(normal, scale, gain, grad_normed)
        low = grad.astype(bf16)
        branch[here, :] = low
        attended_out[here, :] = dot_right(low, weight[own_rows, :]).astype(bf16)

        @pl.when(core == t // 2)
        def _():
            grad_out[(t % 2) * tile : (t % 2 + 1) * tile, :] = grad
            sums = jnp.concatenate(
                [
                    jnp.sum(low.astype(f32), axis=0, keepdims=True),
                    jnp.sum(grad_outputs, axis=0, keepdims=True),
                    jnp.sum(grad_normed * normal, axis=0, keepdims=True),
                    jnp.sum(grad_normed, axis=0, keepdims=True),
                    jnp.zeros((4, width), f32),
                ],
                axis=0,
            )
            sums_out[...] = sums if t % 2 == 0 else sums_out[...] + sums

    weight_grad = dot_left(att[...], branch[...]).astype(bf16)
    shape = send_out.shape[:1] + (2,) + send_out.shape[1:]
    sorted_grad = weight_grad.reshape(shape) if blocks == 4 else None
    if blocks == 4:
        for c in range(2):

            @pl.when(core == c)
            def _():
                keep_out[...] = sorted_grad[:, c]
                send_out[...] = sorted_grad[:, 1 - c]

    else:
        keep_out[...] = weight_grad
        send_out[...] = weight_grad


def middle_back(info, back, back_far, middle, turned, att, weight, cot, patches, blocks):
    rows, width = middle.shape
    part = width // 2
    slab = (2, part // 4, width) if blocks == 4 else (part, width)
    return call(
        functools.partial(middle_back_kernel, blocks, patches),
        [
            (shaped((rows // 2, width), f32), vmem()),
            (shaped((rows, part), bf16), vmem()),
            (shaped(slab, bf16), vmem()),
            (shaped(slab, bf16), vmem()),
            (shaped((8, width), f32), vmem()),
        ],
        [LOAD] * 7,
        [info, back, back_far, middle, turned, att, weight, cot],
        scratch=[pltpu.VMEM((rows, width), bf16)],
        cost=(4 * rows * width * part, 14 * MIB),
    )


def project_kernel(info, dq, dk, dv, weight, keep_out, send_out):
    core = info[0]
    rows, part = dq.shape
    half_rows = rows // 2

    def product(first):
        here = pl.ds(pl.multiple_of(first, 128), half_rows)
        return (
            dot_right(dq[here, :], weight[:, :part])
            + dot_right(dk[here, :], weight[:, part : 2 * part])
            + dot_right(dv[here, :], weight[:, 2 * part : 3 * part])
        )

    send_out[...] = product((1 - core) * half_rows).astype(bf16)
    keep_out[...] = product(core * half_rows)


def project_back(info, dq, dk, dv, weight):
    rows, part = dq.shape
    width = weight.shape[0]
    return call(
        project_kernel,
        [
            (shaped((rows // 2, width), f32), vmem()),
            (shaped((rows // 2, width), bf16), vmem()),
        ],
        [LOAD] * 4,
        [info, dq, dk, dv, weight],
        cost=(6 * rows * width * part, 8 * MIB),
    )


def start_kernel(blocks, patches, spare, info, *refs):
    (keep, far, start, grad_middle, turned, sums, bias_grad, spots, dq, dv, out_keep, out_got) = refs[:12]
    refs = refs[12:]
    low_out, refs = refs[0], refs[1:]
    grads, refs = refs[:-3], refs[-3:]
    held, rows_held, sem = refs
    core, chip = info[0], info[1]
    rows, part = dq.shape
    half_rows, width = keep.shape
    up_rows = width // blocks
    gain = turned[patches + GAIN_ONE : patches + GAIN_ONE + 1, :]
    own = pl.ds(pl.multiple_of(core * half_rows, half_rows), half_rows)
    grad_normed = keep[...] + far[...].astype(f32)
    normal, scale = normalise(start[own, :])
    grad = grad_middle[...] + norm_back(normal, scale, gain, grad_normed)
    low = grad.astype(bf16)
    low_out[...] = low
    ids = lax.broadcasted_iota(jnp.int32, (SMALL, half_rows), 0).astype(f32)
    mine = spots[0:1, pl.ds(pl.multiple_of(core * half_rows, 128), half_rows)]
    one_hot = jnp.where(ids == mine, 1.0, 0.0).astype(bf16)
    rows_held[...] = dot(one_hot, low)
    half = pl.ds(pl.multiple_of(core * part, 128), part)
    rows_held[patches : patches + 8, :] = jnp.zeros((8, width), f32)

    def put(i, row):
        rows_held[patches + i : patches + i + 1, :] = row

    rows_held[patches + QUERY_BIAS : patches + QUERY_BIAS + 1, half] = jnp.sum(
        dq[...].astype(f32), axis=0, keepdims=True
    )
    rows_held[patches + VALUE_BIAS : patches + VALUE_BIAS + 1, half] = jnp.sum(
        dv[...].astype(f32), axis=0, keepdims=True
    )
    put(OUTPUT_BIAS, sums[0:1, :])
    put(DOWN_BIAS, sums[1:2, :])
    put(GAIN_TWO, sums[2:3, :])
    put(SHIFT_TWO, sums[3:4, :])
    put(GAIN_ONE, jnp.sum(grad_normed * normal, axis=0, keepdims=True))
    put(SHIFT_ONE, jnp.sum(grad_normed, axis=0, keepdims=True))
    rows_held[patches + 8 : patches + 8 + spare, :] = bias_grad[:spare, :]
    held[:, :SMALL] = rows_held[...].T.astype(bf16)
    if blocks == 4:
        slab = up_rows // 2
        for x in range(2):
            for side, ref in ((core, out_keep), (1 - core, out_got)):
                begin = pl.multiple_of((2 * side + x) * up_rows, up_rows)
                held[pl.ds(begin, slab), SMALL:] = ref[x, :, : width // 2]
                held[pl.ds(begin + slab, slab), SMALL:] = ref[x, :, width // 2 :]
    if blocks == 4:
        run_copies([copy for copy, _ in fold_copies(held, grads, chip, sem)])
    else:
        run_copies([pltpu.make_async_copy(held, grads[0], sem.at[0])])


def start_back(info, blocks, args, patches, spare):
    half_rows, width = args[0].shape
    columns = SMALL + width // 2 if blocks == 4 else SMALL
    outs = [shaped((width, columns), bf16)]
    if blocks == 4:
        outs = fold_shapes(width // 4, (columns,))
    return call(
        functools.partial(start_kernel, blocks, patches, spare),
        [(shaped((half_rows, width), bf16), vmem())]
        + [(one, anywhere()) for one in outs],
        [LOAD] * len(args),
        [info] + list(args),
        scratch=[
            pltpu.VMEM((width, columns), bf16),
            pltpu.VMEM((SMALL, width), f32),
            pltpu.SemaphoreType.DMA((8,)),
        ],
        cost=(2 * half_rows * width * SMALL, 10 * MIB),
    )


def split_kernel(plan, count, shift, info, *refs):
    place = lax.rem(info[2] >> shift, count)
    inputs, held = refs[: -1 - count], refs[-1]
    outs = refs[-1 - count : -1]
    column = 0
    for parts in plan:
        totals = []
        for terms in parts:
            total = 0.0
            for index, begin, rows in terms:
                total = total + inputs[index][begin : begin + rows, :].astype(f32)
            totals.append(total)
        whole = totals[0] if len(totals) == 1 else jnp.concatenate(totals)
        lanes = whole.shape[-1]
        held[..., column : column + lanes] = whole.reshape(held.shape[:-1] + (lanes,))
        column += lanes
    lead = (slice(None),) * (len(held.shape) - 3)
    for k in range(count):
        outs[k][...] = held[lead + (k ^ place,)].astype(outs[k].dtype)


def split(info, groups, shape, shift=0):
    arrays, plan, columns = [], [], 0
    for group in groups:
        base = len(arrays)
        parts = group.parts if isinstance(group, Fold) else [[(i, 0, None) for i in range(len(group))]]
        terms = group.terms if isinstance(group, Fold) else group
        flat = [array.reshape((-1,) + array.shape[-1:]) for array in terms]
        half = flat[0].shape[0] // 2
        plan.append(
            [
                [
                    (base + i, 0, flat[i].shape[0]) if begin is None else (base + i, begin * half, half)
                    for i, begin, _ in [(i, None if size is None else begin, size) for i, begin, size in part]
                ]
                for part in parts
            ]
        )
        arrays += flat
        columns += flat[0].shape[-1]
    count, total = shape[-2], columns
    for extent in shape:
        total *= extent
    one = shape[:-2] + (shape[-1], columns)
    return call(
        functools.partial(split_kernel, plan, count, shift),
        [(shaped(one, f32 if k == 0 else bf16), vmem()) for k in range(count)],
        [LOAD] * len(arrays),
        [info] + arrays,
        scratch=[pltpu.VMEM(shape + (columns,), f32)],
        limit=20,
        cost=(0, 8 * total),
    )


def swap(values, axis, bits):
    size = lax.axis_size(axis)
    return lax.ppermute(values, axis, [(i, i ^ bits) for i in range(size)])


def spread_perm(turn):
    pairs = []
    for w in range(lax.axis_size("wide")):
        for z in range(PLACES):
            there = (w - w % 2 + z // 2, 2 * (w % 2) + (turn ^ (z % 2)))
            pairs.append((w * PLACES + z, there[0] * PLACES + there[1]))
    return pairs


def unspread_turn(part, turn):
    return lax.ppermute(part, ("wide", "narrow"), [(b, a) for a, b in spread_perm(turn)])


def unspread_join(got, place):
    odd = (place % 2) == 1
    return jnp.stack([jnp.where(odd, got[1], got[0]), jnp.where(odd, got[0], got[1])])


def along(piece, bits):
    held = {0: piece}
    for bit in bits:
        held.update({index ^ (bit // 2): swap(part, "wide", bit) for index, part in list(held.items())})
    return [held[index] for index in range(len(held))]


def direct(piece, chips):
    return [piece] + [swap(piece, "wide", 2 * index) for index in range(1, chips)]


def fold(pieces, bits):
    held = dict(enumerate(pieces))
    for number, bit in enumerate(bits):
        step = bit // 2
        got = {i: swap(held[i ^ step], "wide", bit) for i in held if not i & step}
        if number == len(bits) - 1:
            return [held[0], got[0]]
        held = {i: (held[i].astype(f32) + got[i].astype(f32)).astype(bf16) for i in got}
    return [held[0]]


def after(values, *others):
    return lax.optimization_barrier((values,) + others)[0]


def together(*values):
    return lax.optimization_barrier(values)


class Fold:
    def __init__(self, outs, bits):
        self.outs, self.bits = list(outs), bits
        self.plane = len(outs) == 5
        if self.plane:
            self.near = [swap(outs[1], "wide", 2), swap(outs[2], "wide", 4)]

    def pairs(self):
        return [(self.outs[3], self.near[0]), (self.outs[4], self.near[1])] if self.plane else []

    def cross(self, sums):
        if self.plane:
            self.far = [swap(sums[0], "wide", 4), swap(sums[1], "wide", 2)]
            self.terms = [self.outs[0], *self.near, *self.far]
            first = [(0, 0, 1), (1, 1, 1), (3, 0, 1)]
            self.parts = [first, [(0, 1, 1), (2, 1, 1), (4, 0, 1)]]
        else:
            self.terms = fold(self.outs, self.bits)
            self.parts = [[(i, 0, None) for i in range(len(self.terms))]]


def local(
    tokens,
    positions,
    segments,
    position_table,
    input_weight,
    query_bias,
    value_bias,
    output_weight,
    output_bias,
    first_gain,
    first_shift,
    up_weight,
    up_bias,
    down_weight,
    down_bias,
    second_gain,
    second_shift,
    cotangent,
):
    size = lax.axis_size("wide")
    chips = size // 2
    bits = [2**i for i in range(1, size.bit_length() - 1)]
    seq_count, block, width = tokens.shape
    hidden = up_weight.shape[1]
    patches = position_table.shape[1]
    full = segments.shape[1]
    rows = width // (size * PLACES)
    part = width // 2
    own_hidden = hidden // 2
    wide, place = lax.axis_index("wide"), lax.axis_index("narrow")
    core, chip = wide % 2, wide // 2
    first_core = core == 0
    blocks = 4 if chips == 4 else 1
    info = jnp.stack([core, chip if blocks == 4 else 0 * chip, place, chip]).astype(jnp.int32)

    def pick(values, index, axis=0):
        return lax.dynamic_index_in_dim(values, index, axis, keepdims=False)

    def by_chip(pieces):
        flat = [piece.reshape((-1,) + piece.shape[-1:]) for piece in pieces]
        if blocks == 4:
            return flat
        whole = jnp.take(jnp.stack(flat), jnp.arange(chips) ^ chip, axis=0)
        return [whole.reshape((-1,) + flat[0].shape[1:])]

    def by_distance(outs, shape):
        if blocks == 4:
            return [out.reshape(shape) for out in outs]
        whole = outs[0].reshape((chips,) + shape)
        return [pick(whole, index ^ chip) for index in range(chips)]

    vectors = (
        query_bias,
        value_bias,
        output_bias,
        first_gain,
        first_shift,
        down_bias,
        second_gain,
        second_shift,
    )
    spare = up_bias.shape[0] // rows
    plane = blocks == 4
    up_sorted = up_weight
    if not plane:
        up_sorted = up_weight.reshape(rows, 4, chips // 4, 2, -1)
        up_sorted = jnp.swapaxes(up_sorted, 2, 3).reshape(rows, hidden)

    def cross_one(piece):
        if blocks == 4:
            return [piece, swap(piece, "wide", 2), swap(piece, "wide", 4)]
        return along(piece, bits)

    def cross_two(pieces):
        if blocks == 4:
            own, x, y = pieces
            first, second = cut(info, x, y)
            return [own, x, y, swap(first, "wide", 2), swap(second, "wide", 4)]
        return pieces

    def place_axis(piece):
        return piece.reshape(piece.shape[:-4] + (PLACES,) + piece.shape[-2:])

    def folded(outs, shape):
        if plane:
            return Fold(outs, bits)
        whole = outs[0].reshape((chips,) + shape)
        return Fold([pick(whole, index ^ chip) for index in range(chips)], bits)

    def crossed(folds, *values):
        count = len(values)
        near = [array for one in folds if one.plane for array in one.near]
        values = together(*values, *near)
        values, near = values[:count], list(values[count:])
        if plane:
            for one in folds:
                one.near, near = near[:2], near[2:]
            sums = add_firsts(info, [pair for one in folds for pair in one.pairs()])
        for i, one in enumerate(folds):
            one.cross(sums[2 * i : 2 * i + 2] if plane else None)
        return values

    def arrived(folds, *values):
        if not plane:
            return values
        count = len(values)
        far = [array for one in folds for array in one.far]
        values = together(*values, *far)
        values, far = values[:count], list(values[count:])
        for one in folds:
            one.far, far = far[:2], far[2:]
            one.terms = [*one.terms[:3], *one.far]
        return values

    rows_in = jnp.stack([*vectors, *(up_bias[i * rows : (i + 1) * rows] for i in range(spare))])
    in_keep, in_send = pack_in(info, input_weight, position_table, rows_in)
    in_far = swap(in_send, "wide", 1)
    raw_parts = together(down_weight, output_weight, up_sorted, tokens, in_keep)
    raw = jnp.concatenate(raw_parts[:2]) if plane else raw_parts[0]
    up_keep, up_send = pack_up(info, raw_parts[2])
    first, second = sent(info, raw_parts[3], positions, segments)
    in_far, raw, up_send = together(in_far, raw, up_send)

    in_pair = arrange(info, [in_keep, in_far], 0, 0)
    in_got = [in_pair] + [swap(in_pair, "narrow", k) for k in range(1, PLACES)]
    raw_far = swap(raw, "narrow", 2)
    up_far = swap(up_send, "wide", 1)
    up_far, raw_far, first, *in_got = together(up_far, raw_far, first, *in_got)

    in_piece = arrange(info, in_got)
    in_chips = direct(in_piece, chips) if plane else along(in_piece, bits)
    raw_half = arrange(info, [raw, raw_far], 1)
    raw_far = swap(raw_half, "narrow", 1)
    low = lax.ppermute(first, ("wide", "narrow"), spread_perm(0))
    up_pair = arrange(info, [up_keep, up_far], 0, 0)
    low, raw_far, up_pair, second = together(low, raw_far, up_pair, second)

    up_far = swap(up_pair, "narrow", 2)
    high = lax.ppermute(second, ("wide", "narrow"), spread_perm(1))
    if plane:
        raw_far, *in_chips = together(settle(info, raw_half, raw_far), *in_chips)
        down_chips = cross_one(raw_far)
    else:
        down_chips = along(place_axis(arrange(info, [raw_half, raw_far])), bits)
    high, up_far = together(high, up_far)

    up_half = arrange(info, [up_pair, up_far], 1)
    up_far = swap(up_half, "narrow", 1)
    low_far, high_far = swap(low, "wide", 1), swap(high, "wide", 1)
    low_far, high_far, cotangent = together(low_far, high_far, cotangent)
    token_blocks = [low, high, low_far, high_far]
    cot_first, cot_second = pick_turns(info, cotangent)
    cot_low = lax.ppermute(cot_first, ("wide", "narrow"), spread_perm(0))
    in_blocks = by_chip(in_chips)
    q, k, v, start, normed, in_full, turned, seg, spots = front(
        info, token_blocks, in_blocks, patches
    )
    q, k, v, seg, cot_second, up_far, *down_chips = together(
        q, k, v, seg, cot_second, up_far, *down_chips
    )

    up_chips = cross_one(place_axis(arrange(info, [up_half, up_far])))
    cot_high = lax.ppermute(cot_second, ("wide", "narrow"), spread_perm(1))
    if plane:
        down_chips = cross_two(down_chips)
    att, total = attend(info, q, k, v, seg)
    count = len(down_chips)
    att, cot_low, cot_high, *rest = together(att, cot_low, cot_high, *down_chips, *up_chips)
    down_chips, up_chips = rest[:count], rest[count:]

    att_far = swap(att, "wide", 1)
    if plane:
        out_rows = last_blocks(info, *down_chips[:3], down_chips[4])
        out_weights = [out_rows, swap(out_rows, "wide", 1)]
    else:
        out_weights = [lax.all_gather(output_weight, ("wide", "narrow"), axis=0, tiled=True)]
    if plane:
        up_chips = cross_two(up_chips)
    cots = [cot_low, cot_high, swap(cot_low, "wide", 1), swap(cot_high, "wide", 1)]
    if plane:
        up_blocks = [part.reshape((-1,) + part.shape[-1:]) for part in up_chips]
        down_blocks = down_chips
    else:
        up_blocks = by_chip(up_chips)
        down_blocks = [by_chip(down_chips)[0].reshape(4 * PLACES, -1, width)]
    middle, normed_two, up_bias_own, out_full = middle_front(
        info, att, att_far, start, turned, out_weights, own_hidden, patches, chips
    )
    keep, send, slope, up_full, down_full, cot, *down_grads = feed_front(
        info, normed_two, up_bias_own, cots, up_blocks, down_blocks, blocks
    )
    down_rows = own_hidden // (chips * PLACES)
    down_fold = folded(down_grads, (PLACES, down_rows, width))
    fed = feed_back(info, slope, cot, up_full, down_full, chips)
    back, back_low, grad_hidden, bias_grad, send, normed_two = crossed(
        [down_fold], *fed, send, normed_two
    )
    back_far = swap(back_low, "wide", 1)
    out_far = swap(send, "wide", 1)
    up_grads = weight_grad(info, normed_two, [grad_hidden], blocks)
    back_far, out_far, *up_grads = arrived([down_fold], back_far, out_far, *up_grads)
    up_fold = folded(up_grads, (2, PLACES, rows, own_hidden))
    down_keep, down_send = split(info, [down_fold], (2, 2, down_rows))
    down_got = swap(down_send, "narrow", 1)
    grad_middle, grad_att, out_keep, out_send, sums = middle_back(
        info, back, back_far, middle, turned, att, out_full, cot, patches, blocks
    )
    out_far, grad_att = together(out_far, grad_att)
    out_turns = output_turns(info, middle, keep, out_far, turned, patches)
    out_turns = [unspread_turn(part, turn) for turn, part in enumerate(out_turns)]
    if blocks == 1:
        shape = (chips // 2, 2, PLACES * rows, width)
        out_keep = pick(out_keep.reshape(shape), core, 1)
        out_send = pick(out_send.reshape(shape), 1 - core, 1)
    grad_att, down_got = crossed([up_fold], grad_att, down_got)
    dq, dk, dv = attend_back(info, q, k, v, att, grad_att, total, seg)
    dq, dk, dv, out_send, normed, *out_turns = arrived(
        [up_fold], dq, dk, dv, out_send, normed, *out_turns
    )
    start_keep, start_send = project_back(info, dq, dk, dv, in_full)
    start_far, out_got = swap(start_send, "wide", 1), swap(out_send, "wide", 1)
    down_keep, down_send = split(info, [[down_keep, down_got]], (2, down_rows), 1)
    up_keep, up_send = split(info, [up_fold], (2, 2, 2, rows))
    start_far, out_got, up_send, down_send = together(start_far, out_got, up_send, down_send)
    up_got = swap(up_send, "narrow", 1)
    down_got = swap(down_send, "narrow", 2)
    args = [start_keep, start_far, start, grad_middle, turned, sums, bias_grad, spots, dq, dv]
    started = start_back(info, blocks, args + [out_keep, out_got], patches, spare)
    if not plane:
        out_grad = jnp.where(
            first_core,
            jnp.concatenate([out_keep, out_got]),
            jnp.concatenate([out_got, out_keep]),
        ).reshape(chips, PLACES, rows, 2, part)
        out_grad = jnp.transpose(out_grad, (0, 3, 1, 2, 4)).reshape(width, part)
        started = [started[0], jnp.concatenate([started[1], out_grad], axis=1)]
    normed, grad_blocks, *small_grads = together(normed, *started)
    small_fold = folded(small_grads, (2, PLACES, rows, SMALL + part))
    grad_first, grad_second = pick_turns(info, grad_blocks.reshape(2, block, width))
    grad_first = unspread_turn(grad_first, 0)
    in_grads = weight_grad(info, normed, [dq, dk, dv], blocks)
    up_got, down_got, *in_grads = crossed([small_fold], up_got, down_got, *in_grads)
    in_fold = folded(in_grads, (2, PLACES, rows, 3 * part))
    up_keep, up_send = split(info, [[up_keep, up_got]], (2, 2, rows), 1)
    grad_first, grad_second, up_send = crossed(
        [in_fold], *arrived([small_fold], grad_first, grad_second, up_send)
    )
    grad_second = unspread_turn(grad_second, 1)
    up_got = swap(up_send, "narrow", 2)
    (down_keep,) = arrived([in_fold], down_keep)
    in_cut = split(info, [in_fold, small_fold], (2, PLACES, rows))
    in_got = [swap(in_cut[index], "narrow", index) for index in range(1, PLACES)]
    in_keep, down_keep, up_keep, up_got, grad_first, grad_second, *out_turns = together(
        in_cut[0], down_keep, up_keep, up_got, grad_first, grad_second, *out_turns
    )
    outputs = unspread_join(out_turns, place)
    grad_tokens = unspread_join([grad_first, grad_second], place)
    down_share = down_keep + down_got.astype(f32)
    up_total = up_keep + up_got.astype(f32)
    up_keep = pick(up_total, core)
    up_got = swap(pick(up_total, 1 - core).astype(bf16), "wide", 1).astype(f32)
    up_both = [up_keep.reshape(rows, chips, 1, -1), up_got.reshape(rows, chips, 1, -1)]
    up_share = jnp.where(
        first_core, jnp.concatenate(up_both, axis=2), jnp.concatenate(up_both[::-1], axis=2)
    ).reshape(rows, hidden)
    outputs, grad_tokens, down_share, up_share, *in_got = together(
        outputs, grad_tokens, down_share, up_share, *in_got
    )
    in_total = in_keep
    for array in in_got:
        in_total = in_total + array.astype(f32)
    sent_columns = 3 * part + SMALL
    in_keep = pick(in_total, core)
    in_far = pick(in_total, 1 - core)[:, :sent_columns].astype(bf16)
    in_far = swap(in_far, "wide", 1).astype(f32)
    in_both = [in_keep[:, : 3 * part].reshape(rows, 3, 1, part), in_far[:, : 3 * part].reshape(rows, 3, 1, part)]
    in_share = jnp.where(
        first_core, jnp.concatenate(in_both, axis=2), jnp.concatenate(in_both[::-1], axis=2)
    ).reshape(rows, 3 * width)
    small_share = in_keep[:, 3 * part : sent_columns] + in_far[:, 3 * part :]
    out_share = jnp.concatenate([in_total[0, :, sent_columns:], in_total[1, :, sent_columns:]], axis=1)
    tail = [small_share[:, patches + i] for i in range(8)]
    return (
        outputs,
        grad_tokens,
        small_share[:, :patches],
        in_share,
        tail[QUERY_BIAS],
        tail[VALUE_BIAS],
        out_share,
        tail[OUTPUT_BIAS],
        tail[GAIN_ONE],
        tail[SHIFT_ONE],
        up_share,
        small_share[:, patches + 8 : patches + 8 + spare].T.reshape(-1),
        down_share,
        tail[DOWN_BIAS],
        tail[GAIN_TWO],
        tail[SHIFT_TWO],
    )


def solution(mesh):
    both = ("wide", "narrow")
    matrix = P(both, None)
    vector = P(both)
    block = P("wide", "narrow", None)
    gains = [matrix, matrix] + [vector] * 2 + [matrix] + [vector] * 3 + [matrix, vector, matrix]
    gains += [vector] * 3
    return jax.shard_map(
        local,
        mesh=mesh,
        in_specs=tuple([block, P("wide", "narrow"), P("wide", None)] + gains + [block]),
        out_specs=tuple([block, block] + gains),
        check_vma=False,
    )
```

```python
import functools

import jax
import jax.numpy as jnp
from jax import lax
from jax.experimental import pallas as pl
from jax.experimental.pallas import tpu as pltpu
from jax.sharding import PartitionSpec as P

HEADS = 12
PLACES = 4
epsilon = 1e-05
masked_score = -1e30

f32 = jnp.float32
bf16 = jnp.bfloat16
MIB = 1 << 20
LOAD, HELD = "load", "held"
QUERY_BIAS, VALUE_BIAS, OUTPUT_BIAS, GAIN_ONE, SHIFT_ONE, DOWN_BIAS, GAIN_TWO, SHIFT_TWO = range(8)
SMALL = 128


def dot(left, right):
    return jnp.dot(left, right, preferred_element_type=f32)


def dot_left(left, right):
    return lax.dot_general(left, right, (((0,), (0,)), ((), ())), preferred_element_type=f32)


def dot_right(left, right):
    return lax.dot_general(left, right, (((1,), (1,)), ((), ())), preferred_element_type=f32)


def call(kernel, outs, ins, args, scratch=(), grid=None, limit=14, cost=None):
    loads = []
    specs = [pl.BlockSpec(memory_space=pltpu.SMEM)]
    for index, (spec, array) in enumerate(zip(ins, args[1:], strict=True)):
        if spec == LOAD:
            whole = False
            spec = pl.BlockSpec(memory_space=pl.ANY if whole else pltpu.VMEM)
            if whole:
                loads.append(index)
        elif spec == HELD:
            spec = pl.BlockSpec(memory_space=pl.ANY)
        specs.append(spec)
    count, news = len(ins), len(loads)

    def loaded(info, *refs):
        refs, held, sem = list(refs[: -1 - news]), refs[-1 - news : -1], refs[-1]
        copies = []
        for i, index in enumerate(loads):
            copies.append(pltpu.make_async_copy(refs[index], held[i], sem.at[i]))
            refs[index] = held[i]
        run_copies(copies)
        kernel(info, *refs)

    extra = [pltpu.VMEM(args[1 + i].shape, args[1 + i].dtype) for i in loads]
    if loads:
        extra.append(pltpu.SemaphoreType.DMA((news,)))
    return pl.pallas_call(
        loaded if loads else kernel,
        out_shape=[shape for shape, _ in outs],
        in_specs=specs,
        out_specs=[spec for _, spec in outs],
        scratch_shapes=list(scratch) + extra,
        **({"grid": grid} if grid else {}),
        compiler_params=pltpu.CompilerParams(vmem_limit_bytes=limit * MIB),
        cost_estimate=pl.CostEstimate(
            flops=int(cost[0]), bytes_accessed=int(cost[1]), transcendentals=0
        ),
    )(*args)


def shaped(shape, kind):
    return jax.ShapeDtypeStruct(shape, kind)


def vmem():
    return pl.BlockSpec(memory_space=pltpu.VMEM)


def anywhere():
    return pl.BlockSpec(memory_space=pl.ANY)


def normalise(values):
    average = jnp.mean(values, axis=-1, keepdims=True)
    centered = values - average
    variance = jnp.mean(centered * centered, axis=-1, keepdims=True)
    scale = lax.rsqrt(variance + epsilon)
    return centered * scale, scale


def norm_back(normal, scale, gain, grad):
    inner = grad * gain
    return scale * (
        inner
        - jnp.mean(inner, axis=-1, keepdims=True)
        - normal * jnp.mean(inner * normal, axis=-1, keepdims=True)
    )


def fold_shapes(rows, rest):
    return [shaped((count,) + rest, bf16) for count in (rows, rows, rows, rows // 2, rows // 2)]


def fold_copies(held, outs, chip, sem):
    rows = outs[0].shape[0]
    half = rows // 2
    at = lambda distance, second: pl.ds(
        pl.multiple_of((distance ^ chip) * rows + second * half, half), half
    )
    whole = pl.ds(pl.multiple_of(chip * rows, rows), rows)
    first, second = pl.ds(0, half), pl.ds(half, half)
    own, to_x, to_y, y_left, x_left = outs
    pairs = [
        (0, held.at[whole], own),
        (3, held.at[at(3, 0)], to_x.at[first]),
        (1, held.at[at(1, 0)], to_x.at[second]),
        (3, held.at[at(3, 1)], to_y.at[first]),
        (2, held.at[at(2, 1)], to_y.at[second]),
        (2, held.at[at(2, 0)], y_left),
        (1, held.at[at(1, 1)], x_left),
    ]
    return [
        (pltpu.make_async_copy(a, b, sem.at[i]), distance)
        for i, (distance, a, b) in enumerate(pairs)
    ]


def run_copies(copies):
    for copy in copies:
        copy.start()
    for copy in copies:
        copy.wait()


def pack_in_kernel(patches, info, weight, table, rows_in, keep, send):
    core = info[0]
    part = weight.shape[1] // 6
    turned = rows_in[...].astype(f32).T
    empty = jnp.zeros((weight.shape[0], SMALL - patches - turned.shape[1]), f32)
    small = jnp.concatenate([table[...].astype(f32), turned, empty], axis=1).astype(bf16)
    for ref, side in ((keep, core), (send, 1 - core)):
        for i in range(3):
            there = pl.ds(pl.multiple_of((2 * i + side) * part, 128), part)
            ref[:, i * part : (i + 1) * part] = weight[:, there]
        ref[:, 3 * part :] = small


def pack_in(info, weight, table, rows_in):
    rows, columns = weight.shape[0], weight.shape[1] // 2 + SMALL
    return call(
        functools.partial(pack_in_kernel, table.shape[1]),
        [(shaped((rows, columns), bf16), vmem())] * 2,
        [vmem()] * 3,
        [info, weight, table, rows_in],
        limit=8,
        cost=(0, MIB),
    )


def pack_up_kernel(info, up, keep, send):
    step = keep.shape[1] // 4
    for ref, side in ((keep, info[0]), (send, 1 - info[0])):
        for q in range(4):
            there = pl.ds(pl.multiple_of((2 * q + side) * step, 128), step)
            ref[:, q * step : (q + 1) * step] = up[:, there]


def pack_up(info, up):
    out = (shaped((up.shape[0], up.shape[1] // 2), bf16), vmem())
    return call(pack_up_kernel, [out] * 2, [vmem()], [info, up], limit=8, cost=(0, MIB))


def sent_kernel(info, tokens, positions, segments, first, second, extra):
    place = info[2]
    block, width = tokens.shape[1], tokens.shape[2]
    full = segments.shape[1]
    extra[...] = jnp.zeros_like(extra)
    for k, out in enumerate((first, second)):
        index = k ^ (place % 2)
        row = segments[pl.ds(index, 1), :]
        row = (row - row[:, 0:1]).astype(f32)
        extra[0:1, :block] = positions[pl.ds(index, 1), :].astype(f32)
        extra[1:2, :] = row[:, :width]
        extra[2:3, : full - width] = row[:, width:]
        out[:block, :] = tokens[index]
        out[block:, :] = extra[...].astype(bf16)


def sent(info, tokens, positions, segments):
    _, block, width = tokens.shape
    one = (shaped((block + 16, width), bf16), vmem())
    return call(
        sent_kernel,
        [one, one],
        [vmem()] * 3,
        [info, tokens, positions, segments],
        scratch=[pltpu.VMEM((16, width), f32)],
        limit=8,
        cost=(0, 2 * MIB),
    )


def arrange_kernel(slot, shift, info, *refs):
    ins, out = refs[:-1], refs[-1]
    lead = len(out.shape) - 3
    place = lax.rem(info[slot] >> shift, len(ins))
    for k, ref in enumerate(ins):
        out[(slice(None),) * lead + (k ^ place,)] = ref[...]


def arrange(info, pieces, shift=0, slot=2):
    shape = pieces[0].shape
    shape = shape[:-2] + (len(pieces),) + shape[-2:]
    total = 1
    for extent in shape:
        total *= extent
    return call(
        functools.partial(arrange_kernel, slot, shift),
        [(shaped(shape, bf16), vmem())],
        [vmem()] * len(pieces),
        [info] + list(pieces),
        limit=8,
        cost=(0, 4 * total),
    )[0]


def settle_kernel(info, own, far, out):
    odd = lax.rem(info[2], 2)
    block = out.shape[1]
    rows = own.shape[1] - block
    for k, ref in enumerate((own, far)):
        for high in range(2):
            out[2 * high + (k ^ odd)] = ref[high, :block, :]
    both = (own, far)
    for high in range(2):
        pair = [ref[high, block:, :].astype(f32) for ref in both]
        for low in range(2):
            row = jnp.where(odd == low, pair[0], pair[1]).astype(bf16)
            begin = (2 * high + low) * rows
            out[PLACES, begin : begin + rows, :] = row


def settle(info, own, far):
    _, rows, width = own.shape
    block = rows * PLACES // (PLACES + 1)
    return call(
        settle_kernel,
        [(shaped((PLACES + 1, block, width), bf16), vmem())],
        [vmem()] * 2,
        [info, own, far],
        limit=8,
        cost=(0, 2 * MIB),
    )[0]


def last_kernel(info, own, x, y, d, out):
    for distance, ref in enumerate((own, x, y, d)):
        out[distance ^ info[1]] = ref[ref.shape[0] - 1]


def last_blocks(info, own, x, y, d):
    return call(
        last_kernel,
        [(shaped((4,) + own.shape[1:], bf16), vmem())],
        [vmem()] * 4,
        [info, own, x, y, d],
        limit=8,
        cost=(0, MIB),
    )[0]


def cut_kernel(info, x, y, first, second):
    half = first.shape[0]
    first[...] = y[:half]
    second[...] = x[half:]


def cut(info, x, y):
    half = x.shape[0] // 2
    outs = [
        (shaped((half,) + x.shape[1:], bf16), vmem()),
        (shaped((x.shape[0] - half,) + x.shape[1:], bf16), vmem()),
    ]
    return call(cut_kernel, outs, [LOAD] * 2, [info, x, y], limit=8, cost=(0, MIB))


def add_kernel(info, *refs):
    for i in range(0, len(refs), 3):
        a, b, out = refs[i : i + 3]
        out[...] = (a[...].astype(f32) + b[: out.shape[0]].astype(f32)).astype(bf16)


def add_firsts(info, pairs):
    def kernel(info, *refs):
        outs = refs[2 * len(pairs) :]
        add_kernel(info, *[ref for i, out in enumerate(outs) for ref in (*refs[2 * i : 2 * i + 2], out)])

    return call(
        kernel,
        [(shaped(a.shape, bf16), vmem()) for a, _ in pairs],
        [LOAD] * (2 * len(pairs)),
        [info] + [array for pair in pairs for array in pair],
        limit=8,
        cost=(0, MIB),
    )


def pick_kernel(info, blocks, first, second):
    odd = lax.rem(info[2], 2)
    first[...] = blocks[odd]
    second[...] = blocks[1 - odd]


def pick_turns(info, blocks):
    out = (shaped(blocks.shape[1:], bf16), vmem())
    return call(pick_kernel, [out] * 2, [LOAD], [info, blocks], limit=8, cost=(0, MIB))


def output_kernel(patches, info, middle, keep, far, turned, first, second):
    core, odd = info[0], lax.rem(info[2], 2)
    half = keep.shape[0]
    block = half // 2
    bias = turned[patches + DOWN_BIAS : patches + DOWN_BIAS + 1, :]
    for ref, which in ((first, odd), (second, 1 - odd)):
        here = pl.ds(pl.multiple_of(which * block, block), block)
        there = pl.ds(pl.multiple_of(core * half + which * block, block), block)
        ref[...] = (middle[there, :] + keep[here, :] + far[here, :].astype(f32) + bias).astype(bf16)


def output_turns(info, middle, keep, far, turned, patches):
    out = (shaped((keep.shape[0] // 2, keep.shape[1]), bf16), vmem())
    return call(
        functools.partial(output_kernel, patches),
        [out] * 2,
        [LOAD] * 4,
        [info, middle, keep, far, turned],
        limit=8,
        cost=(0, 6 * MIB),
    )


def front_kernel(blocks, patches, info, *refs):
    tokens_in, refs = refs[:4], refs[4:]
    weights_in, refs = refs[:blocks], refs[blocks:]
    q_out, k_out, v_out, start_out, normed_out, weight, turned_out, seg_out, spot_out = refs[:9]
    held, sem, weight_sem = refs[9:]
    core, chip, place = info[0], info[1], info[2]
    block, columns = held.shape[1] - 16, weight.shape[1] - SMALL
    part = columns // 3
    copies = []
    for i in range(4):
        side = core if i < 2 else 1 - core
        there = 2 * side + ((i % 2) ^ (place % 2))
        copies.append(pltpu.make_async_copy(tokens_in[i], held.at[there], sem.at[i]))
    copies += piece_copies(weights_in, weight, info, weight_sem)
    run_copies(copies)
    small = weight[:, columns:]
    turned_out[...] = small.astype(f32).T
    vector = lambda i: turned_out[patches + i : patches + i + 1, :]
    half = pl.ds(pl.multiple_of(core * part, 128), part)
    query_bias = turned_out[patches + QUERY_BIAS : patches + QUERY_BIAS + 1, half]
    value_bias = turned_out[patches + VALUE_BIAS : patches + VALUE_BIAS + 1, half]
    gain, shift = vector(GAIN_ONE), vector(SHIFT_ONE)
    extra = held[0, block : block + 16, :].astype(f32)
    width = extra.shape[1]
    segment = jnp.concatenate([extra[1:2, :], extra[2:3, : 4 * block - width]], axis=1)
    seg_out[...] = jnp.broadcast_to(segment, seg_out.shape)
    ids = lax.broadcasted_iota(jnp.int32, (SMALL, block), 0).astype(f32)
    for b in range(4):
        here = slice(b * block, (b + 1) * block)
        spot = held[b, block : block + 16, :].astype(f32)[0:1, :block]
        spot_out[:, here] = jnp.broadcast_to(spot, (8, block))
        one_hot = jnp.where(ids == spot, 1.0, 0.0).astype(bf16)
        embedded = lax.dot_general(
            one_hot, small, (((0,), (1,)), ((), ())), preferred_element_type=f32
        )
        start = held[b, :block, :].astype(f32) + embedded
        start_out[here, :] = start
        normal, _ = normalise(start)
        normed = (normal * gain + shift).astype(bf16)
        normed_out[here, :] = normed
        projected = dot(normed, weight[:, :columns])
        query = (projected[:, :part] + query_bias).astype(bf16).astype(f32) * 0.125
        q_out[here, :] = query.astype(bf16)
        k_out[here, :] = projected[:, part : 2 * part].astype(bf16)
        v_out[here, :] = (projected[:, 2 * part :] + value_bias).astype(bf16)


def front(info, tokens, weights, patches):
    blocks = len(weights)
    block, width = tokens[0].shape[0] - 16, tokens[0].shape[1]
    columns = weights[0].shape[1]
    part = (columns - SMALL) // 3
    rows = 4 * block
    return call(
        functools.partial(front_kernel, blocks, patches),
        [
            (shaped((rows, part), bf16), vmem()),
            (shaped((rows, part), bf16), vmem()),
            (shaped((rows, part), bf16), vmem()),
            (shaped((rows, width), f32), vmem()),
            (shaped((rows, width), bf16), vmem()),
            (shaped((width, columns), bf16), vmem()),
            (shaped((SMALL, width), f32), vmem()),
            (shaped((8, rows), f32), vmem()),
            (shaped((8, rows), f32), vmem()),
        ],
        [HELD] * (4 + blocks),
        [info] + list(tokens) + list(weights),
        scratch=[
            pltpu.VMEM((4, block + 16, width), bf16),
            pltpu.SemaphoreType.DMA((4,)),
            pltpu.SemaphoreType.DMA((blocks,)),
        ],
        cost=(2 * rows * width * columns, 12 * MIB),
    )


def fill_bias(bias, seg):
    block = bias.shape[1]
    wide = seg[...]
    tall = jnp.broadcast_to(wide[0:1, :], (128, wide.shape[1])).T[:, 0:1]
    base = 0
    for b in range(4):
        many = (b + 1) * block
        key = lax.broadcasted_iota(jnp.int32, (many, block), 0)
        ask = lax.broadcasted_iota(jnp.int32, (many, block), 1) + b * block
        same = tall[:many] == wide[0:1, b * block : (b + 1) * block]
        bias[base : base + many, :] = jnp.where((key <= ask) & same, 0.0, masked_score)
        base += many


def turn(values):
    return values.astype(f32).T.astype(bf16)


def attend_kernel(info, q, k, v, seg, out, total, bias):
    block = bias.shape[1]

    @pl.when(pl.program_id(0) == 0)
    def _():
        fill_bias(bias, seg)

    turned_q, turned_v = turn(q[...]), turn(v[...])
    side = lax.broadcasted_iota(jnp.int32, (128, block), 0) // 64
    base = 0
    for b in range(4):
        many = (b + 1) * block
        here = slice(b * block, (b + 1) * block)
        mixed = []
        for h in range(2):
            ask = jnp.where(side == h, turned_q[:, here].astype(f32), 0.0).astype(bf16)
            scores = dot(k[:many, :], ask) + bias[base : base + many, :]
            top = jnp.max(scores, axis=0, keepdims=True)
            raised = jnp.exp(scores - top)
            mass = jnp.sum(raised, axis=0, keepdims=True)
            total[0, h : h + 1, here] = top + jnp.log(mass)
            part = dot(turned_v[64 * h : 64 * h + 64, :many], raised.astype(bf16))
            mixed.append(part * (1.0 / mass))
        out[here, :] = jnp.concatenate(mixed, axis=0).T.astype(bf16)
        base += many


def attend(info, q, k, v, seg):
    rows, part = q.shape
    pairs = part // 128
    column = pl.BlockSpec((rows, 128), lambda i: (0, i))
    whole = pl.BlockSpec(seg.shape, lambda i: (0, 0))
    return call(
        attend_kernel,
        [
            (shaped((rows, part), bf16), column),
            (shaped((pairs, 8, rows), f32), pl.BlockSpec((1, 8, rows), lambda i: (i, 0, 0))),
        ],
        [column, column, column, whole],
        [info, q, k, v, seg],
        scratch=[pltpu.VMEM((10 * rows // 4, rows // 4), f32)],
        grid=(pairs,),
        cost=(6 * rows * rows * part, 4 * MIB),
    )


def attend_back_kernel(info, q, k, v, o, g, total, seg, dq, dk, dv, bias, dk_sum, dv_sum):
    block = bias.shape[1]

    @pl.when(pl.program_id(0) == 0)
    def _():
        fill_bias(bias, seg)

    wide_g = g[...].astype(f32).T
    product = wide_g * o[...].astype(f32).T
    inner = [jnp.sum(product[64 * h : 64 * h + 64], axis=0, keepdims=True) for h in range(2)]
    turned_q, turned_k = turn(q[...]), turn(k[...])
    turned_g = wide_g.astype(bf16)
    side = lax.broadcasted_iota(jnp.int32, (128, block), 0) // 64
    flat = lax.broadcasted_iota(jnp.int32, (block, 128), 1) // 64
    dk_sum[...] = jnp.zeros_like(dk_sum)
    dv_sum[...] = jnp.zeros_like(dv_sum)
    base = 0
    for b in range(4):
        many = (b + 1) * block
        here = slice(b * block, (b + 1) * block)
        low_probs, low_scores, own_qs, own_gs = [], [], [], []
        for h in range(2):
            ask = jnp.where(side == h, turned_q[:, here].astype(f32), 0.0).astype(bf16)
            ask_g = jnp.where(side == h, turned_g[:, here].astype(f32), 0.0).astype(bf16)
            scores = dot(k[:many, :], ask) + bias[base : base + many, :]
            probs = jnp.exp(scores - total[0, h : h + 1, here])
            grad_probs = dot(v[:many, :], ask_g)
            grad_scores = (probs * (grad_probs - inner[h][:, here])).astype(bf16)
            own_qs.append(jnp.where(flat == h, q[here, :].astype(f32), 0.0).astype(bf16))
            own_gs.append(jnp.where(flat == h, g[here, :].astype(f32), 0.0).astype(bf16))
            low_probs.append(probs.astype(bf16))
            low_scores.append(grad_scores)
        dv_sum[:many, :] += dot(jnp.concatenate(low_probs, axis=1), jnp.concatenate(own_gs))
        dk_sum[:many, :] += dot(jnp.concatenate(low_scores, axis=1), jnp.concatenate(own_qs))
        both = dot(turned_k[:, :many], jnp.concatenate(low_scores, axis=1))
        half = both.shape[1] // 2
        mixed = jnp.concatenate([both[:64, :half], both[64:, half:]], axis=0)
        dq[here, :] = (mixed.T * 0.125).astype(bf16)
        base += many
    dk[...] = dk_sum[...].astype(bf16)
    dv[...] = dv_sum[...].astype(bf16)


def attend_back(info, q, k, v, o, g, total, seg):
    rows, part = q.shape
    pairs = part // 128
    column = pl.BlockSpec((rows, 128), lambda i: (0, i))
    whole = pl.BlockSpec(seg.shape, lambda i: (0, 0))
    out = (shaped((rows, part), bf16), column)
    return call(
        attend_back_kernel,
        [out, out, out],
        [column] * 5 + [pl.BlockSpec((1, 8, rows), lambda i: (i, 0, 0)), whole],
        [info, q, k, v, o, g, total, seg],
        scratch=[
            pltpu.VMEM((10 * rows // 4, rows // 4), f32),
            pltpu.VMEM((rows, 128), f32),
            pltpu.VMEM((rows, 128), f32),
        ],
        grid=(pairs,),
        cost=(15 * rows * rows * part, 6 * MIB),
    )


def cotangent_copies(info, pieces, held, sems):
    core, place = info[0], info[2]
    copies = []
    for i in range(4):
        side = core if i < 2 else 1 - core
        there = 2 * side + ((i % 2) ^ (place % 2))
        copies.append(pltpu.make_async_copy(pieces[i], held.at[there], sems[i]))
    return copies


def gelu_parts(values):
    scale = 0.7978845608028654
    square = values * values
    slope = jnp.tanh(values * (scale + (scale * 0.044715) * square))
    half = 0.5 * (1.0 + slope)
    grad = half + 0.5 * values * (1.0 - slope * slope) * (
        scale + (3.0 * scale * 0.044715) * square
    )
    return values * half, grad


def piece_copies(pieces, target, info, sem, lanes=None):
    chip = info[1]
    rows = pieces[0].shape[0]
    copies, base = [], 0
    for i, ref in enumerate(pieces):
        distance = min(i, 3)
        begin = pl.multiple_of((distance ^ chip) * rows, rows)
        if i == 4:
            begin = pl.multiple_of(begin + rows // 2, rows // 2)
        source = ref if lanes is None else ref.at[:, lanes]
        there = target.at[pl.ds(begin, ref.shape[0])]
        copies.append(pltpu.make_async_copy(source, there, sem.at[i]))
    return copies


def block_copies(pieces, target, info, sem):
    if len(pieces) == 1:
        return [pltpu.make_async_copy(pieces[0], target, sem.at[0])]
    copies = []
    for i, ref in enumerate(pieces):
        begin = (min(i, 3) ^ info[1]) * PLACES + (2 if i == 4 else 0)
        count = 2 if i >= 3 else PLACES
        copies.append(
            pltpu.make_async_copy(ref.at[pl.ds(0, count)], target.at[pl.ds(begin, count)], sem.at[i])
        )
    return copies


def hidden_places(core, hidden, width, chips):
    spare = 2 * hidden // width
    share = hidden // chips
    device = share // PLACES
    rows = device // spare
    unit = lax.broadcasted_iota(jnp.int32, (hidden, 1), 0)
    rest = lax.rem(unit, share)
    row = ((2 * (unit // share) + core) * PLACES + rest // device) * rows + lax.rem(rest, rows)
    lane = lax.broadcasted_iota(jnp.int32, (hidden, width), 1)
    return jnp.where(lane == row, 1.0, 0.0).astype(bf16)


def hidden_turns(spare, hidden, chips):
    device = hidden // (chips * PLACES)
    unit = lax.broadcasted_iota(jnp.int32, (spare, hidden), 1)
    return lax.rem(unit, device) // (device // spare) == lax.broadcasted_iota(
        jnp.int32, (spare, hidden), 0
    )


def middle_kernel(patches, chips, hidden, info, att, att_far, start, turned, *refs):
    weights, refs = refs[:-4], refs[-4:]
    middle_out, normed_out, bias_out, weight_out = refs
    core = info[0]
    rows, width = start.shape
    part, tile = width // 2, rows // 4
    if len(weights) == 2:
        block = weights[0].shape[1]
        for side, ref in ((core, weights[0]), (1 - core, weights[1])):
            for q in range(4):
                begin = pl.multiple_of((2 * q + side) * block, block)
                weight_out[pl.ds(begin, block), :] = ref[q]
    else:
        weight_out[...] = weights[0][...]
    spare = 2 * hidden // width
    biases = turned[patches + 8 : patches + 8 + spare, :].astype(bf16)
    spread_out = dot_right(biases, hidden_places(core, hidden, width, chips))
    bias = jnp.sum(
        jnp.where(hidden_turns(spare, hidden, chips), spread_out, 0.0), axis=0, keepdims=True
    )
    bias_out[...] = jnp.broadcast_to(bias, bias_out.shape)
    vector = lambda i: turned[patches + i : patches + i + 1, :]
    own = pl.ds(pl.multiple_of(core * part, 128), part)
    far = pl.ds(pl.multiple_of((1 - core) * part, 128), part)
    gain, shift, out_bias = vector(GAIN_TWO), vector(SHIFT_TWO), vector(OUTPUT_BIAS)
    for t in range(4):
        here = slice(t * tile, (t + 1) * tile)
        mixed = dot(att[here, :], weight_out[own, :]) + dot(att_far[here, :], weight_out[far, :])
        middle = start[here, :] + mixed + out_bias
        middle_out[here, :] = middle
        normal, _ = normalise(middle)
        normed_out[here, :] = (normal * gain + shift).astype(bf16)


def middle_front(info, att, att_far, start, turned, weights, hidden, patches, chips):
    rows, width = start.shape
    return call(
        functools.partial(middle_kernel, patches, chips, hidden),
        [
            (shaped((rows, width), f32), vmem()),
            (shaped((rows, width), bf16), vmem()),
            (shaped((8, hidden), f32), vmem()),
            (shaped((width, width), bf16), vmem()),
        ],
        [LOAD] * (4 + len(weights)),
        [info, att, att_far, start, turned] + list(weights),
        cost=(2 * rows * width * width, 12 * MIB),
    )


def feed_front_kernel(ups, downs, blocks, info, normed, up_bias, *refs):
    cot_in, refs = refs[:4], refs[4:]
    up_in, refs = refs[:ups], refs[ups:]
    down_in, refs = refs[:downs], refs[downs:]
    keep_out, send_out, slope_out, up, down, cot, refs = *refs[:6], refs[6:]
    down_grads, (act, far_sum, down_grad, cot_sem, up_sem, down_sem) = refs[:-6], refs[-6:]
    core, chip = info[0], info[1]
    rows, width = normed.shape
    hidden = up.shape[1]
    chunk = hidden // 4
    half = rows // 2
    early = piece_copies(up_in, up, info, up_sem)
    late = block_copies(down_in, down, info, down_sem)
    late += cotangent_copies(info, cot_in, cot, [cot_sem.at[i] for i in range(4)])
    for copy in early + late:
        copy.start()
    for copy in early:
        copy.wait()
    own = pl.ds(pl.multiple_of(core * half, half), half)
    far = pl.ds(pl.multiple_of((1 - core) * half, half), half)
    outs = []
    pair = 2 * chunk
    for step, distances in enumerate(((3, 2), (1, 0))):
        which = (1 - step) ^ (chip // 2)
        lanes = pl.ds(pl.multiple_of(which * pair, 128), pair)
        blocks_here = pl.ds(pl.multiple_of(which * 2 * PLACES, 2 * PLACES), 2 * PLACES)
        for side, here in enumerate((own, far)):
            value, slope = gelu_parts(dot(normed[here, :], up[:, lanes]) + up_bias[0:1, lanes])
            value = value.astype(bf16)
            act[here, :] = value
            slope_out[here, lanes] = slope.astype(bf16)
            if step == 0 and side == 0:
                for copy in late:
                    copy.wait()
            part = dot(value, down[blocks_here].reshape(pair, width))
            if side == 0:
                keep_out[...] = part if step == 0 else keep_out[...] + part
            elif step == 0:
                far_sum[...] = part
            else:
                send_out[...] = (far_sum[...] + part).astype(bf16)
        grad = dot_left(act[...], cot[...].reshape(rows, width)).astype(bf16)
        down_grad[blocks_here] = grad.reshape(2 * PLACES, chunk // PLACES, width)
        if blocks == 4:
            ready = [
                copy
                for copy, where in fold_copies(down_grad, down_grads, chip, down_sem)
                if where in distances
            ]
            for copy in ready:
                copy.start()
            outs += ready
    if blocks != 4:
        outs.append(pltpu.make_async_copy(down_grad, down_grads[0], down_sem.at[0]))
        outs[0].start()
    for copy in outs:
        copy.wait()


def feed_front(info, normed, up_bias, cots, ups, downs, blocks):
    rows, width = normed.shape
    hidden = up_bias.shape[1]
    whole = (4 * PLACES, hidden // (4 * PLACES), width)
    grads = fold_shapes(PLACES, whole[1:]) if blocks == 4 else [shaped(whole, bf16)]
    return call(
        functools.partial(feed_front_kernel, len(ups), len(downs), blocks),
        [
            (shaped((rows // 2, width), f32), vmem()),
            (shaped((rows // 2, width), bf16), vmem()),
            (shaped((rows, hidden), bf16), vmem()),
            (shaped((width, hidden), bf16), vmem()),
            (shaped(whole, bf16), vmem()),
            (shaped((4, rows // 4, width), bf16), vmem()),
        ]
        + [(one, anywhere()) for one in grads],
        [LOAD] * 2 + [HELD] * (4 + len(ups) + len(downs)),
        [info, normed, up_bias] + list(cots) + list(ups) + list(downs),
        scratch=[
            pltpu.VMEM((rows, hidden // 2), bf16),
            pltpu.VMEM((rows // 2, width), f32),
            pltpu.VMEM(whole, bf16),
            pltpu.SemaphoreType.DMA((4,)),
            pltpu.SemaphoreType.DMA((len(ups),)),
            pltpu.SemaphoreType.DMA((8,)),
        ],
        limit=16,
        cost=(6 * rows * width * hidden, 24 * MIB),
    )


def feed_back_kernel(chips, info, slope, cot, up, down, back_out, low_out, grad_out, bias_out):
    rows, hidden = slope.shape
    width = up.shape[0]
    chunk = hidden // 2
    flat = cot[...].reshape(rows, width)
    sums = []
    for q in range(2):
        lanes = slice(q * chunk, (q + 1) * chunk)
        down_part = down[2 * q * PLACES : 2 * (q + 1) * PLACES].reshape(chunk, width)
        grad = (dot_right(flat, down_part) * slope[:, lanes].astype(f32)).astype(bf16)
        grad_out[:, lanes] = grad
        sums.append(jnp.sum(grad.astype(f32), axis=0, keepdims=True))
        back = dot_right(grad, up[:, lanes])
        if q == 0:
            back_out[...] = back
        else:
            back = back_out[...] + back
            back_out[...] = back
            low_out[...] = back.astype(bf16)
    spare = 2 * hidden // width
    turns = hidden_turns(spare, hidden, chips)
    biases = jnp.where(turns, jnp.concatenate(sums, axis=1), 0.0)
    high = biases.astype(bf16)
    both = jnp.concatenate([high.astype(f32), biases - high.astype(f32)]).astype(bf16)
    placed = dot(both, hidden_places(info[0], hidden, width, chips))
    bias_out[...] = jnp.zeros_like(bias_out)
    bias_out[:spare, :] = placed[:spare] + placed[spare:]


def feed_back(info, slope, cot, up, down, chips):
    rows, hidden = slope.shape
    width = up.shape[0]
    return call(
        functools.partial(feed_back_kernel, chips),
        [
            (shaped((rows, width), f32), vmem()),
            (shaped((rows, width), bf16), vmem()),
            (shaped((rows, hidden), bf16), vmem()),
            (shaped((8, width), f32), vmem()),
        ],
        [LOAD] * 4,
        [info, slope, cot, up, down],
        limit=12,
        cost=(4 * rows * width * hidden, 24 * MIB),
    )


def weight_kernel(blocks, count, info, left, *refs):
    parts, outs, held, sem = refs[:count], refs[count:-2], refs[-2], refs[-1]
    if count > 1:
        right = jnp.concatenate([ref[...] for ref in parts], axis=1)
        held[...] = dot_left(left[...], right).astype(bf16)
    else:
        for begin in range(0, held.shape[1], 768):
            lanes = slice(begin, begin + 768)
            held[:, lanes] = dot_left(left[...], parts[0][:, lanes]).astype(bf16)
    if blocks == 4:
        run_copies([copy for copy, _ in fold_copies(held, outs, info[1], sem)])
    else:
        run_copies([pltpu.make_async_copy(held, outs[0], sem.at[0])])


def weight_grad(info, left, parts, blocks):
    rows, width = left.shape
    columns = sum(part.shape[1] for part in parts)
    outs = [shaped((width, columns), bf16)]
    if blocks == 4:
        outs = fold_shapes(width // 4, (columns,))
    return call(
        functools.partial(weight_kernel, blocks, len(parts)),
        [(one, anywhere()) for one in outs],
        [LOAD] * (1 + len(parts)),
        [info, left] + list(parts),
        scratch=[pltpu.VMEM((width, columns), bf16), pltpu.SemaphoreType.DMA((8,))],
        cost=(2 * rows * width * columns, 8 * MIB),
    )


def middle_back_kernel(blocks, patches, info, back, back_far, middle, turned, att, weight, cot, *refs):
    grad_out, attended_out, keep_out, send_out, sums_out, branch = refs
    core = info[0]
    rows, width = middle.shape
    tile = rows // 4
    part = width // 2
    gain = turned[patches + GAIN_TWO : patches + GAIN_TWO + 1, :]
    own_rows = pl.ds(pl.multiple_of(core * part, 128), part)
    for t in range(4):
        here = slice(t * tile, (t + 1) * tile)
        grad_normed = back[here, :] + back_far[here, :].astype(f32)
        normal, scale = normalise(middle[here, :])
        grad_outputs = cot[t].astype(f32)
        grad = grad_outputs + norm_back(normal, scale, gain, grad_normed)
        low = grad.astype(bf16)
        branch[here, :] = low
        attended_out[here, :] = dot_right(low, weight[own_rows, :]).astype(bf16)

        @pl.when(core == t // 2)
        def _():
            grad_out[(t % 2) * tile : (t % 2 + 1) * tile, :] = grad
            sums = jnp.concatenate(
                [
                    jnp.sum(low.astype(f32), axis=0, keepdims=True),
                    jnp.sum(grad_outputs, axis=0, keepdims=True),
                    jnp.sum(grad_normed * normal, axis=0, keepdims=True),
                    jnp.sum(grad_normed, axis=0, keepdims=True),
                    jnp.zeros((4, width), f32),
                ],
                axis=0,
            )
            sums_out[...] = sums if t % 2 == 0 else sums_out[...] + sums

    weight_grad = dot_left(att[...], branch[...]).astype(bf16)
    shape = send_out.shape[:1] + (2,) + send_out.shape[1:]
    sorted_grad = weight_grad.reshape(shape) if blocks == 4 else None
    if blocks == 4:
        for c in range(2):

            @pl.when(core == c)
            def _():
                keep_out[...] = sorted_grad[:, c]
                send_out[...] = sorted_grad[:, 1 - c]

    else:
        keep_out[...] = weight_grad
        send_out[...] = weight_grad


def middle_back(info, back, back_far, middle, turned, att, weight, cot, patches, blocks):
    rows, width = middle.shape
    part = width // 2
    slab = (2, part // 4, width) if blocks == 4 else (part, width)
    return call(
        functools.partial(middle_back_kernel, blocks, patches),
        [
            (shaped((rows // 2, width), f32), vmem()),
            (shaped((rows, part), bf16), vmem()),
            (shaped(slab, bf16), vmem()),
            (shaped(slab, bf16), vmem()),
            (shaped((8, width), f32), vmem()),
        ],
        [LOAD] * 7,
        [info, back, back_far, middle, turned, att, weight, cot],
        scratch=[pltpu.VMEM((rows, width), bf16)],
        cost=(4 * rows * width * part, 14 * MIB),
    )


def project_kernel(info, dq, dk, dv, weight, keep_out, send_out):
    core = info[0]
    rows, part = dq.shape
    half_rows = rows // 2

    def product(first):
        here = pl.ds(pl.multiple_of(first, 128), half_rows)
        return (
            dot_right(dq[here, :], weight[:, :part])
            + dot_right(dk[here, :], weight[:, part : 2 * part])
            + dot_right(dv[here, :], weight[:, 2 * part : 3 * part])
        )

    send_out[...] = product((1 - core) * half_rows).astype(bf16)
    keep_out[...] = product(core * half_rows)


def project_back(info, dq, dk, dv, weight):
    rows, part = dq.shape
    width = weight.shape[0]
    return call(
        project_kernel,
        [
            (shaped((rows // 2, width), f32), vmem()),
            (shaped((rows // 2, width), bf16), vmem()),
        ],
        [LOAD] * 4,
        [info, dq, dk, dv, weight],
        cost=(6 * rows * width * part, 8 * MIB),
    )


def start_kernel(blocks, patches, spare, info, *refs):
    (keep, far, start, grad_middle, turned, sums, bias_grad, spots, dq, dv, out_keep, out_got) = refs[:12]
    refs = refs[12:]
    low_out, refs = refs[0], refs[1:]
    grads, refs = refs[:-3], refs[-3:]
    held, rows_held, sem = refs
    core, chip = info[0], info[1]
    rows, part = dq.shape
    half_rows, width = keep.shape
    up_rows = width // blocks
    gain = turned[patches + GAIN_ONE : patches + GAIN_ONE + 1, :]
    own = pl.ds(pl.multiple_of(core * half_rows, half_rows), half_rows)
    grad_normed = keep[...] + far[...].astype(f32)
    normal, scale = normalise(start[own, :])
    grad = grad_middle[...] + norm_back(normal, scale, gain, grad_normed)
    low = grad.astype(bf16)
    low_out[...] = low
    ids = lax.broadcasted_iota(jnp.int32, (SMALL, half_rows), 0).astype(f32)
    mine = spots[0:1, pl.ds(pl.multiple_of(core * half_rows, 128), half_rows)]
    one_hot = jnp.where(ids == mine, 1.0, 0.0).astype(bf16)
    rows_held[...] = dot(one_hot, low)
    half = pl.ds(pl.multiple_of(core * part, 128), part)
    rows_held[patches : patches + 8, :] = jnp.zeros((8, width), f32)

    def put(i, row):
        rows_held[patches + i : patches + i + 1, :] = row

    rows_held[patches + QUERY_BIAS : patches + QUERY_BIAS + 1, half] = jnp.sum(
        dq[...].astype(f32), axis=0, keepdims=True
    )
    rows_held[patches + VALUE_BIAS : patches + VALUE_BIAS + 1, half] = jnp.sum(
        dv[...].astype(f32), axis=0, keepdims=True
    )
    put(OUTPUT_BIAS, sums[0:1, :])
    put(DOWN_BIAS, sums[1:2, :])
    put(GAIN_TWO, sums[2:3, :])
    put(SHIFT_TWO, sums[3:4, :])
    put(GAIN_ONE, jnp.sum(grad_normed * normal, axis=0, keepdims=True))
    put(SHIFT_ONE, jnp.sum(grad_normed, axis=0, keepdims=True))
    rows_held[patches + 8 : patches + 8 + spare, :] = bias_grad[:spare, :]
    held[:, :SMALL] = rows_held[...].T.astype(bf16)
    if blocks == 4:
        slab = up_rows // 2
        for x in range(2):
            for side, ref in ((core, out_keep), (1 - core, out_got)):
                begin = pl.multiple_of((2 * side + x) * up_rows, up_rows)
                held[pl.ds(begin, slab), SMALL:] = ref[x, :, : width // 2]
                held[pl.ds(begin + slab, slab), SMALL:] = ref[x, :, width // 2 :]
    if blocks == 4:
        run_copies([copy for copy, _ in fold_copies(held, grads, chip, sem)])
    else:
        run_copies([pltpu.make_async_copy(held, grads[0], sem.at[0])])


def start_back(info, blocks, args, patches, spare):
    half_rows, width = args[0].shape
    columns = SMALL + width // 2 if blocks == 4 else SMALL
    outs = [shaped((width, columns), bf16)]
    if blocks == 4:
        outs = fold_shapes(width // 4, (columns,))
    return call(
        functools.partial(start_kernel, blocks, patches, spare),
        [(shaped((half_rows, width), bf16), vmem())]
        + [(one, anywhere()) for one in outs],
        [LOAD] * len(args),
        [info] + list(args),
        scratch=[
            pltpu.VMEM((width, columns), bf16),
            pltpu.VMEM((SMALL, width), f32),
            pltpu.SemaphoreType.DMA((8,)),
        ],
        cost=(2 * half_rows * width * SMALL, 10 * MIB),
    )


def split_kernel(plan, count, shift, info, *refs):
    place = lax.rem(info[2] >> shift, count)
    inputs, held = refs[: -1 - count], refs[-1]
    outs = refs[-1 - count : -1]
    column = 0
    for parts in plan:
        totals = []
        for terms in parts:
            total = 0.0
            for index, begin, rows in terms:
                total = total + inputs[index][begin : begin + rows, :].astype(f32)
            totals.append(total)
        whole = totals[0] if len(totals) == 1 else jnp.concatenate(totals)
        lanes = whole.shape[-1]
        held[..., column : column + lanes] = whole.reshape(held.shape[:-1] + (lanes,))
        column += lanes
    lead = (slice(None),) * (len(held.shape) - 3)
    for k in range(count):
        outs[k][...] = held[lead + (k ^ place,)].astype(outs[k].dtype)


def split(info, groups, shape, shift=0):
    arrays, plan, columns = [], [], 0
    for group in groups:
        base = len(arrays)
        parts = group.parts if isinstance(group, Fold) else [[(i, 0, None) for i in range(len(group))]]
        terms = group.terms if isinstance(group, Fold) else group
        flat = [array.reshape((-1,) + array.shape[-1:]) for array in terms]
        half = flat[0].shape[0] // 2
        plan.append(
            [
                [
                    (base + i, 0, flat[i].shape[0]) if begin is None else (base + i, begin * half, half)
                    for i, begin, _ in [(i, None if size is None else begin, size) for i, begin, size in part]
                ]
                for part in parts
            ]
        )
        arrays += flat
        columns += flat[0].shape[-1]
    count, total = shape[-2], columns
    for extent in shape:
        total *= extent
    one = shape[:-2] + (shape[-1], columns)
    return call(
        functools.partial(split_kernel, plan, count, shift),
        [(shaped(one, f32 if k == 0 else bf16), vmem()) for k in range(count)],
        [LOAD] * len(arrays),
        [info] + arrays,
        scratch=[pltpu.VMEM(shape + (columns,), f32)],
        limit=20,
        cost=(0, 8 * total),
    )


def swap(values, axis, bits):
    size = lax.axis_size(axis)
    return lax.ppermute(values, axis, [(i, i ^ bits) for i in range(size)])


def spread_perm(turn):
    pairs = []
    for w in range(lax.axis_size("wide")):
        for z in range(PLACES):
            there = (w - w % 2 + z // 2, 2 * (w % 2) + (turn ^ (z % 2)))
            pairs.append((w * PLACES + z, there[0] * PLACES + there[1]))
    return pairs


def unspread_turn(part, turn):
    return lax.ppermute(part, ("wide", "narrow"), [(b, a) for a, b in spread_perm(turn)])


def unspread_join(got, place):
    odd = (place % 2) == 1
    return jnp.stack([jnp.where(odd, got[1], got[0]), jnp.where(odd, got[0], got[1])])


def along(piece, bits):
    held = {0: piece}
    for bit in bits:
        held.update({index ^ (bit // 2): swap(part, "wide", bit) for index, part in list(held.items())})
    return [held[index] for index in range(len(held))]


def direct(piece, chips):
    return [piece] + [swap(piece, "wide", 2 * index) for index in range(1, chips)]


def fold(pieces, bits):
    held = dict(enumerate(pieces))
    for number, bit in enumerate(bits):
        step = bit // 2
        got = {i: swap(held[i ^ step], "wide", bit) for i in held if not i & step}
        if number == len(bits) - 1:
            return [held[0], got[0]]
        held = {i: (held[i].astype(f32) + got[i].astype(f32)).astype(bf16) for i in got}
    return [held[0]]


def after(values, *others):
    return lax.optimization_barrier((values,) + others)[0]


def together(*values):
    return lax.optimization_barrier(values)


class Fold:
    def __init__(self, outs, bits):
        self.outs, self.bits = list(outs), bits
        self.plane = len(outs) == 5
        if self.plane:
            self.near = [swap(outs[1], "wide", 2), swap(outs[2], "wide", 4)]

    def pairs(self):
        return [(self.outs[3], self.near[0]), (self.outs[4], self.near[1])] if self.plane else []

    def cross(self, sums):
        if self.plane:
            self.far = [swap(sums[0], "wide", 4), swap(sums[1], "wide", 2)]
            self.terms = [self.outs[0], *self.near, *self.far]
            first = [(0, 0, 1), (1, 1, 1), (3, 0, 1)]
            self.parts = [first, [(0, 1, 1), (2, 1, 1), (4, 0, 1)]]
        else:
            self.terms = fold(self.outs, self.bits)
            self.parts = [[(i, 0, None) for i in range(len(self.terms))]]


def local(
    tokens,
    positions,
    segments,
    position_table,
    input_weight,
    query_bias,
    value_bias,
    output_weight,
    output_bias,
    first_gain,
    first_shift,
    up_weight,
    up_bias,
    down_weight,
    down_bias,
    second_gain,
    second_shift,
    cotangent,
):
    size = lax.axis_size("wide")
    chips = size // 2
    bits = [2**i for i in range(1, size.bit_length() - 1)]
    seq_count, block, width = tokens.shape
    hidden = up_weight.shape[1]
    patches = position_table.shape[1]
    full = segments.shape[1]
    rows = width // (size * PLACES)
    part = width // 2
    own_hidden = hidden // 2
    wide, place = lax.axis_index("wide"), lax.axis_index("narrow")
    core, chip = wide % 2, wide // 2
    first_core = core == 0
    blocks = 4 if chips == 4 else 1
    info = jnp.stack([core, chip if blocks == 4 else 0 * chip, place, chip]).astype(jnp.int32)

    def pick(values, index, axis=0):
        return lax.dynamic_index_in_dim(values, index, axis, keepdims=False)

    def by_chip(pieces):
        flat = [piece.reshape((-1,) + piece.shape[-1:]) for piece in pieces]
        if blocks == 4:
            return flat
        whole = jnp.take(jnp.stack(flat), jnp.arange(chips) ^ chip, axis=0)
        return [whole.reshape((-1,) + flat[0].shape[1:])]

    def by_distance(outs, shape):
        if blocks == 4:
            return [out.reshape(shape) for out in outs]
        whole = outs[0].reshape((chips,) + shape)
        return [pick(whole, index ^ chip) for index in range(chips)]

    vectors = (
        query_bias,
        value_bias,
        output_bias,
        first_gain,
        first_shift,
        down_bias,
        second_gain,
        second_shift,
    )
    spare = up_bias.shape[0] // rows
    plane = blocks == 4
    up_sorted = up_weight
    if not plane:
        up_sorted = up_weight.reshape(rows, 4, chips // 4, 2, -1)
        up_sorted = jnp.swapaxes(up_sorted, 2, 3).reshape(rows, hidden)

    def cross_one(piece):
        if blocks == 4:
            return [piece, swap(piece, "wide", 2), swap(piece, "wide", 4)]
        return along(piece, bits)

    def cross_two(pieces):
        if blocks == 4:
            own, x, y = pieces
            first, second = cut(info, x, y)
            return [own, x, y, swap(first, "wide", 2), swap(second, "wide", 4)]
        return pieces

    def place_axis(piece):
        return piece.reshape(piece.shape[:-4] + (PLACES,) + piece.shape[-2:])

    def folded(outs, shape):
        if plane:
            return Fold(outs, bits)
        whole = outs[0].reshape((chips,) + shape)
        return Fold([pick(whole, index ^ chip) for index in range(chips)], bits)

    def crossed(folds, *values):
        count = len(values)
        near = [array for one in folds if one.plane for array in one.near]
        values = together(*values, *near)
        values, near = values[:count], list(values[count:])
        if plane:
            for one in folds:
                one.near, near = near[:2], near[2:]
            sums = add_firsts(info, [pair for one in folds for pair in one.pairs()])
        for i, one in enumerate(folds):
            one.cross(sums[2 * i : 2 * i + 2] if plane else None)
        return values

    def arrived(folds, *values):
        if not plane:
            return values
        count = len(values)
        far = [array for one in folds for array in one.far]
        values = together(*values, *far)
        values, far = values[:count], list(values[count:])
        for one in folds:
            one.far, far = far[:2], far[2:]
            one.terms = [*one.terms[:3], *one.far]
        return values

    rows_in = jnp.stack([*vectors, *(up_bias[i * rows : (i + 1) * rows] for i in range(spare))])
    in_keep, in_send = pack_in(info, input_weight, position_table, rows_in)
    in_far = swap(in_send, "wide", 1)
    raw_parts = together(down_weight, output_weight, up_sorted, tokens, in_keep)
    raw = jnp.concatenate(raw_parts[:2]) if plane else raw_parts[0]
    up_keep, up_send = pack_up(info, raw_parts[2])
    first, second = sent(info, raw_parts[3], positions, segments)
    in_far, raw, up_send = together(in_far, raw, up_send)

    in_pair = arrange(info, [in_keep, in_far], 0, 0)
    in_got = [in_pair] + [swap(in_pair, "narrow", k) for k in range(1, PLACES)]
    raw_far = swap(raw, "narrow", 2)
    up_far = swap(up_send, "wide", 1)
    up_far, raw_far, first, *in_got = together(up_far, raw_far, first, *in_got)

    in_piece = arrange(info, in_got)
    in_chips = direct(in_piece, chips) if plane else along(in_piece, bits)
    raw_half = arrange(info, [raw, raw_far], 1)
    raw_far = swap(raw_half, "narrow", 1)
    low = lax.ppermute(first, ("wide", "narrow"), spread_perm(0))
    up_pair = arrange(info, [up_keep, up_far], 0, 0)
    low, raw_far, up_pair, second = together(low, raw_far, up_pair, second)

    up_far = swap(up_pair, "narrow", 2)
    high = lax.ppermute(second, ("wide", "narrow"), spread_perm(1))
    if plane:
        raw_far, *in_chips = together(settle(info, raw_half, raw_far), *in_chips)
        down_chips = cross_one(raw_far)
    else:
        down_chips = along(place_axis(arrange(info, [raw_half, raw_far])), bits)
    high, up_far = together(high, up_far)

    up_half = arrange(info, [up_pair, up_far], 1)
    up_far = swap(up_half, "narrow", 1)
    low_far, high_far = swap(low, "wide", 1), swap(high, "wide", 1)
    low_far, high_far, cotangent = together(low_far, high_far, cotangent)
    token_blocks = [low, high, low_far, high_far]
    cot_first, cot_second = pick_turns(info, cotangent)
    cot_low = lax.ppermute(cot_first, ("wide", "narrow"), spread_perm(0))
    in_blocks = by_chip(in_chips)
    q, k, v, start, normed, in_full, turned, seg, spots = front(
        info, token_blocks, in_blocks, patches
    )
    q, k, v, seg, cot_second, up_far, *down_chips = together(
        q, k, v, seg, cot_second, up_far, *down_chips
    )

    up_chips = cross_one(place_axis(arrange(info, [up_half, up_far])))
    cot_high = lax.ppermute(cot_second, ("wide", "narrow"), spread_perm(1))
    if plane:
        down_chips = cross_two(down_chips)
    att, total = attend(info, q, k, v, seg)
    count = len(down_chips)
    att, cot_low, cot_high, *rest = together(att, cot_low, cot_high, *down_chips, *up_chips)
    down_chips, up_chips = rest[:count], rest[count:]

    if plane:
        up_own, up_x, up_y = up_chips
        up_first, up_second = cut(info, up_x, up_y)
        att, cot_low, cot_high, up_first, up_second, *down_chips = together(
            att, cot_low, cot_high, up_first, up_second, *down_chips
        )
        up_chips = [up_own, up_x, up_y, swap(up_first, "wide", 2), swap(up_second, "wide", 4)]
    att_far = swap(att, "wide", 1)
    if plane:
        out_rows = last_blocks(info, *down_chips[:3], down_chips[4])
        out_weights = [out_rows, swap(out_rows, "wide", 1)]
    else:
        out_weights = [lax.all_gather(output_weight, ("wide", "narrow"), axis=0, tiled=True)]
    cots = [cot_low, cot_high, swap(cot_low, "wide", 1), swap(cot_high, "wide", 1)]
    if plane:
        up_blocks = [part.reshape((-1,) + part.shape[-1:]) for part in up_chips]
        down_blocks = down_chips
    else:
        up_blocks = by_chip(up_chips)
        down_blocks = [by_chip(down_chips)[0].reshape(4 * PLACES, -1, width)]
    middle, normed_two, up_bias_own, out_full = middle_front(
        info, att, att_far, start, turned, out_weights, own_hidden, patches, chips
    )
    keep, send, slope, up_full, down_full, cot, *down_grads = feed_front(
        info, normed_two, up_bias_own, cots, up_blocks, down_blocks, blocks
    )
    down_rows = own_hidden // (chips * PLACES)
    down_fold = folded(down_grads, (PLACES, down_rows, width))
    fed = feed_back(info, slope, cot, up_full, down_full, chips)
    back, back_low, grad_hidden, bias_grad, send, normed_two = crossed(
        [down_fold], *fed, send, normed_two
    )
    back_far = swap(back_low, "wide", 1)
    out_far = swap(send, "wide", 1)
    up_grads = weight_grad(info, normed_two, [grad_hidden], blocks)
    back_far, out_far, *up_grads = arrived([down_fold], back_far, out_far, *up_grads)
    up_fold = folded(up_grads, (2, PLACES, rows, own_hidden))
    down_keep, down_send = split(info, [down_fold], (2, 2, down_rows))
    down_got = swap(down_send, "narrow", 1)
    grad_middle, grad_att, out_keep, out_send, sums = middle_back(
        info, back, back_far, middle, turned, att, out_full, cot, patches, blocks
    )
    out_far, grad_att = together(out_far, grad_att)
    out_turns = output_turns(info, middle, keep, out_far, turned, patches)
    out_turns = [unspread_turn(part, turn) for turn, part in enumerate(out_turns)]
    if blocks == 1:
        shape = (chips // 2, 2, PLACES * rows, width)
        out_keep = pick(out_keep.reshape(shape), core, 1)
        out_send = pick(out_send.reshape(shape), 1 - core, 1)
    grad_att, down_got = crossed([up_fold], grad_att, down_got)
    dq, dk, dv = attend_back(info, q, k, v, att, grad_att, total, seg)
    dq, dk, dv, out_send, normed, *out_turns = arrived(
        [up_fold], dq, dk, dv, out_send, normed, *out_turns
    )
    start_keep, start_send = project_back(info, dq, dk, dv, in_full)
    start_far, out_got = swap(start_send, "wide", 1), swap(out_send, "wide", 1)
    down_keep, down_send = split(info, [[down_keep, down_got]], (2, down_rows), 1)
    up_keep, up_send = split(info, [up_fold], (2, 2, 2, rows))
    start_far, out_got, up_send, down_send = together(start_far, out_got, up_send, down_send)
    up_got = swap(up_send, "narrow", 1)
    down_got = swap(down_send, "narrow", 2)
    args = [start_keep, start_far, start, grad_middle, turned, sums, bias_grad, spots, dq, dv]
    started = start_back(info, blocks, args + [out_keep, out_got], patches, spare)
    if not plane:
        out_grad = jnp.where(
            first_core,
            jnp.concatenate([out_keep, out_got]),
            jnp.concatenate([out_got, out_keep]),
        ).reshape(chips, PLACES, rows, 2, part)
        out_grad = jnp.transpose(out_grad, (0, 3, 1, 2, 4)).reshape(width, part)
        started = [started[0], jnp.concatenate([started[1], out_grad], axis=1)]
    normed, grad_blocks, *small_grads = together(normed, *started)
    small_fold = folded(small_grads, (2, PLACES, rows, SMALL + part))
    grad_first, grad_second = pick_turns(info, grad_blocks.reshape(2, block, width))
    grad_first = unspread_turn(grad_first, 0)
    in_grads = weight_grad(info, normed, [dq, dk, dv], blocks)
    up_got, down_got, *in_grads = crossed([small_fold], up_got, down_got, *in_grads)
    in_fold = folded(in_grads, (2, PLACES, rows, 3 * part))
    up_keep, up_send = split(info, [[up_keep, up_got]], (2, 2, rows), 1)
    grad_first, grad_second, up_send = crossed(
        [in_fold], *arrived([small_fold], grad_first, grad_second, up_send)
    )
    grad_second = unspread_turn(grad_second, 1)
    up_got = swap(up_send, "narrow", 2)
    (down_keep,) = arrived([in_fold], down_keep)
    in_cut = split(info, [in_fold, small_fold], (2, PLACES, rows))
    in_got = [swap(in_cut[index], "narrow", index) for index in range(1, PLACES)]
    in_keep, down_keep, up_keep, up_got, grad_first, grad_second, *out_turns = together(
        in_cut[0], down_keep, up_keep, up_got, grad_first, grad_second, *out_turns
    )
    outputs = unspread_join(out_turns, place)
    grad_tokens = unspread_join([grad_first, grad_second], place)
    down_share = down_keep + down_got.astype(f32)
    up_total = up_keep + up_got.astype(f32)
    up_keep = pick(up_total, core)
    up_got = swap(pick(up_total, 1 - core).astype(bf16), "wide", 1).astype(f32)
    up_both = [up_keep.reshape(rows, chips, 1, -1), up_got.reshape(rows, chips, 1, -1)]
    up_share = jnp.where(
        first_core, jnp.concatenate(up_both, axis=2), jnp.concatenate(up_both[::-1], axis=2)
    ).reshape(rows, hidden)
    outputs, grad_tokens, down_share, up_share, *in_got = together(
        outputs, grad_tokens, down_share, up_share, *in_got
    )
    in_total = in_keep
    for array in in_got:
        in_total = in_total + array.astype(f32)
    sent_columns = 3 * part + SMALL
    in_keep = pick(in_total, core)
    in_far = pick(in_total, 1 - core)[:, :sent_columns].astype(bf16)
    in_far = swap(in_far, "wide", 1).astype(f32)
    in_both = [in_keep[:, : 3 * part].reshape(rows, 3, 1, part), in_far[:, : 3 * part].reshape(rows, 3, 1, part)]
    in_share = jnp.where(
        first_core, jnp.concatenate(in_both, axis=2), jnp.concatenate(in_both[::-1], axis=2)
    ).reshape(rows, 3 * width)
    small_share = in_keep[:, 3 * part : sent_columns] + in_far[:, 3 * part :]
    out_share = jnp.concatenate([in_total[0, :, sent_columns:], in_total[1, :, sent_columns:]], axis=1)
    tail = [small_share[:, patches + i] for i in range(8)]
    return (
        outputs,
        grad_tokens,
        small_share[:, :patches],
        in_share,
        tail[QUERY_BIAS],
        tail[VALUE_BIAS],
        out_share,
        tail[OUTPUT_BIAS],
        tail[GAIN_ONE],
        tail[SHIFT_ONE],
        up_share,
        small_share[:, patches + 8 : patches + 8 + spare].T.reshape(-1),
        down_share,
        tail[DOWN_BIAS],
        tail[GAIN_TWO],
        tail[SHIFT_TWO],
    )


def solution(mesh):
    both = ("wide", "narrow")
    matrix = P(both, None)
    vector = P(both)
    block = P("wide", "narrow", None)
    gains = [matrix, matrix] + [vector] * 2 + [matrix] + [vector] * 3 + [matrix, vector, matrix]
    gains += [vector] * 3
    return jax.shard_map(
        local,
        mesh=mesh,
        in_specs=tuple([block, P("wide", "narrow"), P("wide", None)] + gains + [block]),
        out_specs=tuple([block, block] + gains),
        check_vma=False,
    )
```
